32 devices in a mesh: dp: 8 (over z, x), tensor: 4 (over y, core).
Axes of the slice: x: 2, y: 2, z: 4, core: 2. Of those that a mesh axis runs over, the one named last changes fastest.
Arguments:
- inputs: bfloat16 [8, 1024, 1024], P('dp', 'tensor'), may hold values from -16 to 16
- cotangent: bfloat16 [8, 1024, 1024], P('dp', 'tensor'), may hold values from -6 to 6
- lengths: int32 [8], P('dp'), may hold values from 256 to 1024, as said below
- gain_attn: float32 [1024], replicated, may hold values from 0.5 to 1.5
- w_query: bfloat16 [1024, 1024], P(None, 'tensor'), may hold values from -0.1875 to 0.1875
- w_key: bfloat16 [1024, 1024], P(None, 'tensor'), may hold values from -0.1875 to 0.1875
- w_value: bfloat16 [1024, 1024], P(None, 'tensor'), may hold values from -0.1875 to 0.1875
- w_out: bfloat16 [1024, 1024], P('tensor'), may hold values from -0.75 to 0.75
- persist_keys: bfloat16 [8, 16, 128], P('tensor'), may hold values from -5 to 5
- persist_values: bfloat16 [8, 16, 128], P('tensor'), may hold values from -5 to 5
- gain_ffn: float32 [1024], replicated, may hold values from 0.5 to 1.5
- w_gate: bfloat16 [1024, 2816], P(None, 'tensor'), may hold values from -0.1875 to 0.1875
- w_up: bfloat16 [1024, 2816], P(None, 'tensor'), may hold values from -0.1875 to 0.1875
- w_down: bfloat16 [2816, 1024], P('tensor'), may hold values from -0.109375 to 0.109375
- momentum: float32 [8, 16, 8], P('dp', None, 'tensor'), may hold values from 0.5 to 0.95
- decay: float32 [8, 16, 8], P('dp', None, 'tensor'), may hold values from 0 to 0.5
- step_size: float32 [8, 16, 8], P('dp', None, 'tensor'), may hold values from 0.02 to 0.2
Outputs:
- output: bfloat16 [8, 1024, 1024], P('dp', 'tensor')
- input_grad: bfloat16 [8, 1024, 1024], P('dp', 'tensor')
- grad_gain_attn: float32 [1024], replicated
- grad_query: float32 [1024, 1024], P(None, 'tensor')
- grad_key: float32 [1024, 1024], P(None, 'tensor')
- grad_value: float32 [1024, 1024], P(None, 'tensor')
- grad_out: float32 [1024, 1024], P('tensor')
- grad_persist_keys: float32 [8, 16, 128], P('tensor')
- grad_persist_values: float32 [8, 16, 128], P('tensor')
- grad_gain_ffn: float32 [1024], replicated
- grad_gate: float32 [1024, 2816], P(None, 'tensor')
- grad_up: float32 [1024, 2816], P(None, 'tensor')
- grad_down: float32 [2816, 1024], P('tensor')
- rms_stats: float32 [5], replicated
The draws below stay inside these ranges and needn't reach their ends.
Inputs may be any that keep to these rules, and one draw needn't show every extreme that they name: `lengths`: each sequence's count of valid slots; in every draw one sequence fills all 1024 slots.
All inputs are finite; a program needn't handle non-finite values.
Results may differ from the reference program's by a relative error of at most 0.017.
Values may be sent and summed in bfloat16 or wider, within the bound.
A program may use at most 128 MiB of HBM per device.

```python
import math
import jax
import jax.numpy as jnp
from jax import lax

HEAD_COUNT = 8
HS = 128
D = 1024
FF = 2816
NP = 16
L = 1024
SEQUENCE_COUNT = 8
MEMORY_BLOCKS = 16


def draw_inputs(key, part):
    key = jax.random.fold_in(key, 11)
    noise_key, level_key = jax.random.split(key)
    rank = jnp.arange(SEQUENCE_COUNT, dtype=jnp.float32) / max(SEQUENCE_COUNT - 1, 1)
    jitter = jax.random.uniform(level_key, (SEQUENCE_COUNT,), jnp.float32, -0.15, 0.15)
    values = jax.random.normal(noise_key, (SEQUENCE_COUNT, L, D), jnp.float32)
    level = 0.6 * 3.0 ** rank * jnp.exp(jitter)
    return (values * level[:, None, None]).astype(jnp.bfloat16)


def draw_lengths(key, part):
    key = jax.random.fold_in(key, 23)
    span_key, pick_key = jax.random.split(key)
    drawn = jax.random.randint(span_key, (SEQUENCE_COUNT,), L // 4, L + 1, dtype=jnp.int32)
    chosen = jax.random.randint(pick_key, (), 0, SEQUENCE_COUNT, dtype=jnp.int32)
    return jnp.where(jnp.arange(SEQUENCE_COUNT, dtype=jnp.int32) == chosen, L, drawn).astype(jnp.int32)


def draw_decay(key, part):
    key = jax.random.fold_in(key, 37)
    seed_key, perturb_key, spike_key = jax.random.split(key, 3)
    lowest, highest_rate = (0.001, 0.3)
    base = jnp.exp(jax.random.uniform(seed_key, (SEQUENCE_COUNT, 1, HEAD_COUNT), jnp.float32, math.log(lowest), math.log(highest_rate)))
    jitter = jax.random.uniform(perturb_key, (SEQUENCE_COUNT, MEMORY_BLOCKS, HEAD_COUNT), jnp.float32, 0.5, 1.5)
    spike_sample = jax.random.uniform(spike_key, (SEQUENCE_COUNT, MEMORY_BLOCKS, HEAD_COUNT), jnp.float32)
    spike_rate = base * jitter
    return jnp.where(spike_sample < 0.08, jnp.maximum(spike_rate, 0.35), spike_rate).astype(jnp.float32)


def levels(stream_key, extent, shards, least, top_value):
    def one(dim, shards_of):
        draws = jax.random.uniform(jax.random.fold_in(jax.random.fold_in(stream_key, 6), dim), (shards_of,), jnp.float32, least / len(shards), top_value / len(shards))
        return jnp.repeat(jnp.exp(draws), extent[dim] // shards_of).reshape((-1,) + (1,) * (len(extent) - dim - 1))

    level = one(*shards[0])
    for cut in shards[1:]:
        level = level * one(*cut)
    return level


def normal_values(key, dims, deviation, bound, cuts=(), held_as=jnp.bfloat16):
    values = jax.random.normal(key, dims, jnp.float32) * deviation
    if len(cuts) > 0:
        values = levels(key, dims, cuts, -0.22, 0.18) * values
    return jnp.clip(values, min=-bound, max=bound).astype(held_as)


def setup_inputs(seed: int = 0) -> dict:
    key_list = jax.random.split(jax.random.key(seed), 18)
    return {
        "inputs": draw_inputs(jax.random.fold_in(key_list[17], 71), 0),
        "cotangent": normal_values(key_list[1], (SEQUENCE_COUNT, L, D), 1.0, 6.0, ((0, 8), (1, 4))),
        "lengths": draw_lengths(jax.random.fold_in(key_list[17], 71), 0),
        "gain_attn": jnp.clip(1.0 + 0.1 * jax.random.normal(key_list[3], (D,), jnp.float32), 0.5, 1.5),
        "w_query": normal_values(key_list[4], (D, D), D ** -0.5, 0.1875, ((1, 4),)),
        "w_key": normal_values(key_list[5], (D, D), D ** -0.5, 0.1875, ((1, 4),)),
        "w_value": normal_values(key_list[6], (D, D), D ** -0.5, 0.1875, ((1, 4),)),
        "w_out": normal_values(key_list[7], (D, D), (D // 16) ** -0.5, 0.75, ((0, 4),)),
        "persist_keys": normal_values(key_list[8], (HEAD_COUNT, NP, HS), 1.0, 5.0, ((0, 4),)),
        "persist_values": normal_values(key_list[9], (HEAD_COUNT, NP, HS), 1.0, 5.0, ((0, 4),)),
        "gain_ffn": jnp.clip(1.0 + 0.1 * jax.random.normal(key_list[10], (D,), jnp.float32), 0.5, 1.5),
        "w_gate": normal_values(key_list[11], (D, FF), D ** -0.5, 0.1875, ((1, 4),)),
        "w_up": normal_values(key_list[12], (D, FF), D ** -0.5, 0.1875, ((1, 4),)),
        "w_down": normal_values(key_list[13], (FF, D), FF ** -0.5, 0.109375, ((0, 4),)),
        "momentum": jnp.clip(0.5 + 0.45 * jax.random.uniform(key_list[14], (SEQUENCE_COUNT, MEMORY_BLOCKS, HEAD_COUNT), jnp.float32) ** levels(key_list[14], (SEQUENCE_COUNT, MEMORY_BLOCKS, HEAD_COUNT), ((0, 8), (2, 4)), -0.2, 0.2), 0.5, 0.95),
        "decay": draw_decay(jax.random.fold_in(key_list[17], 71), 0),
        "step_size": jnp.clip(jnp.exp(math.log(0.2) - 2.3025851 * jax.random.uniform(key_list[16], (SEQUENCE_COUNT, MEMORY_BLOCKS, HEAD_COUNT), jnp.float32) ** levels(key_list[16], (SEQUENCE_COUNT, MEMORY_BLOCKS, HEAD_COUNT), ((0, 8), (2, 4)), -0.2, 0.2)), 0.02, 0.2),
    }


norm_eps = 1e-05
unit_eps = 1e-06
highest = lax.Precision.HIGHEST

@jax.custom_vjp
def low(v):
    return lax.optimization_barrier(v.astype(jnp.bfloat16)).astype(jnp.float32)

@jax.custom_vjp
def low_back(v):
    return v

def low_keep(v):
    return (low(v), None)

def low_pass(kept, grad):
    return (grad,)

def back_keep(v):
    return (v, None)

def back_low(kept, grad):
    return (low(grad),)
low.defvjp(low_keep, low_pass)
low_back.defvjp(back_keep, back_low)

def product(left, right):
    return jnp.dot(left, right, precision=highest, preferred_element_type=jnp.float32)

def rms_norm(value, gain):
    return value * lax.rsqrt(lax.optimization_barrier(jnp.mean(value * value, axis=-1, keepdims=True)) + norm_eps) * gain

def visible(first, count, keys_total, persistent):
    query_pos = first + jnp.arange(count, dtype=jnp.int32)
    key_pos = jnp.arange(keys_total, dtype=jnp.int32) - persistent
    return key_pos[None, :] <= query_pos[:, None]

def recall(queries, keys, values, valid, momentum, decay, step_size):
    heads, seq_len, size = queries.shape
    blocks = momentum.shape[0]
    width = seq_len // blocks
    query_unit = queries * lax.rsqrt(lax.optimization_barrier(jnp.sum(queries * queries, axis=-1, keepdims=True)) + unit_eps)
    key_unit = keys * lax.rsqrt(lax.optimization_barrier(jnp.sum(keys * keys, axis=-1, keepdims=True)) + unit_eps)

    def split_parts(value):
        return value.reshape(heads, blocks, width, size).transpose(1, 0, 2, 3)

    def advance(carry, pieces):
        memory, velocity = carry
        query_blk, key_blk, value_blk, valid_blk, persist, forget, spike_rate = pieces
        reads = jnp.einsum('hcd,hde->hce', query_blk, memory, precision=highest)
        error = (jnp.einsum('hcd,hde->hce', key_blk, memory, precision=highest) - value_blk) * valid_blk[None, :, None]
        gradient = jnp.einsum('hcd,hce->hde', key_blk, error, precision=highest)
        velocity = persist[:, None, None] * velocity - spike_rate[:, None, None] * gradient
        memory = (1.0 - forget)[:, None, None] * memory + velocity
        return ((memory, velocity), reads)
    zero = jnp.zeros((heads, size, size), jnp.float32)
    carried, reads = lax.scan(jax.checkpoint(advance), (zero, zero), (split_parts(query_unit), split_parts(key_unit), split_parts(values), valid.reshape(blocks, width), momentum, decay, step_size))
    return reads.transpose(1, 0, 2, 3).reshape(heads, seq_len, size)

def attend(query_heads, keys_all, values_all):
    block = min(512, L)

    def one_block(first):
        rows_q = lax.dynamic_slice_in_dim(query_heads, first, block, 1)
        scores = low_back(jnp.einsum('hqd,hkd->hqk', rows_q, keys_all, precision=highest) * HS ** (-0.5))
        scores = jnp.where(visible(first, block, L + NP, NP)[None], scores, -1e+30)
        probs = low(jax.nn.softmax(scores, axis=-1))
        return jnp.einsum('hqk,hkd->hqd', probs, values_all, precision=highest)
    starts = jnp.arange(L // block, dtype=jnp.int32) * block
    blocks_out = lax.map(jax.checkpoint(one_block), starts)
    return blocks_out.transpose(1, 0, 2, 3).reshape(HEAD_COUNT, L, HS)

def layer(resid, gain_attn, w_query, w_key, w_value, w_out, persist_keys, persist_values, gain_ffn, w_gate, w_up, w_down, valid, momentum, decay, step_size):

    def to_heads(value):
        return value.reshape(L, HEAD_COUNT, HS).transpose(1, 0, 2)
    normed_attn = low(rms_norm(resid, gain_attn))
    query = low(low_back(product(normed_attn, w_query)))
    key = low(low_back(product(normed_attn, w_key)))
    value = low(low_back(product(normed_attn, w_value)))
    query_heads = to_heads(query)
    key_heads = to_heads(key)
    value_heads = to_heads(value)
    keys_all = jnp.concatenate([persist_keys, key_heads], axis=1)
    values_all = jnp.concatenate([persist_values, value_heads], axis=1)
    attended = attend(query_heads, keys_all, values_all)
    reads = recall(query_heads, key_heads, value_heads, valid, momentum, decay, step_size)
    mixed = low(low_back(attended + reads)).transpose(1, 0, 2).reshape(L, D)
    branch_attn = low_back(product(mixed, w_out))
    middle = resid + branch_attn
    normed_ffn = low(rms_norm(middle, gain_ffn))
    gate = low_back(product(normed_ffn, w_gate))
    up = low_back(product(normed_ffn, w_up))
    hidden = low(jax.nn.silu(gate) * up)
    branch_ffn = low_back(product(hidden, w_down))
    result = middle + branch_ffn
    return (result, (middle, branch_attn, branch_ffn))

def reference(inputs, cotangent, lengths, gain_attn, w_query, w_key, w_value, w_out, persist_keys, persist_values, gain_ffn, w_gate, w_up, w_down, momentum, decay, step_size):
    weights = tuple((weight.astype(jnp.float32) for weight in (gain_attn, w_query, w_key, w_value, w_out, persist_keys, persist_values, gain_ffn, w_gate, w_up, w_down)))

    def one_sequence(carry, sliced):
        totals, squares, counted = carry
        resid_in, upstream, length, persist, forget, spike_rate = sliced
        resid = resid_in.astype(jnp.float32)
        valid = (jnp.arange(L, dtype=jnp.int32) < length).astype(jnp.float32)

        def forward(resid_arg, *params):
            return layer(resid_arg, *params, valid, persist, forget, spike_rate)
        result, back, extras = jax.vjp(forward, resid, *weights, has_aux=True)
        middle, branch_attn, branch_ffn = extras
        grads = back(upstream.astype(jnp.float32) * valid[:, None])
        totals = tuple((total + grad for total, grad in zip(totals, grads[1:])))

        def masked(value):
            return jnp.sum(valid[:, None] * (value * value))
        squares = squares + jnp.stack([masked(resid), masked(middle), masked(result), masked(branch_attn), masked(branch_ffn)])
        counted = counted + jnp.sum(valid)
        return ((totals, squares, counted), (result.astype(jnp.bfloat16), grads[0].astype(jnp.bfloat16)))
    start = (tuple((jnp.zeros_like(weight) for weight in weights)), jnp.zeros((5,), jnp.float32), jnp.zeros((), jnp.float32))
    finals, stacked = lax.scan(one_sequence, start, (inputs, cotangent, lengths, momentum, decay, step_size))
    totals, squares, counted = finals
    rms_stats = jnp.sqrt(squares / (counted * D))
    return (stacked[0], stacked[1], totals[0], totals[1], totals[2], totals[3], totals[4], totals[5], totals[6], totals[7], totals[8], totals[9], totals[10], rms_stats)
```

```python
import functools
import jax
import jax.numpy as jnp
from jax import lax
from jax.sharding import PartitionSpec as P
import jax.experimental.pallas as pl
import jax.experimental.pallas.tpu as pltpu

norm_eps = 1e-05
unit_eps = 1e-06
f32 = jnp.float32
bf16 = jnp.bfloat16
log2_e = 1.4426950408889634


def dot_nn(left, right):
    return lax.dot_general(left, right, (((1,), (0,)), ((), ())), preferred_element_type=f32)


def dot_nt(left, right):
    return lax.dot_general(left, right, (((1,), (1,)), ((), ())), preferred_element_type=f32)


def dot_tn(left, right):
    return lax.dot_general(left, right, (((0,), (0,)), ((), ())), preferred_element_type=f32)


def halves(value):
    high = value.astype(bf16)
    return high, (value - high.astype(f32)).astype(bf16)


def dot3(dot, left, right):
    (lh, ll), (rh, rl) = left, right
    return dot(lh, rh) + dot(ll, rh) + dot(lh, rl)


def unit_rows(value):
    wide = value.astype(f32)
    scale = lax.rsqrt(jnp.sum(wide * wide, axis=-1, keepdims=True) + unit_eps)
    return wide * scale, scale


def block_rows(start, width):
    return pl.ds(pl.multiple_of(start, width), width)


def forward_kernel(
    heads, blocks, parts,
    place, length, momentum, decay, step_size, qkv, persist_k, persist_v,
    mixed, log_total, states, grams,
    ordered, reads,
):
    seq_len, wide = qkv.shape
    size = persist_k.shape[2]
    cols = heads * size
    rows = seq_len // parts
    width = seq_len // blocks
    me = place[0]
    count = length[0]
    for b in range(parts):
        ordered[b * rows:(b + 1) * rows, :] = qkv[block_rows(jnp.bitwise_xor(me, b) * rows, rows), :]

    carried = [(jnp.zeros((size, size), f32), jnp.zeros((size, size), f32)) for _ in range(heads)]
    for c in range(blocks):
        span = slice(c * width, (c + 1) * width)
        live = (c * width + lax.broadcasted_iota(jnp.int32, (width, 1), 0) < count).astype(f32)
        for h in range(heads):
            col = h * size
            key_unit, _ = unit_rows(ordered[span, cols + col:cols + col + size])
            query_unit, _ = unit_rows(ordered[span, col:col + size])
            value = ordered[span, 2 * cols + col:2 * cols + col + size]
            key_h, key_l = halves(key_unit)
            live_h, live_l = halves(key_unit * live)
            gram = dot3(dot_tn, (live_h, live_l), (key_h, key_l))
            target = dot_tn(value, live_h) + dot_tn(value, live_l)
            memory, velocity = carried[h]
            states[h, c] = memory
            grams[h, c] = gram
            parts_m = halves(memory)
            reads[span, col:col + size] = dot_nt(query_unit.astype(bf16), parts_m[0])
            change = dot3(dot_nn, parts_m, halves(gram)) - target
            velocity = momentum[c, h] * velocity - step_size[c, h] * change
            memory = (1.0 - decay[c, h]) * memory + velocity
            carried[h] = (memory, velocity)

    factor = size ** (-0.5) * log2_e
    diagonal = lax.broadcasted_iota(jnp.int32, (rows, rows), 0) <= lax.broadcasted_iota(jnp.int32, (rows, rows), 1)
    for h in range(heads):
        col = h * size
        value_t = ordered[:, 2 * cols + col:2 * cols + col + size].T
        persist_t = persist_v[h].astype(f32).T.astype(bf16)
        for i in range(parts):
            span = slice(i * rows, (i + 1) * rows)
            seen = (i + 1) * rows
            query = ordered[span, col:col + size]
            scores = dot_nt(ordered[:seen, cols + col:cols + col + size], query)
            last = jnp.where(diagonal, scores[seen - rows:], -1e30)
            scores = last if i == 0 else jnp.concatenate([scores[:seen - rows], last], axis=0)
            extra = dot_nt(persist_k[h], query)
            top = jnp.maximum(jnp.max(scores, axis=0, keepdims=True), jnp.max(extra, axis=0, keepdims=True))
            lifted = jnp.exp2((scores - top) * factor)
            lifted_extra = jnp.exp2((extra - top) * factor)
            total = jnp.sum(lifted, axis=0, keepdims=True) + jnp.sum(lifted_extra, axis=0, keepdims=True)
            attended = dot_nn(value_t[:, :seen], lifted.astype(bf16)) + dot_nn(persist_t, lifted_extra.astype(bf16))
            attended = attended * (1.0 / total)
            log_total[h:h + 1, span] = top * factor + jnp.log2(total)
            together = attended.T + reads[span, col:col + size]
            mixed[block_rows(jnp.bitwise_xor(me, i) * rows, rows), col:col + size] = together.astype(bf16)


def backward_kernel(
    heads, blocks, parts,
    place, length, momentum, decay, step_size, qkv, mixed_grad, persist_k, persist_v,
    log_total, states, grams,
    qkv_grad, persist_k_grad, persist_v_grad,
    ordered, upstream, slopes, key_sum, value_sum, query_sum,
):
    seq_len, wide = qkv.shape
    size = persist_k.shape[2]
    cols = heads * size
    rows = seq_len // parts
    width = seq_len // blocks
    me = place[0]
    count = length[0]
    for b in range(parts):
        source = block_rows(jnp.bitwise_xor(me, b) * rows, rows)
        ordered[b * rows:(b + 1) * rows, :] = qkv[source, :]
        upstream[b * rows:(b + 1) * rows, :] = mixed_grad[source, :]

    carried = [(jnp.zeros((size, size), f32), jnp.zeros((size, size), f32)) for _ in range(heads)]
    for c in reversed(range(blocks)):
        span = slice(c * width, (c + 1) * width)
        for h in range(heads):
            col = h * size
            query_unit, _ = unit_rows(ordered[span, col:col + size])
            query_h, query_l = halves(query_unit)
            rise = upstream[span, col:col + size]
            entry = dot_tn(rise, query_h) + dot_tn(rise, query_l)
            memory, velocity = carried[h]
            velocity = velocity + memory
            change = (-step_size[c, h]) * velocity
            slopes[h, c] = change
            memory = (1.0 - decay[c, h]) * memory + entry + dot3(dot_nn, halves(change), halves(grams[h, c]))
            velocity = momentum[c, h] * velocity
            carried[h] = (memory, velocity)

    for h in range(heads):
        col = h * size
        for c in range(blocks):
            span = slice(c * width, (c + 1) * width)
            live = (c * width + lax.broadcasted_iota(jnp.int32, (width, 1), 0) < count).astype(f32)
            query_unit, query_scale = unit_rows(ordered[span, col:col + size])
            key_unit, key_scale = unit_rows(ordered[span, cols + col:cols + col + size])
            value = ordered[span, 2 * cols + col:2 * cols + col + size].astype(f32)
            rise = upstream[span, col:col + size]
            state = states[h, c].astype(bf16)
            slope = slopes[h, c].astype(bf16)
            key_b = key_unit.astype(bf16)
            error = (dot_nt(key_b, state) - value) * live
            error_grad = dot_nt(key_b, slope) * live
            unit_grad = dot_nn(error.astype(bf16), slope) + dot_nn(error_grad.astype(bf16), state)
            key_sum[span, :] = key_scale * (unit_grad - key_unit * jnp.sum(unit_grad * key_unit, axis=-1, keepdims=True))
            value_sum[span, :] = -error_grad
            read_grad = dot_nn(rise, state)
            query_sum[span, :] = query_scale * (read_grad - query_unit * jnp.sum(read_grad * query_unit, axis=-1, keepdims=True))

        factor = size ** (-0.5)
        diagonal = lax.broadcasted_iota(jnp.int32, (rows, rows), 0) <= lax.broadcasted_iota(jnp.int32, (rows, rows), 1)
        key_t = ordered[:, cols + col:cols + col + size].T
        persist_t = persist_k[h].astype(f32).T.astype(bf16)
        persist_k_total = jnp.zeros(persist_k.shape[1:], f32)
        persist_v_total = jnp.zeros(persist_k.shape[1:], f32)
        for i in range(parts):
            span = slice(i * rows, (i + 1) * rows)
            seen = (i + 1) * rows
            query = ordered[span, col:col + size]
            rise = upstream[span, col:col + size]
            scores = dot_nt(ordered[:seen, cols + col:cols + col + size], query)
            last = jnp.where(diagonal, scores[seen - rows:], -1e30)
            scores = last if i == 0 else jnp.concatenate([scores[:seen - rows], last], axis=0)
            extra = dot_nt(persist_k[h], query)
            base = log_total[h:h + 1, span]
            probs = jnp.exp2(scores * (factor * log2_e) - base)
            probs_extra = jnp.exp2(extra * (factor * log2_e) - base)
            probs_grad = dot_nt(ordered[:seen, 2 * cols + col:2 * cols + col + size], rise)
            extra_grad = dot_nt(persist_v[h], rise)
            weighted = probs * probs_grad
            weighted_extra = probs_extra * extra_grad
            inner = jnp.sum(weighted, axis=0, keepdims=True) + jnp.sum(weighted_extra, axis=0, keepdims=True)
            scores_grad = (weighted - probs * inner).astype(bf16)
            scores_extra = (weighted_extra - probs_extra * inner).astype(bf16)
            query_t = dot_nn(key_t[:, :seen], scores_grad) + dot_nn(persist_t, scores_extra)
            query_sum[span, :] += query_t.T * factor
            key_sum[:seen, :] += dot_nn(scores_grad, query) * factor
            value_sum[:seen, :] += dot_nn(probs.astype(bf16), rise)
            persist_k_total += dot_nn(scores_extra, query) * factor
            persist_v_total += dot_nn(probs_extra.astype(bf16), rise)
        persist_k_grad[h] = persist_k_total
        persist_v_grad[h] = persist_v_total
        for b in range(parts):
            span = slice(b * rows, (b + 1) * rows)
            target = block_rows(jnp.bitwise_xor(me, b) * rows, rows)
            qkv_grad[target, col:col + size] = query_sum[span, :].astype(bf16)
            qkv_grad[target, cols + col:cols + col + size] = key_sum[span, :].astype(bf16)
            qkv_grad[target, 2 * cols + col:2 * cols + col + size] = value_sum[span, :].astype(bf16)


vmem = functools.partial(pl.BlockSpec, memory_space=pltpu.VMEM)
smem = functools.partial(pl.BlockSpec, memory_space=pltpu.SMEM)
vmem_limit = 56 << 20


def attend_and_recall(place, length, momentum, decay, step_size, qkv, persist_k, persist_v, parts):
    heads, _, size = persist_k.shape
    seq_len = qkv.shape[0]
    blocks = momentum.shape[0]
    cols = heads * size
    return pl.pallas_call(
        functools.partial(forward_kernel, heads, blocks, parts),
        out_shape=(
            jax.ShapeDtypeStruct((seq_len, cols), bf16),
            jax.ShapeDtypeStruct((heads, seq_len), f32),
            jax.ShapeDtypeStruct((heads, blocks, size, size), f32),
            jax.ShapeDtypeStruct((heads, blocks, size, size), f32),
        ),
        in_specs=[smem()] * 5 + [vmem()] * 3,
        out_specs=(vmem(),) * 4,
        scratch_shapes=[pltpu.VMEM((seq_len, 3 * cols), bf16), pltpu.VMEM((seq_len, cols), f32)],
        compiler_params=pltpu.CompilerParams(vmem_limit_bytes=vmem_limit),
        cost_estimate=pl.CostEstimate(flops=12_000_000_000, bytes_accessed=8_000_000, transcendentals=2_000_000),
        name="attend_recall",
    )(place, length, momentum, decay, step_size, qkv, persist_k, persist_v)


def attend_and_recall_back(
    place, length, momentum, decay, step_size, qkv, mixed_grad, persist_k, persist_v, log_total, states, grams, parts
):
    heads, persistent, size = persist_k.shape
    seq_len = qkv.shape[0]
    blocks = momentum.shape[0]
    cols = heads * size
    return pl.pallas_call(
        functools.partial(backward_kernel, heads, blocks, parts),
        out_shape=(
            jax.ShapeDtypeStruct((seq_len, 3 * cols), bf16),
            jax.ShapeDtypeStruct((heads, persistent, size), f32),
            jax.ShapeDtypeStruct((heads, persistent, size), f32),
        ),
        in_specs=[smem()] * 5 + [vmem()] * 7,
        out_specs=(vmem(),) * 3,
        scratch_shapes=[
            pltpu.VMEM((seq_len, 3 * cols), bf16),
            pltpu.VMEM((seq_len, cols), bf16),
            pltpu.VMEM((heads, blocks, size, size), f32),
            pltpu.VMEM((seq_len, size), f32),
            pltpu.VMEM((seq_len, size), f32),
            pltpu.VMEM((seq_len, size), f32),
        ],
        compiler_params=pltpu.CompilerParams(vmem_limit_bytes=vmem_limit),
        cost_estimate=pl.CostEstimate(flops=25_000_000_000, bytes_accessed=12_000_000, transcendentals=2_000_000),
        name="attend_recall_back",
    )(place, length, momentum, decay, step_size, qkv, mixed_grad, persist_k, persist_v, log_total, states, grams)


def swap(value, axis, bit):
    count = lax.axis_size(axis)
    return lax.ppermute(value, axis, [(i, i ^ bit) for i in range(count)])


def norm_scale(value):
    return lax.rsqrt(jnp.mean(value * value, axis=-1, keepdims=True) + norm_eps)


def norm_back(value, scale, gain, upstream):
    weighted = upstream * gain
    return scale * weighted - value * (scale * scale * scale) * jnp.mean(
        weighted * value, axis=-1, keepdims=True
    )


def gather_rows(own):
    far = swap(own, "tensor", 2)
    near = swap(own, "tensor", 1)
    both = swap(far, "tensor", 1)
    return jnp.concatenate([own, near], 0), jnp.concatenate([far, both], 0)


def scatter_rows(near, far):
    rows = near.shape[0] // 2
    far_sum = far[:rows] + swap(far[rows:].astype(bf16), "tensor", 1).astype(f32)
    far_in = swap(far_sum.astype(bf16), "tensor", 2).astype(f32)
    near_in = swap(near[rows:].astype(bf16), "tensor", 1).astype(f32)
    return near[:rows] + near_in + far_in


def sum_everywhere(value):
    for axis in ("tensor", "dp"):
        count = lax.axis_size(axis)
        if count & (count - 1):
            value = lax.psum(value, axis)
        else:
            bit = 1
            while bit < count:
                value = value + swap(value, axis, bit)
                bit *= 2
    return value


def body(
    inputs, cotangent, lengths, gain_attn, w_query, w_key, w_value, w_out, persist_keys, persist_values,
    gain_ffn, w_gate, w_up, w_down, momentum, decay, step_size,
):
    parts = lax.axis_size("tensor")
    rows = inputs.shape[1]
    width = inputs.shape[2]
    half = 2 * rows
    cols = w_query.shape[1]
    place = lax.axis_index("tensor")
    first_row = place * rows
    own_valid = (first_row + jnp.arange(rows, dtype=jnp.int32) < lengths[0]).astype(f32)[:, None]
    places = place.astype(jnp.int32).reshape(1)
    rates = (places, lengths, momentum[0], decay[0], step_size[0])

    def mul(left, right):
        return jnp.dot(left, right, preferred_element_type=f32)

    def mul_nt(left, right):
        return jnp.einsum("ab,cb->ac", left, right, preferred_element_type=f32)

    def mul_tn(left, right):
        return jnp.einsum("ab,ac->bc", left, right, preferred_element_type=f32)

    resid = inputs[0].astype(f32)
    scale_attn = norm_scale(resid)
    near, far = gather_rows((resid * scale_attn * gain_attn).astype(bf16))
    w_qkv = jnp.concatenate([w_query, w_key, w_value], 1)
    qkv = jnp.concatenate([mul(near, w_qkv).astype(bf16), mul(far, w_qkv).astype(bf16)], 0)
    normed_attn = jnp.concatenate([near, far], 0)
    mixed, log_total, states, grams = attend_and_recall(*rates, qkv, persist_keys, persist_values, parts)
    branch_attn = scatter_rows(mul(mixed[:half], w_out), mul(mixed[half:], w_out))
    middle = resid + branch_attn
    scale_ffn = norm_scale(middle)
    normed_ffn = jnp.concatenate(gather_rows((middle * scale_ffn * gain_ffn).astype(bf16)), 0)

    out_grad = cotangent[0].astype(f32) * own_valid
    out_full = jnp.concatenate(gather_rows(out_grad.astype(bf16)), 0)
    gate = mul(normed_ffn, w_gate)
    up = mul(normed_ffn, w_up)
    sigmoid = jax.nn.sigmoid(gate)
    silu = gate * sigmoid
    hidden = (silu * up).astype(bf16)
    hidden_grad = mul_nt(out_full, w_down)
    grad_down = mul_tn(hidden, out_full)
    gate_grad = (hidden_grad * up * sigmoid * (1.0 + gate * (1.0 - sigmoid))).astype(bf16)
    up_grad = (hidden_grad * silu).astype(bf16)
    grad_gate = mul_tn(normed_ffn, gate_grad)
    grad_up = mul_tn(normed_ffn, up_grad)
    normed_ffn_grad = scatter_rows(
        mul_nt(gate_grad[:half], w_gate) + mul_nt(up_grad[:half], w_up),
        mul_nt(gate_grad[half:], w_gate) + mul_nt(up_grad[half:], w_up),
    )
    ffn_sums = lax.psum((grad_gate.astype(bf16), grad_up.astype(bf16), grad_down.astype(bf16)), "dp")
    branch_ffn = scatter_rows(mul(hidden[:half], w_down), mul(hidden[half:], w_down))
    result = middle + branch_ffn

    gain_ffn_part = jnp.sum(normed_ffn_grad * middle * scale_ffn, axis=0)
    middle_grad = out_grad + norm_back(middle, scale_ffn, gain_ffn, normed_ffn_grad)
    middle_full = jnp.concatenate(gather_rows(middle_grad.astype(bf16)), 0)
    mixed_grad = mul_nt(middle_full, w_out).astype(bf16)
    grad_out = mul_tn(mixed, middle_full)
    qkv_grad, persist_k_grad, persist_v_grad = attend_and_recall_back(
        *rates, qkv, mixed_grad, persist_keys, persist_values, log_total, states, grams, parts
    )
    normed_attn_grad = scatter_rows(mul_nt(qkv_grad[:half], w_qkv), mul_nt(qkv_grad[half:], w_qkv))
    grad_qkv = mul_tn(normed_attn, qkv_grad)
    attn_sums = lax.psum(
        (grad_qkv.astype(bf16), grad_out.astype(bf16), persist_k_grad.astype(bf16), persist_v_grad.astype(bf16)), "dp"
    )
    gain_attn_part = jnp.sum(normed_attn_grad * resid * scale_attn, axis=0)
    input_grad = middle_grad + norm_back(resid, scale_attn, gain_attn, normed_attn_grad)

    def masked(value_in):
        return jnp.sum(own_valid * (value_in * value_in))

    squares = jnp.stack(
        [masked(resid), masked(middle), masked(result), masked(branch_attn), masked(branch_ffn), jnp.sum(own_valid)]
    )
    packed = jnp.concatenate([gain_attn_part, gain_ffn_part, squares, jnp.zeros((122,), f32)])
    small = sum_everywhere(packed.reshape(-1, 128)).reshape(-1)
    rms_stats = jnp.sqrt(small[2 * width:2 * width + 5] / (small[2 * width + 5] * width))
    wide = attn_sums[0].astype(f32)
    return (
        result.astype(bf16)[None],
        input_grad.astype(bf16)[None],
        small[:width],
        wide[:, :cols],
        wide[:, cols:2 * cols],
        wide[:, 2 * cols:],
        attn_sums[1].astype(f32),
        attn_sums[2].astype(f32),
        attn_sums[3].astype(f32),
        small[width:2 * width],
        ffn_sums[0].astype(f32),
        ffn_sums[1].astype(f32),
        ffn_sums[2].astype(f32),
        rms_stats,
    )


def solution(mesh):
    in_specs = (
        P("dp", "tensor", None),
        P("dp", "tensor", None),
        P("dp"),
        P(),
        P(None, "tensor"),
        P(None, "tensor"),
        P(None, "tensor"),
        P("tensor", None),
        P("tensor", None, None),
        P("tensor", None, None),
        P(),
        P(None, "tensor"),
        P(None, "tensor"),
        P("tensor", None),
        P("dp", None, "tensor"),
        P("dp", None, "tensor"),
        P("dp", None, "tensor"),
    )
    out_specs = (
        P("dp", "tensor", None),
        P("dp", "tensor", None),
        P(),
        P(None, "tensor"),
        P(None, "tensor"),
        P(None, "tensor"),
        P("tensor", None),
        P("tensor", None, None),
        P("tensor", None, None),
        P(),
        P(None, "tensor"),
        P(None, "tensor"),
        P("tensor", None),
        P(),
    )
    return jax.shard_map(body, mesh=mesh, in_specs=in_specs, out_specs=out_specs, check_vma=False)
```

```python
import functools
import jax
import jax.numpy as jnp
from jax import lax
from jax.sharding import PartitionSpec as P
import jax.experimental.pallas as pl
import jax.experimental.pallas.tpu as pltpu

norm_eps = 1e-05
unit_eps = 1e-06
f32 = jnp.float32
bf16 = jnp.bfloat16
log2_e = 1.4426950408889634


def dot_nn(left, right):
    return lax.dot_general(left, right, (((1,), (0,)), ((), ())), preferred_element_type=f32)


def dot_nt(left, right):
    return lax.dot_general(left, right, (((1,), (1,)), ((), ())), preferred_element_type=f32)


def dot_tn(left, right):
    return lax.dot_general(left, right, (((0,), (0,)), ((), ())), preferred_element_type=f32)


def halves(value):
    high = value.astype(bf16)
    return high, (value - high.astype(f32)).astype(bf16)


def dot3(dot, left, right):
    (lh, ll), (rh, rl) = left, right
    return dot(lh, rh) + dot(ll, rh) + dot(lh, rl)


def unit_rows(value):
    wide = value.astype(f32)
    scale = lax.rsqrt(jnp.sum(wide * wide, axis=-1, keepdims=True) + unit_eps)
    return wide * scale, scale


def block_rows(start, width):
    return pl.ds(pl.multiple_of(start, width), width)


def forward_kernel(
    heads, blocks, parts,
    place, length, momentum, decay, step_size, qkv, persist_k, persist_v,
    mixed, log_total, states, grams,
    ordered, reads,
):
    seq_len, wide = qkv.shape
    size = persist_k.shape[2]
    cols = heads * size
    rows = seq_len // parts
    width = seq_len // blocks
    me = place[0]
    count = length[0]
    for b in range(parts):
        ordered[b * rows:(b + 1) * rows, :] = qkv[block_rows(jnp.bitwise_xor(me, b) * rows, rows), :]

    carried = [(jnp.zeros((size, size), f32), jnp.zeros((size, size), f32)) for _ in range(heads)]
    for c in range(blocks):
        span = slice(c * width, (c + 1) * width)
        live = (c * width + lax.broadcasted_iota(jnp.int32, (width, 1), 0) < count).astype(f32)
        for h in range(heads):
            col = h * size
            key_unit, _ = unit_rows(ordered[span, cols + col:cols + col + size])
            query_unit, _ = unit_rows(ordered[span, col:col + size])
            value = ordered[span, 2 * cols + col:2 * cols + col + size]
            key_h, key_l = halves(key_unit)
            live_h, live_l = halves(key_unit * live)
            gram = dot3(dot_tn, (live_h, live_l), (key_h, key_l))
            target = dot_tn(value, live_h) + dot_tn(value, live_l)
            memory, velocity = carried[h]
            states[h, c] = memory.astype(bf16)
            grams[h, c] = gram
            parts_m = halves(memory)
            reads[span, col:col + size] = dot_nt(query_unit.astype(bf16), parts_m[0])
            change = dot3(dot_nn, parts_m, halves(gram)) - target
            velocity = momentum[c, h] * velocity - step_size[c, h] * change
            memory = (1.0 - decay[c, h]) * memory + velocity
            carried[h] = (memory, velocity)

    factor = size ** (-0.5) * log2_e
    diagonal = lax.broadcasted_iota(jnp.int32, (rows, rows), 0) <= lax.broadcasted_iota(jnp.int32, (rows, rows), 1)
    for h in range(heads):
        col = h * size
        value_t = ordered[:, 2 * cols + col:2 * cols + col + size].T
        persist_t = persist_v[h].astype(f32).T.astype(bf16)
        for i in range(parts):
            span = slice(i * rows, (i + 1) * rows)
            seen = (i + 1) * rows
            query = ordered[span, col:col + size]
            scores = dot_nt(ordered[:seen, cols + col:cols + col + size], query)
            last = jnp.where(diagonal, scores[seen - rows:], -1e30)
            scores = last if i == 0 else jnp.concatenate([scores[:seen - rows], last], axis=0)
            extra = dot_nt(persist_k[h], query)
            top = jnp.maximum(jnp.max(scores, axis=0, keepdims=True), jnp.max(extra, axis=0, keepdims=True))
            lifted = jnp.exp2((scores - top) * factor)
            lifted_extra = jnp.exp2((extra - top) * factor)
            total = jnp.sum(lifted, axis=0, keepdims=True) + jnp.sum(lifted_extra, axis=0, keepdims=True)
            attended = dot_nn(value_t[:, :seen], lifted.astype(bf16)) + dot_nn(persist_t, lifted_extra.astype(bf16))
            attended = attended * (1.0 / total)
            log_total[h:h + 1, span] = top * factor + jnp.log2(total)
            together = attended.T + reads[span, col:col + size]
            mixed[block_rows(jnp.bitwise_xor(me, i) * rows, rows), col:col + size] = together.astype(bf16)


def backward_kernel(
    heads, blocks, parts,
    place, length, momentum, decay, step_size, qkv, mixed_grad, persist_k, persist_v,
    log_total, states, grams,
    qkv_grad, persist_k_grad, persist_v_grad,
    ordered, upstream, slopes, key_sum, value_sum, query_sum,
):
    seq_len, wide = qkv.shape
    size = persist_k.shape[2]
    cols = heads * size
    rows = seq_len // parts
    width = seq_len // blocks
    me = place[0]
    count = length[0]
    for b in range(parts):
        source = block_rows(jnp.bitwise_xor(me, b) * rows, rows)
        ordered[b * rows:(b + 1) * rows, :] = qkv[source, :]
        upstream[b * rows:(b + 1) * rows, :] = mixed_grad[source, :]

    carried = [(jnp.zeros((size, size), f32), jnp.zeros((size, size), f32)) for _ in range(heads)]
    for c in reversed(range(blocks)):
        span = slice(c * width, (c + 1) * width)
        for h in range(heads):
            col = h * size
            query_unit, _ = unit_rows(ordered[span, col:col + size])
            query_h, query_l = halves(query_unit)
            rise = upstream[span, col:col + size]
            entry = dot_tn(rise, query_h) + dot_tn(rise, query_l)
            memory, velocity = carried[h]
            velocity = velocity + memory
            change = (-step_size[c, h]) * velocity
            slopes[h, c] = change
            memory = (1.0 - decay[c, h]) * memory + entry + dot3(dot_nn, halves(change), halves(grams[h, c]))
            velocity = momentum[c, h] * velocity
            carried[h] = (memory, velocity)

    for h in range(heads):
        col = h * size
        for c in range(blocks):
            span = slice(c * width, (c + 1) * width)
            live = (c * width + lax.broadcasted_iota(jnp.int32, (width, 1), 0) < count).astype(f32)
            query_unit, query_scale = unit_rows(ordered[span, col:col + size])
            key_unit, key_scale = unit_rows(ordered[span, cols + col:cols + col + size])
            value = ordered[span, 2 * cols + col:2 * cols + col + size].astype(f32)
            rise = upstream[span, col:col + size]
            state = states[h, c]
            slope = slopes[h, c].astype(bf16)
            key_b = key_unit.astype(bf16)
            error = (dot_nt(key_b, state) - value) * live
            error_grad = dot_nt(key_b, slope) * live
            unit_grad = dot_nn(error.astype(bf16), slope) + dot_nn(error_grad.astype(bf16), state)
            key_sum[span, :] = key_scale * (unit_grad - key_unit * jnp.sum(unit_grad * key_unit, axis=-1, keepdims=True))
            value_sum[span, :] = -error_grad
            read_grad = dot_nn(rise, state)
            query_sum[span, :] = query_scale * (read_grad - query_unit * jnp.sum(read_grad * query_unit, axis=-1, keepdims=True))

        factor = size ** (-0.5)
        diagonal = lax.broadcasted_iota(jnp.int32, (rows, rows), 0) <= lax.broadcasted_iota(jnp.int32, (rows, rows), 1)
        key_t = ordered[:, cols + col:cols + col + size].T
        persist_t = persist_k[h].astype(f32).T.astype(bf16)
        persist_k_total = jnp.zeros(persist_k.shape[1:], f32)
        persist_v_total = jnp.zeros(persist_k.shape[1:], f32)
        for i in range(parts):
            span = slice(i * rows, (i + 1) * rows)
            seen = (i + 1) * rows
            query = ordered[span, col:col + size]
            rise = upstream[span, col:col + size]
            scores = dot_nt(ordered[:seen, cols + col:cols + col + size], query)
            last = jnp.where(diagonal, scores[seen - rows:], -1e30)
            scores = last if i == 0 else jnp.concatenate([scores[:seen - rows], last], axis=0)
            extra = dot_nt(persist_k[h], query)
            base = log_total[h:h + 1, span]
            probs = jnp.exp2(scores * (factor * log2_e) - base)
            probs_extra = jnp.exp2(extra * (factor * log2_e) - base)
            probs_grad = dot_nt(ordered[:seen, 2 * cols + col:2 * cols + col + size], rise)
            extra_grad = dot_nt(persist_v[h], rise)
            weighted = probs * probs_grad
            weighted_extra = probs_extra * extra_grad
            inner = jnp.sum(weighted, axis=0, keepdims=True) + jnp.sum(weighted_extra, axis=0, keepdims=True)
            scores_grad = (weighted - probs * inner).astype(bf16)
            scores_extra = (weighted_extra - probs_extra * inner).astype(bf16)
            query_t = dot_nn(key_t[:, :seen], scores_grad) + dot_nn(persist_t, scores_extra)
            query_sum[span, :] += query_t.T * factor
            key_sum[:seen, :] += dot_nn(scores_grad, query) * factor
            value_sum[:seen, :] += dot_nn(probs.astype(bf16), rise)
            persist_k_total += dot_nn(scores_extra, query) * factor
            persist_v_total += dot_nn(probs_extra.astype(bf16), rise)
        persist_k_grad[h] = persist_k_total
        persist_v_grad[h] = persist_v_total
        for b in range(parts):
            span = slice(b * rows, (b + 1) * rows)
            target = block_rows(jnp.bitwise_xor(me, b) * rows, rows)
            qkv_grad[target, col:col + size] = query_sum[span, :].astype(bf16)
            qkv_grad[target, cols + col:cols + col + size] = key_sum[span, :].astype(bf16)
            qkv_grad[target, 2 * cols + col:2 * cols + col + size] = value_sum[span, :].astype(bf16)


vmem = functools.partial(pl.BlockSpec, memory_space=pltpu.VMEM)
smem = functools.partial(pl.BlockSpec, memory_space=pltpu.SMEM)
vmem_limit = 56 << 20


def attend_and_recall(place, length, momentum, decay, step_size, qkv, persist_k, persist_v, parts):
    heads, _, size = persist_k.shape
    seq_len = qkv.shape[0]
    blocks = momentum.shape[0]
    cols = heads * size
    return pl.pallas_call(
        functools.partial(forward_kernel, heads, blocks, parts),
        out_shape=(
            jax.ShapeDtypeStruct((seq_len, cols), bf16),
            jax.ShapeDtypeStruct((heads, seq_len), f32),
            jax.ShapeDtypeStruct((heads, blocks, size, size), bf16),
            jax.ShapeDtypeStruct((heads, blocks, size, size), f32),
        ),
        in_specs=[smem()] * 5 + [vmem()] * 3,
        out_specs=(vmem(),) * 4,
        scratch_shapes=[pltpu.VMEM((seq_len, 3 * cols), bf16), pltpu.VMEM((seq_len, cols), f32)],
        compiler_params=pltpu.CompilerParams(vmem_limit_bytes=vmem_limit),
        cost_estimate=pl.CostEstimate(flops=12_000_000_000, bytes_accessed=8_000_000, transcendentals=2_000_000),
        name="attend_recall",
    )(place, length, momentum, decay, step_size, qkv, persist_k, persist_v)


def attend_and_recall_back(
    place, length, momentum, decay, step_size, qkv, mixed_grad, persist_k, persist_v, log_total, states, grams, parts
):
    heads, persistent, size = persist_k.shape
    seq_len = qkv.shape[0]
    blocks = momentum.shape[0]
    cols = heads * size
    return pl.pallas_call(
        functools.partial(backward_kernel, heads, blocks, parts),
        out_shape=(
            jax.ShapeDtypeStruct((seq_len, 3 * cols), bf16),
            jax.ShapeDtypeStruct((heads, persistent, size), f32),
            jax.ShapeDtypeStruct((heads, persistent, size), f32),
        ),
        in_specs=[smem()] * 5 + [vmem()] * 7,
        out_specs=(vmem(),) * 3,
        scratch_shapes=[
            pltpu.VMEM((seq_len, 3 * cols), bf16),
            pltpu.VMEM((seq_len, cols), bf16),
            pltpu.VMEM((heads, blocks, size, size), f32),
            pltpu.VMEM((seq_len, size), f32),
            pltpu.VMEM((seq_len, size), f32),
            pltpu.VMEM((seq_len, size), f32),
        ],
        compiler_params=pltpu.CompilerParams(vmem_limit_bytes=vmem_limit),
        cost_estimate=pl.CostEstimate(flops=25_000_000_000, bytes_accessed=12_000_000, transcendentals=2_000_000),
        name="attend_recall_back",
    )(place, length, momentum, decay, step_size, qkv, mixed_grad, persist_k, persist_v, log_total, states, grams)


def ring_place(index, count):
    odd = index % 2
    return (1 - odd) * (index // 2) + odd * (count - 1 - index // 2)


def ring_index(place, count):
    late = place // (count // 2)
    return (1 - late) * (2 * place) + late * (2 * (count - 1 - place) + 1)


def flip(index, bit):
    return index + bit * (1 - 2 * ((index // bit) % 2))


def bits_below(count):
    return [1 << k for k in range(count.bit_length() - 1)]


def relative(index, block):
    for bit in (1, 2):
        if block & bit:
            index = flip(index, bit)
    return index


def remote(source, target, send_sem, recv_sem, device):
    return pltpu.make_async_remote_copy(
        src_ref=source, dst_ref=target, send_sem=send_sem, recv_sem=recv_sem,
        device_id=device, device_id_type=pl.DeviceIdType.MESH,
    )


class Ring:
    def __init__(self, count, by_rows, source, out, slots, send_sem, recv_sem):
        self.count, self.by_rows = count, by_rows
        self.source, self.out, self.slots = source, out, slots
        self.send_sem, self.recv_sem = send_sem, recv_sem
        index = lax.axis_index("dp")
        self.place = ring_place(index, count)
        self.peers = (
            {"dp": ring_index((self.place + 1) % count, count)},
            {"dp": ring_index((self.place + count - 1) % count, count)},
        )
        self.step = 0
        self.copies = [None, None]

    def piece(self, ref, way, chunk):
        rows, cols = ref.shape
        chunk = chunk % self.count
        if self.by_rows:
            size = rows // (2 * self.count)
            return ref.at[pl.ds(pl.multiple_of(chunk * (2 * size) + way * size, size), size), :]
        size, width = rows // 2, cols // self.count
        return ref.at[way * size:(way + 1) * size, pl.ds(pl.multiple_of(chunk * width, width), width)]

    def chunk(self, way, step):
        return self.place + self.count + (2 * self.count - step if way == 0 else step)

    def launch(self, way, step, source, target):
        copy = remote(source, target, self.send_sem.at[way, step], self.recv_sem.at[way, step], self.peers[way])
        copy.start()
        self.copies[way] = copy

    def start(self):
        for way in range(2):
            self.launch(way, 0, self.piece(self.source, way, self.chunk(way, 0)), self.slots.at[way, 0])

    def advance(self):
        count, step = self.count, self.step
        for way in range(2):
            self.copies[way].wait_recv()
            self.copies[way].wait_send()
            if step < count - 1:
                chunk = self.chunk(way, step + 1)
                total = self.slots[way, step].astype(f32) + self.piece(self.source, way, chunk)[...].astype(f32)
                if step < count - 2:
                    self.slots[way, step] = total.astype(bf16)
                    source, target = self.slots.at[way, step], self.slots.at[way, step + 1]
                else:
                    source = target = self.piece(self.out, way, chunk)
                    source[...] = total.astype(bf16)
            else:
                source = target = self.piece(self.out, way, self.chunk(way, step + 1 - count))
            if step < 2 * count - 3:
                self.launch(way, step + 1, source, target)
        self.step += 1
        return self.step < 2 * count - 2


class SmallSum:
    def __init__(self, value, slots, shared, send_sem, recv_sem, count, parts):
        self.value, self.slots, self.shared = value, slots, shared
        self.send_sem, self.recv_sem = send_sem, recv_sem
        index, inner = lax.axis_index("dp"), lax.axis_index("tensor")
        self.inner = len(bits_below(parts))
        self.peers = [{"tensor": flip(inner, bit)} for bit in bits_below(parts)]
        self.peers += [{"dp": flip(index, bit)} for bit in bits_below(count)]
        self.step = 0

    def start(self):
        used = slice(0, self.shared if self.step < self.inner else self.value.shape[0])
        self.used = used
        self.copy = remote(
            self.value.at[used], self.slots.at[self.step, used], self.send_sem.at[self.step],
            self.recv_sem.at[self.step], self.peers[self.step],
        )
        self.copy.start()

    def advance(self):
        self.copy.wait()
        self.value[self.used] += self.slots[self.step, self.used]
        self.step += 1
        if self.step < len(self.peers):
            self.start()
        return self.step < len(self.peers)


class Rounds:
    def __init__(self):
        self.queue = []

    def add(self, *flows):
        for flow in flows:
            flow.start()
            self.queue.append(flow)

    def tick(self, count=1):
        for _ in range(count):
            if self.queue:
                flow = self.queue.pop(0)
                if flow.advance():
                    self.queue.append(flow)

    def finish(self):
        while self.queue:
            self.tick()


def rows_scale(value):
    return lax.rsqrt(jnp.mean(value * value, axis=-1, keepdims=True) + norm_eps)


def scatter_blocks(block, rows, sent, landed, send_sem, recv_sem, hold, rounds, waits):
    inner = lax.axis_index("tensor")
    sibling, across = {"tensor": flip(inner, 1)}, {"tensor": flip(inner, 2)}

    def copy(k, device):
        return remote(sent.at[k], landed.at[k], send_sem.at[k], recv_sem.at[k], device)

    sent[0] = block(3).astype(bf16)
    first = copy(0, sibling)
    first.start()
    hold[...] = block(2)
    first.wait()
    sent[1] = (hold[...] + landed[0].astype(f32)).astype(bf16)
    second = copy(1, across)
    second.start()
    rounds.tick(1)
    sent[2] = block(1).astype(bf16)
    third = copy(2, sibling)
    third.start()
    hold[...] = block(0)
    rounds.tick(waits)
    third.wait()
    second.wait()
    return hold[...] + landed[2].astype(f32) + landed[1].astype(f32)


def tail_kernel(
    heads, blocks, parts, count, shared, pace,
    length, momentum, decay, step_size,
    gain_attn, gain_ffn, squares, persist_k, persist_v, log_total,
    gate_source, up_source, down_source,
    gate_grad_h, up_grad_h, w_gate_h, w_up_h, middle_h, cotangent_h,
    w_out_h, mixed_h, qkv_h, states_h, grams_h, normed_attn_h, w_qkv_h, inputs_h,
    gate_out, up_out, down_out, wide_out, out_out, small, input_grad,
    gate_grad, up_grad, w_gate, w_up, middle, cotangent,
    w_out, mixed, ordered, states, grams, normed_attn, w_qkv, inputs,
    gate_slots, up_slots, down_slots, wide_slots, out_slots, small_slots,
    wide_source, out_source, sent_a, landed_a, sent_b, landed_b, hold, middle_grad, middle_full, upstream,
    slopes, key_sum, value_sum, query_sum, qkv_grad,
    load_sem, ring_send, ring_recv, small_send, small_recv, move_send, move_recv,
):
    size = persist_k.shape[2]
    cols = heads * size
    seq_len, width = middle_full.shape
    rows = seq_len // parts
    span_rows = seq_len // blocks
    inner = lax.axis_index("tensor")
    valid_count = length[0]
    sibling, across = {"tensor": flip(inner, 1)}, {"tensor": flip(inner, 2)}

    rounds = Rounds()
    rings = [
        Ring(count, by_rows, source, out, slots, ring_send.at[k], ring_recv.at[k])
        for k, (by_rows, source, out, slots) in enumerate((
            (False, gate_source, gate_out, gate_slots),
            (False, up_source, up_out, up_slots),
            (False, down_source, down_out, down_slots),
            (False, out_source, out_out, out_slots),
            (True, wide_source, wide_out, wide_slots),
        ))
    ]
    small_sum = SmallSum(small, small_slots, shared, small_send, small_recv, count, parts)
    barrier = pltpu.get_barrier_semaphore()
    peers = list(rings[0].peers) + small_sum.peers
    for peer in peers:
        pl.semaphore_signal(barrier, inc=1, device_id=peer, device_id_type=pl.DeviceIdType.MESH)

    loads = []

    def load(source, target):
        copy = pltpu.make_async_copy(source, target, load_sem.at[len(loads)])
        copy.start()
        loads.append(copy)
        return copy

    first_loads = [
        load(gate_grad_h, gate_grad), load(w_gate_h, w_gate), load(up_grad_h, up_grad), load(w_up_h, w_up)
    ]
    second_loads = [load(middle_h, middle), load(cotangent_h, cotangent)]
    third_loads = [load(w_out_h, w_out), load(mixed_h, mixed), load(states_h, states), load(grams_h, grams)]
    for b in range(parts):
        source = pl.ds(pl.multiple_of(relative(inner, b) * rows, rows), rows)
        third_loads.append(load(qkv_h.at[source, :], ordered.at[b * rows:(b + 1) * rows, :]))
    fourth_loads = [load(normed_attn_h, normed_attn), load(w_qkv_h, w_qkv), load(inputs_h, inputs)]

    pl.semaphore_wait(barrier, len(peers))
    rounds.add(*rings[:3])
    for copy in first_loads:
        copy.wait()

    def ffn_block(b):
        span = slice(b * rows, (b + 1) * rows)
        return dot_nt(gate_grad[span, :], w_gate[...]) + dot_nt(up_grad[span, :], w_up[...])

    normed_grad = scatter_blocks(
        ffn_block, rows, sent_a, landed_a, move_send.at[0], move_recv.at[0], hold, rounds, pace[0]
    )
    for copy in second_loads:
        copy.wait()
    row_place = inner * rows + lax.broadcasted_iota(jnp.int32, (rows, 1), 0)
    own_valid = (row_place < valid_count).astype(f32)
    value = middle[...]
    scale = rows_scale(value)
    weighted = normed_grad * gain_ffn[...]
    gain_row = jnp.sum(normed_grad * value * scale, axis=0, keepdims=True)
    for k in range(width // size):
        small[width // size + k:width // size + k + 1, :] = gain_row[:, k * size:(k + 1) * size]
    grad = cotangent[...].astype(f32) * own_valid + scale * weighted - value * (scale * scale * scale) * jnp.mean(
        weighted * value, axis=-1, keepdims=True
    )
    middle_grad[...] = grad
    middle_full[0:rows, :] = grad.astype(bf16)

    def share(source_block, target_block, k, device):
        return remote(
            middle_full.at[source_block * rows:(source_block + 1) * rows, :],
            middle_full.at[target_block * rows:(target_block + 1) * rows, :],
            move_send.at[2, k], move_recv.at[2, k], device,
        )

    far, near = share(0, 2, 0, across), share(0, 1, 1, sibling)
    far.start()
    near.start()
    rounds.tick(pace[1])
    for copy in third_loads:
        copy.wait()
    near.wait()

    def mixed_block(b):
        target = pl.ds(pl.multiple_of(relative(inner, b) * rows, rows), rows)
        upstream[target, :] = dot_nt(middle_full[b * rows:(b + 1) * rows, :], w_out[...]).astype(bf16)

    mixed_block(0)
    mixed_block(1)
    far.wait()
    both = share(2, 3, 2, sibling)
    both.start()
    mixed_block(2)
    both.wait()
    mixed_block(3)
    rounds.tick(pace[2])
    out_source[...] = dot_tn(mixed[...], middle_full[...]).astype(bf16)
    rounds.add(rings[3])

    carried = [(jnp.zeros((size, size), f32), jnp.zeros((size, size), f32)) for _ in range(heads)]
    for c in reversed(range(blocks)):
        span = slice(c * span_rows, (c + 1) * span_rows)
        for h in range(heads):
            col = h * size
            query_unit, _ = unit_rows(ordered[span, col:col + size])
            query_h, query_l = halves(query_unit)
            rise = upstream[span, col:col + size]
            entry = dot_tn(rise, query_h) + dot_tn(rise, query_l)
            memory, velocity = carried[h]
            velocity = velocity + memory
            change = (-step_size[c, h]) * velocity
            slopes[h, c] = change.astype(bf16)
            memory = (1.0 - decay[c, h]) * memory + entry + dot3(dot_nn, halves(change), halves(grams[h, c]))
            velocity = momentum[c, h] * velocity
            carried[h] = (memory, velocity)
        if c % pace[3] == 0:
            rounds.tick(pace[4])

    factor = size ** (-0.5)
    diagonal = lax.broadcasted_iota(jnp.int32, (rows, rows), 0) <= lax.broadcasted_iota(jnp.int32, (rows, rows), 1)
    base_row = shared
    for h in range(heads):
        col = h * size
        for c in range(blocks):
            span = slice(c * span_rows, (c + 1) * span_rows)
            live = (c * span_rows + lax.broadcasted_iota(jnp.int32, (span_rows, 1), 0) < valid_count).astype(f32)
            query_unit, query_scale = unit_rows(ordered[span, col:col + size])
            key_unit, key_scale = unit_rows(ordered[span, cols + col:cols + col + size])
            value = ordered[span, 2 * cols + col:2 * cols + col + size].astype(f32)
            rise = upstream[span, col:col + size]
            state = states[h, c]
            slope = slopes[h, c]
            error = (dot_nt(key_unit.astype(bf16), state) - value) * live
            error_grad = dot_nt(key_unit.astype(bf16), slope) * live
            unit_grad = dot_nn(error.astype(bf16), slope) + dot_nn(error_grad.astype(bf16), state)
            key_sum[span, :] = key_scale * (
                unit_grad - key_unit * jnp.sum(unit_grad * key_unit, axis=-1, keepdims=True)
            )
            value_sum[span, :] = -error_grad
            read_grad = dot_nn(rise, state)
            query_sum[span, :] = query_scale * (
                read_grad - query_unit * jnp.sum(read_grad * query_unit, axis=-1, keepdims=True)
            )
            if c % pace[3] == 0:
                rounds.tick(pace[4])

        key_t = ordered[:, cols + col:cols + col + size].T
        persist_t = persist_k[h].astype(f32).T.astype(bf16)
        persist_k_total = jnp.zeros(persist_k.shape[1:], f32)
        persist_v_total = jnp.zeros(persist_k.shape[1:], f32)
        for i in range(parts):
            span = slice(i * rows, (i + 1) * rows)
            seen = (i + 1) * rows
            query = ordered[span, col:col + size]
            rise = upstream[span, col:col + size]
            scores = dot_nt(ordered[:seen, cols + col:cols + col + size], query)
            last = jnp.where(diagonal, scores[seen - rows:], -1e30)
            scores = last if i == 0 else jnp.concatenate([scores[:seen - rows], last], axis=0)
            extra = dot_nt(persist_k[h], query)
            base = log_total[h:h + 1, span]
            probs = jnp.exp2(scores * (factor * log2_e) - base)
            probs_extra = jnp.exp2(extra * (factor * log2_e) - base)
            probs_grad = dot_nt(ordered[:seen, 2 * cols + col:2 * cols + col + size], rise)
            extra_grad = dot_nt(persist_v[h], rise)
            weighted = probs * probs_grad
            weighted_extra = probs_extra * extra_grad
            inner_sum = jnp.sum(weighted, axis=0, keepdims=True) + jnp.sum(weighted_extra, axis=0, keepdims=True)
            scores_grad = (weighted - probs * inner_sum).astype(bf16)
            scores_extra = (weighted_extra - probs_extra * inner_sum).astype(bf16)
            query_t = dot_nn(key_t[:, :seen], scores_grad) + dot_nn(persist_t, scores_extra)
            query_sum[span, :] += query_t.T * factor
            key_sum[:seen, :] += dot_nn(scores_grad, query) * factor
            value_sum[:seen, :] += dot_nn(probs.astype(bf16), rise)
            persist_k_total += dot_nn(scores_extra, query) * factor
            persist_v_total += dot_nn(probs_extra.astype(bf16), rise)
            rounds.tick(pace[5])
        many = persist_k.shape[1]
        small[base_row + h * many:base_row + (h + 1) * many, :] = persist_k_total
        small[base_row + (heads + h) * many:base_row + (heads + h + 1) * many, :] = persist_v_total
        for b in range(parts):
            span = slice(b * rows, (b + 1) * rows)
            target = pl.ds(pl.multiple_of(relative(inner, b) * rows, rows), rows)
            qkv_grad[target, col:col + size] = query_sum[span, :].astype(bf16)
            qkv_grad[target, cols + col:cols + col + size] = key_sum[span, :].astype(bf16)
            qkv_grad[target, 2 * cols + col:2 * cols + col + size] = value_sum[span, :].astype(bf16)

    for copy in fourth_loads:
        copy.wait()
    for b in range(parts):
        span = slice(b * rows, (b + 1) * rows)
        grad = dot_tn(normed_attn[:, span], qkv_grad[...])
        wide_source[span, :] = grad.astype(bf16)
        gain_row = jnp.sum((grad * w_qkv[span, :].astype(f32)).T, axis=0, keepdims=True) / gain_attn[:, span]
        for k in range(rows // size):
            row = b * (rows // size) + k
            small[row:row + 1, :] = gain_row[:, k * size:(k + 1) * size]
        rounds.tick(pace[6])
    small[2 * width // size:shared, :] = squares[...]
    rounds.add(rings[4], small_sum)

    def attn_block(b):
        return dot_nt(qkv_grad[b * rows:(b + 1) * rows, :], w_qkv[...])

    normed_grad = scatter_blocks(
        attn_block, rows, sent_b, landed_b, move_send.at[1], move_recv.at[1], hold, rounds, pace[7]
    )
    value = inputs[...].astype(f32)
    scale = rows_scale(value)
    weighted = normed_grad * gain_attn[...]
    input_grad[...] = (
        middle_grad[...] + scale * weighted
        - value * (scale * scale * scale) * jnp.mean(weighted * value, axis=-1, keepdims=True)
    ).astype(bf16)
    rounds.finish()


def backward_tail(
    length, momentum, decay, step_size, gain_attn, gain_ffn, squares, persist_k, persist_v, log_total,
    gate_source, up_source, down_source, streamed, count, parts,
):
    heads, many, size = persist_k.shape
    blocks = momentum.shape[0]
    cols = heads * size
    gate_grad, up_grad, w_gate, w_up, middle, cotangent, w_out, mixed, qkv, states, grams, normed_attn, w_qkv, inputs = streamed
    seq_len, width = normed_attn.shape
    rows = seq_len // parts
    hidden = gate_grad.shape[1]
    shared = 2 * width // size + squares.shape[0]
    small_rows = shared + 2 * heads * many
    flows = len(bits_below(count)) + len(bits_below(parts))

    def like(value):
        return pltpu.VMEM(value.shape, value.dtype)

    def row_slots(value):
        return pltpu.VMEM((2, count - 1, value[0] // (2 * count), value[1]), bf16)

    def col_slots(value):
        return pltpu.VMEM((2, count - 1, value[0] // 2, value[1] // count), bf16)

    def semaphores(*shape):
        return pltpu.SemaphoreType.DMA(shape)

    return pl.pallas_call(
        functools.partial(tail_kernel, heads, blocks, parts, count, shared, pace),
        out_shape=(
            jax.ShapeDtypeStruct(gate_source.shape, bf16),
            jax.ShapeDtypeStruct(up_source.shape, bf16),
            jax.ShapeDtypeStruct(down_source.shape, bf16),
            jax.ShapeDtypeStruct((width, 3 * cols), bf16),
            jax.ShapeDtypeStruct((cols, width), bf16),
            jax.ShapeDtypeStruct((small_rows, size), f32),
            jax.ShapeDtypeStruct((rows, width), bf16),
        ),
        in_specs=[smem()] * 4 + [vmem()] * 9 + [pl.BlockSpec(memory_space=pl.ANY)] * len(streamed),
        out_specs=(vmem(),) * 7,
        scratch_shapes=[like(value) for value in streamed] + [
            col_slots(gate_source.shape), col_slots(up_source.shape), col_slots(down_source.shape),
            row_slots((width, 3 * cols)), col_slots((cols, width)),
            pltpu.VMEM((flows, small_rows, size), f32),
            pltpu.VMEM((width, 3 * cols), bf16), pltpu.VMEM((cols, width), bf16),
            pltpu.VMEM((3, rows, width), bf16), pltpu.VMEM((3, rows, width), bf16),
            pltpu.VMEM((3, rows, width), bf16), pltpu.VMEM((3, rows, width), bf16),
            pltpu.VMEM((rows, width), f32), pltpu.VMEM((rows, width), f32), pltpu.VMEM((seq_len, width), bf16),
            pltpu.VMEM((seq_len, cols), bf16), pltpu.VMEM((heads, blocks, size, size), bf16),
            pltpu.VMEM((seq_len, size), f32), pltpu.VMEM((seq_len, size), f32), pltpu.VMEM((seq_len, size), f32),
            pltpu.VMEM((seq_len, 3 * cols), bf16),
            semaphores(len(streamed) + parts), semaphores(5, 2, 2 * count - 2), semaphores(5, 2, 2 * count - 2),
            semaphores(flows), semaphores(flows), semaphores(3, 3), semaphores(3, 3),
        ],
        compiler_params=pltpu.CompilerParams(
            vmem_limit_bytes=tail_limit, collective_id=0, has_side_effects=True
        ),
        cost_estimate=pl.CostEstimate(flops=90_000_000_000, bytes_accessed=40_000_000, transcendentals=2_000_000),
        name="backward_tail",
    )(
        length, momentum, decay, step_size, gain_attn, gain_ffn, squares, persist_k, persist_v, log_total,
        gate_source, up_source, down_source, *streamed,
    )


pace = (4, 4, 1, 4, 1, 1, 1, 6)
tail_limit = 62 << 20


def swap(value, axis, bit):
    count = lax.axis_size(axis)
    return lax.ppermute(value, axis, [(i, i ^ bit) for i in range(count)])


def norm_back(value, scale, gain, upstream):
    weighted = upstream * gain
    return scale * weighted - value * (scale * scale * scale) * jnp.mean(
        weighted * value, axis=-1, keepdims=True
    )


def gather_rows(own):
    far = swap(own, "tensor", 2)
    near = swap(own, "tensor", 1)
    both = swap(far, "tensor", 1)
    return jnp.concatenate([own, near], 0), jnp.concatenate([far, both], 0)


def scatter_rows(near, far):
    rows = near.shape[0] // 2
    far_sum = far[:rows] + swap(far[rows:].astype(bf16), "tensor", 1).astype(f32)
    far_in = swap(far_sum.astype(bf16), "tensor", 2).astype(f32)
    near_in = swap(near[rows:].astype(bf16), "tensor", 1).astype(f32)
    return near[:rows] + near_in + far_in


def mul(left, right):
    return jnp.dot(left, right, preferred_element_type=f32)


def mul_nt(left, right):
    return jnp.einsum("ab,cb->ac", left, right, preferred_element_type=f32)


def mul_tn(left, right):
    return jnp.einsum("ab,ac->bc", left, right, preferred_element_type=f32)


def fits_ring(count, parts, *shapes):
    if count & (count - 1) or parts != 4 or count < 4:
        return False
    return all(rows % (32 * count) == 0 or (rows % 32 == 0 and cols % (128 * count) == 0) for rows, cols in shapes)


def body(
    inputs, cotangent, lengths, gain_attn, w_query, w_key, w_value, w_out, persist_keys, persist_values,
    gain_ffn, w_gate, w_up, w_down, momentum, decay, step_size,
):
    parts = lax.axis_size("tensor")
    count = lax.axis_size("dp")
    rows = inputs.shape[1]
    width = inputs.shape[2]
    half = 2 * rows
    cols = w_query.shape[1]
    size = persist_keys.shape[2]
    place = lax.axis_index("tensor")
    first_row = place * rows
    own_valid = (first_row + jnp.arange(rows, dtype=jnp.int32) < lengths[0]).astype(f32)[:, None]
    places = place.astype(jnp.int32).reshape(1)
    rates = (places, lengths, momentum[0], decay[0], step_size[0])

    resid = inputs[0].astype(f32)
    scale_attn = rows_scale(resid)
    near, far = gather_rows((resid * scale_attn * gain_attn).astype(bf16))
    w_qkv = jnp.concatenate([w_query, w_key, w_value], 1)
    qkv = jnp.concatenate([mul(near, w_qkv).astype(bf16), mul(far, w_qkv).astype(bf16)], 0)
    normed_attn = jnp.concatenate([near, far], 0)
    mixed, log_total, states, grams = attend_and_recall(*rates, qkv, persist_keys, persist_values, parts)
    branch_attn = scatter_rows(mul(mixed[:half], w_out), mul(mixed[half:], w_out))
    middle = resid + branch_attn
    scale_ffn = rows_scale(middle)
    normed_ffn = jnp.concatenate(gather_rows((middle * scale_ffn * gain_ffn).astype(bf16)), 0)

    out_grad = cotangent[0].astype(f32) * own_valid
    out_full = jnp.concatenate(gather_rows(out_grad.astype(bf16)), 0)
    gate = mul(normed_ffn, w_gate)
    up = mul(normed_ffn, w_up)
    sigmoid = jax.nn.sigmoid(gate)
    silu = gate * sigmoid
    hidden = (silu * up).astype(bf16)
    branch_ffn = scatter_rows(mul(hidden[:half], w_down), mul(hidden[half:], w_down))
    result = middle + branch_ffn
    hidden_grad = mul_nt(out_full, w_down)
    gate_grad = (hidden_grad * up * sigmoid * (1.0 + gate * (1.0 - sigmoid))).astype(bf16)
    up_grad = (hidden_grad * silu).astype(bf16)

    def masked(value_in):
        return jnp.sum(own_valid * (value_in * value_in))

    squares = jnp.stack(
        [masked(resid), masked(middle), masked(result), masked(branch_attn), masked(branch_ffn), jnp.sum(own_valid)]
    )
    squares = jnp.pad(squares, (0, 8 * size - 6)).reshape(8, size)
    grad_down = mul_tn(hidden, out_full).astype(bf16)
    grad_gate = mul_tn(gate_grad, normed_ffn).astype(bf16)
    grad_up = mul_tn(up_grad, normed_ffn).astype(bf16)
    if fits_ring(count, parts, grad_down.shape, (width, 3 * cols), (cols, width)):
        gate_sum, up_sum, down_sum, wide, out_sum, small, input_grad = backward_tail(
            *rates[1:], gain_attn[None], gain_ffn[None], squares, persist_keys, persist_values, log_total,
            grad_gate, grad_up, grad_down,
            (gate_grad, up_grad, w_gate, w_up, middle, cotangent[0], w_out, mixed, qkv, states, grams,
             normed_attn, w_qkv, inputs[0]),
            count, parts,
        )
        shared = small.shape[0] - 2 * persist_keys.shape[0] * persist_keys.shape[1]
        persist_sums = small[shared:].reshape((2,) + persist_keys.shape)
        small = small[:shared].reshape(-1)
    else:
        normed_ffn_grad = scatter_rows(
            mul_nt(gate_grad[:half], w_gate) + mul_nt(up_grad[:half], w_up),
            mul_nt(gate_grad[half:], w_gate) + mul_nt(up_grad[half:], w_up),
        )
        gain_ffn_part = jnp.sum(normed_ffn_grad * middle * scale_ffn, axis=0)
        middle_grad = out_grad + norm_back(middle, scale_ffn, gain_ffn, normed_ffn_grad)
        middle_full = jnp.concatenate(gather_rows(middle_grad.astype(bf16)), 0)
        mixed_grad = mul_nt(middle_full, w_out).astype(bf16)
        qkv_grad, persist_k_grad, persist_v_grad = attend_and_recall_back(
            *rates, qkv, mixed_grad, persist_keys, persist_values, log_total, states, grams, parts
        )
        normed_attn_grad = scatter_rows(mul_nt(qkv_grad[:half], w_qkv), mul_nt(qkv_grad[half:], w_qkv))
        gain_attn_part = jnp.sum(normed_attn_grad * resid * scale_attn, axis=0)
        input_grad = (middle_grad + norm_back(resid, scale_attn, gain_attn, normed_attn_grad)).astype(bf16)
        gate_sum, up_sum, down_sum, wide, out_sum, persist_sums = lax.psum(
            (grad_gate, grad_up, grad_down, mul_tn(normed_attn, qkv_grad).astype(bf16),
             mul_tn(mixed, middle_full).astype(bf16), jnp.stack([persist_k_grad, persist_v_grad])), "dp"
        )
        small = lax.psum(jnp.concatenate([gain_attn_part, gain_ffn_part, squares.reshape(-1)]), ("dp", "tensor"))
    rms_stats = jnp.sqrt(small[2 * width:2 * width + 5] / (small[2 * width + 5] * width))
    wide = wide.astype(f32)
    return (
        result.astype(bf16)[None],
        input_grad[None],
        small[:width],
        wide[:, :cols],
        wide[:, cols:2 * cols],
        wide[:, 2 * cols:],
        out_sum.astype(f32),
        persist_sums[0],
        persist_sums[1],
        small[width:2 * width],
        gate_sum.astype(f32).T,
        up_sum.astype(f32).T,
        down_sum.astype(f32),
        rms_stats,
    )


def solution(mesh):
    in_specs = (
        P("dp", "tensor", None),
        P("dp", "tensor", None),
        P("dp"),
        P(),
        P(None, "tensor"),
        P(None, "tensor"),
        P(None, "tensor"),
        P("tensor", None),
        P("tensor", None, None),
        P("tensor", None, None),
        P(),
        P(None, "tensor"),
        P(None, "tensor"),
        P("tensor", None),
        P("dp", None, "tensor"),
        P("dp", None, "tensor"),
        P("dp", None, "tensor"),
    )
    out_specs = (
        P("dp", "tensor", None),
        P("dp", "tensor", None),
        P(),
        P(None, "tensor"),
        P(None, "tensor"),
        P(None, "tensor"),
        P("tensor", None),
        P("tensor", None, None),
        P("tensor", None, None),
        P(),
        P(None, "tensor"),
        P(None, "tensor"),
        P("tensor", None),
        P(),
    )
    return jax.shard_map(body, mesh=mesh, in_specs=in_specs, out_specs=out_specs, check_vma=False)
```

```python
import functools
import jax
import jax.numpy as jnp
from jax import lax
from jax.sharding import PartitionSpec as P
import jax.experimental.pallas as pl
import jax.experimental.pallas.tpu as pltpu

norm_eps = 1e-05
unit_eps = 1e-06
f32 = jnp.float32
bf16 = jnp.bfloat16
log2_e = 1.4426950408889634


def dot_nn(left, right):
    return lax.dot_general(left, right, (((1,), (0,)), ((), ())), preferred_element_type=f32)


def dot_nt(left, right):
    return lax.dot_general(left, right, (((1,), (1,)), ((), ())), preferred_element_type=f32)


def dot_tn(left, right):
    return lax.dot_general(left, right, (((0,), (0,)), ((), ())), preferred_element_type=f32)


def halves(value):
    high = value.astype(bf16)
    return high, (value - high.astype(f32)).astype(bf16)


def dot3(dot, left, right):
    (lh, ll), (rh, rl) = left, right
    return dot(lh, rh) + dot(ll, rh) + dot(lh, rl)


def unit_rows(value):
    wide = value.astype(f32)
    scale = lax.rsqrt(jnp.sum(wide * wide, axis=-1, keepdims=True) + unit_eps)
    return wide * scale, scale


def block_rows(start, width):
    return pl.ds(pl.multiple_of(start, width), width)


def forward_kernel(
    heads, blocks, parts,
    place, length, momentum, decay, step_size, qkv, persist_k, persist_v,
    mixed, log_total, states, grams,
    ordered, reads,
):
    seq_len, wide = qkv.shape
    size = persist_k.shape[2]
    cols = heads * size
    rows = seq_len // parts
    width = seq_len // blocks
    me = place[0]
    count = length[0]
    for b in range(parts):
        ordered[b * rows:(b + 1) * rows, :] = qkv[block_rows(jnp.bitwise_xor(me, b) * rows, rows), :]

    carried = [(jnp.zeros((size, size), f32), jnp.zeros((size, size), f32)) for _ in range(heads)]
    for c in range(blocks):
        span = slice(c * width, (c + 1) * width)
        live = (c * width + lax.broadcasted_iota(jnp.int32, (width, 1), 0) < count).astype(f32)
        for h in range(heads):
            col = h * size
            key_unit, _ = unit_rows(ordered[span, cols + col:cols + col + size])
            query_unit, _ = unit_rows(ordered[span, col:col + size])
            value = ordered[span, 2 * cols + col:2 * cols + col + size]
            key_h, key_l = halves(key_unit)
            live_h, live_l = halves(key_unit * live)
            gram = dot3(dot_tn, (live_h, live_l), (key_h, key_l))
            target = dot_tn(value, live_h) + dot_tn(value, live_l)
            memory, velocity = carried[h]
            states[h, c] = memory.astype(bf16)
            grams[h, c] = gram
            parts_m = halves(memory)
            reads[span, col:col + size] = dot_nt(query_unit.astype(bf16), parts_m[0])
            change = dot3(dot_nn, parts_m, halves(gram)) - target
            velocity = momentum[c, h] * velocity - step_size[c, h] * change
            memory = (1.0 - decay[c, h]) * memory + velocity
            carried[h] = (memory, velocity)

    factor = size ** (-0.5) * log2_e
    diagonal = lax.broadcasted_iota(jnp.int32, (rows, rows), 0) <= lax.broadcasted_iota(jnp.int32, (rows, rows), 1)
    for h in range(heads):
        col = h * size
        value_t = ordered[:, 2 * cols + col:2 * cols + col + size].T
        persist_t = persist_v[h].astype(f32).T.astype(bf16)
        for i in range(parts):
            span = slice(i * rows, (i + 1) * rows)
            seen = (i + 1) * rows
            query = ordered[span, col:col + size]
            scores = dot_nt(ordered[:seen, cols + col:cols + col + size], query)
            last = jnp.where(diagonal, scores[seen - rows:], -1e30)
            scores = last if i == 0 else jnp.concatenate([scores[:seen - rows], last], axis=0)
            extra = dot_nt(persist_k[h], query)
            top = jnp.maximum(jnp.max(scores, axis=0, keepdims=True), jnp.max(extra, axis=0, keepdims=True))
            lifted = jnp.exp2((scores - top) * factor)
            lifted_extra = jnp.exp2((extra - top) * factor)
            total = jnp.sum(lifted, axis=0, keepdims=True) + jnp.sum(lifted_extra, axis=0, keepdims=True)
            attended = dot_nn(value_t[:, :seen], lifted.astype(bf16)) + dot_nn(persist_t, lifted_extra.astype(bf16))
            attended = attended * (1.0 / total)
            log_total[h:h + 1, span] = top * factor + jnp.log2(total)
            together = attended.T + reads[span, col:col + size]
            mixed[block_rows(jnp.bitwise_xor(me, i) * rows, rows), col:col + size] = together.astype(bf16)


def backward_kernel(
    heads, blocks, parts,
    place, length, momentum, decay, step_size, qkv, mixed_grad, persist_k, persist_v,
    log_total, states, grams,
    qkv_grad, persist_k_grad, persist_v_grad,
    ordered, upstream, slopes, key_sum, value_sum, query_sum,
):
    seq_len, wide = qkv.shape
    size = persist_k.shape[2]
    cols = heads * size
    rows = seq_len // parts
    width = seq_len // blocks
    me = place[0]
    count = length[0]
    for b in range(parts):
        source = block_rows(jnp.bitwise_xor(me, b) * rows, rows)
        ordered[b * rows:(b + 1) * rows, :] = qkv[source, :]
        upstream[b * rows:(b + 1) * rows, :] = mixed_grad[source, :]

    carried = [(jnp.zeros((size, size), f32), jnp.zeros((size, size), f32)) for _ in range(heads)]
    for c in reversed(range(blocks)):
        span = slice(c * width, (c + 1) * width)
        for h in range(heads):
            col = h * size
            query_unit, _ = unit_rows(ordered[span, col:col + size])
            query_h, query_l = halves(query_unit)
            rise = upstream[span, col:col + size]
            entry = dot_tn(rise, query_h) + dot_tn(rise, query_l)
            memory, velocity = carried[h]
            velocity = velocity + memory
            change = (-step_size[c, h]) * velocity
            slopes[h, c] = change
            memory = (1.0 - decay[c, h]) * memory + entry + dot3(dot_nn, halves(change), halves(grams[h, c]))
            velocity = momentum[c, h] * velocity
            carried[h] = (memory, velocity)

    for h in range(heads):
        col = h * size
        for c in range(blocks):
            span = slice(c * width, (c + 1) * width)
            live = (c * width + lax.broadcasted_iota(jnp.int32, (width, 1), 0) < count).astype(f32)
            query_unit, query_scale = unit_rows(ordered[span, col:col + size])
            key_unit, key_scale = unit_rows(ordered[span, cols + col:cols + col + size])
            value = ordered[span, 2 * cols + col:2 * cols + col + size].astype(f32)
            rise = upstream[span, col:col + size]
            state = states[h, c]
            slope = slopes[h, c].astype(bf16)
            key_b = key_unit.astype(bf16)
            error = (dot_nt(key_b, state) - value) * live
            error_grad = dot_nt(key_b, slope) * live
            unit_grad = dot_nn(error.astype(bf16), slope) + dot_nn(error_grad.astype(bf16), state)
            key_sum[span, :] = key_scale * (unit_grad - key_unit * jnp.sum(unit_grad * key_unit, axis=-1, keepdims=True))
            value_sum[span, :] = -error_grad
            read_grad = dot_nn(rise, state)
            query_sum[span, :] = query_scale * (read_grad - query_unit * jnp.sum(read_grad * query_unit, axis=-1, keepdims=True))

        factor = size ** (-0.5)
        diagonal = lax.broadcasted_iota(jnp.int32, (rows, rows), 0) <= lax.broadcasted_iota(jnp.int32, (rows, rows), 1)
        key_t = ordered[:, cols + col:cols + col + size].T
        persist_t = persist_k[h].astype(f32).T.astype(bf16)
        persist_k_total = jnp.zeros(persist_k.shape[1:], f32)
        persist_v_total = jnp.zeros(persist_k.shape[1:], f32)
        for i in range(parts):
            span = slice(i * rows, (i + 1) * rows)
            seen = (i + 1) * rows
            query = ordered[span, col:col + size]
            rise = upstream[span, col:col + size]
            scores = dot_nt(ordered[:seen, cols + col:cols + col + size], query)
            last = jnp.where(diagonal, scores[seen - rows:], -1e30)
            scores = last if i == 0 else jnp.concatenate([scores[:seen - rows], last], axis=0)
            extra = dot_nt(persist_k[h], query)
            base = log_total[h:h + 1, span]
            probs = jnp.exp2(scores * (factor * log2_e) - base)
            probs_extra = jnp.exp2(extra * (factor * log2_e) - base)
            probs_grad = dot_nt(ordered[:seen, 2 * cols + col:2 * cols + col + size], rise)
            extra_grad = dot_nt(persist_v[h], rise)
            weighted = probs * probs_grad
            weighted_extra = probs_extra * extra_grad
            inner = jnp.sum(weighted, axis=0, keepdims=True) + jnp.sum(weighted_extra, axis=0, keepdims=True)
            scores_grad = (weighted - probs * inner).astype(bf16)
            scores_extra = (weighted_extra - probs_extra * inner).astype(bf16)
            query_t = dot_nn(key_t[:, :seen], scores_grad) + dot_nn(persist_t, scores_extra)
            query_sum[span, :] += query_t.T * factor
            key_sum[:seen, :] += dot_nn(scores_grad, query) * factor
            value_sum[:seen, :] += dot_nn(probs.astype(bf16), rise)
            persist_k_total += dot_nn(scores_extra, query) * factor
            persist_v_total += dot_nn(probs_extra.astype(bf16), rise)
        persist_k_grad[h] = persist_k_total
        persist_v_grad[h] = persist_v_total
        for b in range(parts):
            span = slice(b * rows, (b + 1) * rows)
            target = block_rows(jnp.bitwise_xor(me, b) * rows, rows)
            qkv_grad[target, col:col + size] = query_sum[span, :].astype(bf16)
            qkv_grad[target, cols + col:cols + col + size] = key_sum[span, :].astype(bf16)
            qkv_grad[target, 2 * cols + col:2 * cols + col + size] = value_sum[span, :].astype(bf16)


vmem = functools.partial(pl.BlockSpec, memory_space=pltpu.VMEM)
smem = functools.partial(pl.BlockSpec, memory_space=pltpu.SMEM)
vmem_limit = 56 << 20


def attend_and_recall(place, length, momentum, decay, step_size, qkv, persist_k, persist_v, parts):
    heads, _, size = persist_k.shape
    seq_len = qkv.shape[0]
    blocks = momentum.shape[0]
    cols = heads * size
    return pl.pallas_call(
        functools.partial(forward_kernel, heads, blocks, parts),
        out_shape=(
            jax.ShapeDtypeStruct((seq_len, cols), bf16),
            jax.ShapeDtypeStruct((heads, seq_len), f32),
            jax.ShapeDtypeStruct((heads, blocks, size, size), bf16),
            jax.ShapeDtypeStruct((heads, blocks, size, size), f32),
        ),
        in_specs=[smem()] * 5 + [vmem()] * 3,
        out_specs=(vmem(),) * 4,
        scratch_shapes=[pltpu.VMEM((seq_len, 3 * cols), bf16), pltpu.VMEM((seq_len, cols), f32)],
        compiler_params=pltpu.CompilerParams(vmem_limit_bytes=vmem_limit),
        cost_estimate=pl.CostEstimate(flops=12_000_000_000, bytes_accessed=8_000_000, transcendentals=2_000_000),
        name="attend_recall",
    )(place, length, momentum, decay, step_size, qkv, persist_k, persist_v)


def attend_and_recall_back(
    place, length, momentum, decay, step_size, qkv, mixed_grad, persist_k, persist_v, log_total, states, grams, parts
):
    heads, persistent, size = persist_k.shape
    seq_len = qkv.shape[0]
    blocks = momentum.shape[0]
    cols = heads * size
    return pl.pallas_call(
        functools.partial(backward_kernel, heads, blocks, parts),
        out_shape=(
            jax.ShapeDtypeStruct((seq_len, 3 * cols), bf16),
            jax.ShapeDtypeStruct((heads, persistent, size), f32),
            jax.ShapeDtypeStruct((heads, persistent, size), f32),
        ),
        in_specs=[smem()] * 5 + [vmem()] * 7,
        out_specs=(vmem(),) * 3,
        scratch_shapes=[
            pltpu.VMEM((seq_len, 3 * cols), bf16),
            pltpu.VMEM((seq_len, cols), bf16),
            pltpu.VMEM((heads, blocks, size, size), f32),
            pltpu.VMEM((seq_len, size), f32),
            pltpu.VMEM((seq_len, size), f32),
            pltpu.VMEM((seq_len, size), f32),
        ],
        compiler_params=pltpu.CompilerParams(vmem_limit_bytes=vmem_limit),
        cost_estimate=pl.CostEstimate(flops=25_000_000_000, bytes_accessed=12_000_000, transcendentals=2_000_000),
        name="attend_recall_back",
    )(place, length, momentum, decay, step_size, qkv, mixed_grad, persist_k, persist_v, log_total, states, grams)


def ring_place(index, count):
    odd = index % 2
    return (1 - odd) * (index // 2) + odd * (count - 1 - index // 2)


def ring_index(place, count):
    late = place // (count // 2)
    return (1 - late) * (2 * place) + late * (2 * (count - 1 - place) + 1)


def flip(index, bit):
    return index + bit * (1 - 2 * ((index // bit) % 2))


def bits_below(count):
    return [1 << k for k in range(count.bit_length() - 1)]


def relative(index, block):
    for bit in (1, 2):
        if block & bit:
            index = flip(index, bit)
    return index


def remote(source, target, send_sem, recv_sem, device):
    return pltpu.make_async_remote_copy(
        src_ref=source, dst_ref=target, send_sem=send_sem, recv_sem=recv_sem,
        device_id=device, device_id_type=pl.DeviceIdType.MESH,
    )


class Ring:
    def __init__(self, count, by_rows, source, out, slots, send_sem, recv_sem):
        self.count, self.by_rows = count, by_rows
        self.source, self.out, self.slots = source, out, slots
        self.send_sem, self.recv_sem = send_sem, recv_sem
        index = lax.axis_index("dp")
        self.place = ring_place(index, count)
        self.peers = (
            {"dp": ring_index((self.place + 1) % count, count)},
            {"dp": ring_index((self.place + count - 1) % count, count)},
        )
        self.step = 0
        self.copies = [None, None]
        self.sent = []

    def piece(self, ref, way, chunk):
        rows, cols = ref.shape
        chunk = chunk % self.count
        if self.by_rows:
            size = rows // (2 * self.count)
            return ref.at[pl.ds(pl.multiple_of(chunk * (2 * size) + way * size, size), size), :]
        size, width = rows // 2, cols // self.count
        return ref.at[way * size:(way + 1) * size, pl.ds(pl.multiple_of(chunk * width, width), width)]

    def chunk(self, way, step):
        return self.place + self.count + (2 * self.count - step if way == 0 else step)

    def launch(self, way, step, source, target):
        copy = remote(source, target, self.send_sem.at[way, step], self.recv_sem.at[way, step], self.peers[way])
        copy.start()
        self.copies[way] = copy
        self.sent.append(copy)

    def start(self):
        for way in range(2):
            self.launch(way, 0, self.piece(self.source, way, self.chunk(way, 0)), self.slots.at[way, 0])

    def advance(self):
        count, step = self.count, self.step
        for way in range(2):
            self.copies[way].wait_recv()
            if step < count - 1:
                chunk = self.chunk(way, step + 1)
                total = self.slots[way, step].astype(f32) + self.piece(self.source, way, chunk)[...].astype(f32)
                if step < count - 2:
                    self.slots[way, step] = total.astype(bf16)
                    source, target = self.slots.at[way, step], self.slots.at[way, step + 1]
                else:
                    source = target = self.piece(self.out, way, chunk)
                    source[...] = total.astype(bf16)
            else:
                source = target = self.piece(self.out, way, self.chunk(way, step + 1 - count))
            if step < 2 * count - 3:
                self.launch(way, step + 1, source, target)
        self.step += 1
        if self.step < 2 * count - 2:
            return True
        for copy in self.sent:
            copy.wait_send()
        return False


class SmallSum:
    def __init__(self, value, slots, shared, send_sem, recv_sem, count, parts):
        self.value, self.slots, self.shared = value, slots, shared
        self.send_sem, self.recv_sem = send_sem, recv_sem
        index, inner = lax.axis_index("dp"), lax.axis_index("tensor")
        self.inner = len(bits_below(parts))
        self.peers = [{"tensor": flip(inner, bit)} for bit in bits_below(parts)]
        self.peers += [{"dp": flip(index, bit)} for bit in bits_below(count)]
        self.step = 0

    def start(self):
        used = slice(0, self.shared if self.step < self.inner else self.value.shape[0])
        self.used = used
        self.copy = remote(
            self.value.at[used], self.slots.at[self.step, used], self.send_sem.at[self.step],
            self.recv_sem.at[self.step], self.peers[self.step],
        )
        self.copy.start()

    def advance(self):
        self.copy.wait()
        self.value[self.used] += self.slots[self.step, self.used]
        self.step += 1
        if self.step < len(self.peers):
            self.start()
        return self.step < len(self.peers)


class Rounds:
    def __init__(self):
        self.queue = []

    def add(self, *flows):
        for flow in flows:
            flow.start()
            self.queue.append(flow)

    def tick(self, count=1):
        for _ in range(count):
            if self.queue:
                flow = self.queue.pop(0)
                if flow.advance():
                    self.queue.append(flow)

    def finish(self):
        while self.queue:
            self.tick()


def rows_scale(value):
    return lax.rsqrt(jnp.mean(value * value, axis=-1, keepdims=True) + norm_eps)


class Scatter:
    def __init__(self, sent, landed, hold, send_sem, recv_sem):
        self.sent, self.landed, self.hold = sent, landed, hold
        self.send_sem, self.recv_sem = send_sem, recv_sem
        inner = lax.axis_index("tensor")
        self.sibling, self.across = {"tensor": flip(inner, 1)}, {"tensor": flip(inner, 2)}

    def copy(self, k, device):
        return remote(self.sent.at[k], self.landed.at[k], self.send_sem.at[k], self.recv_sem.at[k], device)

    def begin(self, block):
        self.sent[0] = block(3).astype(bf16)
        first = self.copy(0, self.sibling)
        first.start()
        self.hold[...] = block(2)
        first.wait()
        self.sent[1] = (self.hold[...] + self.landed[0].astype(f32)).astype(bf16)
        self.second = self.copy(1, self.across)
        self.second.start()
        self.sent[2] = block(1).astype(bf16)
        self.third = self.copy(2, self.sibling)
        self.third.start()
        self.hold[...] = block(0)

    def finish(self):
        self.third.wait()
        self.second.wait()
        return self.hold[...] + self.landed[2].astype(f32) + self.landed[1].astype(f32)


class Gather:
    def __init__(self, full, parts, send_sem, recv_sem):
        self.full, self.rows = full, full.shape[0] // parts
        self.send_sem, self.recv_sem = send_sem, recv_sem
        inner = lax.axis_index("tensor")
        self.sibling, self.across = {"tensor": flip(inner, 1)}, {"tensor": flip(inner, 2)}

    def block(self, b):
        return self.full.at[b * self.rows:(b + 1) * self.rows, :]

    def copy(self, source, target, k, device):
        return remote(self.block(source), self.block(target), self.send_sem.at[k], self.recv_sem.at[k], device)

    def begin(self):
        self.far, self.near = self.copy(0, 2, 0, self.across), self.copy(0, 1, 1, self.sibling)
        self.far.start()
        self.near.start()

    def forward(self):
        self.far.wait()
        self.both = self.copy(2, 3, 2, self.sibling)
        self.both.start()


def layer_kernel(
    heads, blocks, parts, count, shared, pace,
    length, momentum, decay, step_size,
    inputs, cotangent, gain_attn, gain_ffn, persist_k, persist_v,
    w_query_h, w_key_h, w_value_h, w_out_h, w_gate_h, w_up_h, w_down_h,
    gate_out, up_out, down_out, wide_out, out_out, small, result, input_grad,
    w_qkv, w_out, w_gate, w_up, w_down,
    normed_attn, ordered, mixed, states, grams, log_total,
    middle, hold, middle_grad, normed_ffn, out_full, gate_grad, up_grad, hidden,
    gate_source, up_source, down_source, wide_source, out_source,
    gate_slots, up_slots, down_slots, wide_slots, out_slots, small_slots,
    sent_a, landed_a, sent_b, landed_b, middle_full, upstream, slopes, key_sum, value_sum, query_sum, qkv_grad,
    load_sem, ring_send, ring_recv, small_send, small_recv, move_send, move_recv,
):
    size = persist_k.shape[2]
    many = persist_k.shape[1]
    cols = heads * size
    seq_len, width = middle_full.shape
    units = gate_grad.shape[0]
    rows = seq_len // parts
    span_rows = seq_len // blocks
    inner = lax.axis_index("tensor")
    valid_count = length[0]
    factor = size ** (-0.5)
    reads = middle_grad

    rounds = Rounds()
    rings = [
        Ring(count, by_rows, source, out, slots, ring_send.at[k], ring_recv.at[k])
        for k, (by_rows, source, out, slots) in enumerate((
            (False, down_source, down_out, down_slots),
            (False, gate_source, gate_out, gate_slots),
            (False, up_source, up_out, up_slots),
            (False, out_source, out_out, out_slots),
            (True, wide_source, wide_out, wide_slots),
        ))
    ]
    small_sum = SmallSum(small, small_slots, shared, small_send, small_recv, count, parts)
    barrier = pltpu.get_barrier_semaphore()
    peers = list(rings[0].peers) + small_sum.peers
    for peer in peers:
        pl.semaphore_signal(barrier, inc=1, device_id=peer, device_id_type=pl.DeviceIdType.MESH)

    loads = []

    def load(source, target):
        copy = pltpu.make_async_copy(source, target, load_sem.at[len(loads)])
        copy.start()
        loads.append(copy)
        return copy

    qkv_loads = [
        load(source, w_qkv.at[:, k * cols:(k + 1) * cols]) for k, source in enumerate((w_query_h, w_key_h, w_value_h))
    ]
    out_load = load(w_out_h, w_out)
    ffn_loads = [load(w_gate_h, w_gate), load(w_up_h, w_up), load(w_down_h, w_down)]

    def true_rows(b):
        return pl.ds(pl.multiple_of(relative(inner, b) * rows, rows), rows)

    def block_of(b):
        return slice(b * rows, (b + 1) * rows)

    row_place = inner * rows + lax.broadcasted_iota(jnp.int32, (rows, 1), 0)
    own_valid = (row_place < valid_count).astype(f32)
    stat_row = 2 * width // size

    def note(k, value):
        total = jnp.sum(jnp.sum(value, axis=1, keepdims=True) * own_valid, axis=0, keepdims=True)
        small[stat_row + k:stat_row + k + 1, :] = jnp.broadcast_to(total, (1, size))

    resid = inputs[...].astype(f32)
    normed_attn[0:rows, :] = (resid * rows_scale(resid) * gain_attn[...]).astype(bf16)
    gather_attn = Gather(normed_attn, parts, move_send.at[0], move_recv.at[0])
    pl.semaphore_wait(barrier, len(peers))
    gather_attn.begin()
    out_full[0:rows, :] = (cotangent[...].astype(f32) * own_valid).astype(bf16)
    small[stat_row:stat_row + 8, :] = jnp.zeros((8, size), f32)
    note(0, resid * resid)
    note(5, jnp.ones((rows, 1), f32))
    for copy in qkv_loads:
        copy.wait()

    def qkv_block(b):
        ordered[true_rows(b), :] = dot_nn(normed_attn[block_of(b), :], w_qkv[...]).astype(bf16)

    qkv_block(0)
    gather_attn.near.wait()
    qkv_block(1)
    gather_attn.forward()
    qkv_block(2)
    gather_cot = Gather(out_full, parts, move_send.at[1], move_recv.at[1])
    gather_cot.begin()
    gather_attn.both.wait()
    qkv_block(3)

    carried = [(jnp.zeros((size, size), f32), jnp.zeros((size, size), f32)) for _ in range(heads)]
    for c in range(blocks):
        span = slice(c * span_rows, (c + 1) * span_rows)
        live = (c * span_rows + lax.broadcasted_iota(jnp.int32, (span_rows, 1), 0) < valid_count).astype(f32)
        tile, offset = c * span_rows // rows, c * span_rows % rows
        for h in range(heads):
            col = h * size
            key_unit, _ = unit_rows(ordered[span, cols + col:cols + col + size])
            query_unit, _ = unit_rows(ordered[span, col:col + size])
            value = ordered[span, 2 * cols + col:2 * cols + col + size]
            key_h, key_l = halves(key_unit)
            live_h, live_l = halves(key_unit * live)
            gram = dot3(dot_tn, (live_h, live_l), (key_h, key_l))
            target = dot_tn(value, live_h) + dot_tn(value, live_l)
            memory, velocity = carried[h]
            states[h, c] = memory.astype(bf16)
            grams[h, c] = gram
            parts_m = halves(memory)
            reads[offset:offset + span_rows, tile * cols + col:tile * cols + col + size] = dot_nt(
                query_unit.astype(bf16), parts_m[0]
            )
            change = dot3(dot_nn, parts_m, halves(gram)) - target
            velocity = momentum[c, h] * velocity - step_size[c, h] * change
            memory = (1.0 - decay[c, h]) * memory + velocity
            carried[h] = (memory, velocity)

    diagonal = lax.broadcasted_iota(jnp.int32, (rows, rows), 0) <= lax.broadcasted_iota(jnp.int32, (rows, rows), 1)

    def masked_scores(h, i, query):
        seen = (i + 1) * rows
        scores = dot_nt(ordered[:seen, cols + h * size:cols + (h + 1) * size], query)
        last = jnp.where(diagonal, scores[seen - rows:], -1e30)
        return last if i == 0 else jnp.concatenate([scores[:seen - rows], last], axis=0)

    for h in range(heads):
        col = h * size
        value_t = ordered[:, 2 * cols + col:2 * cols + col + size].T
        persist_t = persist_v[h].astype(f32).T.astype(bf16)
        for i in range(parts):
            seen = (i + 1) * rows
            query = ordered[block_of(i), col:col + size]
            scores = masked_scores(h, i, query)
            extra = dot_nt(persist_k[h], query)
            top = jnp.maximum(jnp.max(scores, axis=0, keepdims=True), jnp.max(extra, axis=0, keepdims=True))
            lifted = jnp.exp2((scores - top) * (factor * log2_e))
            lifted_extra = jnp.exp2((extra - top) * (factor * log2_e))
            total = jnp.sum(lifted, axis=0, keepdims=True) + jnp.sum(lifted_extra, axis=0, keepdims=True)
            attended = dot_nn(value_t[:, :seen], lifted.astype(bf16)) + dot_nn(persist_t, lifted_extra.astype(bf16))
            attended = attended * (1.0 / total)
            log_total[h:h + 1, block_of(i)] = top * (factor * log2_e) + jnp.log2(total)
            together = attended.T + reads[:, i * cols + col:i * cols + col + size]
            mixed[true_rows(i), col:col + size] = together.astype(bf16)
    gather_cot.near.wait()
    gather_cot.forward()

    out_load.wait()
    scatter = Scatter(sent_a, landed_a, hold, move_send.at[2], move_recv.at[2])
    scatter.begin(lambda b: dot_nn(mixed[block_of(b), :], w_out[...]))
    for copy in ffn_loads:
        copy.wait()
    branch = scatter.finish()
    note(3, branch * branch)
    value = inputs[...].astype(f32) + branch
    middle[...] = value
    note(1, value * value)
    normed_ffn[0:rows, :] = (value * rows_scale(value) * gain_ffn[...]).astype(bf16)
    gather_ffn = Gather(normed_ffn, parts, move_send.at[3], move_recv.at[3])
    gather_ffn.begin()
    gather_cot.both.wait()
    gather_ffn.near.wait()

    piece = units // 4

    def feed(half):
        tokens = slice(half * 2 * rows, (half + 1) * 2 * rows)
        for k in range(4):
            span = slice(k * piece, (k + 1) * piece)
            gate = dot_nt(w_gate[span, :], normed_ffn[tokens, :])
            up = dot_nt(w_up[span, :], normed_ffn[tokens, :])
            hidden_grad = dot_nt(w_down[span, :], out_full[tokens, :])
            sigmoid = jax.nn.sigmoid(gate)
            silu = gate * sigmoid
            hidden[span, tokens] = (silu * up).astype(bf16)
            up_grad[span, tokens] = (hidden_grad * silu).astype(bf16)
            gate_grad[span, tokens] = (hidden_grad * up * sigmoid * (1.0 + gate * (1.0 - sigmoid))).astype(bf16)

    feed(0)
    gather_ffn.forward()
    gather_ffn.both.wait()
    feed(1)
    for source, left, right, ring in (
        (down_source, hidden, out_full, rings[0]), (gate_source, gate_grad, normed_ffn, rings[1]),
        (up_source, up_grad, normed_ffn, rings[2]),
    ):
        source[...] = dot_nn(left[...], right[...]).astype(bf16)
        rounds.add(ring)

    scatter = Scatter(sent_b, landed_b, hold, move_send.at[4], move_recv.at[4])
    scatter.begin(
        lambda b: dot_tn(gate_grad[:, block_of(b)], w_gate[...]) + dot_tn(up_grad[:, block_of(b)], w_up[...])
    )
    rounds.tick(pace[0])
    normed_grad = scatter.finish()
    value = middle[...]
    scale = rows_scale(value)
    weighted = normed_grad * gain_ffn[...]
    gain_row = jnp.sum(normed_grad * value * scale, axis=0, keepdims=True)
    for k in range(width // size):
        small[width // size + k:width // size + k + 1, :] = gain_row[:, k * size:(k + 1) * size]
    grad = cotangent[...].astype(f32) * own_valid + scale * weighted - value * (scale * scale * scale) * jnp.mean(
        weighted * value, axis=-1, keepdims=True
    )
    middle_grad[...] = grad
    middle_full[0:rows, :] = grad.astype(bf16)
    gather_middle = Gather(middle_full, parts, move_send.at[5], move_recv.at[5])
    gather_middle.begin()
    rounds.tick(pace[1])
    gather_middle.near.wait()

    def mixed_block(b):
        upstream[true_rows(b), :] = dot_nt(middle_full[block_of(b), :], w_out[...]).astype(bf16)

    mixed_block(0)
    mixed_block(1)
    gather_middle.forward()
    mixed_block(2)
    gather_middle.both.wait()
    mixed_block(3)
    scatter = Scatter(sent_a, landed_a, hold, move_send.at[6], move_recv.at[6])
    scatter.begin(lambda b: dot_tn(hidden[:, block_of(b)], w_down[...]))
    rounds.tick(pace[2])
    out_source[...] = dot_tn(mixed[...], middle_full[...]).astype(bf16)
    rounds.add(rings[3])

    carried = [(jnp.zeros((size, size), f32), jnp.zeros((size, size), f32)) for _ in range(heads)]
    for c in reversed(range(blocks)):
        span = slice(c * span_rows, (c + 1) * span_rows)
        for h in range(heads):
            col = h * size
            query_unit, _ = unit_rows(ordered[span, col:col + size])
            query_h, query_l = halves(query_unit)
            rise = upstream[span, col:col + size]
            entry = dot_tn(rise, query_h) + dot_tn(rise, query_l)
            memory, velocity = carried[h]
            velocity = velocity + memory
            change = (-step_size[c, h]) * velocity
            slopes[h, c] = change.astype(bf16)
            memory = (1.0 - decay[c, h]) * memory + entry + dot3(dot_nn, halves(change), halves(grams[h, c]))
            velocity = momentum[c, h] * velocity
            carried[h] = (memory, velocity)
        if c % pace[3] == 0:
            rounds.tick(pace[4])

    for h in range(heads):
        col = h * size
        for c in range(blocks):
            span = slice(c * span_rows, (c + 1) * span_rows)
            live = (c * span_rows + lax.broadcasted_iota(jnp.int32, (span_rows, 1), 0) < valid_count).astype(f32)
            query_unit, query_scale = unit_rows(ordered[span, col:col + size])
            key_unit, key_scale = unit_rows(ordered[span, cols + col:cols + col + size])
            value = ordered[span, 2 * cols + col:2 * cols + col + size].astype(f32)
            rise = upstream[span, col:col + size]
            state = states[h, c]
            slope = slopes[h, c]
            error = (dot_nt(key_unit.astype(bf16), state) - value) * live
            error_grad = dot_nt(key_unit.astype(bf16), slope) * live
            unit_grad = dot_nn(error.astype(bf16), slope) + dot_nn(error_grad.astype(bf16), state)
            key_sum[span, :] = key_scale * (
                unit_grad - key_unit * jnp.sum(unit_grad * key_unit, axis=-1, keepdims=True)
            )
            value_sum[span, :] = -error_grad
            read_grad = dot_nn(rise, state)
            query_sum[span, :] = query_scale * (
                read_grad - query_unit * jnp.sum(read_grad * query_unit, axis=-1, keepdims=True)
            )
            if c % pace[3] == 0:
                rounds.tick(pace[4])

        key_t = ordered[:, cols + col:cols + col + size].T
        persist_t = persist_k[h].astype(f32).T.astype(bf16)
        persist_k_total = jnp.zeros(persist_k.shape[1:], f32)
        persist_v_total = jnp.zeros(persist_k.shape[1:], f32)
        for i in range(parts):
            span = block_of(i)
            seen = (i + 1) * rows
            query = ordered[span, col:col + size]
            rise = upstream[span, col:col + size]
            scores = masked_scores(h, i, query)
            extra = dot_nt(persist_k[h], query)
            base = log_total[h:h + 1, span]
            probs = jnp.exp2(scores * (factor * log2_e) - base)
            probs_extra = jnp.exp2(extra * (factor * log2_e) - base)
            probs_grad = dot_nt(ordered[:seen, 2 * cols + col:2 * cols + col + size], rise)
            extra_grad = dot_nt(persist_v[h], rise)
            weighted = probs * probs_grad
            weighted_extra = probs_extra * extra_grad
            inner_sum = jnp.sum(weighted, axis=0, keepdims=True) + jnp.sum(weighted_extra, axis=0, keepdims=True)
            scores_grad = (weighted - probs * inner_sum).astype(bf16)
            scores_extra = (weighted_extra - probs_extra * inner_sum).astype(bf16)
            query_t = dot_nn(key_t[:, :seen], scores_grad) + dot_nn(persist_t, scores_extra)
            query_sum[span, :] += query_t.T * factor
            key_sum[:seen, :] += dot_nn(scores_grad, query) * factor
            value_sum[:seen, :] += dot_nn(probs.astype(bf16), rise)
            persist_k_total += dot_nn(scores_extra, query) * factor
            persist_v_total += dot_nn(probs_extra.astype(bf16), rise)
            rounds.tick(pace[5])
        small[shared + h * many:shared + (h + 1) * many, :] = persist_k_total
        small[shared + (heads + h) * many:shared + (heads + h + 1) * many, :] = persist_v_total
        for b in range(parts):
            target = true_rows(b)
            qkv_grad[target, col:col + size] = query_sum[block_of(b), :].astype(bf16)
            qkv_grad[target, cols + col:cols + col + size] = key_sum[block_of(b), :].astype(bf16)
            qkv_grad[target, 2 * cols + col:2 * cols + col + size] = value_sum[block_of(b), :].astype(bf16)

    branch = scatter.finish()
    note(4, branch * branch)
    value = middle[...] + branch
    note(2, value * value)
    result[...] = value.astype(bf16)

    for b in range(parts):
        span = block_of(b)
        grad = dot_tn(normed_attn[:, span], qkv_grad[...])
        wide_source[span, :] = grad.astype(bf16)
        gain_row = jnp.sum((grad * w_qkv[span, :].astype(f32)).T, axis=0, keepdims=True) / gain_attn[:, span]
        for k in range(rows // size):
            row = b * (rows // size) + k
            small[row:row + 1, :] = gain_row[:, k * size:(k + 1) * size]
        rounds.tick(pace[6])
    rounds.add(rings[4], small_sum)
    scatter = Scatter(sent_b, landed_b, hold, move_send.at[7], move_recv.at[7])
    scatter.begin(lambda b: dot_nt(qkv_grad[block_of(b), :], w_qkv[...]))
    rounds.tick(pace[7])
    normed_grad = scatter.finish()
    value = inputs[...].astype(f32)
    scale = rows_scale(value)
    weighted = normed_grad * gain_attn[...]
    input_grad[...] = (
        middle_grad[...] + scale * weighted
        - value * (scale * scale * scale) * jnp.mean(weighted * value, axis=-1, keepdims=True)
    ).astype(bf16)
    rounds.finish()


def whole_layer(
    length, momentum, decay, step_size, inputs, cotangent, gain_attn, gain_ffn, persist_k, persist_v,
    w_query, w_key, w_value, w_out, w_gate, w_up, w_down, count, parts,
):
    heads, many, size = persist_k.shape
    blocks = momentum.shape[0]
    cols = heads * size
    rows, width = inputs.shape
    seq_len = rows * parts
    units = w_gate.shape[0]
    shared = 2 * width // size + 8
    small_rows = shared + 2 * heads * many
    flows = len(bits_below(count)) + len(bits_below(parts))

    def row_slots(*shape):
        return pltpu.VMEM((2, count - 1, shape[0] // (2 * count), shape[1]), bf16)

    def col_slots(*shape):
        return pltpu.VMEM((2, count - 1, shape[0] // 2, shape[1] // count), bf16)

    def low(*shape):
        return pltpu.VMEM(shape, bf16)

    def full(*shape):
        return pltpu.VMEM(shape, f32)

    def semaphores(*shape):
        return pltpu.SemaphoreType.DMA(shape)

    ffn = (units, width)
    return pl.pallas_call(
        functools.partial(layer_kernel, heads, blocks, parts, count, shared, pace),
        out_shape=(
            jax.ShapeDtypeStruct(ffn, bf16),
            jax.ShapeDtypeStruct(ffn, bf16),
            jax.ShapeDtypeStruct(ffn, bf16),
            jax.ShapeDtypeStruct((width, 3 * cols), bf16),
            jax.ShapeDtypeStruct((cols, width), bf16),
            jax.ShapeDtypeStruct((small_rows, size), f32),
            jax.ShapeDtypeStruct((rows, width), bf16),
            jax.ShapeDtypeStruct((rows, width), bf16),
        ),
        in_specs=[smem()] * 4 + [vmem()] * 6 + [pl.BlockSpec(memory_space=pl.ANY)] * 7,
        out_specs=(vmem(),) * 8,
        scratch_shapes=[
            low(width, 3 * cols), low(cols, width), low(*ffn), low(*ffn), low(*ffn),
            low(seq_len, width), low(seq_len, 3 * cols), low(seq_len, cols),
            low(heads, blocks, size, size), full(heads, blocks, size, size), full(heads, seq_len),
            full(rows, width), full(rows, width), full(rows, width), low(seq_len, width), low(seq_len, width),
            low(units, seq_len), low(units, seq_len), low(units, seq_len),
            low(*ffn), low(*ffn), low(*ffn), low(width, 3 * cols), low(cols, width),
            col_slots(*ffn), col_slots(*ffn), col_slots(*ffn), row_slots(width, 3 * cols), col_slots(cols, width),
            full(flows, small_rows, size),
            low(3, rows, width), low(3, rows, width), low(3, rows, width), low(3, rows, width),
            low(seq_len, width), low(seq_len, cols), low(heads, blocks, size, size),
            full(seq_len, size), full(seq_len, size), full(seq_len, size), low(seq_len, 3 * cols),
            semaphores(7), semaphores(5, 2, 2 * count - 2), semaphores(5, 2, 2 * count - 2),
            semaphores(flows), semaphores(flows), semaphores(8, 3), semaphores(8, 3),
        ],
        compiler_params=pltpu.CompilerParams(
            vmem_limit_bytes=layer_limit, collective_id=0, has_side_effects=True
        ),
        cost_estimate=pl.CostEstimate(flops=150_000_000_000, bytes_accessed=40_000_000, transcendentals=4_000_000),
        name="whole_layer",
    )(
        length, momentum, decay, step_size, inputs, cotangent, gain_attn, gain_ffn, persist_k, persist_v,
        w_query, w_key, w_value, w_out, w_gate, w_up, w_down,
    )


pace = (4, 4, 1, 4, 1, 1, 1, 6)
layer_limit = 63 << 20


def swap(value, axis, bit):
    count = lax.axis_size(axis)
    return lax.ppermute(value, axis, [(i, i ^ bit) for i in range(count)])


def norm_back(value, scale, gain, upstream):
    weighted = upstream * gain
    return scale * weighted - value * (scale * scale * scale) * jnp.mean(
        weighted * value, axis=-1, keepdims=True
    )


def gather_rows(own):
    far = swap(own, "tensor", 2)
    near = swap(own, "tensor", 1)
    both = swap(far, "tensor", 1)
    return jnp.concatenate([own, near], 0), jnp.concatenate([far, both], 0)


def scatter_rows(near, far):
    rows = near.shape[0] // 2
    far_sum = far[:rows] + swap(far[rows:].astype(bf16), "tensor", 1).astype(f32)
    far_in = swap(far_sum.astype(bf16), "tensor", 2).astype(f32)
    near_in = swap(near[rows:].astype(bf16), "tensor", 1).astype(f32)
    return near[:rows] + near_in + far_in


def mul(left, right):
    return jnp.dot(left, right, preferred_element_type=f32)


def mul_nt(left, right):
    return jnp.einsum("ab,cb->ac", left, right, preferred_element_type=f32)


def mul_tn(left, right):
    return jnp.einsum("ab,ac->bc", left, right, preferred_element_type=f32)


def fits_ring(count, parts, *shapes):
    if count & (count - 1) or parts != 4 or count < 4:
        return False
    return all(rows % (32 * count) == 0 or (rows % 32 == 0 and cols % (128 * count) == 0) for rows, cols in shapes)


def body(
    inputs, cotangent, lengths, gain_attn, w_query, w_key, w_value, w_out, persist_keys, persist_values,
    gain_ffn, w_gate, w_up, w_down, momentum, decay, step_size,
):
    parts = lax.axis_size("tensor")
    count = lax.axis_size("dp")
    rows = inputs.shape[1]
    width = inputs.shape[2]
    half = 2 * rows
    cols = w_query.shape[1]
    size = persist_keys.shape[2]
    place = lax.axis_index("tensor")
    first_row = place * rows
    own_valid = (first_row + jnp.arange(rows, dtype=jnp.int32) < lengths[0]).astype(f32)[:, None]
    places = place.astype(jnp.int32).reshape(1)
    rates = (places, lengths, momentum[0], decay[0], step_size[0])

    if fits_ring(count, parts, (w_down.shape), (width, 3 * cols), (cols, width)):
        gate_sum, up_sum, down_sum, wide, out_sum, small, result, input_grad = whole_layer(
            *rates[1:], inputs[0], cotangent[0], gain_attn[None], gain_ffn[None], persist_keys, persist_values,
            w_query, w_key, w_value, w_out, w_gate.T, w_up.T, w_down, count, parts,
        )
        shared = small.shape[0] - 2 * persist_keys.shape[0] * persist_keys.shape[1]
        persist_sums = small[shared:].reshape((2,) + persist_keys.shape)
        squares = small[2 * width // size:2 * width // size + 6, 0]
        gains = small[:2 * width // size].reshape(-1)
    else:
        resid = inputs[0].astype(f32)
        scale_attn = rows_scale(resid)
        near, far = gather_rows((resid * scale_attn * gain_attn).astype(bf16))
        w_qkv = jnp.concatenate([w_query, w_key, w_value], 1)
        qkv = jnp.concatenate([mul(near, w_qkv).astype(bf16), mul(far, w_qkv).astype(bf16)], 0)
        normed_attn = jnp.concatenate([near, far], 0)
        mixed, log_total, states, grams = attend_and_recall(*rates, qkv, persist_keys, persist_values, parts)
        branch_attn = scatter_rows(mul(mixed[:half], w_out), mul(mixed[half:], w_out))
        middle = resid + branch_attn
        scale_ffn = rows_scale(middle)
        normed_ffn = jnp.concatenate(gather_rows((middle * scale_ffn * gain_ffn).astype(bf16)), 0)

        out_grad = cotangent[0].astype(f32) * own_valid
        out_full = jnp.concatenate(gather_rows(out_grad.astype(bf16)), 0)
        gate = mul(normed_ffn, w_gate)
        up = mul(normed_ffn, w_up)
        sigmoid = jax.nn.sigmoid(gate)
        silu = gate * sigmoid
        hidden = (silu * up).astype(bf16)
        branch_ffn = scatter_rows(mul(hidden[:half], w_down), mul(hidden[half:], w_down))
        result = middle + branch_ffn
        hidden_grad = mul_nt(out_full, w_down)
        gate_grad = (hidden_grad * up * sigmoid * (1.0 + gate * (1.0 - sigmoid))).astype(bf16)
        up_grad = (hidden_grad * silu).astype(bf16)

        def masked(value_in):
            return jnp.sum(own_valid * (value_in * value_in))

        squares = jnp.stack(
            [masked(resid), masked(middle), masked(result), masked(branch_attn), masked(branch_ffn), jnp.sum(own_valid)]
        )
        grad_down = mul_tn(hidden, out_full).astype(bf16)
        grad_gate = mul_tn(gate_grad, normed_ffn).astype(bf16)
        grad_up = mul_tn(up_grad, normed_ffn).astype(bf16)
        normed_ffn_grad = scatter_rows(
            mul_nt(gate_grad[:half], w_gate) + mul_nt(up_grad[:half], w_up),
            mul_nt(gate_grad[half:], w_gate) + mul_nt(up_grad[half:], w_up),
        )
        gain_ffn_part = jnp.sum(normed_ffn_grad * middle * scale_ffn, axis=0)
        middle_grad = out_grad + norm_back(middle, scale_ffn, gain_ffn, normed_ffn_grad)
        middle_full = jnp.concatenate(gather_rows(middle_grad.astype(bf16)), 0)
        mixed_grad = mul_nt(middle_full, w_out).astype(bf16)
        qkv_grad, persist_k_grad, persist_v_grad = attend_and_recall_back(
            *rates, qkv, mixed_grad, persist_keys, persist_values, log_total, states, grams, parts
        )
        normed_attn_grad = scatter_rows(mul_nt(qkv_grad[:half], w_qkv), mul_nt(qkv_grad[half:], w_qkv))
        gain_attn_part = jnp.sum(normed_attn_grad * resid * scale_attn, axis=0)
        input_grad = (middle_grad + norm_back(resid, scale_attn, gain_attn, normed_attn_grad)).astype(bf16)
        gate_sum, up_sum, down_sum, wide, out_sum, persist_sums = lax.psum(
            (grad_gate, grad_up, grad_down, mul_tn(normed_attn, qkv_grad).astype(bf16),
             mul_tn(mixed, middle_full).astype(bf16), jnp.stack([persist_k_grad, persist_v_grad])), "dp"
        )
        gains, squares = lax.psum((jnp.concatenate([gain_attn_part, gain_ffn_part]), squares), ("dp", "tensor"))
    rms_stats = jnp.sqrt(squares[:5] / (squares[5] * width))
    wide = wide.astype(f32)
    return (
        result.astype(bf16)[None],
        input_grad[None],
        gains[:width],
        wide[:, :cols],
        wide[:, cols:2 * cols],
        wide[:, 2 * cols:],
        out_sum.astype(f32),
        persist_sums[0],
        persist_sums[1],
        gains[width:],
        gate_sum.astype(f32).T,
        up_sum.astype(f32).T,
        down_sum.astype(f32),
        rms_stats,
    )


def solution(mesh):
    in_specs = (
        P("dp", "tensor", None),
        P("dp", "tensor", None),
        P("dp"),
        P(),
        P(None, "tensor"),
        P(None, "tensor"),
        P(None, "tensor"),
        P("tensor", None),
        P("tensor", None, None),
        P("tensor", None, None),
        P(),
        P(None, "tensor"),
        P(None, "tensor"),
        P("tensor", None),
        P("dp", None, "tensor"),
        P("dp", None, "tensor"),
        P("dp", None, "tensor"),
    )
    out_specs = (
        P("dp", "tensor", None),
        P("dp", "tensor", None),
        P(),
        P(None, "tensor"),
        P(None, "tensor"),
        P(None, "tensor"),
        P("tensor", None),
        P("tensor", None, None),
        P("tensor", None, None),
        P(),
        P(None, "tensor"),
        P(None, "tensor"),
        P("tensor", None),
        P(),
    )
    return jax.shard_map(body, mesh=mesh, in_specs=in_specs, out_specs=out_specs, check_vma=False)
```

```python
import functools
import jax
import jax.numpy as jnp
from jax import lax
from jax.sharding import PartitionSpec as P
import jax.experimental.pallas as pl
import jax.experimental.pallas.tpu as pltpu

norm_eps = 1e-05
unit_eps = 1e-06
f32 = jnp.float32
bf16 = jnp.bfloat16
log2_e = 1.4426950408889634


def dot_nn(left, right):
    return lax.dot_general(left, right, (((1,), (0,)), ((), ())), preferred_element_type=f32)


def dot_nt(left, right):
    return lax.dot_general(left, right, (((1,), (1,)), ((), ())), preferred_element_type=f32)


def dot_tn(left, right):
    return lax.dot_general(left, right, (((0,), (0,)), ((), ())), preferred_element_type=f32)


def halves(value):
    high = value.astype(bf16)
    return high, (value - high.astype(f32)).astype(bf16)


def dot3(dot, left, right):
    (lh, ll), (rh, rl) = left, right
    return dot(lh, rh) + dot(ll, rh) + dot(lh, rl)


def unit_rows(value):
    wide = value.astype(f32)
    scale = lax.rsqrt(jnp.sum(wide * wide, axis=-1, keepdims=True) + unit_eps)
    return wide * scale, scale


def block_rows(start, width):
    return pl.ds(pl.multiple_of(start, width), width)


def forward_kernel(
    heads, blocks, parts,
    place, length, momentum, decay, step_size, qkv, persist_k, persist_v,
    mixed, log_total, states, grams,
    ordered, reads,
):
    seq_len, wide = qkv.shape
    size = persist_k.shape[2]
    cols = heads * size
    rows = seq_len // parts
    width = seq_len // blocks
    me = place[0]
    count = length[0]
    for b in range(parts):
        ordered[b * rows:(b + 1) * rows, :] = qkv[block_rows(jnp.bitwise_xor(me, b) * rows, rows), :]

    carried = [(jnp.zeros((size, size), f32), jnp.zeros((size, size), f32)) for _ in range(heads)]
    for c in range(blocks):
        span = slice(c * width, (c + 1) * width)
        live = (c * width + lax.broadcasted_iota(jnp.int32, (width, 1), 0) < count).astype(f32)
        for h in range(heads):
            col = h * size
            key_unit, _ = unit_rows(ordered[span, cols + col:cols + col + size])
            query_unit, _ = unit_rows(ordered[span, col:col + size])
            value = ordered[span, 2 * cols + col:2 * cols + col + size]
            key_h, key_l = halves(key_unit)
            live_h, live_l = halves(key_unit * live)
            gram = dot3(dot_tn, (live_h, live_l), (key_h, key_l))
            target = dot_tn(value, live_h) + dot_tn(value, live_l)
            memory, velocity = carried[h]
            states[h, c] = memory.astype(bf16)
            grams[h, c] = gram
            parts_m = halves(memory)
            reads[span, col:col + size] = dot_nt(query_unit.astype(bf16), parts_m[0])
            change = dot3(dot_nn, parts_m, halves(gram)) - target
            velocity = momentum[c, h] * velocity - step_size[c, h] * change
            memory = (1.0 - decay[c, h]) * memory + velocity
            carried[h] = (memory, velocity)

    factor = size ** (-0.5) * log2_e
    diagonal = lax.broadcasted_iota(jnp.int32, (rows, rows), 0) <= lax.broadcasted_iota(jnp.int32, (rows, rows), 1)
    for h in range(heads):
        col = h * size
        value_t = ordered[:, 2 * cols + col:2 * cols + col + size].T
        persist_t = persist_v[h].astype(f32).T.astype(bf16)
        for i in range(parts):
            span = slice(i * rows, (i + 1) * rows)
            seen = (i + 1) * rows
            query = ordered[span, col:col + size]
            scores = dot_nt(ordered[:seen, cols + col:cols + col + size], query)
            last = jnp.where(diagonal, scores[seen - rows:], -1e30)
            scores = last if i == 0 else jnp.concatenate([scores[:seen - rows], last], axis=0)
            extra = dot_nt(persist_k[h], query)
            top = jnp.maximum(jnp.max(scores, axis=0, keepdims=True), jnp.max(extra, axis=0, keepdims=True))
            lifted = jnp.exp2((scores - top) * factor)
            lifted_extra = jnp.exp2((extra - top) * factor)
            total = jnp.sum(lifted, axis=0, keepdims=True) + jnp.sum(lifted_extra, axis=0, keepdims=True)
            attended = dot_nn(value_t[:, :seen], lifted.astype(bf16)) + dot_nn(persist_t, lifted_extra.astype(bf16))
            attended = attended * (1.0 / total)
            log_total[h:h + 1, span] = top * factor + jnp.log2(total)
            together = attended.T + reads[span, col:col + size]
            mixed[block_rows(jnp.bitwise_xor(me, i) * rows, rows), col:col + size] = together.astype(bf16)


def backward_kernel(
    heads, blocks, parts,
    place, length, momentum, decay, step_size, qkv, mixed_grad, persist_k, persist_v,
    log_total, states, grams,
    qkv_grad, persist_k_grad, persist_v_grad,
    ordered, upstream, slopes, key_sum, value_sum, query_sum,
):
    seq_len, wide = qkv.shape
    size = persist_k.shape[2]
    cols = heads * size
    rows = seq_len // parts
    width = seq_len // blocks
    me = place[0]
    count = length[0]
    for b in range(parts):
        source = block_rows(jnp.bitwise_xor(me, b) * rows, rows)
        ordered[b * rows:(b + 1) * rows, :] = qkv[source, :]
        upstream[b * rows:(b + 1) * rows, :] = mixed_grad[source, :]

    carried = [(jnp.zeros((size, size), f32), jnp.zeros((size, size), f32)) for _ in range(heads)]
    for c in reversed(range(blocks)):
        span = slice(c * width, (c + 1) * width)
        for h in range(heads):
            col = h * size
            query_unit, _ = unit_rows(ordered[span, col:col + size])
            query_h, query_l = halves(query_unit)
            rise = upstream[span, col:col + size]
            entry = dot_tn(rise, query_h) + dot_tn(rise, query_l)
            memory, velocity = carried[h]
            velocity = velocity + memory
            change = (-step_size[c, h]) * velocity
            slopes[h, c] = change
            memory = (1.0 - decay[c, h]) * memory + entry + dot3(dot_nn, halves(change), halves(grams[h, c]))
            velocity = momentum[c, h] * velocity
            carried[h] = (memory, velocity)

    for h in range(heads):
        col = h * size
        for c in range(blocks):
            span = slice(c * width, (c + 1) * width)
            live = (c * width + lax.broadcasted_iota(jnp.int32, (width, 1), 0) < count).astype(f32)
            query_unit, query_scale = unit_rows(ordered[span, col:col + size])
            key_unit, key_scale = unit_rows(ordered[span, cols + col:cols + col + size])
            value = ordered[span, 2 * cols + col:2 * cols + col + size].astype(f32)
            rise = upstream[span, col:col + size]
            state = states[h, c]
            slope = slopes[h, c].astype(bf16)
            key_b = key_unit.astype(bf16)
            error = (dot_nt(key_b, state) - value) * live
            error_grad = dot_nt(key_b, slope) * live
            unit_grad = dot_nn(error.astype(bf16), slope) + dot_nn(error_grad.astype(bf16), state)
            key_sum[span, :] = key_scale * (unit_grad - key_unit * jnp.sum(unit_grad * key_unit, axis=-1, keepdims=True))
            value_sum[span, :] = -error_grad
            read_grad = dot_nn(rise, state)
            query_sum[span, :] = query_scale * (read_grad - query_unit * jnp.sum(read_grad * query_unit, axis=-1, keepdims=True))

        factor = size ** (-0.5)
        diagonal = lax.broadcasted_iota(jnp.int32, (rows, rows), 0) <= lax.broadcasted_iota(jnp.int32, (rows, rows), 1)
        key_t = ordered[:, cols + col:cols + col + size].T
        persist_t = persist_k[h].astype(f32).T.astype(bf16)
        persist_k_total = jnp.zeros(persist_k.shape[1:], f32)
        persist_v_total = jnp.zeros(persist_k.shape[1:], f32)
        for i in range(parts):
            span = slice(i * rows, (i + 1) * rows)
            seen = (i + 1) * rows
            query = ordered[span, col:col + size]
            rise = upstream[span, col:col + size]
            scores = dot_nt(ordered[:seen, cols + col:cols + col + size], query)
            last = jnp.where(diagonal, scores[seen - rows:], -1e30)
            scores = last if i == 0 else jnp.concatenate([scores[:seen - rows], last], axis=0)
            extra = dot_nt(persist_k[h], query)
            base = log_total[h:h + 1, span]
            probs = jnp.exp2(scores * (factor * log2_e) - base)
            probs_extra = jnp.exp2(extra * (factor * log2_e) - base)
            probs_grad = dot_nt(ordered[:seen, 2 * cols + col:2 * cols + col + size], rise)
            extra_grad = dot_nt(persist_v[h], rise)
            weighted = probs * probs_grad
            weighted_extra = probs_extra * extra_grad
            inner = jnp.sum(weighted, axis=0, keepdims=True) + jnp.sum(weighted_extra, axis=0, keepdims=True)
            scores_grad = (weighted - probs * inner).astype(bf16)
            scores_extra = (weighted_extra - probs_extra * inner).astype(bf16)
            query_t = dot_nn(key_t[:, :seen], scores_grad) + dot_nn(persist_t, scores_extra)
            query_sum[span, :] += query_t.T * factor
            key_sum[:seen, :] += dot_nn(scores_grad, query) * factor
            value_sum[:seen, :] += dot_nn(probs.astype(bf16), rise)
            persist_k_total += dot_nn(scores_extra, query) * factor
            persist_v_total += dot_nn(probs_extra.astype(bf16), rise)
        persist_k_grad[h] = persist_k_total
        persist_v_grad[h] = persist_v_total
        for b in range(parts):
            span = slice(b * rows, (b + 1) * rows)
            target = block_rows(jnp.bitwise_xor(me, b) * rows, rows)
            qkv_grad[target, col:col + size] = query_sum[span, :].astype(bf16)
            qkv_grad[target, cols + col:cols + col + size] = key_sum[span, :].astype(bf16)
            qkv_grad[target, 2 * cols + col:2 * cols + col + size] = value_sum[span, :].astype(bf16)


vmem = functools.partial(pl.BlockSpec, memory_space=pltpu.VMEM)
smem = functools.partial(pl.BlockSpec, memory_space=pltpu.SMEM)
vmem_limit = 56 << 20


def attend_and_recall(place, length, momentum, decay, step_size, qkv, persist_k, persist_v, parts):
    heads, _, size = persist_k.shape
    seq_len = qkv.shape[0]
    blocks = momentum.shape[0]
    cols = heads * size
    return pl.pallas_call(
        functools.partial(forward_kernel, heads, blocks, parts),
        out_shape=(
            jax.ShapeDtypeStruct((seq_len, cols), bf16),
            jax.ShapeDtypeStruct((heads, seq_len), f32),
            jax.ShapeDtypeStruct((heads, blocks, size, size), bf16),
            jax.ShapeDtypeStruct((heads, blocks, size, size), f32),
        ),
        in_specs=[smem()] * 5 + [vmem()] * 3,
        out_specs=(vmem(),) * 4,
        scratch_shapes=[pltpu.VMEM((seq_len, 3 * cols), bf16), pltpu.VMEM((seq_len, cols), f32)],
        compiler_params=pltpu.CompilerParams(vmem_limit_bytes=vmem_limit),
        cost_estimate=pl.CostEstimate(flops=12_000_000_000, bytes_accessed=8_000_000, transcendentals=2_000_000),
        name="attend_recall",
    )(place, length, momentum, decay, step_size, qkv, persist_k, persist_v)


def attend_and_recall_back(
    place, length, momentum, decay, step_size, qkv, mixed_grad, persist_k, persist_v, log_total, states, grams, parts
):
    heads, persistent, size = persist_k.shape
    seq_len = qkv.shape[0]
    blocks = momentum.shape[0]
    cols = heads * size
    return pl.pallas_call(
        functools.partial(backward_kernel, heads, blocks, parts),
        out_shape=(
            jax.ShapeDtypeStruct((seq_len, 3 * cols), bf16),
            jax.ShapeDtypeStruct((heads, persistent, size), f32),
            jax.ShapeDtypeStruct((heads, persistent, size), f32),
        ),
        in_specs=[smem()] * 5 + [vmem()] * 7,
        out_specs=(vmem(),) * 3,
        scratch_shapes=[
            pltpu.VMEM((seq_len, 3 * cols), bf16),
            pltpu.VMEM((seq_len, cols), bf16),
            pltpu.VMEM((heads, blocks, size, size), f32),
            pltpu.VMEM((seq_len, size), f32),
            pltpu.VMEM((seq_len, size), f32),
            pltpu.VMEM((seq_len, size), f32),
        ],
        compiler_params=pltpu.CompilerParams(vmem_limit_bytes=vmem_limit),
        cost_estimate=pl.CostEstimate(flops=25_000_000_000, bytes_accessed=12_000_000, transcendentals=2_000_000),
        name="attend_recall_back",
    )(place, length, momentum, decay, step_size, qkv, mixed_grad, persist_k, persist_v, log_total, states, grams)


def ring_place(index, count):
    odd = index % 2
    return (1 - odd) * (index // 2) + odd * (count - 1 - index // 2)


def ring_index(place, count):
    late = place // (count // 2)
    return (1 - late) * (2 * place) + late * (2 * (count - 1 - place) + 1)


def flip(index, bit):
    return index + bit * (1 - 2 * ((index // bit) % 2))


def bits_below(count):
    return [1 << k for k in range(count.bit_length() - 1)]


def relative(index, block):
    for bit in (1, 2):
        if block & bit:
            index = flip(index, bit)
    return index


def remote(source, target, send_sem, recv_sem, device):
    return pltpu.make_async_remote_copy(
        src_ref=source, dst_ref=target, send_sem=send_sem, recv_sem=recv_sem,
        device_id=device, device_id_type=pl.DeviceIdType.MESH,
    )


class Ring:
    def __init__(self, count, by_rows, source, out, slots, send_sem, recv_sem):
        self.count, self.by_rows = count, by_rows
        self.source, self.out, self.slots = source, out, slots
        self.send_sem, self.recv_sem = send_sem, recv_sem
        index = lax.axis_index("dp")
        self.place = ring_place(index, count)
        self.peers = (
            {"dp": ring_index((self.place + 1) % count, count)},
            {"dp": ring_index((self.place + count - 1) % count, count)},
        )
        self.step = 0
        self.copies = [None, None]
        self.sent = []

    def piece(self, ref, way, chunk):
        rows, cols = ref.shape
        chunk = chunk % self.count
        if self.by_rows:
            size = rows // (2 * self.count)
            return ref.at[pl.ds(pl.multiple_of(chunk * (2 * size) + way * size, size), size), :]
        size, width = rows // 2, cols // self.count
        return ref.at[way * size:(way + 1) * size, pl.ds(pl.multiple_of(chunk * width, width), width)]

    def chunk(self, way, step):
        return self.place + self.count + (2 * self.count - step if way == 0 else step)

    def launch(self, way, step, source, target):
        copy = remote(source, target, self.send_sem.at[way, step], self.recv_sem.at[way, step], self.peers[way])
        copy.start()
        self.copies[way] = copy
        self.sent.append(copy)

    def start(self):
        for way in range(2):
            self.launch(way, 0, self.piece(self.source, way, self.chunk(way, 0)), self.slots.at[way, 0])

    def advance(self):
        count, step = self.count, self.step
        for way in range(2):
            self.copies[way].wait_recv()
            if step < count - 1:
                chunk = self.chunk(way, step + 1)
                total = self.slots[way, step].astype(f32) + self.piece(self.source, way, chunk)[...].astype(f32)
                if step < count - 2:
                    self.slots[way, step] = total.astype(bf16)
                    source, target = self.slots.at[way, step], self.slots.at[way, step + 1]
                else:
                    source = target = self.piece(self.out, way, chunk)
                    source[...] = total.astype(bf16)
            else:
                source = target = self.piece(self.out, way, self.chunk(way, step + 1 - count))
            if step < 2 * count - 3:
                self.launch(way, step + 1, source, target)
        self.step += 1
        if self.step < 2 * count - 2:
            return True
        for copy in self.sent:
            copy.wait_send()
        return False


class SmallSum:
    def __init__(self, value, slots, shared, send_sem, recv_sem, count, parts):
        self.value, self.slots, self.shared = value, slots, shared
        self.send_sem, self.recv_sem = send_sem, recv_sem
        index, inner = lax.axis_index("dp"), lax.axis_index("tensor")
        self.inner = len(bits_below(parts))
        self.peers = [{"tensor": flip(inner, bit)} for bit in bits_below(parts)]
        self.peers += [{"dp": flip(index, bit)} for bit in bits_below(count)]
        self.step = 0

    def start(self):
        used = slice(0, self.shared if self.step < self.inner else self.value.shape[0])
        self.used = used
        self.copy = remote(
            self.value.at[used], self.slots.at[self.step, used], self.send_sem.at[self.step],
            self.recv_sem.at[self.step], self.peers[self.step],
        )
        self.copy.start()

    def advance(self):
        self.copy.wait()
        self.value[self.used] += self.slots[self.step, self.used]
        self.step += 1
        if self.step < len(self.peers):
            self.start()
        return self.step < len(self.peers)


class Rounds:
    def __init__(self):
        self.queue = []

    def add(self, *flows):
        for flow in flows:
            flow.start()
            self.queue.append(flow)

    def tick(self, count=1):
        for _ in range(count):
            if self.queue:
                flow = self.queue.pop(0)
                if flow.advance():
                    self.queue.append(flow)

    def finish(self):
        while self.queue:
            self.tick()


def rows_scale(value):
    return lax.rsqrt(jnp.mean(value * value, axis=-1, keepdims=True) + norm_eps)


class Scatter:
    def __init__(self, sent, landed, hold, send_sem, recv_sem):
        self.sent, self.landed, self.hold = sent, landed, hold
        self.send_sem, self.recv_sem = send_sem, recv_sem
        self.rows = hold.shape[0] // 2
        inner = lax.axis_index("tensor")
        self.sibling, self.across = {"tensor": flip(inner, 1)}, {"tensor": flip(inner, 2)}

    def span(self, j):
        return slice(j * self.rows, (j + 1) * self.rows)

    def copy(self, k, j, device):
        return remote(
            self.sent.at[k, self.span(j)], self.landed.at[k, self.span(j)],
            self.send_sem.at[k, j], self.recv_sem.at[k, j], device,
        )

    def begin(self, block, tick):
        first = [self.copy(0, j, self.sibling) for j in range(2)]
        self.second = [self.copy(1, j, self.across) for j in range(2)]
        self.third = [self.copy(2, j, self.sibling) for j in range(2)]
        for j in range(2):
            self.sent[0, self.span(j)] = block(3, j).astype(bf16)
            first[j].start()
        for j in range(2):
            self.hold[self.span(j), :] = block(2, j)
        tick()
        for j in range(2):
            first[j].wait()
            self.sent[1, self.span(j)] = (
                self.hold[self.span(j), :] + self.landed[0, self.span(j)].astype(f32)
            ).astype(bf16)
            self.second[j].start()
        for j in range(2):
            self.sent[2, self.span(j)] = block(1, j).astype(bf16)
            self.third[j].start()
        tick()
        for j in range(2):
            self.hold[self.span(j), :] = block(0, j)

    def finish(self, j):
        span = self.span(j)
        self.third[j].wait()
        self.second[j].wait()
        return self.hold[span, :] + self.landed[2, span].astype(f32) + self.landed[1, span].astype(f32)


class Gather:
    def __init__(self, full, parts, send_sem, recv_sem):
        self.full, self.rows = full, full.shape[0] // (2 * parts)
        self.send_sem, self.recv_sem = send_sem, recv_sem
        inner = lax.axis_index("tensor")
        self.sibling, self.across = {"tensor": flip(inner, 1)}, {"tensor": flip(inner, 2)}
        self.far, self.near, self.both = [None] * 2, [None] * 2, [None] * 2

    def copy(self, source, target, k, j, device):
        def piece(b):
            first = (2 * b + j) * self.rows
            return self.full.at[first:first + self.rows, :]

        return remote(piece(source), piece(target), self.send_sem.at[k, j], self.recv_sem.at[k, j], device)

    def begin(self, j):
        self.far[j], self.near[j] = self.copy(0, 2, 0, j, self.across), self.copy(0, 1, 1, j, self.sibling)
        self.far[j].start()
        self.near[j].start()

    def forward(self):
        for j in range(2):
            self.far[j].wait()
            self.both[j] = self.copy(2, 3, 2, j, self.sibling)
            self.both[j].start()

    def wait(self, copies):
        for copy in copies:
            copy.wait()


def layer_kernel(
    heads, blocks, parts, count, shared, pace,
    length, momentum, decay, step_size,
    inputs, cotangent, gain_attn, gain_ffn, persist_k, persist_v,
    w_query_h, w_key_h, w_value_h, w_out_h, w_gate_h, w_up_h, w_down_h,
    gate_out, up_out, down_out, query_out, key_out, value_out, out_out, small, result, input_grad,
    w_qkv, w_out, w_gate, w_up, w_down,
    normed_attn, ordered, mixed, states, grams, log_total,
    middle, hold, middle_grad, normed_ffn, out_full, gate_grad, up_grad, hidden,
    gate_source, up_source, down_source, query_source, key_source, value_source, out_source,
    gate_slots, up_slots, down_slots, query_slots, key_slots, value_slots, out_slots, small_slots,
    sent_a, landed_a, sent_b, landed_b, middle_full, upstream, slopes, key_sum, value_sum, query_sum, qkv_grad,
    load_sem, ring_send, ring_recv, small_send, small_recv, move_send, move_recv,
):
    size = persist_k.shape[2]
    many = persist_k.shape[1]
    cols = heads * size
    seq_len, width = middle_full.shape
    units = gate_grad.shape[0]
    rows = seq_len // parts
    span_rows = seq_len // blocks
    inner = lax.axis_index("tensor")
    valid_count = length[0]
    factor = size ** (-0.5)

    rounds = Rounds()
    rings = [
        Ring(count, by_rows, source, out, slots, ring_send.at[k], ring_recv.at[k])
        for k, (by_rows, source, out, slots) in enumerate((
            (False, down_source, down_out, down_slots),
            (False, gate_source, gate_out, gate_slots),
            (False, up_source, up_out, up_slots),
            (False, out_source, out_out, out_slots),
            (True, query_source, query_out, query_slots),
            (True, key_source, key_out, key_slots),
            (True, value_source, value_out, value_slots),
        ))
    ]
    small_sum = SmallSum(small, small_slots, shared, small_send, small_recv, count, parts)
    barrier = pltpu.get_barrier_semaphore()
    peers = list(rings[0].peers) + small_sum.peers
    for peer in peers:
        pl.semaphore_signal(barrier, inc=1, device_id=peer, device_id_type=pl.DeviceIdType.MESH)

    loads = []

    def load(source, target):
        copy = pltpu.make_async_copy(source, target, load_sem.at[len(loads)])
        copy.start()
        loads.append(copy)
        return copy

    qkv_loads = [
        load(source, w_qkv.at[:, k * cols:(k + 1) * cols]) for k, source in enumerate((w_query_h, w_key_h, w_value_h))
    ]
    out_load = load(w_out_h, w_out)
    ffn_loads = [load(w_gate_h, w_gate), load(w_up_h, w_up), load(w_down_h, w_down)]

    def true_rows(b):
        return pl.ds(pl.multiple_of(relative(inner, b) * rows, rows), rows)

    def block_of(b):
        return slice(b * rows, (b + 1) * rows)

    row_place = inner * rows + lax.broadcasted_iota(jnp.int32, (rows, 1), 0)
    own_valid = (row_place < valid_count).astype(f32)
    stat_row = 2 * width // size

    def half_rows(j):
        return slice(j * (rows // 2), (j + 1) * (rows // 2))

    def part_of(b, j):
        return slice((2 * b + j) * (rows // 2), (2 * b + j + 1) * (rows // 2))

    def note(k, value, j):
        total = jnp.sum(jnp.sum(value, axis=1, keepdims=True) * own_valid[half_rows(j)], axis=0, keepdims=True)
        small[stat_row + k:stat_row + k + 1, :] += jnp.broadcast_to(total, (1, size))

    gather_attn = Gather(normed_attn, parts, move_send.at[0], move_recv.at[0])
    small[stat_row:stat_row + 8, :] = jnp.zeros((8, size), f32)

    def attn_norm(j):
        resid = inputs[half_rows(j), :].astype(f32)
        normed_attn[half_rows(j), :] = (resid * rows_scale(resid) * gain_attn[...]).astype(bf16)
        note(0, resid * resid, j)

    attn_norm(0)
    pl.semaphore_wait(barrier, len(peers))
    gather_attn.begin(0)
    attn_norm(1)
    gather_attn.begin(1)
    out_full[0:rows, :] = (cotangent[...].astype(f32) * own_valid).astype(bf16)
    for j in range(2):
        note(5, jnp.ones((rows // 2, 1), f32), j)
    for copy in qkv_loads:
        copy.wait()

    def qkv_block(b):
        made = dot_nn(normed_attn[block_of(b), :], w_qkv[...])
        ordered[true_rows(b), :] = made.astype(bf16)
        for k in range(rows // span_rows):
            c = relative(inner, b) * (rows // span_rows) + k
            live = (c * span_rows + lax.broadcasted_iota(jnp.int32, (span_rows, 1), 0) < valid_count).astype(f32)
            for h in range(heads):
                span, col = slice(k * span_rows, (k + 1) * span_rows), h * size
                key_unit, _ = unit_rows(made[span, cols + col:cols + col + size].astype(bf16))
                value = made[span, 2 * cols + col:2 * cols + col + size].astype(bf16)
                key_h, key_l = halves(key_unit)
                live_h, live_l = halves(key_unit * live)
                grams[h, c] = dot3(dot_tn, (live_h, live_l), (key_h, key_l))
                slopes[h, c] = (dot_tn(value, live_h) + dot_tn(value, live_l)).astype(bf16)

    qkv_block(0)
    gather_attn.wait(gather_attn.near)
    qkv_block(1)
    gather_attn.forward()
    gather_cot = Gather(out_full, parts, move_send.at[1], move_recv.at[1])
    for j in range(2):
        gather_cot.begin(j)
    qkv_block(2)
    gather_attn.wait(gather_attn.both)
    qkv_block(3)

    carried = [(jnp.zeros((size, size), f32), jnp.zeros((size, size), f32)) for _ in range(heads)]
    for c in range(blocks):
        for h in range(heads):
            memory, velocity = carried[h]
            parts_m = halves(memory)
            states[h, c] = parts_m[0]
            change = dot3(dot_nn, parts_m, halves(grams[h, c])) - slopes[h, c].astype(f32)
            velocity = momentum[h, c] * velocity - step_size[h, c] * change
            memory = (1.0 - decay[h, c]) * memory + velocity
            carried[h] = (memory, velocity)

    diagonal = lax.broadcasted_iota(jnp.int32, (rows, rows), 0) <= lax.broadcasted_iota(jnp.int32, (rows, rows), 1)

    def masked_scores(h, i, query):
        seen = (i + 1) * rows
        scores = dot_nt(ordered[:seen, cols + h * size:cols + (h + 1) * size], query)
        last = jnp.where(diagonal, scores[seen - rows:], -1e30)
        return last if i == 0 else jnp.concatenate([scores[:seen - rows], last], axis=0)

    for h in range(heads):
        col = h * size
        value_t = ordered[:, 2 * cols + col:2 * cols + col + size].T
        persist_t = persist_v[h].astype(f32).T.astype(bf16)
        for i in range(parts):
            seen = (i + 1) * rows
            query = ordered[block_of(i), col:col + size]
            scores = masked_scores(h, i, query)
            extra = dot_nt(persist_k[h], query)
            top = jnp.maximum(jnp.max(scores, axis=0, keepdims=True), jnp.max(extra, axis=0, keepdims=True))
            lifted = jnp.exp2((scores - top) * (factor * log2_e))
            lifted_extra = jnp.exp2((extra - top) * (factor * log2_e))
            total = jnp.sum(lifted, axis=0, keepdims=True) + jnp.sum(lifted_extra, axis=0, keepdims=True)
            attended = dot_nn(value_t[:, :seen], lifted.astype(bf16)) + dot_nn(persist_t, lifted_extra.astype(bf16))
            attended = attended * (1.0 / total)
            log_total[h:h + 1, block_of(i)] = top * (factor * log2_e) + jnp.log2(total)
            query_unit = unit_rows(query)[0].astype(bf16)
            reads = [
                dot_nt(query_unit[k * span_rows:(k + 1) * span_rows], states[h, i * (rows // span_rows) + k])
                for k in range(rows // span_rows)
            ]
            together = attended.T + jnp.concatenate(reads, axis=0)
            mixed[true_rows(i), col:col + size] = together.astype(bf16)

    out_load.wait()
    scatter = Scatter(sent_a, landed_a, hold, move_send.at[2], move_recv.at[2])
    scatter.begin(lambda b, j: dot_nn(mixed[part_of(b, j), :], w_out[...]), rounds.tick)
    gather_cot.wait(gather_cot.near)
    gather_cot.forward()
    gather_ffn = Gather(normed_ffn, parts, move_send.at[3], move_recv.at[3])
    for j in range(2):
        branch = scatter.finish(j)
        value = inputs[half_rows(j), :].astype(f32) + branch
        middle[half_rows(j), :] = value
        normed_ffn[half_rows(j), :] = (value * rows_scale(value) * gain_ffn[...]).astype(bf16)
        gather_ffn.begin(j)
        note(3, branch * branch, j)
        note(1, value * value, j)
    for copy in ffn_loads:
        copy.wait()
    gather_cot.wait(gather_cot.both)
    gather_ffn.wait(gather_ffn.near)

    piece = units // 4

    def feed(half):
        tokens = slice(half * 2 * rows, (half + 1) * 2 * rows)
        for k in range(4):
            span = slice(k * piece, (k + 1) * piece)
            gate = dot_nt(w_gate[span, :], normed_ffn[tokens, :])
            up = dot_nt(w_up[span, :], normed_ffn[tokens, :])
            hidden_grad = dot_nt(w_down[span, :], out_full[tokens, :])
            sigmoid = jax.nn.sigmoid(gate)
            silu = gate * sigmoid
            hidden[span, tokens] = (silu * up).astype(bf16)
            up_grad[span, tokens] = (hidden_grad * silu).astype(bf16)
            gate_grad[span, tokens] = (hidden_grad * up * sigmoid * (1.0 + gate * (1.0 - sigmoid))).astype(bf16)

    feed(0)
    gather_ffn.forward()
    gather_ffn.wait(gather_ffn.both)
    feed(1)
    for source, left, right, ring in (
        (down_source, hidden, out_full, rings[0]), (gate_source, gate_grad, normed_ffn, rings[1]),
        (up_source, up_grad, normed_ffn, rings[2]),
    ):
        source[...] = dot_nn(left[...], right[...]).astype(bf16)
        rounds.add(ring)

    scatter = Scatter(sent_b, landed_b, hold, move_send.at[4], move_recv.at[4])
    scatter.begin(
        lambda b, j: dot_tn(gate_grad[:, part_of(b, j)], w_gate[...]) + dot_tn(up_grad[:, part_of(b, j)], w_up[...]),
        rounds.tick,
    )
    rounds.tick(pace[0])
    gather_middle = Gather(middle_full, parts, move_send.at[5], move_recv.at[5])
    gain_row = jnp.zeros((1, width), f32)
    for j in range(2):
        normed_grad = scatter.finish(j)
        value = middle[half_rows(j), :]
        scale = rows_scale(value)
        weighted = normed_grad * gain_ffn[...]
        grad = (
            cotangent[half_rows(j), :].astype(f32) * own_valid[half_rows(j)] + scale * weighted
            - value * (scale * scale * scale) * jnp.mean(weighted * value, axis=-1, keepdims=True)
        )
        middle_grad[half_rows(j), :] = grad
        middle_full[half_rows(j), :] = grad.astype(bf16)
        gather_middle.begin(j)
        gain_row = gain_row + jnp.sum(normed_grad * value * scale, axis=0, keepdims=True)
        if j == 0:
            rounds.tick(pace[8])
    for k in range(width // size):
        small[width // size + k:width // size + k + 1, :] = gain_row[:, k * size:(k + 1) * size]
    rounds.tick(pace[1])
    gather_middle.wait(gather_middle.near)

    def mixed_block(b):
        upstream[true_rows(b), :] = dot_nt(middle_full[block_of(b), :], w_out[...]).astype(bf16)

    mixed_block(0)
    mixed_block(1)
    gather_middle.forward()
    mixed_block(2)
    gather_middle.wait(gather_middle.both)
    mixed_block(3)
    scatter = Scatter(sent_a, landed_a, hold, move_send.at[6], move_recv.at[6])
    scatter.begin(lambda b, j: dot_tn(hidden[:, part_of(b, j)], w_down[...]), rounds.tick)
    rounds.tick(pace[2])
    out_source[...] = dot_tn(mixed[...], middle_full[...]).astype(bf16)
    rounds.add(rings[3])

    carried = [(jnp.zeros((size, size), f32), jnp.zeros((size, size), f32)) for _ in range(heads)]
    for c in reversed(range(blocks)):
        span = slice(c * span_rows, (c + 1) * span_rows)
        for h in range(heads):
            col = h * size
            query_unit, _ = unit_rows(ordered[span, col:col + size])
            query_h, query_l = halves(query_unit)
            rise = upstream[span, col:col + size]
            entry = dot_tn(rise, query_h) + dot_tn(rise, query_l)
            memory, velocity = carried[h]
            velocity = velocity + memory
            change = (-step_size[h, c]) * velocity
            slopes[h, c] = change.astype(bf16)
            memory = (1.0 - decay[h, c]) * memory + entry + dot3(dot_nn, halves(change), halves(grams[h, c]))
            velocity = momentum[h, c] * velocity
            carried[h] = (memory, velocity)
        rounds.tick(pace[3][c])

    for h in range(heads):
        col = h * size
        for c in range(blocks):
            span = slice(c * span_rows, (c + 1) * span_rows)
            live = (c * span_rows + lax.broadcasted_iota(jnp.int32, (span_rows, 1), 0) < valid_count).astype(f32)
            query_unit, query_scale = unit_rows(ordered[span, col:col + size])
            key_unit, key_scale = unit_rows(ordered[span, cols + col:cols + col + size])
            value = ordered[span, 2 * cols + col:2 * cols + col + size].astype(f32)
            rise = upstream[span, col:col + size]
            state = states[h, c]
            slope = slopes[h, c]
            error = (dot_nt(key_unit.astype(bf16), state) - value) * live
            error_grad = dot_nt(key_unit.astype(bf16), slope) * live
            unit_grad = dot_nn(error.astype(bf16), slope) + dot_nn(error_grad.astype(bf16), state)
            key_sum[span, :] = key_scale * (
                unit_grad - key_unit * jnp.sum(unit_grad * key_unit, axis=-1, keepdims=True)
            )
            value_sum[span, :] = -error_grad
            read_grad = dot_nn(rise, state)
            query_sum[span, :] = query_scale * (
                read_grad - query_unit * jnp.sum(read_grad * query_unit, axis=-1, keepdims=True)
            )
            rounds.tick(pace[4][c])

        key_t = ordered[:, cols + col:cols + col + size].T
        persist_t = persist_k[h].astype(f32).T.astype(bf16)
        persist_k_total = jnp.zeros(persist_k.shape[1:], f32)
        persist_v_total = jnp.zeros(persist_k.shape[1:], f32)
        for i in range(parts):
            span = block_of(i)
            seen = (i + 1) * rows
            query = ordered[span, col:col + size]
            rise = upstream[span, col:col + size]
            scores = masked_scores(h, i, query)
            extra = dot_nt(persist_k[h], query)
            base = log_total[h:h + 1, span]
            probs = jnp.exp2(scores * (factor * log2_e) - base)
            probs_extra = jnp.exp2(extra * (factor * log2_e) - base)
            probs_grad = dot_nt(ordered[:seen, 2 * cols + col:2 * cols + col + size], rise)
            extra_grad = dot_nt(persist_v[h], rise)
            weighted = probs * probs_grad
            weighted_extra = probs_extra * extra_grad
            inner_sum = jnp.sum(weighted, axis=0, keepdims=True) + jnp.sum(weighted_extra, axis=0, keepdims=True)
            scores_grad = (weighted - probs * inner_sum).astype(bf16)
            scores_extra = (weighted_extra - probs_extra * inner_sum).astype(bf16)
            query_t = dot_nn(key_t[:, :seen], scores_grad) + dot_nn(persist_t, scores_extra)
            query_sum[span, :] += query_t.T * factor
            key_sum[:seen, :] += dot_nn(scores_grad, query) * factor
            value_sum[:seen, :] += dot_nn(probs.astype(bf16), rise)
            persist_k_total += dot_nn(scores_extra, query) * factor
            persist_v_total += dot_nn(probs_extra.astype(bf16), rise)
            rounds.tick(pace[5][i])
        small[shared + h * many:shared + (h + 1) * many, :] = persist_k_total
        small[shared + (heads + h) * many:shared + (heads + h + 1) * many, :] = persist_v_total
        for b in range(parts):
            target = true_rows(b)
            qkv_grad[target, col:col + size] = query_sum[block_of(b), :].astype(bf16)
            qkv_grad[target, cols + col:cols + col + size] = key_sum[block_of(b), :].astype(bf16)
            qkv_grad[target, 2 * cols + col:2 * cols + col + size] = value_sum[block_of(b), :].astype(bf16)

    for j in range(2):
        branch = scatter.finish(j)
        note(4, branch * branch, j)
        value = middle[half_rows(j), :] + branch
        note(2, value * value, j)
        result[half_rows(j), :] = value.astype(bf16)

    for b in range(parts):
        span = block_of(b)
        grad = dot_tn(normed_attn[:, span], qkv_grad[...])
        for k, source in enumerate((query_source, key_source, value_source)):
            source[span, :] = grad[:, k * cols:(k + 1) * cols].astype(bf16)
        gain_row = jnp.sum((grad * w_qkv[span, :].astype(f32)).T, axis=0, keepdims=True) / gain_attn[:, span]
        for k in range(rows // size):
            row = b * (rows // size) + k
            small[row:row + 1, :] = gain_row[:, k * size:(k + 1) * size]
        rounds.tick(pace[6])
    rounds.add(small_sum, *rings[4:])
    scatter = Scatter(sent_b, landed_b, hold, move_send.at[7], move_recv.at[7])
    scatter.begin(lambda b, j: dot_nt(qkv_grad[part_of(b, j), :], w_qkv[...]), rounds.tick)
    rounds.tick(pace[7])
    for j in range(2):
        normed_grad = scatter.finish(j)
        value = inputs[half_rows(j), :].astype(f32)
        scale = rows_scale(value)
        weighted = normed_grad * gain_attn[...]
        input_grad[half_rows(j), :] = (
            middle_grad[half_rows(j), :] + scale * weighted
            - value * (scale * scale * scale) * jnp.mean(weighted * value, axis=-1, keepdims=True)
        ).astype(bf16)
    rounds.finish()


def whole_layer(
    length, momentum, decay, step_size, inputs, cotangent, gain_attn, gain_ffn, persist_k, persist_v,
    w_query, w_key, w_value, w_out, w_gate, w_up, w_down, count, parts,
):
    heads, many, size = persist_k.shape
    blocks = momentum.shape[1]
    cols = heads * size
    rows, width = inputs.shape
    seq_len = rows * parts
    units = w_gate.shape[0]
    shared = 2 * width // size + 8
    small_rows = shared + 2 * heads * many
    flows = len(bits_below(count)) + len(bits_below(parts))

    def row_slots(*shape):
        return pltpu.VMEM((2, count - 1, shape[0] // (2 * count), shape[1]), bf16)

    def col_slots(*shape):
        return pltpu.VMEM((2, count - 1, shape[0] // 2, shape[1] // count), bf16)

    def low(*shape):
        return pltpu.VMEM(shape, bf16)

    def full(*shape):
        return pltpu.VMEM(shape, f32)

    def semaphores(*shape):
        return pltpu.SemaphoreType.DMA(shape)

    ffn = (units, width)
    return pl.pallas_call(
        functools.partial(layer_kernel, heads, blocks, parts, count, shared, pace),
        out_shape=(
            jax.ShapeDtypeStruct(ffn, bf16),
            jax.ShapeDtypeStruct(ffn, bf16),
            jax.ShapeDtypeStruct(ffn, bf16),
            jax.ShapeDtypeStruct((width, cols), bf16),
            jax.ShapeDtypeStruct((width, cols), bf16),
            jax.ShapeDtypeStruct((width, cols), bf16),
            jax.ShapeDtypeStruct((cols, width), bf16),
            jax.ShapeDtypeStruct((small_rows, size), f32),
            jax.ShapeDtypeStruct((rows, width), bf16),
            jax.ShapeDtypeStruct((rows, width), bf16),
        ),
        in_specs=[smem()] * 4 + [vmem()] * 6 + [pl.BlockSpec(memory_space=pl.ANY)] * 7,
        out_specs=(vmem(),) * 10,
        scratch_shapes=[
            low(width, 3 * cols), low(cols, width), low(*ffn), low(*ffn), low(*ffn),
            low(seq_len, width), low(seq_len, 3 * cols), low(seq_len, cols),
            low(heads, blocks, size, size), full(heads, blocks, size, size), full(heads, seq_len),
            full(rows, width), full(rows, width), full(rows, width), low(seq_len, width), low(seq_len, width),
            low(units, seq_len), low(units, seq_len), low(units, seq_len),
            low(*ffn), low(*ffn), low(*ffn), low(width, cols), low(width, cols), low(width, cols), low(cols, width),
            col_slots(*ffn), col_slots(*ffn), col_slots(*ffn),
            row_slots(width, cols), row_slots(width, cols), row_slots(width, cols), col_slots(cols, width),
            full(flows, small_rows, size),
            low(3, rows, width), low(3, rows, width), low(3, rows, width), low(3, rows, width),
            low(seq_len, width), low(seq_len, cols), low(heads, blocks, size, size),
            full(seq_len, size), full(seq_len, size), full(seq_len, size), low(seq_len, 3 * cols),
            semaphores(7), semaphores(7, 2, 2 * count - 2), semaphores(7, 2, 2 * count - 2),
            semaphores(flows), semaphores(flows), semaphores(8, 3, 2), semaphores(8, 3, 2),
        ],
        compiler_params=pltpu.CompilerParams(
            vmem_limit_bytes=layer_limit, collective_id=0, has_side_effects=True
        ),
        cost_estimate=pl.CostEstimate(flops=150_000_000_000, bytes_accessed=40_000_000, transcendentals=4_000_000),
        name="whole_layer",
    )(
        length, momentum, decay, step_size, inputs, cotangent, gain_attn, gain_ffn, persist_k, persist_v,
        w_query, w_key, w_value, w_out, w_gate, w_up, w_down,
    )


def finish_kernel(casts, moves, *refs):
    total = casts + moves
    sources, small = refs[:total], refs[total]
    targets, refs = refs[total + 1:2 * total + 1], refs[2 * total + 1:]
    gain_attn, gain_ffn, persist_k, persist_v, roots = refs[:5]
    held, cast, semaphores = refs[5:5 + total], refs[5 + total:5 + total + casts], refs[5 + total + casts]
    arrive = [pltpu.make_async_copy(sources[k], held[k], semaphores.at[0, k]) for k in range(total)]
    leave = [
        pltpu.make_async_copy(cast[k] if k < casts else held[k], targets[k], semaphores.at[1, k])
        for k in range(total)
    ]
    for copy in arrive:
        copy.start()
    lines = gain_attn.shape[0]
    heads, many, size = persist_k.shape
    gain_attn[...] = small[0:lines, :]
    gain_ffn[...] = small[lines:2 * lines, :]
    stats = small[2 * lines:2 * lines + 8, :]
    stats = jnp.sqrt(stats / (stats[5:6, :] * (lines * size)))
    for k in range(5):
        roots[k] = stats[k, 0]
    for h in range(heads):
        first = 2 * lines + 8 + h * many
        persist_k[h] = small[first:first + many, :]
        persist_v[h] = small[first + heads * many:first + (heads + 1) * many, :]
    for k in range(total):
        arrive[k].wait()
        if k < casts:
            cast[k][...] = held[k][...].astype(f32)
        leave[k].start()
    for copy in leave:
        copy.wait()


def finish(sums, rest, small, persist_shape):
    casts, moves = len(sums), len(rest)
    size = small.shape[1]
    lines = (small.shape[0] - 2 * persist_shape[0] * persist_shape[1] - 8) // 2
    anywhere = pl.BlockSpec(memory_space=pl.ANY)
    return pl.pallas_call(
        functools.partial(finish_kernel, casts, moves),
        out_shape=tuple(jax.ShapeDtypeStruct(value.shape, f32) for value in sums)
        + tuple(jax.ShapeDtypeStruct(value.shape, value.dtype) for value in rest)
        + (jax.ShapeDtypeStruct((lines, size), f32),) * 2
        + (jax.ShapeDtypeStruct(persist_shape, f32),) * 2
        + (jax.ShapeDtypeStruct((5,), f32),),
        in_specs=[anywhere] * (casts + moves) + [vmem()],
        out_specs=(anywhere,) * (casts + moves) + (vmem(),) * 4 + (smem(),),
        scratch_shapes=[pltpu.VMEM(value.shape, value.dtype) for value in (*sums, *rest)]
        + [pltpu.VMEM(value.shape, f32) for value in sums]
        + [pltpu.SemaphoreType.DMA((2, casts + moves))],
        compiler_params=pltpu.CompilerParams(vmem_limit_bytes=vmem_limit),
        name="finish",
    )(*sums, *rest, small)


pace = (4, 6, 0, (0, 0, 0, 1) * 4, (0, 0, 0, 0, 0, 0, 0, 1) * 2, (0, 1, 1, 1), 1, 8, 2)
layer_limit = 63 << 20


def swap(value, axis, bit):
    count = lax.axis_size(axis)
    return lax.ppermute(value, axis, [(i, i ^ bit) for i in range(count)])


def norm_back(value, scale, gain, upstream):
    weighted = upstream * gain
    return scale * weighted - value * (scale * scale * scale) * jnp.mean(
        weighted * value, axis=-1, keepdims=True
    )


def gather_rows(own):
    far = swap(own, "tensor", 2)
    near = swap(own, "tensor", 1)
    both = swap(far, "tensor", 1)
    return jnp.concatenate([own, near], 0), jnp.concatenate([far, both], 0)


def scatter_rows(near, far):
    rows = near.shape[0] // 2
    far_sum = far[:rows] + swap(far[rows:].astype(bf16), "tensor", 1).astype(f32)
    far_in = swap(far_sum.astype(bf16), "tensor", 2).astype(f32)
    near_in = swap(near[rows:].astype(bf16), "tensor", 1).astype(f32)
    return near[:rows] + near_in + far_in


def mul(left, right):
    return jnp.dot(left, right, preferred_element_type=f32)


def mul_nt(left, right):
    return jnp.einsum("ab,cb->ac", left, right, preferred_element_type=f32)


def mul_tn(left, right):
    return jnp.einsum("ab,ac->bc", left, right, preferred_element_type=f32)


def fits_ring(count, parts, *shapes):
    if count & (count - 1) or parts != 4 or count < 4:
        return False
    return all(rows % (32 * count) == 0 or (rows % 32 == 0 and cols % (128 * count) == 0) for rows, cols in shapes)


def body(
    inputs, cotangent, lengths, gain_attn, w_query, w_key, w_value, w_out, persist_keys, persist_values,
    gain_ffn, w_gate, w_up, w_down, momentum, decay, step_size,
):
    parts = lax.axis_size("tensor")
    count = lax.axis_size("dp")
    rows = inputs.shape[1]
    width = inputs.shape[2]
    half = 2 * rows
    cols = w_query.shape[1]
    size = persist_keys.shape[2]
    place = lax.axis_index("tensor")
    first_row = place * rows
    own_valid = (first_row + jnp.arange(rows, dtype=jnp.int32) < lengths[0]).astype(f32)[:, None]
    places = place.astype(jnp.int32).reshape(1)
    rates = (places, lengths, momentum[0], decay[0], step_size[0])

    if fits_ring(count, parts, (w_down.shape), (width, 3 * cols), (cols, width)):
        *sums, small, result, input_grad = whole_layer(
            lengths, momentum[0].T, decay[0].T, step_size[0].T, inputs[0], cotangent[0], gain_attn[None], gain_ffn[None], persist_keys, persist_values,
            w_query, w_key, w_value, w_out, w_gate.T, w_up.T, w_down, count, parts,
        )
        gate_sum, up_sum, down_sum, query_sum, key_sum, value_sum, out_sum, *rest = finish(
            sums, (result, input_grad), small, persist_keys.shape
        )
        result, input_grad, gain_attn_sum, gain_ffn_sum, persist_k_sum, persist_v_sum, rms_stats = rest
    else:
        resid = inputs[0].astype(f32)
        scale_attn = rows_scale(resid)
        near, far = gather_rows((resid * scale_attn * gain_attn).astype(bf16))
        w_qkv = jnp.concatenate([w_query, w_key, w_value], 1)
        qkv = jnp.concatenate([mul(near, w_qkv).astype(bf16), mul(far, w_qkv).astype(bf16)], 0)
        normed_attn = jnp.concatenate([near, far], 0)
        mixed, log_total, states, grams = attend_and_recall(*rates, qkv, persist_keys, persist_values, parts)
        branch_attn = scatter_rows(mul(mixed[:half], w_out), mul(mixed[half:], w_out))
        middle = resid + branch_attn
        scale_ffn = rows_scale(middle)
        normed_ffn = jnp.concatenate(gather_rows((middle * scale_ffn * gain_ffn).astype(bf16)), 0)

        out_grad = cotangent[0].astype(f32) * own_valid
        out_full = jnp.concatenate(gather_rows(out_grad.astype(bf16)), 0)
        gate = mul(normed_ffn, w_gate)
        up = mul(normed_ffn, w_up)
        sigmoid = jax.nn.sigmoid(gate)
        silu = gate * sigmoid
        hidden = (silu * up).astype(bf16)
        branch_ffn = scatter_rows(mul(hidden[:half], w_down), mul(hidden[half:], w_down))
        result = middle + branch_ffn
        hidden_grad = mul_nt(out_full, w_down)
        gate_grad = (hidden_grad * up * sigmoid * (1.0 + gate * (1.0 - sigmoid))).astype(bf16)
        up_grad = (hidden_grad * silu).astype(bf16)

        def masked(value_in):
            return jnp.sum(own_valid * (value_in * value_in))

        squares = jnp.stack(
            [masked(resid), masked(middle), masked(result), masked(branch_attn), masked(branch_ffn), jnp.sum(own_valid)]
        )
        grad_down = mul_tn(hidden, out_full).astype(bf16)
        grad_gate = mul_tn(gate_grad, normed_ffn).astype(bf16)
        grad_up = mul_tn(up_grad, normed_ffn).astype(bf16)
        normed_ffn_grad = scatter_rows(
            mul_nt(gate_grad[:half], w_gate) + mul_nt(up_grad[:half], w_up),
            mul_nt(gate_grad[half:], w_gate) + mul_nt(up_grad[half:], w_up),
        )
        gain_ffn_part = jnp.sum(normed_ffn_grad * middle * scale_ffn, axis=0)
        middle_grad = out_grad + norm_back(middle, scale_ffn, gain_ffn, normed_ffn_grad)
        middle_full = jnp.concatenate(gather_rows(middle_grad.astype(bf16)), 0)
        mixed_grad = mul_nt(middle_full, w_out).astype(bf16)
        qkv_grad, persist_k_grad, persist_v_grad = attend_and_recall_back(
            *rates, qkv, mixed_grad, persist_keys, persist_values, log_total, states, grams, parts
        )
        normed_attn_grad = scatter_rows(mul_nt(qkv_grad[:half], w_qkv), mul_nt(qkv_grad[half:], w_qkv))
        gain_attn_part = jnp.sum(normed_attn_grad * resid * scale_attn, axis=0)
        input_grad = (middle_grad + norm_back(resid, scale_attn, gain_attn, normed_attn_grad)).astype(bf16)
        gate_sum, up_sum, down_sum, wide, out_sum, persist_sums = lax.psum(
            (grad_gate, grad_up, grad_down, mul_tn(normed_attn, qkv_grad).astype(bf16),
             mul_tn(mixed, middle_full).astype(bf16), jnp.stack([persist_k_grad, persist_v_grad])), "dp"
        )
        query_sum, key_sum, value_sum = wide[:, :cols], wide[:, cols:2 * cols], wide[:, 2 * cols:]
        gains, squares = lax.psum((jnp.concatenate([gain_attn_part, gain_ffn_part]), squares), ("dp", "tensor"))
        gain_attn_sum, gain_ffn_sum = gains[:width], gains[width:]
        persist_k_sum, persist_v_sum = persist_sums[0], persist_sums[1]
        rms_stats = jnp.sqrt(squares[:5] / (squares[5] * width))
    return (
        result.astype(bf16)[None],
        input_grad[None],
        gain_attn_sum.reshape(-1),
        query_sum.astype(f32),
        key_sum.astype(f32),
        value_sum.astype(f32),
        out_sum.astype(f32),
        persist_k_sum,
        persist_v_sum,
        gain_ffn_sum.reshape(-1),
        gate_sum.astype(f32).T,
        up_sum.astype(f32).T,
        down_sum.astype(f32),
        rms_stats,
    )


def solution(mesh):
    in_specs = (
        P("dp", "tensor", None),
        P("dp", "tensor", None),
        P("dp"),
        P(),
        P(None, "tensor"),
        P(None, "tensor"),
        P(None, "tensor"),
        P("tensor", None),
        P("tensor", None, None),
        P("tensor", None, None),
        P(),
        P(None, "tensor"),
        P(None, "tensor"),
        P("tensor", None),
        P("dp", None, "tensor"),
        P("dp", None, "tensor"),
        P("dp", None, "tensor"),
    )
    out_specs = (
        P("dp", "tensor", None),
        P("dp", "tensor", None),
        P(),
        P(None, "tensor"),
        P(None, "tensor"),
        P(None, "tensor"),
        P("tensor", None),
        P("tensor", None, None),
        P("tensor", None, None),
        P(),
        P(None, "tensor"),
        P(None, "tensor"),
        P("tensor", None),
        P(),
    )
    return jax.shard_map(body, mesh=mesh, in_specs=in_specs, out_specs=out_specs, check_vma=False)
```

```python
import functools
import jax
import jax.numpy as jnp
from jax import lax
from jax.sharding import PartitionSpec as P
import jax.experimental.pallas as pl
import jax.experimental.pallas.tpu as pltpu

norm_eps = 1e-05
unit_eps = 1e-06
f32 = jnp.float32
bf16 = jnp.bfloat16
log2_e = 1.4426950408889634


def dot_nn(left, right):
    return lax.dot_general(left, right, (((1,), (0,)), ((), ())), preferred_element_type=f32)


def dot_nt(left, right):
    return lax.dot_general(left, right, (((1,), (1,)), ((), ())), preferred_element_type=f32)


def dot_tn(left, right):
    return lax.dot_general(left, right, (((0,), (0,)), ((), ())), preferred_element_type=f32)


def halves(value):
    high = value.astype(bf16)
    return high, (value - high.astype(f32)).astype(bf16)


def dot3(dot, left, right):
    (lh, ll), (rh, rl) = left, right
    return dot(lh, rh) + dot(ll, rh) + dot(lh, rl)


def unit_rows(value):
    wide = value.astype(f32)
    scale = lax.rsqrt(jnp.sum(wide * wide, axis=-1, keepdims=True) + unit_eps)
    return wide * scale, scale


def block_rows(start, width):
    return pl.ds(pl.multiple_of(start, width), width)


def forward_kernel(
    heads, blocks, parts,
    place, length, momentum, decay, step_size, qkv, persist_k, persist_v,
    mixed, log_total, states, grams,
    ordered, reads,
):
    seq_len, wide = qkv.shape
    size = persist_k.shape[2]
    cols = heads * size
    rows = seq_len // parts
    width = seq_len // blocks
    me = place[0]
    count = length[0]
    for b in range(parts):
        ordered[b * rows:(b + 1) * rows, :] = qkv[block_rows(jnp.bitwise_xor(me, b) * rows, rows), :]

    carried = [(jnp.zeros((size, size), f32), jnp.zeros((size, size), f32)) for _ in range(heads)]
    for c in range(blocks):
        span = slice(c * width, (c + 1) * width)
        live = (c * width + lax.broadcasted_iota(jnp.int32, (width, 1), 0) < count).astype(f32)
        for h in range(heads):
            col = h * size
            key_unit, _ = unit_rows(ordered[span, cols + col:cols + col + size])
            query_unit, _ = unit_rows(ordered[span, col:col + size])
            value = ordered[span, 2 * cols + col:2 * cols + col + size]
            key_h, key_l = halves(key_unit)
            live_h, live_l = halves(key_unit * live)
            gram = dot3(dot_tn, (live_h, live_l), (key_h, key_l))
            target = dot_tn(value, live_h) + dot_tn(value, live_l)
            memory, velocity = carried[h]
            states[h, c] = memory.astype(bf16)
            grams[h, c] = gram
            parts_m = halves(memory)
            reads[span, col:col + size] = dot_nt(query_unit.astype(bf16), parts_m[0])
            change = dot3(dot_nn, parts_m, halves(gram)) - target
            velocity = momentum[c, h] * velocity - step_size[c, h] * change
            memory = (1.0 - decay[c, h]) * memory + velocity
            carried[h] = (memory, velocity)

    factor = size ** (-0.5) * log2_e
    diagonal = lax.broadcasted_iota(jnp.int32, (rows, rows), 0) <= lax.broadcasted_iota(jnp.int32, (rows, rows), 1)
    for h in range(heads):
        col = h * size
        value_t = ordered[:, 2 * cols + col:2 * cols + col + size].T
        persist_t = persist_v[h].astype(f32).T.astype(bf16)
        for i in range(parts):
            span = slice(i * rows, (i + 1) * rows)
            seen = (i + 1) * rows
            query = ordered[span, col:col + size]
            scores = dot_nt(ordered[:seen, cols + col:cols + col + size], query)
            last = jnp.where(diagonal, scores[seen - rows:], -1e30)
            scores = last if i == 0 else jnp.concatenate([scores[:seen - rows], last], axis=0)
            extra = dot_nt(persist_k[h], query)
            top = jnp.maximum(jnp.max(scores, axis=0, keepdims=True), jnp.max(extra, axis=0, keepdims=True))
            lifted = jnp.exp2((scores - top) * factor)
            lifted_extra = jnp.exp2((extra - top) * factor)
            total = jnp.sum(lifted, axis=0, keepdims=True) + jnp.sum(lifted_extra, axis=0, keepdims=True)
            attended = dot_nn(value_t[:, :seen], lifted.astype(bf16)) + dot_nn(persist_t, lifted_extra.astype(bf16))
            attended = attended * (1.0 / total)
            log_total[h:h + 1, span] = top * factor + jnp.log2(total)
            together = attended.T + reads[span, col:col + size]
            mixed[block_rows(jnp.bitwise_xor(me, i) * rows, rows), col:col + size] = together.astype(bf16)


def backward_kernel(
    heads, blocks, parts,
    place, length, momentum, decay, step_size, qkv, mixed_grad, persist_k, persist_v,
    log_total, states, grams,
    qkv_grad, persist_k_grad, persist_v_grad,
    ordered, upstream, slopes, key_sum, value_sum, query_sum,
):
    seq_len, wide = qkv.shape
    size = persist_k.shape[2]
    cols = heads * size
    rows = seq_len // parts
    width = seq_len // blocks
    me = place[0]
    count = length[0]
    for b in range(parts):
        source = block_rows(jnp.bitwise_xor(me, b) * rows, rows)
        ordered[b * rows:(b + 1) * rows, :] = qkv[source, :]
        upstream[b * rows:(b + 1) * rows, :] = mixed_grad[source, :]

    carried = [(jnp.zeros((size, size), f32), jnp.zeros((size, size), f32)) for _ in range(heads)]
    for c in reversed(range(blocks)):
        span = slice(c * width, (c + 1) * width)
        for h in range(heads):
            col = h * size
            query_unit, _ = unit_rows(ordered[span, col:col + size])
            query_h, query_l = halves(query_unit)
            rise = upstream[span, col:col + size]
            entry = dot_tn(rise, query_h) + dot_tn(rise, query_l)
            memory, velocity = carried[h]
            velocity = velocity + memory
            change = (-step_size[c, h]) * velocity
            slopes[h, c] = change
            memory = (1.0 - decay[c, h]) * memory + entry + dot3(dot_nn, halves(change), halves(grams[h, c]))
            velocity = momentum[c, h] * velocity
            carried[h] = (memory, velocity)

    for h in range(heads):
        col = h * size
        for c in range(blocks):
            span = slice(c * width, (c + 1) * width)
            live = (c * width + lax.broadcasted_iota(jnp.int32, (width, 1), 0) < count).astype(f32)
            query_unit, query_scale = unit_rows(ordered[span, col:col + size])
            key_unit, key_scale = unit_rows(ordered[span, cols + col:cols + col + size])
            value = ordered[span, 2 * cols + col:2 * cols + col + size].astype(f32)
            rise = upstream[span, col:col + size]
            state = states[h, c]
            slope = slopes[h, c].astype(bf16)
            key_b = key_unit.astype(bf16)
            error = (dot_nt(key_b, state) - value) * live
            error_grad = dot_nt(key_b, slope) * live
            unit_grad = dot_nn(error.astype(bf16), slope) + dot_nn(error_grad.astype(bf16), state)
            key_sum[span, :] = key_scale * (unit_grad - key_unit * jnp.sum(unit_grad * key_unit, axis=-1, keepdims=True))
            value_sum[span, :] = -error_grad
            read_grad = dot_nn(rise, state)
            query_sum[span, :] = query_scale * (read_grad - query_unit * jnp.sum(read_grad * query_unit, axis=-1, keepdims=True))

        factor = size ** (-0.5)
        diagonal = lax.broadcasted_iota(jnp.int32, (rows, rows), 0) <= lax.broadcasted_iota(jnp.int32, (rows, rows), 1)
        key_t = ordered[:, cols + col:cols + col + size].T
        persist_t = persist_k[h].astype(f32).T.astype(bf16)
        persist_k_total = jnp.zeros(persist_k.shape[1:], f32)
        persist_v_total = jnp.zeros(persist_k.shape[1:], f32)
        for i in range(parts):
            span = slice(i * rows, (i + 1) * rows)
            seen = (i + 1) * rows
            query = ordered[span, col:col + size]
            rise = upstream[span, col:col + size]
            scores = dot_nt(ordered[:seen, cols + col:cols + col + size], query)
            last = jnp.where(diagonal, scores[seen - rows:], -1e30)
            scores = last if i == 0 else jnp.concatenate([scores[:seen - rows], last], axis=0)
            extra = dot_nt(persist_k[h], query)
            base = log_total[h:h + 1, span]
            probs = jnp.exp2(scores * (factor * log2_e) - base)
            probs_extra = jnp.exp2(extra * (factor * log2_e) - base)
            probs_grad = dot_nt(ordered[:seen, 2 * cols + col:2 * cols + col + size], rise)
            extra_grad = dot_nt(persist_v[h], rise)
            weighted = probs * probs_grad
            weighted_extra = probs_extra * extra_grad
            inner = jnp.sum(weighted, axis=0, keepdims=True) + jnp.sum(weighted_extra, axis=0, keepdims=True)
            scores_grad = (weighted - probs * inner).astype(bf16)
            scores_extra = (weighted_extra - probs_extra * inner).astype(bf16)
            query_t = dot_nn(key_t[:, :seen], scores_grad) + dot_nn(persist_t, scores_extra)
            query_sum[span, :] += query_t.T * factor
            key_sum[:seen, :] += dot_nn(scores_grad, query) * factor
            value_sum[:seen, :] += dot_nn(probs.astype(bf16), rise)
            persist_k_total += dot_nn(scores_extra, query) * factor
            persist_v_total += dot_nn(probs_extra.astype(bf16), rise)
        persist_k_grad[h] = persist_k_total
        persist_v_grad[h] = persist_v_total
        for b in range(parts):
            span = slice(b * rows, (b + 1) * rows)
            target = block_rows(jnp.bitwise_xor(me, b) * rows, rows)
            qkv_grad[target, col:col + size] = query_sum[span, :].astype(bf16)
            qkv_grad[target, cols + col:cols + col + size] = key_sum[span, :].astype(bf16)
            qkv_grad[target, 2 * cols + col:2 * cols + col + size] = value_sum[span, :].astype(bf16)


vmem = functools.partial(pl.BlockSpec, memory_space=pltpu.VMEM)
smem = functools.partial(pl.BlockSpec, memory_space=pltpu.SMEM)
vmem_limit = 56 << 20


def attend_and_recall(place, length, momentum, decay, step_size, qkv, persist_k, persist_v, parts):
    heads, _, size = persist_k.shape
    seq_len = qkv.shape[0]
    blocks = momentum.shape[0]
    cols = heads * size
    return pl.pallas_call(
        functools.partial(forward_kernel, heads, blocks, parts),
        out_shape=(
            jax.ShapeDtypeStruct((seq_len, cols), bf16),
            jax.ShapeDtypeStruct((heads, seq_len), f32),
            jax.ShapeDtypeStruct((heads, blocks, size, size), bf16),
            jax.ShapeDtypeStruct((heads, blocks, size, size), f32),
        ),
        in_specs=[smem()] * 5 + [vmem()] * 3,
        out_specs=(vmem(),) * 4,
        scratch_shapes=[pltpu.VMEM((seq_len, 3 * cols), bf16), pltpu.VMEM((seq_len, cols), f32)],
        compiler_params=pltpu.CompilerParams(vmem_limit_bytes=vmem_limit),
        cost_estimate=pl.CostEstimate(flops=12_000_000_000, bytes_accessed=8_000_000, transcendentals=2_000_000),
        name="attend_recall",
    )(place, length, momentum, decay, step_size, qkv, persist_k, persist_v)


def attend_and_recall_back(
    place, length, momentum, decay, step_size, qkv, mixed_grad, persist_k, persist_v, log_total, states, grams, parts
):
    heads, persistent, size = persist_k.shape
    seq_len = qkv.shape[0]
    blocks = momentum.shape[0]
    cols = heads * size
    return pl.pallas_call(
        functools.partial(backward_kernel, heads, blocks, parts),
        out_shape=(
            jax.ShapeDtypeStruct((seq_len, 3 * cols), bf16),
            jax.ShapeDtypeStruct((heads, persistent, size), f32),
            jax.ShapeDtypeStruct((heads, persistent, size), f32),
        ),
        in_specs=[smem()] * 5 + [vmem()] * 7,
        out_specs=(vmem(),) * 3,
        scratch_shapes=[
            pltpu.VMEM((seq_len, 3 * cols), bf16),
            pltpu.VMEM((seq_len, cols), bf16),
            pltpu.VMEM((heads, blocks, size, size), f32),
            pltpu.VMEM((seq_len, size), f32),
            pltpu.VMEM((seq_len, size), f32),
            pltpu.VMEM((seq_len, size), f32),
        ],
        compiler_params=pltpu.CompilerParams(vmem_limit_bytes=vmem_limit),
        cost_estimate=pl.CostEstimate(flops=25_000_000_000, bytes_accessed=12_000_000, transcendentals=2_000_000),
        name="attend_recall_back",
    )(place, length, momentum, decay, step_size, qkv, mixed_grad, persist_k, persist_v, log_total, states, grams)


def ring_place(index, count):
    odd = index % 2
    return (1 - odd) * (index // 2) + odd * (count - 1 - index // 2)


def ring_index(place, count):
    late = place // (count // 2)
    return (1 - late) * (2 * place) + late * (2 * (count - 1 - place) + 1)


def flip(index, bit):
    return index + bit * (1 - 2 * ((index // bit) % 2))


def bits_below(count):
    return [1 << k for k in range(count.bit_length() - 1)]


def relative(index, block):
    for bit in (1, 2):
        if block & bit:
            index = flip(index, bit)
    return index


def remote(source, target, send_sem, recv_sem, device):
    return pltpu.make_async_remote_copy(
        src_ref=source, dst_ref=target, send_sem=send_sem, recv_sem=recv_sem,
        device_id=device, device_id_type=pl.DeviceIdType.MESH,
    )


class Ring:
    def __init__(self, count, by_rows, source, out, slots, send_sem, recv_sem, home, home_sem):
        self.homeward = pltpu.make_async_copy(out, home, home_sem)
        self.count, self.by_rows = count, by_rows
        self.source, self.out, self.slots = source, out, slots
        self.send_sem, self.recv_sem = send_sem, recv_sem
        index = lax.axis_index("dp")
        self.place = ring_place(index, count)
        self.peers = (
            {"dp": ring_index((self.place + 1) % count, count)},
            {"dp": ring_index((self.place + count - 1) % count, count)},
        )
        self.step = 0
        self.copies = [None, None]
        self.sent = []

    def piece(self, ref, way, chunk):
        rows, cols = ref.shape
        chunk = chunk % self.count
        if self.by_rows:
            size = rows // (2 * self.count)
            return ref.at[pl.ds(pl.multiple_of(chunk * (2 * size) + way * size, size), size), :]
        size, width = rows // 2, cols // self.count
        return ref.at[way * size:(way + 1) * size, pl.ds(pl.multiple_of(chunk * width, width), width)]

    def chunk(self, way, step):
        return self.place + self.count + (2 * self.count - step if way == 0 else step)

    def launch(self, way, step, source, target):
        copy = remote(source, target, self.send_sem.at[way, step], self.recv_sem.at[way, step], self.peers[way])
        copy.start()
        self.copies[way] = copy
        self.sent.append(copy)

    def start_way(self, way):
        self.launch(way, 0, self.piece(self.source, way, self.chunk(way, 0)), self.slots.at[way, 0])

    def start(self):
        for way in range(2):
            self.start_way(way)

    def advance(self):
        count, step = self.count, self.step
        for way in range(2):
            self.copies[way].wait_recv()
            if step < count - 1:
                chunk = self.chunk(way, step + 1)
                total = self.slots[way, step].astype(f32) + self.piece(self.source, way, chunk)[...].astype(f32)
                if step < count - 2:
                    self.slots[way, step] = total.astype(bf16)
                    source, target = self.slots.at[way, step], self.slots.at[way, step + 1]
                else:
                    source = target = self.piece(self.out, way, chunk)
                    source[...] = total.astype(bf16)
            else:
                source = target = self.piece(self.out, way, self.chunk(way, step + 1 - count))
            if step < 2 * count - 3:
                self.launch(way, step + 1, source, target)
        self.step += 1
        if self.step < 2 * count - 2:
            return True
        for copy in self.sent:
            copy.wait_send()
        self.homeward.start()
        return False

    def left(self):
        return 2 * self.count - 2 - self.step


class SmallSum:
    def __init__(self, value, slots, shared, send_sem, recv_sem, count, parts):
        self.value, self.slots, self.shared = value, slots, shared
        self.send_sem, self.recv_sem = send_sem, recv_sem
        index, inner = lax.axis_index("dp"), lax.axis_index("tensor")
        self.inner = len(bits_below(parts))
        self.peers = [{"tensor": flip(inner, bit)} for bit in bits_below(parts)]
        self.peers += [{"dp": flip(index, bit)} for bit in bits_below(count)]
        self.step = 0

    def start(self):
        used = slice(0, self.shared if self.step < self.inner else self.value.shape[0])
        self.used = used
        self.copy = remote(
            self.value.at[used], self.slots.at[self.step, used], self.send_sem.at[self.step],
            self.recv_sem.at[self.step], self.peers[self.step],
        )
        self.copy.start()

    def left(self):
        return len(self.peers) - self.step

    def advance(self):
        self.copy.wait()
        self.value[self.used] += self.slots[self.step, self.used]
        self.step += 1
        if self.step < len(self.peers):
            self.start()
        return self.step < len(self.peers)


class Rounds:
    def __init__(self):
        self.queue = []

    def add(self, *flows):
        for flow in flows:
            flow.start()
            self.queue.append(flow)

    def spread(self, fast, slow):
        fast = [flow for flow in fast if flow in self.queue]
        slow = [flow for flow in slow if flow in self.queue]
        counts = {flow: flow.left() for flow in fast + slow}
        rest = [flow for k in range(max([counts[flow] for flow in slow], default=0)) for flow in slow if k < counts[flow]]
        turns = max(counts[flow] for flow in fast)
        self.queue = []
        for k in range(turns):
            self.queue += [flow for flow in fast if k < counts[flow]]
            self.queue += rest[k * len(rest) // turns:(k + 1) * len(rest) // turns]

    def mix(self, flow):
        for k in range(flow.left()):
            self.queue.insert(min(6 * k + 4, len(self.queue)), flow)

    def tick(self, count=1):
        for _ in range(count):
            if self.queue:
                flow = self.queue.pop(0)
                if flow.advance() and flow not in self.queue:
                    self.queue.append(flow)

    def finish(self):
        while self.queue:
            self.tick()


def rows_scale(value):
    return lax.rsqrt(jnp.mean(value * value, axis=-1, keepdims=True) + norm_eps)


class Scatter:
    def __init__(self, sent, landed, hold, send_sem, recv_sem):
        self.sent, self.landed, self.hold = sent, landed, hold
        self.send_sem, self.recv_sem = send_sem, recv_sem
        self.rows = hold.shape[0] // 2
        inner = lax.axis_index("tensor")
        self.sibling, self.across = {"tensor": flip(inner, 1)}, {"tensor": flip(inner, 2)}

    def span(self, j):
        return slice(j * self.rows, (j + 1) * self.rows)

    def copy(self, k, j, device):
        return remote(
            self.sent.at[k, self.span(j)], self.landed.at[k, self.span(j)],
            self.send_sem.at[k, j], self.recv_sem.at[k, j], device,
        )

    def begin(self, block, tick):
        first = [self.copy(0, j, self.sibling) for j in range(2)]
        self.second = [self.copy(1, j, self.across) for j in range(2)]
        self.third = [self.copy(2, j, self.sibling) for j in range(2)]
        for j in range(2):
            self.sent[0, self.span(j)] = block(3, j).astype(bf16)
            first[j].start()
        for j in range(2):
            self.hold[self.span(j), :] = block(2, j)
        tick()
        for j in range(2):
            first[j].wait()
            self.sent[1, self.span(j)] = (
                self.hold[self.span(j), :] + self.landed[0, self.span(j)].astype(f32)
            ).astype(bf16)
            self.second[j].start()
        for j in range(2):
            self.sent[2, self.span(j)] = block(1, j).astype(bf16)
            self.third[j].start()
        tick()
        for j in range(2):
            self.hold[self.span(j), :] = block(0, j)

    def finish(self, j):
        span = self.span(j)
        self.third[j].wait()
        self.second[j].wait()
        return self.hold[span, :] + self.landed[2, span].astype(f32) + self.landed[1, span].astype(f32)


class Gather:
    def __init__(self, full, parts, send_sem, recv_sem):
        self.full, self.rows = full, full.shape[0] // (2 * parts)
        self.send_sem, self.recv_sem = send_sem, recv_sem
        inner = lax.axis_index("tensor")
        self.sibling, self.across = {"tensor": flip(inner, 1)}, {"tensor": flip(inner, 2)}
        self.far, self.near, self.both = [None] * 2, [None] * 2, [None] * 2

    def copy(self, source, target, k, j, device):
        def piece(b):
            first = (2 * b + j) * self.rows
            return self.full.at[first:first + self.rows, :]

        return remote(piece(source), piece(target), self.send_sem.at[k, j], self.recv_sem.at[k, j], device)

    def begin(self, j):
        self.far[j], self.near[j] = self.copy(0, 2, 0, j, self.across), self.copy(0, 1, 1, j, self.sibling)
        self.far[j].start()
        self.near[j].start()

    def forward(self, then=lambda j: None):
        for j in range(2):
            self.far[j].wait()
            then(j)
            self.both[j] = self.copy(2, 3, 2, j, self.sibling)
            self.both[j].start()

    def wait(self, copies):
        for copy in copies:
            copy.wait()


def dot_pair(high, low, right):
    return dot_nn(jnp.concatenate([high, low], axis=1), jnp.concatenate([right, right], axis=0))


def layer_kernel(
    heads, blocks, parts, count, shared, pace,
    length, momentum, decay, step_size,
    inputs_h, cotangent_h, gain_attn, gain_ffn, persist_k, persist_v,
    w_query_h, w_key_h, w_value_h, w_out_h, w_gate_h, w_up_h, w_down_h,
    gate_home, up_home, down_home, query_home, key_home, value_home, out_home, result_home, input_grad_home, small,
    w_qkv, w_out, w_gate, w_up, w_down,
    normed_attn, ordered, mixed, states, grams, log_total,
    middle, hold, middle_grad, normed_ffn, out_full, gate_grad, up_grad, hidden,
    gate_source, up_source, down_source, query_source, key_source, value_source, out_source,
    gate_slots, up_slots, down_slots, query_slots, key_slots, value_slots, out_slots, small_slots,
    gate_out, up_out, down_out, query_out, key_out, value_out, out_out, result, input_grad,
    inputs, cotangent, sent_a, landed_a, sent_b, landed_b, middle_full, upstream, slopes, key_sum, value_sum, query_sum, qkv_grad,
    load_sem, home_sem, ring_send, ring_recv, small_send, small_recv, move_send, move_recv,
):
    size = persist_k.shape[2]
    many = persist_k.shape[1]
    cols = heads * size
    seq_len, width = middle_full.shape
    units = gate_grad.shape[0]
    rows = seq_len // parts
    span_rows = seq_len // blocks
    inner = lax.axis_index("tensor")
    valid_count = length[0]
    factor = size ** (-0.5)

    rounds = Rounds()
    rings = [
        Ring(count, by_rows, source, out, slots, ring_send.at[k], ring_recv.at[k], home, home_sem.at[k])
        for k, (by_rows, source, out, slots, home) in enumerate((
            (False, down_source, down_out, down_slots, down_home),
            (False, gate_source, gate_out, gate_slots, gate_home),
            (False, up_source, up_out, up_slots, up_home),
            (False, out_source, out_out, out_slots, out_home),
            (True, query_source, query_out, query_slots, query_home),
            (True, key_source, key_out, key_slots, key_home),
            (True, value_source, value_out, value_slots, value_home),
        ))
    ]
    small_sum = SmallSum(small, small_slots, shared, small_send, small_recv, count, parts)
    barrier = pltpu.get_barrier_semaphore()
    peers = list(rings[0].peers) + small_sum.peers
    for peer in peers:
        pl.semaphore_signal(barrier, inc=1, device_id=peer, device_id_type=pl.DeviceIdType.MESH)

    loads = []

    def load(source, target):
        copy = pltpu.make_async_copy(source, target, load_sem.at[len(loads)])
        copy.start()
        loads.append(copy)
        return copy

    input_load, cotangent_load = load(inputs_h, inputs), load(cotangent_h, cotangent)
    qkv_loads = [
        load(source, w_qkv.at[:, k * cols:(k + 1) * cols]) for k, source in enumerate((w_query_h, w_key_h, w_value_h))
    ]
    out_load = load(w_out_h, w_out)
    ffn_loads = [load(w_gate_h, w_gate), load(w_up_h, w_up), load(w_down_h, w_down)]

    def true_rows(b):
        return pl.ds(pl.multiple_of(relative(inner, b) * rows, rows), rows)

    def block_of(b):
        return slice(b * rows, (b + 1) * rows)

    row_place = inner * rows + lax.broadcasted_iota(jnp.int32, (rows, 1), 0)
    own_valid = (row_place < valid_count).astype(f32)
    stat_row = 2 * width // size

    def half_rows(j):
        return slice(j * (rows // 2), (j + 1) * (rows // 2))

    def part_of(b, j):
        return slice((2 * b + j) * (rows // 2), (2 * b + j + 1) * (rows // 2))

    def note(k, value, j):
        total = jnp.sum(jnp.sum(value, axis=1, keepdims=True) * own_valid[half_rows(j)], axis=0, keepdims=True)
        small[stat_row + k:stat_row + k + 1, :] += jnp.broadcast_to(total, (1, size))

    gather_attn = Gather(normed_attn, parts, move_send.at[0], move_recv.at[0])
    small[stat_row:stat_row + 8, :] = jnp.zeros((8, size), f32)

    def attn_norm(j):
        resid = inputs[half_rows(j), :].astype(f32)
        normed_attn[half_rows(j), :] = (resid * rows_scale(resid) * gain_attn[...]).astype(bf16)
        note(0, resid * resid, j)

    input_load.wait()
    attn_norm(0)
    pl.semaphore_wait(barrier, len(peers))
    gather_attn.begin(0)
    attn_norm(1)
    gather_attn.begin(1)
    cotangent_load.wait()
    out_full[0:rows, :] = (cotangent[...].astype(f32) * own_valid).astype(bf16)
    for j in range(2):
        note(5, jnp.ones((rows // 2, 1), f32), j)
    for copy in qkv_loads:
        copy.wait()

    def qkv_block(b):
        made = dot_nn(normed_attn[block_of(b), :], w_qkv[...])
        ordered[true_rows(b), :] = made.astype(bf16)
        first = relative(inner, b) * (rows // span_rows)
        place = lax.broadcasted_iota(jnp.int32, (rows, 1), 0)
        live = (relative(inner, b) * rows + place < valid_count).astype(f32)
        for h in range(heads):
            col = h * size
            key_unit, _ = unit_rows(made[:, cols + col:cols + col + size].astype(bf16))
            value = made[:, 2 * cols + col:2 * cols + col + size].astype(bf16)
            live_unit = (key_unit * live).astype(bf16)
            empty = jnp.zeros((span_rows, size), bf16)
            spread = jnp.concatenate([
                jnp.concatenate([
                    live_unit[k * span_rows:(k + 1) * span_rows] if k == m else empty for m in range(rows // span_rows)
                ], axis=1) for k in range(rows // span_rows)
            ], axis=0)
            both = dot_nn(jnp.concatenate([value, key_unit.astype(bf16)], axis=1).T, spread).astype(bf16)
            for k in range(rows // span_rows):
                slopes[h, first + k] = both[:size, k * size:(k + 1) * size]
                grams[h, first + k] = both[size:, k * size:(k + 1) * size]

    qkv_block(0)
    gather_attn.wait(gather_attn.near)
    qkv_block(1)
    gather_cot = Gather(out_full, parts, move_send.at[1], move_recv.at[1])
    gather_attn.forward(gather_cot.begin)
    qkv_block(2)
    gather_attn.wait(gather_attn.both)
    qkv_block(3)

    diagonal = lax.broadcasted_iota(jnp.int32, (rows, rows), 0) <= lax.broadcasted_iota(jnp.int32, (rows, rows), 1)
    tiles = [(h, i) for i in range(parts) for h in range(heads)]

    def masked_scores(h, i, query):
        seen = (i + 1) * rows
        scores = dot_nt(ordered[:seen, cols + h * size:cols + (h + 1) * size], query)
        last = jnp.where(diagonal, scores[seen - rows:], -1e30)
        return last if i == 0 else jnp.concatenate([scores[:seen - rows], last], axis=0)

    value_t = [ordered[:, 2 * cols + h * size:2 * cols + (h + 1) * size].T for h in range(heads)]
    persist_t = [persist_v[h].astype(f32).T.astype(bf16) for h in range(heads)]

    def attend(h, i):
        seen, col = (i + 1) * rows, h * size
        query = ordered[block_of(i), col:col + size]
        scores = masked_scores(h, i, query)
        extra = dot_nt(persist_k[h], query)
        top = jnp.maximum(jnp.max(scores, axis=0, keepdims=True), jnp.max(extra, axis=0, keepdims=True))
        lifted = jnp.exp2((scores - top) * (factor * log2_e))
        lifted_extra = jnp.exp2((extra - top) * (factor * log2_e))
        total = jnp.sum(lifted, axis=0, keepdims=True) + jnp.sum(lifted_extra, axis=0, keepdims=True)
        attended = dot_nn(value_t[h][:, :seen], lifted.astype(bf16)) + dot_nn(persist_t[h], lifted_extra.astype(bf16))
        log_total[h:h + 1, block_of(i)] = top * (factor * log2_e) + jnp.log2(total)
        query_sum[block_of(i), col:col + size] = (attended * (1.0 / total)).T

    carried = [(jnp.zeros((size, size), f32), jnp.zeros((size, size), f32)) for _ in range(heads)]
    for c in range(blocks):
        for h in range(heads):
            memory, velocity = carried[h]
            high, low_part = halves(memory)
            states[h, c] = high
            change = dot_pair(high, low_part, grams[h, c]) - slopes[h, c].astype(f32)
            velocity = momentum[h, c] * velocity - step_size[h, c] * change
            memory = (1.0 - decay[h, c]) * memory + velocity
            carried[h] = (memory, velocity)
        for h, i in tiles[c * len(tiles) // blocks:(c + 1) * len(tiles) // blocks]:
            attend(h, i)
    def mix(b):
        span, first = true_rows(b), relative(inner, b) * (rows // span_rows)
        for h in range(heads):
            wide = slice(h * size, (h + 1) * size)
            query_unit = unit_rows(ordered[span, wide])[0].astype(bf16)
            reads = [
                dot_nt(query_unit[k * span_rows:(k + 1) * span_rows], states[h, first + k])
                for k in range(rows // span_rows)
            ]
            mixed[block_of(b), wide] = (query_sum[span, wide] + jnp.concatenate(reads, axis=0)).astype(bf16)

    def project(b, j):
        if j == 0:
            mix(b)
        return dot_nn(mixed[part_of(b, j), :], w_out[...])

    out_load.wait()
    scatter = Scatter(sent_a, landed_a, hold, move_send.at[2], move_recv.at[2])
    scatter.begin(project, rounds.tick)
    gather_cot.wait(gather_cot.near)
    gather_cot.forward()
    gather_ffn = Gather(normed_ffn, parts, move_send.at[3], move_recv.at[3])
    for j in range(2):
        branch = scatter.finish(j)
        value = inputs[half_rows(j), :].astype(f32) + branch
        middle[half_rows(j), :] = value
        normed_ffn[half_rows(j), :] = (value * rows_scale(value) * gain_ffn[...]).astype(bf16)
        gather_ffn.begin(j)
        note(3, branch * branch, j)
        note(1, value * value, j)
    for copy in ffn_loads:
        copy.wait()
    gather_cot.wait(gather_cot.both)
    gather_ffn.wait(gather_ffn.near)

    piece = units // 4

    def feed(tokens):
        for k in range(4):
            span = slice(k * piece, (k + 1) * piece)
            gate = dot_nt(w_gate[span, :], normed_ffn[tokens, :])
            up = dot_nt(w_up[span, :], normed_ffn[tokens, :])
            hidden_grad = dot_nt(w_down[span, :], out_full[tokens, :])
            sigmoid = jax.nn.sigmoid(gate)
            silu = gate * sigmoid
            hidden[span, tokens] = (silu * up).astype(bf16)
            up_grad[span, tokens] = (hidden_grad * silu).astype(bf16)
            gate_grad[span, tokens] = (hidden_grad * up * sigmoid * (1.0 + gate * (1.0 - sigmoid))).astype(bf16)

    feed(slice(0, 2 * rows))
    gather_ffn.forward()
    feed(block_of(2))
    gather_ffn.wait(gather_ffn.both)
    feed(block_of(3))
    for source, left, right, ring in (
        (down_source, hidden, out_full, rings[0]), (gate_source, gate_grad, normed_ffn, rings[1]),
        (up_source, up_grad, normed_ffn, rings[2]),
    ):
        for way in range(2):
            span = slice(way * (units // 2), (way + 1) * (units // 2))
            source[span, :] = dot_nn(left[span, :], right[...]).astype(bf16)
            ring.start_way(way)
        rounds.queue.append(ring)

    scatter = Scatter(sent_b, landed_b, hold, move_send.at[4], move_recv.at[4])
    scatter.begin(
        lambda b, j: dot_tn(gate_grad[:, part_of(b, j)], w_gate[...]) + dot_tn(up_grad[:, part_of(b, j)], w_up[...]),
        rounds.tick,
    )
    rounds.tick(pace[0])
    for b in range(parts):
        normed_ffn[:, block_of(b)] = normed_attn[block_of(b), :].T
        rounds.tick(pace[9])
    gather_middle = Gather(middle_full, parts, move_send.at[5], move_recv.at[5])
    gain_row = jnp.zeros((1, width), f32)
    for j in range(2):
        normed_grad = scatter.finish(j)
        value = middle[half_rows(j), :]
        scale = rows_scale(value)
        weighted = normed_grad * gain_ffn[...]
        grad = (
            cotangent[half_rows(j), :].astype(f32) * own_valid[half_rows(j)] + scale * weighted
            - value * (scale * scale * scale) * jnp.mean(weighted * value, axis=-1, keepdims=True)
        )
        middle_grad[half_rows(j), :] = grad
        middle_full[half_rows(j), :] = grad.astype(bf16)
        gather_middle.begin(j)
        gain_row = gain_row + jnp.sum(normed_grad * value * scale, axis=0, keepdims=True)
        if j == 0:
            rounds.tick(pace[8])
    for k in range(width // size):
        small[width // size + k:width // size + k + 1, :] = gain_row[:, k * size:(k + 1) * size]
    rounds.tick(pace[1])
    gather_middle.wait(gather_middle.near)

    def mixed_block(b):
        upstream[true_rows(b), :] = dot_nt(middle_full[block_of(b), :], w_out[...]).astype(bf16)

    mixed_block(0)
    mixed_block(1)
    gather_middle.forward()
    mixed_block(2)
    gather_middle.wait(gather_middle.both)
    mixed_block(3)
    scatter = Scatter(sent_a, landed_a, hold, move_send.at[6], move_recv.at[6])
    scatter.begin(lambda b, j: dot_tn(hidden[:, part_of(b, j)], w_down[...]), rounds.tick)
    rounds.tick(pace[2])
    out_source[...] = dot_tn(mixed[...], middle_full[...]).astype(bf16)
    rounds.add(rings[3])

    key_t = [ordered[:, cols + h * size:cols + (h + 1) * size].T for h in range(heads)]
    persist_t = [persist_k[h].astype(f32).T.astype(bf16) for h in range(heads)]
    persist_sums = [[jnp.zeros((many, size), f32), jnp.zeros((many, size), f32)] for _ in range(heads)]

    def attend_back(h, i):
        span, seen, col = block_of(i), (i + 1) * rows, h * size
        wide = slice(col, col + size)
        query = ordered[span, wide]
        rise = upstream[span, wide]
        scores = masked_scores(h, i, query)
        extra = dot_nt(persist_k[h], query)
        base = log_total[h:h + 1, span]
        probs = jnp.exp2(scores * (factor * log2_e) - base)
        probs_extra = jnp.exp2(extra * (factor * log2_e) - base)
        probs_grad = dot_nt(ordered[:seen, 2 * cols + col:2 * cols + col + size], rise)
        extra_grad = dot_nt(persist_v[h], rise)
        weighted = probs * probs_grad
        weighted_extra = probs_extra * extra_grad
        inner_sum = jnp.sum(weighted, axis=0, keepdims=True) + jnp.sum(weighted_extra, axis=0, keepdims=True)
        scores_grad = (weighted - probs * inner_sum).astype(bf16)
        scores_extra = (weighted_extra - probs_extra * inner_sum).astype(bf16)
        query_t = dot_nn(key_t[h][:, :seen], scores_grad) + dot_nn(persist_t[h], scores_extra)
        query_sum[span, wide] = query_t.T * factor
        key_part = dot_nn(scores_grad, query) * factor
        value_part = dot_nn(probs.astype(bf16), rise)
        for ref, part in ((key_sum, key_part), (value_sum, value_part)):
            ref[span, wide] = part[seen - rows:]
            if i:
                ref[:seen - rows, wide] += part[:seen - rows]
        persist_sums[h][0] += dot_nn(scores_extra, query) * factor
        persist_sums[h][1] += dot_nn(probs_extra.astype(bf16), rise)

    carried = [(jnp.zeros((size, size), f32), jnp.zeros((size, size), f32)) for _ in range(heads)]
    for c in reversed(range(blocks)):
        span = slice(c * span_rows, (c + 1) * span_rows)
        for h in range(heads):
            col = h * size
            query_unit, _ = unit_rows(ordered[span, col:col + size])
            rise = upstream[span, col:col + size]
            entry = dot_tn(rise, query_unit.astype(bf16))
            memory, velocity = carried[h]
            velocity = velocity + memory
            change = (-step_size[h, c]) * velocity
            slopes[h, c] = change.astype(bf16)
            memory = (1.0 - decay[h, c]) * memory + entry + dot_pair(*halves(change), grams[h, c])
            velocity = momentum[h, c] * velocity
            carried[h] = (memory, velocity)
        done = blocks - 1 - c
        for h, i in tiles[done * len(tiles) // blocks:(done + 1) * len(tiles) // blocks]:
            attend_back(h, i)
        rounds.tick(pace[3][done])

    for h in range(heads):
        col = h * size
        wide = slice(col, col + size)
        for c in range(blocks):
            span = slice(c * span_rows, (c + 1) * span_rows)
            live = (c * span_rows + lax.broadcasted_iota(jnp.int32, (span_rows, 1), 0) < valid_count).astype(f32)
            query_unit, query_scale = unit_rows(ordered[span, wide])
            key_unit, key_scale = unit_rows(ordered[span, cols + col:cols + col + size])
            value = ordered[span, 2 * cols + col:2 * cols + col + size].astype(f32)
            rise = upstream[span, wide]
            state = states[h, c]
            slope = slopes[h, c]
            error = (dot_nt(key_unit.astype(bf16), state) - value) * live
            error_grad = dot_nt(key_unit.astype(bf16), slope) * live
            unit_grad = dot_nn(error.astype(bf16), slope) + dot_nn(error_grad.astype(bf16), state)
            key_sum[span, wide] += key_scale * (
                unit_grad - key_unit * jnp.sum(unit_grad * key_unit, axis=-1, keepdims=True)
            )
            value_sum[span, wide] -= error_grad
            read_grad = dot_nn(rise, state)
            query_sum[span, wide] += query_scale * (
                read_grad - query_unit * jnp.sum(read_grad * query_unit, axis=-1, keepdims=True)
            )
            rounds.tick(pace[4][c])
        small[shared + h * many:shared + (h + 1) * many, :] = persist_sums[h][0]
        small[shared + (heads + h) * many:shared + (heads + h + 1) * many, :] = persist_sums[h][1]
    for b in range(parts):
        target = true_rows(b)
        qkv_grad[target, 0:cols] = query_sum[block_of(b), :].astype(bf16)
        qkv_grad[target, cols:2 * cols] = key_sum[block_of(b), :].astype(bf16)
        qkv_grad[target, 2 * cols:3 * cols] = value_sum[block_of(b), :].astype(bf16)

    for j in range(2):
        branch = scatter.finish(j)
        note(4, branch * branch, j)
        value = middle[half_rows(j), :] + branch
        note(2, value * value, j)
        result[half_rows(j), :] = value.astype(bf16)
    homes = [pltpu.make_async_copy(result, result_home, home_sem.at[len(rings)])]
    homes[0].start()

    for b in range(parts):
        span = block_of(b)
        grad = dot_nn(normed_ffn[span, :], qkv_grad[...])
        for k, source in enumerate((query_source, key_source, value_source)):
            source[span, :] = grad[:, k * cols:(k + 1) * cols].astype(bf16)
        rounds.tick(pace[6])
    rounds.add(*rings[4:])
    rounds.spread(rings[3:], rings[:3])
    scatter = Scatter(sent_b, landed_b, hold, move_send.at[7], move_recv.at[7])
    scatter.begin(lambda b, j: dot_nt(qkv_grad[part_of(b, j), :], w_qkv[...]), lambda: rounds.tick(pace[10]))
    for b in range(parts):
        span = block_of(b)
        products = sum(
            source[span, :].astype(f32) * w_qkv[span, k * cols:(k + 1) * cols].astype(f32)
            for k, source in enumerate((query_source, key_source, value_source))
        )
        gain_row = jnp.sum(products.T, axis=0, keepdims=True) / gain_attn[:, span]
        for k in range(rows // size):
            row = b * (rows // size) + k
            small[row:row + 1, :] = gain_row[:, k * size:(k + 1) * size]
        rounds.tick(pace[7])
    small_sum.start()
    rounds.mix(small_sum)
    for j in range(2):
        normed_grad = scatter.finish(j)
        value = inputs[half_rows(j), :].astype(f32)
        scale = rows_scale(value)
        weighted = normed_grad * gain_attn[...]
        input_grad[half_rows(j), :] = (
            middle_grad[half_rows(j), :] + scale * weighted
            - value * (scale * scale * scale) * jnp.mean(weighted * value, axis=-1, keepdims=True)
        ).astype(bf16)
    homes.append(pltpu.make_async_copy(input_grad, input_grad_home, home_sem.at[len(rings) + 1]))
    homes[1].start()
    rounds.finish()
    for copy in homes + [ring.homeward for ring in rings]:
        copy.wait()


def whole_layer(
    length, momentum, decay, step_size, inputs, cotangent, gain_attn, gain_ffn, persist_k, persist_v,
    w_query, w_key, w_value, w_out, w_gate, w_up, w_down, count, parts,
):
    heads, many, size = persist_k.shape
    blocks = momentum.shape[1]
    cols = heads * size
    rows, width = inputs.shape
    seq_len = rows * parts
    units = w_gate.shape[0]
    shared = 2 * width // size + 8
    small_rows = shared + 2 * heads * many
    flows = len(bits_below(count)) + len(bits_below(parts))

    def row_slots(*shape):
        return pltpu.VMEM((2, count - 1, shape[0] // (2 * count), shape[1]), bf16)

    def col_slots(*shape):
        return pltpu.VMEM((2, count - 1, shape[0] // 2, shape[1] // count), bf16)

    def low(*shape):
        return pltpu.VMEM(shape, bf16)

    def full(*shape):
        return pltpu.VMEM(shape, f32)

    def semaphores(*shape):
        return pltpu.SemaphoreType.DMA(shape)

    ffn = (units, width)
    return pl.pallas_call(
        functools.partial(layer_kernel, heads, blocks, parts, count, shared, pace),
        out_shape=(
            jax.ShapeDtypeStruct(ffn, bf16),
            jax.ShapeDtypeStruct(ffn, bf16),
            jax.ShapeDtypeStruct(ffn, bf16),
            jax.ShapeDtypeStruct((width, cols), bf16),
            jax.ShapeDtypeStruct((width, cols), bf16),
            jax.ShapeDtypeStruct((width, cols), bf16),
            jax.ShapeDtypeStruct((cols, width), bf16),
            jax.ShapeDtypeStruct((rows, width), bf16),
            jax.ShapeDtypeStruct((rows, width), bf16),
            jax.ShapeDtypeStruct((small_rows, size), f32),
        ),
        in_specs=[smem()] * 4 + [pl.BlockSpec(memory_space=pl.ANY)] * 2 + [vmem()] * 4 + [pl.BlockSpec(memory_space=pl.ANY)] * 7,
        out_specs=(pl.BlockSpec(memory_space=pl.ANY),) * 9 + (vmem(),),
        scratch_shapes=[
            low(width, 3 * cols), low(cols, width), low(*ffn), low(*ffn), low(*ffn),
            low(seq_len, width), low(seq_len, 3 * cols), low(seq_len, cols),
            low(heads, blocks, size, size), low(heads, blocks, size, size), full(heads, seq_len),
            full(rows, width), full(rows, width), full(rows, width), low(seq_len, width), low(seq_len, width),
            low(units, seq_len), low(units, seq_len), low(units, seq_len),
            low(*ffn), low(*ffn), low(*ffn), low(width, cols), low(width, cols), low(width, cols), low(cols, width),
            col_slots(*ffn), col_slots(*ffn), col_slots(*ffn),
            row_slots(width, cols), row_slots(width, cols), row_slots(width, cols), col_slots(cols, width),
            full(flows, small_rows, size),
            low(*ffn), low(*ffn), low(*ffn), low(width, cols), low(width, cols), low(width, cols), low(cols, width),
            low(rows, width), low(rows, width), low(rows, width), low(rows, width),
            low(3, rows, width), low(3, rows, width), low(3, rows, width), low(3, rows, width),
            low(seq_len, width), low(seq_len, cols), low(heads, blocks, size, size),
            full(seq_len, cols), full(seq_len, cols), full(seq_len, cols), low(seq_len, 3 * cols),
            semaphores(9), semaphores(9), semaphores(7, 2, 2 * count - 2), semaphores(7, 2, 2 * count - 2),
            semaphores(flows), semaphores(flows), semaphores(8, 3, 2), semaphores(8, 3, 2),
        ],
        compiler_params=pltpu.CompilerParams(
            vmem_limit_bytes=layer_limit, collective_id=0, has_side_effects=True
        ),
        cost_estimate=pl.CostEstimate(flops=150_000_000_000, bytes_accessed=40_000_000, transcendentals=4_000_000),
        name="whole_layer",
    )(
        length, momentum, decay, step_size, inputs, cotangent, gain_attn, gain_ffn, persist_k, persist_v,
        w_query, w_key, w_value, w_out, w_gate, w_up, w_down,
    )


def finish_kernel(casts, moves, *refs):
    total = casts + moves
    sources, small = refs[:total], refs[total]
    targets, refs = refs[total + 1:2 * total + 1], refs[2 * total + 1:]
    gain_attn, gain_ffn, persist_k, persist_v, roots = refs[:5]
    held, cast, semaphores = refs[5:5 + total], refs[5 + total:5 + total + casts], refs[5 + total + casts]
    arrive = [pltpu.make_async_copy(sources[k], held[k], semaphores.at[0, k]) for k in range(total)]
    leave = [
        pltpu.make_async_copy(cast[k] if k < casts else held[k], targets[k], semaphores.at[1, k])
        for k in range(total)
    ]
    ahead = total
    for copy in arrive[:ahead]:
        copy.start()
    lines = gain_attn.shape[0]
    heads, many, size = persist_k.shape
    gain_attn[...] = small[0:lines, :]
    gain_ffn[...] = small[lines:2 * lines, :]
    stats = small[2 * lines:2 * lines + 8, :]
    stats = jnp.sqrt(stats / (stats[5:6, :] * (lines * size)))
    for k in range(5):
        roots[k] = stats[k, 0]
    for h in range(heads):
        first = 2 * lines + 8 + h * many
        persist_k[h] = small[first:first + many, :]
        persist_v[h] = small[first + heads * many:first + (heads + 1) * many, :]
    for k in range(total):
        arrive[k].wait()
        if k + ahead < total:
            arrive[k + ahead].start()
        if k < casts:
            cast[k][...] = held[k][...].astype(f32)
        leave[k].start()
    for copy in leave:
        copy.wait()


def finish(sums, rest, small, persist_shape):
    casts, moves = len(sums), len(rest)
    size = small.shape[1]
    lines = (small.shape[0] - 2 * persist_shape[0] * persist_shape[1] - 8) // 2
    anywhere = pl.BlockSpec(memory_space=pl.ANY)
    return pl.pallas_call(
        functools.partial(finish_kernel, casts, moves),
        out_shape=tuple(jax.ShapeDtypeStruct(value.shape, f32) for value in sums)
        + tuple(jax.ShapeDtypeStruct(value.shape, value.dtype) for value in rest)
        + (jax.ShapeDtypeStruct((lines, size), f32),) * 2
        + (jax.ShapeDtypeStruct(persist_shape, f32),) * 2
        + (jax.ShapeDtypeStruct((5,), f32),),
        in_specs=[anywhere] * (casts + moves) + [vmem()],
        out_specs=(anywhere,) * (casts + moves) + (vmem(),) * 4 + (smem(),),
        scratch_shapes=[pltpu.VMEM(value.shape, value.dtype) for value in (*sums, *rest)]
        + [pltpu.VMEM(value.shape, f32) for value in sums]
        + [pltpu.SemaphoreType.DMA((2, casts + moves))],
        compiler_params=pltpu.CompilerParams(vmem_limit_bytes=vmem_limit),
        name="finish",
    )(*sums, *rest, small)


pace = (0, 6, 0, (0, 1) * 8, (0, 0, 0, 0, 0, 0, 0, 1) * 2, None, 1, 3, 2, 1, 3)
layer_limit = 63 << 20


def swap(value, axis, bit):
    count = lax.axis_size(axis)
    return lax.ppermute(value, axis, [(i, i ^ bit) for i in range(count)])


def norm_back(value, scale, gain, upstream):
    weighted = upstream * gain
    return scale * weighted - value * (scale * scale * scale) * jnp.mean(
        weighted * value, axis=-1, keepdims=True
    )


def gather_rows(own):
    far = swap(own, "tensor", 2)
    near = swap(own, "tensor", 1)
    both = swap(far, "tensor", 1)
    return jnp.concatenate([own, near], 0), jnp.concatenate([far, both], 0)


def scatter_rows(near, far):
    rows = near.shape[0] // 2
    far_sum = far[:rows] + swap(far[rows:].astype(bf16), "tensor", 1).astype(f32)
    far_in = swap(far_sum.astype(bf16), "tensor", 2).astype(f32)
    near_in = swap(near[rows:].astype(bf16), "tensor", 1).astype(f32)
    return near[:rows] + near_in + far_in


def mul(left, right):
    return jnp.dot(left, right, preferred_element_type=f32)


def mul_nt(left, right):
    return jnp.einsum("ab,cb->ac", left, right, preferred_element_type=f32)


def mul_tn(left, right):
    return jnp.einsum("ab,ac->bc", left, right, preferred_element_type=f32)


def fits_ring(count, parts, *shapes):
    if count & (count - 1) or parts != 4 or count < 4:
        return False
    return all(rows % (32 * count) == 0 or (rows % 32 == 0 and cols % (128 * count) == 0) for rows, cols in shapes)


def body(
    inputs, cotangent, lengths, gain_attn, w_query, w_key, w_value, w_out, persist_keys, persist_values,
    gain_ffn, w_gate, w_up, w_down, momentum, decay, step_size,
):
    parts = lax.axis_size("tensor")
    count = lax.axis_size("dp")
    rows = inputs.shape[1]
    width = inputs.shape[2]
    half = 2 * rows
    cols = w_query.shape[1]
    size = persist_keys.shape[2]
    place = lax.axis_index("tensor")
    first_row = place * rows
    own_valid = (first_row + jnp.arange(rows, dtype=jnp.int32) < lengths[0]).astype(f32)[:, None]
    places = place.astype(jnp.int32).reshape(1)
    rates = (places, lengths, momentum[0], decay[0], step_size[0])

    if fits_ring(count, parts, (w_down.shape), (width, 3 * cols), (cols, width)):
        *sums, result, input_grad, small = whole_layer(
            lengths, momentum[0].T, decay[0].T, step_size[0].T, inputs[0], cotangent[0], gain_attn[None], gain_ffn[None], persist_keys, persist_values,
            w_query, w_key, w_value, w_out, w_gate.T, w_up.T, w_down, count, parts,
        )
        gate_sum, up_sum, down_sum, query_sum, key_sum, value_sum, out_sum, *rest = finish(
            sums, (result, input_grad), small, persist_keys.shape
        )
        result, input_grad, gain_attn_sum, gain_ffn_sum, persist_k_sum, persist_v_sum, rms_stats = rest
    else:
        resid = inputs[0].astype(f32)
        scale_attn = rows_scale(resid)
        near, far = gather_rows((resid * scale_attn * gain_attn).astype(bf16))
        w_qkv = jnp.concatenate([w_query, w_key, w_value], 1)
        qkv = jnp.concatenate([mul(near, w_qkv).astype(bf16), mul(far, w_qkv).astype(bf16)], 0)
        normed_attn = jnp.concatenate([near, far], 0)
        mixed, log_total, states, grams = attend_and_recall(*rates, qkv, persist_keys, persist_values, parts)
        branch_attn = scatter_rows(mul(mixed[:half], w_out), mul(mixed[half:], w_out))
        middle = resid + branch_attn
        scale_ffn = rows_scale(middle)
        normed_ffn = jnp.concatenate(gather_rows((middle * scale_ffn * gain_ffn).astype(bf16)), 0)

        out_grad = cotangent[0].astype(f32) * own_valid
        out_full = jnp.concatenate(gather_rows(out_grad.astype(bf16)), 0)
        gate = mul(normed_ffn, w_gate)
        up = mul(normed_ffn, w_up)
        sigmoid = jax.nn.sigmoid(gate)
        silu = gate * sigmoid
        hidden = (silu * up).astype(bf16)
        branch_ffn = scatter_rows(mul(hidden[:half], w_down), mul(hidden[half:], w_down))
        result = middle + branch_ffn
        hidden_grad = mul_nt(out_full, w_down)
        gate_grad = (hidden_grad * up * sigmoid * (1.0 + gate * (1.0 - sigmoid))).astype(bf16)
        up_grad = (hidden_grad * silu).astype(bf16)

        def masked(value_in):
            return jnp.sum(own_valid * (value_in * value_in))

        squares = jnp.stack(
            [masked(resid), masked(middle), masked(result), masked(branch_attn), masked(branch_ffn), jnp.sum(own_valid)]
        )
        grad_down = mul_tn(hidden, out_full).astype(bf16)
        grad_gate = mul_tn(gate_grad, normed_ffn).astype(bf16)
        grad_up = mul_tn(up_grad, normed_ffn).astype(bf16)
        normed_ffn_grad = scatter_rows(
            mul_nt(gate_grad[:half], w_gate) + mul_nt(up_grad[:half], w_up),
            mul_nt(gate_grad[half:], w_gate) + mul_nt(up_grad[half:], w_up),
        )
        gain_ffn_part = jnp.sum(normed_ffn_grad * middle * scale_ffn, axis=0)
        middle_grad = out_grad + norm_back(middle, scale_ffn, gain_ffn, normed_ffn_grad)
        middle_full = jnp.concatenate(gather_rows(middle_grad.astype(bf16)), 0)
        mixed_grad = mul_nt(middle_full, w_out).astype(bf16)
        qkv_grad, persist_k_grad, persist_v_grad = attend_and_recall_back(
            *rates, qkv, mixed_grad, persist_keys, persist_values, log_total, states, grams, parts
        )
        normed_attn_grad = scatter_rows(mul_nt(qkv_grad[:half], w_qkv), mul_nt(qkv_grad[half:], w_qkv))
        gain_attn_part = jnp.sum(normed_attn_grad * resid * scale_attn, axis=0)
        input_grad = (middle_grad + norm_back(resid, scale_attn, gain_attn, normed_attn_grad)).astype(bf16)
        gate_sum, up_sum, down_sum, wide, out_sum, persist_sums = lax.psum(
            (grad_gate, grad_up, grad_down, mul_tn(normed_attn, qkv_grad).astype(bf16),
             mul_tn(mixed, middle_full).astype(bf16), jnp.stack([persist_k_grad, persist_v_grad])), "dp"
        )
        query_sum, key_sum, value_sum = wide[:, :cols], wide[:, cols:2 * cols], wide[:, 2 * cols:]
        gains, squares = lax.psum((jnp.concatenate([gain_attn_part, gain_ffn_part]), squares), ("dp", "tensor"))
        gain_attn_sum, gain_ffn_sum = gains[:width], gains[width:]
        persist_k_sum, persist_v_sum = persist_sums[0], persist_sums[1]
        rms_stats = jnp.sqrt(squares[:5] / (squares[5] * width))
    return (
        result.astype(bf16)[None],
        input_grad[None],
        gain_attn_sum.reshape(-1),
        query_sum.astype(f32),
        key_sum.astype(f32),
        value_sum.astype(f32),
        out_sum.astype(f32),
        persist_k_sum,
        persist_v_sum,
        gain_ffn_sum.reshape(-1),
        gate_sum.astype(f32).T,
        up_sum.astype(f32).T,
        down_sum.astype(f32),
        rms_stats,
    )


def solution(mesh):
    in_specs = (
        P("dp", "tensor", None),
        P("dp", "tensor", None),
        P("dp"),
        P(),
        P(None, "tensor"),
        P(None, "tensor"),
        P(None, "tensor"),
        P("tensor", None),
        P("tensor", None, None),
        P("tensor", None, None),
        P(),
        P(None, "tensor"),
        P(None, "tensor"),
        P("tensor", None),
        P("dp", None, "tensor"),
        P("dp", None, "tensor"),
        P("dp", None, "tensor"),
    )
    out_specs = (
        P("dp", "tensor", None),
        P("dp", "tensor", None),
        P(),
        P(None, "tensor"),
        P(None, "tensor"),
        P(None, "tensor"),
        P("tensor", None),
        P("tensor", None, None),
        P("tensor", None, None),
        P(),
        P(None, "tensor"),
        P(None, "tensor"),
        P("tensor", None),
        P(),
    )
    return jax.shard_map(body, mesh=mesh, in_specs=in_specs, out_specs=out_specs, check_vma=False)
```

```python
import functools
import jax
import jax.numpy as jnp
from jax import lax
from jax.sharding import PartitionSpec as P
import jax.experimental.pallas as pl
import jax.experimental.pallas.tpu as pltpu

norm_eps = 1e-05
unit_eps = 1e-06
f32 = jnp.float32
bf16 = jnp.bfloat16
log2_e = 1.4426950408889634


def dot_nn(left, right):
    return lax.dot_general(left, right, (((1,), (0,)), ((), ())), preferred_element_type=f32)


def dot_nt(left, right):
    return lax.dot_general(left, right, (((1,), (1,)), ((), ())), preferred_element_type=f32)


def dot_tn(left, right):
    return lax.dot_general(left, right, (((0,), (0,)), ((), ())), preferred_element_type=f32)


def halves(value):
    high = value.astype(bf16)
    return high, (value - high.astype(f32)).astype(bf16)


def dot3(dot, left, right):
    (lh, ll), (rh, rl) = left, right
    return dot(lh, rh) + dot(ll, rh) + dot(lh, rl)


def unit_rows(value):
    wide = value.astype(f32)
    scale = lax.rsqrt(jnp.sum(wide * wide, axis=-1, keepdims=True) + unit_eps)
    return wide * scale, scale


def block_rows(start, width):
    return pl.ds(pl.multiple_of(start, width), width)


def forward_kernel(
    heads, blocks, parts,
    place, length, momentum, decay, step_size, qkv, persist_k, persist_v,
    mixed, log_total, states, grams,
    ordered, reads,
):
    seq_len, wide = qkv.shape
    size = persist_k.shape[2]
    cols = heads * size
    rows = seq_len // parts
    width = seq_len // blocks
    me = place[0]
    count = length[0]
    for b in range(parts):
        ordered[b * rows:(b + 1) * rows, :] = qkv[block_rows(jnp.bitwise_xor(me, b) * rows, rows), :]

    carried = [(jnp.zeros((size, size), f32), jnp.zeros((size, size), f32)) for _ in range(heads)]
    for c in range(blocks):
        span = slice(c * width, (c + 1) * width)
        live = (c * width + lax.broadcasted_iota(jnp.int32, (width, 1), 0) < count).astype(f32)
        for h in range(heads):
            col = h * size
            key_unit, _ = unit_rows(ordered[span, cols + col:cols + col + size])
            query_unit, _ = unit_rows(ordered[span, col:col + size])
            value = ordered[span, 2 * cols + col:2 * cols + col + size]
            key_h, key_l = halves(key_unit)
            live_h, live_l = halves(key_unit * live)
            gram = dot3(dot_tn, (live_h, live_l), (key_h, key_l))
            target = dot_tn(value, live_h) + dot_tn(value, live_l)
            memory, velocity = carried[h]
            states[h, c] = memory.astype(bf16)
            grams[h, c] = gram
            parts_m = halves(memory)
            reads[span, col:col + size] = dot_nt(query_unit.astype(bf16), parts_m[0])
            change = dot3(dot_nn, parts_m, halves(gram)) - target
            velocity = momentum[c, h] * velocity - step_size[c, h] * change
            memory = (1.0 - decay[c, h]) * memory + velocity
            carried[h] = (memory, velocity)

    factor = size ** (-0.5) * log2_e
    diagonal = lax.broadcasted_iota(jnp.int32, (rows, rows), 0) <= lax.broadcasted_iota(jnp.int32, (rows, rows), 1)
    for h in range(heads):
        col = h * size
        value_t = ordered[:, 2 * cols + col:2 * cols + col + size].T
        persist_t = persist_v[h].astype(f32).T.astype(bf16)
        for i in range(parts):
            span = slice(i * rows, (i + 1) * rows)
            seen = (i + 1) * rows
            query = ordered[span, col:col + size]
            scores = dot_nt(ordered[:seen, cols + col:cols + col + size], query)
            last = jnp.where(diagonal, scores[seen - rows:], -1e30)
            scores = last if i == 0 else jnp.concatenate([scores[:seen - rows], last], axis=0)
            extra = dot_nt(persist_k[h], query)
            top = jnp.maximum(jnp.max(scores, axis=0, keepdims=True), jnp.max(extra, axis=0, keepdims=True))
            lifted = jnp.exp2((scores - top) * factor)
            lifted_extra = jnp.exp2((extra - top) * factor)
            total = jnp.sum(lifted, axis=0, keepdims=True) + jnp.sum(lifted_extra, axis=0, keepdims=True)
            attended = dot_nn(value_t[:, :seen], lifted.astype(bf16)) + dot_nn(persist_t, lifted_extra.astype(bf16))
            attended = attended * (1.0 / total)
            log_total[h:h + 1, span] = top * factor + jnp.log2(total)
            together = attended.T + reads[span, col:col + size]
            mixed[block_rows(jnp.bitwise_xor(me, i) * rows, rows), col:col + size] = together.astype(bf16)


def backward_kernel(
    heads, blocks, parts,
    place, length, momentum, decay, step_size, qkv, mixed_grad, persist_k, persist_v,
    log_total, states, grams,
    qkv_grad, persist_k_grad, persist_v_grad,
    ordered, upstream, slopes, key_sum, value_sum, query_sum,
):
    seq_len, wide = qkv.shape
    size = persist_k.shape[2]
    cols = heads * size
    rows = seq_len // parts
    width = seq_len // blocks
    me = place[0]
    count = length[0]
    for b in range(parts):
        source = block_rows(jnp.bitwise_xor(me, b) * rows, rows)
        ordered[b * rows:(b + 1) * rows, :] = qkv[source, :]
        upstream[b * rows:(b + 1) * rows, :] = mixed_grad[source, :]

    carried = [(jnp.zeros((size, size), f32), jnp.zeros((size, size), f32)) for _ in range(heads)]
    for c in reversed(range(blocks)):
        span = slice(c * width, (c + 1) * width)
        for h in range(heads):
            col = h * size
            query_unit, _ = unit_rows(ordered[span, col:col + size])
            query_h, query_l = halves(query_unit)
            rise = upstream[span, col:col + size]
            entry = dot_tn(rise, query_h) + dot_tn(rise, query_l)
            memory, velocity = carried[h]
            velocity = velocity + memory
            change = (-step_size[c, h]) * velocity
            slopes[h, c] = change
            memory = (1.0 - decay[c, h]) * memory + entry + dot3(dot_nn, halves(change), halves(grams[h, c]))
            velocity = momentum[c, h] * velocity
            carried[h] = (memory, velocity)

    for h in range(heads):
        col = h * size
        for c in range(blocks):
            span = slice(c * width, (c + 1) * width)
            live = (c * width + lax.broadcasted_iota(jnp.int32, (width, 1), 0) < count).astype(f32)
            query_unit, query_scale = unit_rows(ordered[span, col:col + size])
            key_unit, key_scale = unit_rows(ordered[span, cols + col:cols + col + size])
            value = ordered[span, 2 * cols + col:2 * cols + col + size].astype(f32)
            rise = upstream[span, col:col + size]
            state = states[h, c]
            slope = slopes[h, c].astype(bf16)
            key_b = key_unit.astype(bf16)
            error = (dot_nt(key_b, state) - value) * live
            error_grad = dot_nt(key_b, slope) * live
            unit_grad = dot_nn(error.astype(bf16), slope) + dot_nn(error_grad.astype(bf16), state)
            key_sum[span, :] = key_scale * (unit_grad - key_unit * jnp.sum(unit_grad * key_unit, axis=-1, keepdims=True))
            value_sum[span, :] = -error_grad
            read_grad = dot_nn(rise, state)
            query_sum[span, :] = query_scale * (read_grad - query_unit * jnp.sum(read_grad * query_unit, axis=-1, keepdims=True))

        factor = size ** (-0.5)
        diagonal = lax.broadcasted_iota(jnp.int32, (rows, rows), 0) <= lax.broadcasted_iota(jnp.int32, (rows, rows), 1)
        key_t = ordered[:, cols + col:cols + col + size].T
        persist_t = persist_k[h].astype(f32).T.astype(bf16)
        persist_k_total = jnp.zeros(persist_k.shape[1:], f32)
        persist_v_total = jnp.zeros(persist_k.shape[1:], f32)
        for i in range(parts):
            span = slice(i * rows, (i + 1) * rows)
            seen = (i + 1) * rows
            query = ordered[span, col:col + size]
            rise = upstream[span, col:col + size]
            scores = dot_nt(ordered[:seen, cols + col:cols + col + size], query)
            last = jnp.where(diagonal, scores[seen - rows:], -1e30)
            scores = last if i == 0 else jnp.concatenate([scores[:seen - rows], last], axis=0)
            extra = dot_nt(persist_k[h], query)
            base = log_total[h:h + 1, span]
            probs = jnp.exp2(scores * (factor * log2_e) - base)
            probs_extra = jnp.exp2(extra * (factor * log2_e) - base)
            probs_grad = dot_nt(ordered[:seen, 2 * cols + col:2 * cols + col + size], rise)
            extra_grad = dot_nt(persist_v[h], rise)
            weighted = probs * probs_grad
            weighted_extra = probs_extra * extra_grad
            inner = jnp.sum(weighted, axis=0, keepdims=True) + jnp.sum(weighted_extra, axis=0, keepdims=True)
            scores_grad = (weighted - probs * inner).astype(bf16)
            scores_extra = (weighted_extra - probs_extra * inner).astype(bf16)
            query_t = dot_nn(key_t[:, :seen], scores_grad) + dot_nn(persist_t, scores_extra)
            query_sum[span, :] += query_t.T * factor
            key_sum[:seen, :] += dot_nn(scores_grad, query) * factor
            value_sum[:seen, :] += dot_nn(probs.astype(bf16), rise)
            persist_k_total += dot_nn(scores_extra, query) * factor
            persist_v_total += dot_nn(probs_extra.astype(bf16), rise)
        persist_k_grad[h] = persist_k_total
        persist_v_grad[h] = persist_v_total
        for b in range(parts):
            span = slice(b * rows, (b + 1) * rows)
            target = block_rows(jnp.bitwise_xor(me, b) * rows, rows)
            qkv_grad[target, col:col + size] = query_sum[span, :].astype(bf16)
            qkv_grad[target, cols + col:cols + col + size] = key_sum[span, :].astype(bf16)
            qkv_grad[target, 2 * cols + col:2 * cols + col + size] = value_sum[span, :].astype(bf16)


vmem = functools.partial(pl.BlockSpec, memory_space=pltpu.VMEM)
smem = functools.partial(pl.BlockSpec, memory_space=pltpu.SMEM)
vmem_limit = 56 << 20


def attend_and_recall(place, length, momentum, decay, step_size, qkv, persist_k, persist_v, parts):
    heads, _, size = persist_k.shape
    seq_len = qkv.shape[0]
    blocks = momentum.shape[0]
    cols = heads * size
    return pl.pallas_call(
        functools.partial(forward_kernel, heads, blocks, parts),
        out_shape=(
            jax.ShapeDtypeStruct((seq_len, cols), bf16),
            jax.ShapeDtypeStruct((heads, seq_len), f32),
            jax.ShapeDtypeStruct((heads, blocks, size, size), bf16),
            jax.ShapeDtypeStruct((heads, blocks, size, size), f32),
        ),
        in_specs=[smem()] * 5 + [vmem()] * 3,
        out_specs=(vmem(),) * 4,
        scratch_shapes=[pltpu.VMEM((seq_len, 3 * cols), bf16), pltpu.VMEM((seq_len, cols), f32)],
        compiler_params=pltpu.CompilerParams(vmem_limit_bytes=vmem_limit),
        cost_estimate=pl.CostEstimate(flops=12_000_000_000, bytes_accessed=8_000_000, transcendentals=2_000_000),
        name="attend_recall",
    )(place, length, momentum, decay, step_size, qkv, persist_k, persist_v)


def attend_and_recall_back(
    place, length, momentum, decay, step_size, qkv, mixed_grad, persist_k, persist_v, log_total, states, grams, parts
):
    heads, persistent, size = persist_k.shape
    seq_len = qkv.shape[0]
    blocks = momentum.shape[0]
    cols = heads * size
    return pl.pallas_call(
        functools.partial(backward_kernel, heads, blocks, parts),
        out_shape=(
            jax.ShapeDtypeStruct((seq_len, 3 * cols), bf16),
            jax.ShapeDtypeStruct((heads, persistent, size), f32),
            jax.ShapeDtypeStruct((heads, persistent, size), f32),
        ),
        in_specs=[smem()] * 5 + [vmem()] * 7,
        out_specs=(vmem(),) * 3,
        scratch_shapes=[
            pltpu.VMEM((seq_len, 3 * cols), bf16),
            pltpu.VMEM((seq_len, cols), bf16),
            pltpu.VMEM((heads, blocks, size, size), f32),
            pltpu.VMEM((seq_len, size), f32),
            pltpu.VMEM((seq_len, size), f32),
            pltpu.VMEM((seq_len, size), f32),
        ],
        compiler_params=pltpu.CompilerParams(vmem_limit_bytes=vmem_limit),
        cost_estimate=pl.CostEstimate(flops=25_000_000_000, bytes_accessed=12_000_000, transcendentals=2_000_000),
        name="attend_recall_back",
    )(place, length, momentum, decay, step_size, qkv, mixed_grad, persist_k, persist_v, log_total, states, grams)


def ring_place(index, count):
    odd = index % 2
    return (1 - odd) * (index // 2) + odd * (count - 1 - index // 2)


def ring_index(place, count):
    late = place // (count // 2)
    return (1 - late) * (2 * place) + late * (2 * (count - 1 - place) + 1)


def flip(index, bit):
    return index + bit * (1 - 2 * ((index // bit) % 2))


def bits_below(count):
    return [1 << k for k in range(count.bit_length() - 1)]


def relative(index, block):
    for bit in (1, 2):
        if block & bit:
            index = flip(index, bit)
    return index


def remote(source, target, send_sem, recv_sem, device):
    return pltpu.make_async_remote_copy(
        src_ref=source, dst_ref=target, send_sem=send_sem, recv_sem=recv_sem,
        device_id=device, device_id_type=pl.DeviceIdType.MESH,
    )


class Ring:
    def __init__(self, count, by_rows, source, out, slots, send_sem, recv_sem, home, home_sem):
        self.homeward = pltpu.make_async_copy(out, home, home_sem)
        self.count, self.by_rows = count, by_rows
        self.source, self.out, self.slots = source, out, slots
        self.send_sem, self.recv_sem = send_sem, recv_sem
        index = lax.axis_index("dp")
        self.place = ring_place(index, count)
        self.peers = (
            {"dp": ring_index((self.place + 1) % count, count)},
            {"dp": ring_index((self.place + count - 1) % count, count)},
        )
        self.step = 0
        self.copies = [None, None]
        self.sent = [[], []]

    def piece(self, ref, way, chunk):
        rows, cols = ref.shape
        chunk = chunk % self.count
        if self.by_rows:
            size = rows // (2 * self.count)
            return ref.at[pl.ds(pl.multiple_of(chunk * (2 * size) + way * size, size), size), :]
        size, width = rows // 2, cols // self.count
        return ref.at[way * size:(way + 1) * size, pl.ds(pl.multiple_of(chunk * width, width), width)]

    def chunk(self, way, step):
        return self.place + self.count + (2 * self.count - step if way == 0 else step)

    def launch(self, way, step, source, target):
        copy = remote(source, target, self.send_sem.at[way, step % 2], self.recv_sem.at[way, step % self.count], self.peers[way])
        if step > 1:
            self.sent[way].pop(0).wait_send()
        copy.start()
        self.copies[way] = copy
        self.sent[way].append(copy)

    def start_way(self, way):
        self.launch(way, 0, self.piece(self.source, way, self.chunk(way, 0)), self.slots.at[way, 0])

    def start(self):
        for way in range(2):
            self.start_way(way)

    def advance(self):
        count, step = self.count, self.step
        for way in range(2):
            self.copies[way].wait_recv()
            if step < count - 1:
                chunk = self.chunk(way, step + 1)
                total = self.slots[way, step].astype(f32) + self.piece(self.source, way, chunk)[...].astype(f32)
                if step < count - 2:
                    self.slots[way, step] = total.astype(bf16)
                    source, target = self.slots.at[way, step], self.slots.at[way, step + 1]
                else:
                    source = target = self.piece(self.out, way, chunk)
                    source[...] = total.astype(bf16)
            else:
                source = target = self.piece(self.out, way, self.chunk(way, step + 1 - count))
            if step < 2 * count - 3:
                self.launch(way, step + 1, source, target)
        self.step += 1
        if self.step < 2 * count - 2:
            return True
        for copy in self.sent[0] + self.sent[1]:
            copy.wait_send()
        self.homeward.start()
        return False

    def left(self):
        return 2 * self.count - 2 - self.step


class SmallSum:
    def __init__(self, value, slots, shared, send_sem, recv_sem, count, parts):
        self.value, self.slots, self.shared = value, slots, shared
        self.send_sem, self.recv_sem = send_sem, recv_sem
        index, inner = lax.axis_index("dp"), lax.axis_index("tensor")
        self.inner = len(bits_below(parts))
        self.peers = [{"tensor": flip(inner, bit)} for bit in bits_below(parts)]
        self.peers += [{"dp": flip(index, bit)} for bit in bits_below(count)]
        self.step = 0

    def start(self):
        used = slice(0, self.shared if self.step < self.inner else self.value.shape[0])
        self.used = used
        self.copy = remote(
            self.value.at[used], self.slots.at[self.step, used], self.send_sem.at[self.step],
            self.recv_sem.at[self.step], self.peers[self.step],
        )
        self.copy.start()

    def left(self):
        return len(self.peers) - self.step

    def advance(self):
        self.copy.wait()
        self.value[self.used] += self.slots[self.step, self.used]
        self.step += 1
        if self.step < len(self.peers):
            self.start()
        return self.step < len(self.peers)


class Rounds:
    def __init__(self):
        self.queue = []

    def add(self, *flows):
        for flow in flows:
            flow.start()
            self.queue.append(flow)

    def spread(self, fast, slow):
        fast = [flow for flow in fast if flow in self.queue]
        slow = [flow for flow in slow if flow in self.queue]
        counts = {flow: flow.left() for flow in fast + slow}
        rest = [flow for k in range(max([counts[flow] for flow in slow], default=0)) for flow in slow if k < counts[flow]]
        turns = max(counts[flow] for flow in fast)
        self.queue = []
        for k in range(turns):
            self.queue += [flow for flow in fast if k < counts[flow]]
            self.queue += rest[k * len(rest) // turns:(k + 1) * len(rest) // turns]

    def mix(self, flow):
        for k in range(flow.left()):
            self.queue.insert(min(6 * k + 4, len(self.queue)), flow)

    def tick(self, count=1):
        for _ in range(count):
            if self.queue:
                flow = self.queue.pop(0)
                if flow.advance() and flow not in self.queue:
                    self.queue.append(flow)

    def finish(self):
        while self.queue:
            self.tick()


def rows_scale(value):
    return lax.rsqrt(jnp.mean(value * value, axis=-1, keepdims=True) + norm_eps)


class Scatter:
    def __init__(self, sent, landed, hold, send_sem, recv_sem):
        self.sent, self.landed, self.hold = sent, landed, hold
        self.send_sem, self.recv_sem = send_sem, recv_sem
        self.rows = hold.shape[0] // 2
        inner = lax.axis_index("tensor")
        self.sibling, self.across = {"tensor": flip(inner, 1)}, {"tensor": flip(inner, 2)}

    def span(self, j):
        return slice(j * self.rows, (j + 1) * self.rows)

    def copy(self, k, j, device):
        return remote(
            self.sent.at[k, self.span(j)], self.landed.at[k, self.span(j)],
            self.send_sem.at[k, j], self.recv_sem.at[k, j], device,
        )

    def begin(self, block, tick):
        first = [self.copy(0, j, self.sibling) for j in range(2)]
        self.second = [self.copy(1, j, self.across) for j in range(2)]
        self.third = [self.copy(2, j, self.sibling) for j in range(2)]
        for j in range(2):
            self.sent[0, self.span(j)] = block(3, j).astype(bf16)
            first[j].start()
        for j in range(2):
            self.hold[self.span(j), :] = block(2, j)
        tick()
        for j in range(2):
            first[j].wait()
            self.sent[1, self.span(j)] = (
                self.hold[self.span(j), :] + self.landed[0, self.span(j)].astype(f32)
            ).astype(bf16)
            self.second[j].start()
        for j in range(2):
            self.sent[2, self.span(j)] = block(1, j).astype(bf16)
            self.third[j].start()
        tick()
        for j in range(2):
            self.hold[self.span(j), :] = block(0, j)

    def finish(self, j):
        span = self.span(j)
        self.third[j].wait()
        self.second[j].wait()
        return self.hold[span, :] + self.landed[2, span].astype(f32) + self.landed[1, span].astype(f32)


class Gather:
    def __init__(self, full, parts, send_sem, recv_sem):
        self.full, self.rows = full, full.shape[0] // (2 * parts)
        self.send_sem, self.recv_sem = send_sem, recv_sem
        inner = lax.axis_index("tensor")
        self.sibling, self.across = {"tensor": flip(inner, 1)}, {"tensor": flip(inner, 2)}
        self.far, self.near, self.both = [None] * 2, [None] * 2, [None] * 2

    def copy(self, source, target, k, j, device):
        def piece(b):
            first = (2 * b + j) * self.rows
            return self.full.at[first:first + self.rows, :]

        return remote(piece(source), piece(target), self.send_sem.at[k, j], self.recv_sem.at[k, j], device)

    def begin(self, j):
        self.far[j], self.near[j] = self.copy(0, 2, 0, j, self.across), self.copy(0, 1, 1, j, self.sibling)
        self.far[j].start()
        self.near[j].start()

    def forward(self, then=lambda j: None):
        for j in range(2):
            self.far[j].wait()
            then(j)
            self.both[j] = self.copy(2, 3, 2, j, self.sibling)
            self.both[j].start()

    def wait(self, copies):
        for copy in copies:
            copy.wait()


def dot_pair(high, low, right):
    return dot_nn(jnp.concatenate([high, low], axis=1), jnp.concatenate([right, right], axis=0))


def layer_kernel(
    heads, blocks, parts, count, shared, pace,
    length, momentum, decay, step_size,
    inputs_h, cotangent_h, gain_attn, gain_ffn_h, persist_k_h, persist_v_h,
    w_query_h, w_key_h, w_value_h, w_out_h, w_gate_h, w_up_h, w_down_h,
    gate_home, up_home, down_home, query_home, key_home, value_home, out_home, result_home, input_grad_home, small,
    w_qkv, w_out, w_gate, w_up, w_down,
    normed_attn, ordered, mixed, states, grams, log_total,
    middle, hold, middle_grad, normed_ffn, out_full, gate_grad, up_grad, hidden,
    gate_source, up_source, down_source, query_source, key_source, value_source, out_source,
    gate_slots, up_slots, down_slots, query_slots, key_slots, value_slots, out_slots, small_slots,
    gate_out, up_out, down_out, query_out, key_out, value_out, out_out, result, input_grad,
    inputs, cotangent, gain_ffn, persist_k, persist_v, sent_a, landed_a, sent_b, landed_b, middle_full, upstream, slopes, key_sum, value_sum, query_sum, qkv_grad,
    load_sem, home_sem, ring_send, ring_recv, small_send, small_recv, move_send, move_recv,
):
    size = persist_k.shape[2]
    many = persist_k.shape[1]
    cols = heads * size
    seq_len, width = middle_full.shape
    units = gate_grad.shape[0]
    rows = seq_len // parts
    span_rows = seq_len // blocks
    inner = lax.axis_index("tensor")
    valid_count = length[0]
    factor = size ** (-0.5)

    rounds = Rounds()
    rings = [
        Ring(count, by_rows, source, out, slots, ring_send.at[k], ring_recv.at[k], home, home_sem.at[k])
        for k, (by_rows, source, out, slots, home) in enumerate((
            (False, down_source, down_out, down_slots, down_home),
            (False, gate_source, gate_out, gate_slots, gate_home),
            (False, up_source, up_out, up_slots, up_home),
            (False, out_source, out_out, out_slots, out_home),
            (True, query_source, query_out, query_slots, query_home),
            (True, key_source, key_out, key_slots, key_home),
            (True, value_source, value_out, value_slots, value_home),
        ))
    ]
    small_sum = SmallSum(small, small_slots, shared, small_send, small_recv, count, parts)
    barrier = pltpu.get_barrier_semaphore()
    peers = list(rings[0].peers) + small_sum.peers
    for peer in peers:
        pl.semaphore_signal(barrier, inc=1, device_id=peer, device_id_type=pl.DeviceIdType.MESH)

    loads = []

    def load(source, target):
        copy = pltpu.make_async_copy(source, target, load_sem.at[len(loads)])
        copy.start()
        loads.append(copy)
        return copy

    input_load, cotangent_load = load(inputs_h, inputs), load(cotangent_h, cotangent)
    qkv_loads = [
        load(source, w_qkv.at[:, k * cols:(k + 1) * cols]) for k, source in enumerate((w_query_h, w_key_h, w_value_h))
    ]
    persist_loads = [load(persist_k_h, persist_k), load(persist_v_h, persist_v), load(gain_ffn_h, gain_ffn)]
    out_load = load(w_out_h, w_out)
    ffn_loads = [load(w_gate_h, w_gate), load(w_up_h, w_up), load(w_down_h, w_down)]

    def true_rows(b):
        return pl.ds(pl.multiple_of(relative(inner, b) * rows, rows), rows)

    def block_of(b):
        return slice(b * rows, (b + 1) * rows)

    row_place = inner * rows + lax.broadcasted_iota(jnp.int32, (rows, 1), 0)
    own_valid = (row_place < valid_count).astype(f32)
    stat_row = 2 * width // size

    def half_rows(j):
        return slice(j * (rows // 2), (j + 1) * (rows // 2))

    def part_of(b, j):
        return slice((2 * b + j) * (rows // 2), (2 * b + j + 1) * (rows // 2))

    def note(k, value, j):
        total = jnp.sum(jnp.sum(value, axis=1, keepdims=True) * own_valid[half_rows(j)], axis=0, keepdims=True)
        small[stat_row + k:stat_row + k + 1, :] += jnp.broadcast_to(total, (1, size))

    gather_attn = Gather(normed_attn, parts, move_send.at[0], move_recv.at[0])
    small[stat_row:stat_row + 8, :] = jnp.zeros((8, size), f32)

    def attn_norm(j):
        resid = inputs[half_rows(j), :].astype(f32)
        normed_attn[half_rows(j), :] = (resid * rows_scale(resid) * gain_attn[...]).astype(bf16)
        note(0, resid * resid, j)

    input_load.wait()
    attn_norm(0)
    pl.semaphore_wait(barrier, len(peers))
    gather_attn.begin(0)
    attn_norm(1)
    gather_attn.begin(1)
    cotangent_load.wait()
    out_full[0:rows, :] = (cotangent[...].astype(f32) * own_valid).astype(bf16)
    for j in range(2):
        note(5, jnp.ones((rows // 2, 1), f32), j)
    for copy in qkv_loads:
        copy.wait()

    def qkv_block(b):
        made = dot_nn(normed_attn[block_of(b), :], w_qkv[...])
        ordered[true_rows(b), :] = made.astype(bf16)
        first = relative(inner, b) * (rows // span_rows)
        place = lax.broadcasted_iota(jnp.int32, (rows, 1), 0)
        live = (relative(inner, b) * rows + place < valid_count).astype(f32)
        for h in range(heads):
            col = h * size
            key_unit, _ = unit_rows(made[:, cols + col:cols + col + size].astype(bf16))
            value = made[:, 2 * cols + col:2 * cols + col + size].astype(bf16)
            live_unit = (key_unit * live).astype(bf16)
            empty = jnp.zeros((span_rows, size), bf16)
            spread = jnp.concatenate([
                jnp.concatenate([
                    live_unit[k * span_rows:(k + 1) * span_rows] if k == m else empty for m in range(rows // span_rows)
                ], axis=1) for k in range(rows // span_rows)
            ], axis=0)
            both = dot_nn(jnp.concatenate([value, key_unit.astype(bf16)], axis=1).T, spread).astype(bf16)
            for k in range(rows // span_rows):
                slopes[h, first + k] = both[:size, k * size:(k + 1) * size]
                grams[h, first + k] = both[size:, k * size:(k + 1) * size]

    qkv_block(0)
    gather_attn.wait(gather_attn.near)
    qkv_block(1)
    gather_cot = Gather(out_full, parts, move_send.at[1], move_recv.at[1])
    gather_attn.forward(gather_cot.begin)
    qkv_block(2)
    gather_attn.wait(gather_attn.both)
    qkv_block(3)

    for copy in persist_loads:
        copy.wait()
    diagonal = lax.broadcasted_iota(jnp.int32, (rows, rows), 0) <= lax.broadcasted_iota(jnp.int32, (rows, rows), 1)
    tiles = [(h, i) for i in range(parts) for h in range(heads)]

    def masked_scores(h, i, query):
        seen = (i + 1) * rows
        scores = dot_nt(ordered[:seen, cols + h * size:cols + (h + 1) * size], query)
        last = jnp.where(diagonal, scores[seen - rows:], -1e30)
        return last if i == 0 else jnp.concatenate([scores[:seen - rows], last], axis=0)

    value_t = [ordered[:, 2 * cols + h * size:2 * cols + (h + 1) * size].T for h in range(heads)]
    persist_t = [persist_v[h].astype(f32).T.astype(bf16) for h in range(heads)]

    def attend(h, i):
        seen, col = (i + 1) * rows, h * size
        query = ordered[block_of(i), col:col + size]
        scores = masked_scores(h, i, query)
        extra = dot_nt(persist_k[h], query)
        top = jnp.maximum(jnp.max(scores, axis=0, keepdims=True), jnp.max(extra, axis=0, keepdims=True))
        lifted = jnp.exp2((scores - top) * (factor * log2_e))
        lifted_extra = jnp.exp2((extra - top) * (factor * log2_e))
        total = jnp.sum(lifted, axis=0, keepdims=True) + jnp.sum(lifted_extra, axis=0, keepdims=True)
        attended = dot_nn(value_t[h][:, :seen], lifted.astype(bf16)) + dot_nn(persist_t[h], lifted_extra.astype(bf16))
        log_total[h:h + 1, block_of(i)] = top * (factor * log2_e) + jnp.log2(total)
        query_sum[block_of(i), col:col + size] = (attended * (1.0 / total)).T

    carried = [(jnp.zeros((size, size), f32), jnp.zeros((size, size), f32)) for _ in range(heads)]
    for c in range(blocks):
        for h in range(heads):
            memory, velocity = carried[h]
            high, low_part = halves(memory)
            states[h, c] = high
            change = dot_pair(high, low_part, grams[h, c]) - slopes[h, c].astype(f32)
            velocity = momentum[h, c] * velocity - step_size[h, c] * change
            memory = (1.0 - decay[h, c]) * memory + velocity
            carried[h] = (memory, velocity)
        for h, i in tiles[c * len(tiles) // blocks:(c + 1) * len(tiles) // blocks]:
            attend(h, i)
    def mix(b):
        span, first = true_rows(b), relative(inner, b) * (rows // span_rows)
        for h in range(heads):
            wide = slice(h * size, (h + 1) * size)
            query_unit = unit_rows(ordered[span, wide])[0].astype(bf16)
            reads = [
                dot_nt(query_unit[k * span_rows:(k + 1) * span_rows], states[h, first + k])
                for k in range(rows // span_rows)
            ]
            mixed[block_of(b), wide] = (query_sum[span, wide] + jnp.concatenate(reads, axis=0)).astype(bf16)

    def project(b, j):
        if j == 0:
            mix(b)
        return dot_nn(mixed[part_of(b, j), :], w_out[...])

    out_load.wait()
    scatter = Scatter(sent_a, landed_a, hold, move_send.at[2], move_recv.at[2])
    scatter.begin(project, rounds.tick)
    gather_cot.wait(gather_cot.near)
    gather_cot.forward()
    gather_ffn = Gather(normed_ffn, parts, move_send.at[0], move_recv.at[0])
    for j in range(2):
        branch = scatter.finish(j)
        value = inputs[half_rows(j), :].astype(f32) + branch
        middle[half_rows(j), :] = value
        normed_ffn[half_rows(j), :] = (value * rows_scale(value) * gain_ffn[...]).astype(bf16)
        gather_ffn.begin(j)
        note(3, branch * branch, j)
        note(1, value * value, j)
    for copy in ffn_loads:
        copy.wait()
    gather_cot.wait(gather_cot.both)
    gather_ffn.wait(gather_ffn.near)

    piece = units // 4

    def feed(tokens):
        for k in range(4):
            span = slice(k * piece, (k + 1) * piece)
            gate = dot_nt(w_gate[span, :], normed_ffn[tokens, :])
            up = dot_nt(w_up[span, :], normed_ffn[tokens, :])
            hidden_grad = dot_nt(w_down[span, :], out_full[tokens, :])
            sigmoid = jax.nn.sigmoid(gate)
            silu = gate * sigmoid
            hidden[span, tokens] = (silu * up).astype(bf16)
            up_grad[span, tokens] = (hidden_grad * silu).astype(bf16)
            gate_grad[span, tokens] = (hidden_grad * up * sigmoid * (1.0 + gate * (1.0 - sigmoid))).astype(bf16)

    feed(slice(0, 2 * rows))
    gather_ffn.forward()
    feed(block_of(2))
    gather_ffn.wait(gather_ffn.both)
    feed(block_of(3))
    for source, left, right, ring in (
        (down_source, hidden, out_full, rings[0]), (gate_source, gate_grad, normed_ffn, rings[1]),
        (up_source, up_grad, normed_ffn, rings[2]),
    ):
        for way in range(2):
            span = slice(way * (units // 2), (way + 1) * (units // 2))
            source[span, :] = dot_nn(left[span, :], right[...]).astype(bf16)
            ring.start_way(way)
        rounds.queue.append(ring)

    scatter = Scatter(sent_b, landed_b, hold, move_send.at[3], move_recv.at[3])
    scatter.begin(
        lambda b, j: dot_tn(gate_grad[:, part_of(b, j)], w_gate[...]) + dot_tn(up_grad[:, part_of(b, j)], w_up[...]),
        rounds.tick,
    )
    rounds.tick(pace[0])
    for b in range(parts):
        normed_ffn[:, block_of(b)] = normed_attn[block_of(b), :].T
        rounds.tick(pace[9])
    gather_middle = Gather(middle_full, parts, move_send.at[1], move_recv.at[1])
    gain_row = jnp.zeros((1, width), f32)
    for j in range(2):
        normed_grad = scatter.finish(j)
        value = middle[half_rows(j), :]
        scale = rows_scale(value)
        weighted = normed_grad * gain_ffn[...]
        grad = (
            cotangent[half_rows(j), :].astype(f32) * own_valid[half_rows(j)] + scale * weighted
            - value * (scale * scale * scale) * jnp.mean(weighted * value, axis=-1, keepdims=True)
        )
        middle_grad[half_rows(j), :] = grad
        middle_full[half_rows(j), :] = grad.astype(bf16)
        gather_middle.begin(j)
        gain_row = gain_row + jnp.sum(normed_grad * value * scale, axis=0, keepdims=True)
        if j == 0:
            rounds.tick(pace[8])
    for k in range(width // size):
        small[width // size + k:width // size + k + 1, :] = gain_row[:, k * size:(k + 1) * size]
    rounds.tick(pace[1])
    gather_middle.wait(gather_middle.near)

    def mixed_block(b):
        upstream[true_rows(b), :] = dot_nt(middle_full[block_of(b), :], w_out[...]).astype(bf16)

    mixed_block(0)
    mixed_block(1)
    gather_middle.forward()
    mixed_block(2)
    gather_middle.wait(gather_middle.both)
    mixed_block(3)
    scatter = Scatter(sent_a, landed_a, hold, move_send.at[2], move_recv.at[2])
    scatter.begin(lambda b, j: dot_tn(hidden[:, part_of(b, j)], w_down[...]), rounds.tick)
    rounds.tick(pace[2])
    out_source[...] = dot_tn(mixed[...], middle_full[...]).astype(bf16)
    rounds.add(rings[3])

    key_t = [ordered[:, cols + h * size:cols + (h + 1) * size].T for h in range(heads)]
    persist_t = [persist_k[h].astype(f32).T.astype(bf16) for h in range(heads)]
    persist_sums = [[jnp.zeros((many, size), f32), jnp.zeros((many, size), f32)] for _ in range(heads)]

    def attend_back(h, i):
        span, seen, col = block_of(i), (i + 1) * rows, h * size
        wide = slice(col, col + size)
        query = ordered[span, wide]
        rise = upstream[span, wide]
        scores = masked_scores(h, i, query)
        extra = dot_nt(persist_k[h], query)
        base = log_total[h:h + 1, span]
        probs = jnp.exp2(scores * (factor * log2_e) - base)
        probs_extra = jnp.exp2(extra * (factor * log2_e) - base)
        probs_grad = dot_nt(ordered[:seen, 2 * cols + col:2 * cols + col + size], rise)
        extra_grad = dot_nt(persist_v[h], rise)
        weighted = probs * probs_grad
        weighted_extra = probs_extra * extra_grad
        inner_sum = jnp.sum(weighted, axis=0, keepdims=True) + jnp.sum(weighted_extra, axis=0, keepdims=True)
        scores_grad = (weighted - probs * inner_sum).astype(bf16)
        scores_extra = (weighted_extra - probs_extra * inner_sum).astype(bf16)
        query_t = dot_nn(key_t[h][:, :seen], scores_grad) + dot_nn(persist_t[h], scores_extra)
        query_sum[span, wide] = query_t.T * factor
        key_part = dot_nn(scores_grad, query) * factor
        value_part = dot_nn(probs.astype(bf16), rise)
        for ref, part in ((key_sum, key_part), (value_sum, value_part)):
            ref[span, wide] = part[seen - rows:]
            if i:
                ref[:seen - rows, wide] += part[:seen - rows]
        persist_sums[h][0] += dot_nn(scores_extra, query) * factor
        persist_sums[h][1] += dot_nn(probs_extra.astype(bf16), rise)

    carried = [(jnp.zeros((size, size), f32), jnp.zeros((size, size), f32)) for _ in range(heads)]
    for c in reversed(range(blocks)):
        span = slice(c * span_rows, (c + 1) * span_rows)
        for h in range(heads):
            col = h * size
            query_unit, _ = unit_rows(ordered[span, col:col + size])
            rise = upstream[span, col:col + size]
            entry = dot_tn(rise, query_unit.astype(bf16))
            memory, velocity = carried[h]
            velocity = velocity + memory
            change = (-step_size[h, c]) * velocity
            slopes[h, c] = change.astype(bf16)
            memory = (1.0 - decay[h, c]) * memory + entry + dot_pair(*halves(change), grams[h, c])
            velocity = momentum[h, c] * velocity
            carried[h] = (memory, velocity)
        done = blocks - 1 - c
        for h, i in tiles[done * len(tiles) // blocks:(done + 1) * len(tiles) // blocks]:
            attend_back(h, i)
        rounds.tick(pace[3][done])

    for h in range(heads):
        col = h * size
        wide = slice(col, col + size)
        for c in range(blocks):
            span = slice(c * span_rows, (c + 1) * span_rows)
            live = (c * span_rows + lax.broadcasted_iota(jnp.int32, (span_rows, 1), 0) < valid_count).astype(f32)
            query_unit, query_scale = unit_rows(ordered[span, wide])
            key_unit, key_scale = unit_rows(ordered[span, cols + col:cols + col + size])
            value = ordered[span, 2 * cols + col:2 * cols + col + size].astype(f32)
            rise = upstream[span, wide]
            state = states[h, c]
            slope = slopes[h, c]
            error = (dot_nt(key_unit.astype(bf16), state) - value) * live
            error_grad = dot_nt(key_unit.astype(bf16), slope) * live
            unit_grad = dot_nn(error.astype(bf16), slope) + dot_nn(error_grad.astype(bf16), state)
            key_sum[span, wide] += key_scale * (
                unit_grad - key_unit * jnp.sum(unit_grad * key_unit, axis=-1, keepdims=True)
            )
            value_sum[span, wide] -= error_grad
            read_grad = dot_nn(rise, state)
            query_sum[span, wide] += query_scale * (
                read_grad - query_unit * jnp.sum(read_grad * query_unit, axis=-1, keepdims=True)
            )
            rounds.tick(pace[4][c])
        small[shared + h * many:shared + (h + 1) * many, :] = persist_sums[h][0]
        small[shared + (heads + h) * many:shared + (heads + h + 1) * many, :] = persist_sums[h][1]
    for b in range(parts):
        target = true_rows(b)
        qkv_grad[target, 0:cols] = query_sum[block_of(b), :].astype(bf16)
        qkv_grad[target, cols:2 * cols] = key_sum[block_of(b), :].astype(bf16)
        qkv_grad[target, 2 * cols:3 * cols] = value_sum[block_of(b), :].astype(bf16)

    for j in range(2):
        branch = scatter.finish(j)
        note(4, branch * branch, j)
        value = middle[half_rows(j), :] + branch
        note(2, value * value, j)
        result[half_rows(j), :] = value.astype(bf16)
    homes = [pltpu.make_async_copy(result, result_home, home_sem.at[len(rings)])]
    homes[0].start()

    for b in range(parts):
        span = block_of(b)
        grad = dot_nn(normed_ffn[span, :], qkv_grad[...])
        for k, source in enumerate((query_source, key_source, value_source)):
            source[span, :] = grad[:, k * cols:(k + 1) * cols].astype(bf16)
        rounds.tick(pace[6])
    rounds.add(*rings[4:])
    rounds.spread(rings[3:], rings[:3])
    scatter = Scatter(sent_b, landed_b, hold, move_send.at[3], move_recv.at[3])
    scatter.begin(lambda b, j: dot_nt(qkv_grad[part_of(b, j), :], w_qkv[...]), lambda: rounds.tick(pace[10]))
    for b in range(parts):
        span = block_of(b)
        products = sum(
            source[span, :].astype(f32) * w_qkv[span, k * cols:(k + 1) * cols].astype(f32)
            for k, source in enumerate((query_source, key_source, value_source))
        )
        gain_row = jnp.sum(products.T, axis=0, keepdims=True) / gain_attn[:, span]
        for k in range(rows // size):
            row = b * (rows // size) + k
            small[row:row + 1, :] = gain_row[:, k * size:(k + 1) * size]
        rounds.tick(pace[7])
    small_sum.start()
    rounds.mix(small_sum)
    for j in range(2):
        normed_grad = scatter.finish(j)
        value = inputs[half_rows(j), :].astype(f32)
        scale = rows_scale(value)
        weighted = normed_grad * gain_attn[...]
        input_grad[half_rows(j), :] = (
            middle_grad[half_rows(j), :] + scale * weighted
            - value * (scale * scale * scale) * jnp.mean(weighted * value, axis=-1, keepdims=True)
        ).astype(bf16)
    homes.append(pltpu.make_async_copy(input_grad, input_grad_home, home_sem.at[len(rings) + 1]))
    homes[1].start()
    rounds.finish()
    for copy in homes + [ring.homeward for ring in rings]:
        copy.wait()


def whole_layer(
    length, momentum, decay, step_size, inputs, cotangent, gain_attn, gain_ffn, persist_k, persist_v,
    w_query, w_key, w_value, w_out, w_gate, w_up, w_down, count, parts,
):
    heads, many, size = persist_k.shape
    blocks = momentum.shape[1]
    cols = heads * size
    rows, width = inputs.shape
    seq_len = rows * parts
    units = w_gate.shape[0]
    shared = 2 * width // size + 8
    small_rows = shared + 2 * heads * many
    flows = len(bits_below(count)) + len(bits_below(parts))

    def row_slots(*shape):
        return pltpu.VMEM((2, count - 1, shape[0] // (2 * count), shape[1]), bf16)

    def col_slots(*shape):
        return pltpu.VMEM((2, count - 1, shape[0] // 2, shape[1] // count), bf16)

    def low(*shape):
        return pltpu.VMEM(shape, bf16)

    def full(*shape):
        return pltpu.VMEM(shape, f32)

    def semaphores(*shape):
        return pltpu.SemaphoreType.DMA(shape)

    ffn = (units, width)
    return pl.pallas_call(
        functools.partial(layer_kernel, heads, blocks, parts, count, shared, pace),
        out_shape=(
            jax.ShapeDtypeStruct(ffn, bf16),
            jax.ShapeDtypeStruct(ffn, bf16),
            jax.ShapeDtypeStruct(ffn, bf16),
            jax.ShapeDtypeStruct((width, cols), bf16),
            jax.ShapeDtypeStruct((width, cols), bf16),
            jax.ShapeDtypeStruct((width, cols), bf16),
            jax.ShapeDtypeStruct((cols, width), bf16),
            jax.ShapeDtypeStruct((rows, width), bf16),
            jax.ShapeDtypeStruct((rows, width), bf16),
            jax.ShapeDtypeStruct((small_rows, size), f32),
        ),
        in_specs=[smem()] * 4 + [pl.BlockSpec(memory_space=pl.ANY)] * 2 + [vmem()] + [pl.BlockSpec(memory_space=pl.ANY)] * 10,
        out_specs=(pl.BlockSpec(memory_space=pl.ANY),) * 9 + (vmem(),),
        scratch_shapes=[
            low(width, 3 * cols), low(cols, width), low(*ffn), low(*ffn), low(*ffn),
            low(seq_len, width), low(seq_len, 3 * cols), low(seq_len, cols),
            low(heads, blocks, size, size), low(heads, blocks, size, size), full(heads, seq_len),
            full(rows, width), full(rows, width), full(rows, width), low(seq_len, width), low(seq_len, width),
            low(units, seq_len), low(units, seq_len), low(units, seq_len),
            low(*ffn), low(*ffn), low(*ffn), low(width, cols), low(width, cols), low(width, cols), low(cols, width),
            col_slots(*ffn), col_slots(*ffn), col_slots(*ffn),
            row_slots(width, cols), row_slots(width, cols), row_slots(width, cols), col_slots(cols, width),
            full(flows, small_rows, size),
            low(*ffn), low(*ffn), low(*ffn), low(width, cols), low(width, cols), low(width, cols), low(cols, width),
            low(rows, width), low(rows, width), low(rows, width), low(rows, width),
            full(1, width), low(heads, many, size), low(heads, many, size),
            low(3, rows, width), low(3, rows, width), low(3, rows, width), low(3, rows, width),
            low(seq_len, width), low(seq_len, cols), low(heads, blocks, size, size),
            full(seq_len, cols), full(seq_len, cols), full(seq_len, cols), low(seq_len, 3 * cols),
            semaphores(12), semaphores(9), semaphores(7, 2, 2), semaphores(7, 2, count),
            semaphores(flows), semaphores(flows), semaphores(4, 3, 2), semaphores(4, 3, 2),
        ],
        compiler_params=pltpu.CompilerParams(
            vmem_limit_bytes=layer_limit, collective_id=0, has_side_effects=True
        ),
        cost_estimate=pl.CostEstimate(flops=150_000_000_000, bytes_accessed=40_000_000, transcendentals=4_000_000),
        name="whole_layer",
    )(
        length, momentum, decay, step_size, inputs, cotangent, gain_attn, gain_ffn, persist_k, persist_v,
        w_query, w_key, w_value, w_out, w_gate, w_up, w_down,
    )


def finish_kernel(casts, moves, *refs):
    total = casts + moves
    sources, small = refs[:total], refs[total]
    targets, refs = refs[total + 1:2 * total + 1], refs[2 * total + 1:]
    gain_attn, gain_ffn, persist_k, persist_v, roots = refs[:5]
    held, cast, semaphores = refs[5:5 + total], refs[5 + total:5 + total + casts], refs[5 + total + casts]
    arrive = [pltpu.make_async_copy(sources[k], held[k], semaphores.at[0, k]) for k in range(total)]
    leave = [
        pltpu.make_async_copy(cast[k] if k < casts else held[k], targets[k], semaphores.at[1, k])
        for k in range(total)
    ]
    ahead = total
    for copy in arrive[:ahead]:
        copy.start()
    lines = gain_attn.shape[0]
    heads, many, size = persist_k.shape
    gain_attn[...] = small[0:lines, :]
    gain_ffn[...] = small[lines:2 * lines, :]
    stats = small[2 * lines:2 * lines + 8, :]
    stats = jnp.sqrt(stats / (stats[5:6, :] * (lines * size)))
    for k in range(5):
        roots[k] = stats[k, 0]
    for h in range(heads):
        first = 2 * lines + 8 + h * many
        persist_k[h] = small[first:first + many, :]
        persist_v[h] = small[first + heads * many:first + (heads + 1) * many, :]
    for k in range(total):
        arrive[k].wait()
        if k + ahead < total:
            arrive[k + ahead].start()
        if k < casts:
            cast[k][...] = held[k][...].astype(f32)
        leave[k].start()
    for copy in leave:
        copy.wait()


def finish(sums, rest, small, persist_shape):
    casts, moves = len(sums), len(rest)
    size = small.shape[1]
    lines = (small.shape[0] - 2 * persist_shape[0] * persist_shape[1] - 8) // 2
    anywhere = pl.BlockSpec(memory_space=pl.ANY)
    return pl.pallas_call(
        functools.partial(finish_kernel, casts, moves),
        out_shape=tuple(jax.ShapeDtypeStruct(value.shape, f32) for value in sums)
        + tuple(jax.ShapeDtypeStruct(value.shape, value.dtype) for value in rest)
        + (jax.ShapeDtypeStruct((lines, size), f32),) * 2
        + (jax.ShapeDtypeStruct(persist_shape, f32),) * 2
        + (jax.ShapeDtypeStruct((5,), f32),),
        in_specs=[anywhere] * (casts + moves) + [vmem()],
        out_specs=(anywhere,) * (casts + moves) + (vmem(),) * 4 + (smem(),),
        scratch_shapes=[pltpu.VMEM(value.shape, value.dtype) for value in (*sums, *rest)]
        + [pltpu.VMEM(value.shape, f32) for value in sums]
        + [pltpu.SemaphoreType.DMA((2, casts + moves))],
        compiler_params=pltpu.CompilerParams(vmem_limit_bytes=vmem_limit),
        name="finish",
    )(*sums, *rest, small)


pace = (0, 6, 0, (0, 1) * 8, (0, 0, 0, 0, 0, 0, 0, 1) * 2, None, 1, 3, 2, 1, 3)
layer_limit = 63 << 20


def swap(value, axis, bit):
    count = lax.axis_size(axis)
    return lax.ppermute(value, axis, [(i, i ^ bit) for i in range(count)])


def norm_back(value, scale, gain, upstream):
    weighted = upstream * gain
    return scale * weighted - value * (scale * scale * scale) * jnp.mean(
        weighted * value, axis=-1, keepdims=True
    )


def gather_rows(own):
    far = swap(own, "tensor", 2)
    near = swap(own, "tensor", 1)
    both = swap(far, "tensor", 1)
    return jnp.concatenate([own, near], 0), jnp.concatenate([far, both], 0)


def scatter_rows(near, far):
    rows = near.shape[0] // 2
    far_sum = far[:rows] + swap(far[rows:].astype(bf16), "tensor", 1).astype(f32)
    far_in = swap(far_sum.astype(bf16), "tensor", 2).astype(f32)
    near_in = swap(near[rows:].astype(bf16), "tensor", 1).astype(f32)
    return near[:rows] + near_in + far_in


def mul(left, right):
    return jnp.dot(left, right, preferred_element_type=f32)


def mul_nt(left, right):
    return jnp.einsum("ab,cb->ac", left, right, preferred_element_type=f32)


def mul_tn(left, right):
    return jnp.einsum("ab,ac->bc", left, right, preferred_element_type=f32)


def fits_ring(count, parts, *shapes):
    if count & (count - 1) or parts != 4 or count < 4:
        return False
    return all(rows % (32 * count) == 0 or (rows % 32 == 0 and cols % (128 * count) == 0) for rows, cols in shapes)


def body(
    inputs, cotangent, lengths, gain_attn, w_query, w_key, w_value, w_out, persist_keys, persist_values,
    gain_ffn, w_gate, w_up, w_down, momentum, decay, step_size,
):
    parts = lax.axis_size("tensor")
    count = lax.axis_size("dp")
    rows = inputs.shape[1]
    width = inputs.shape[2]
    half = 2 * rows
    cols = w_query.shape[1]
    size = persist_keys.shape[2]
    place = lax.axis_index("tensor")
    first_row = place * rows
    own_valid = (first_row + jnp.arange(rows, dtype=jnp.int32) < lengths[0]).astype(f32)[:, None]
    places = place.astype(jnp.int32).reshape(1)
    rates = (places, lengths, momentum[0], decay[0], step_size[0])

    if fits_ring(count, parts, (w_down.shape), (width, 3 * cols), (cols, width)):
        *sums, result, input_grad, small = whole_layer(
            lengths, momentum[0].T, decay[0].T, step_size[0].T, inputs[0], cotangent[0], gain_attn[None], gain_ffn[None], persist_keys, persist_values,
            w_query, w_key, w_value, w_out, w_gate.T, w_up.T, w_down, count, parts,
        )
        gate_sum, up_sum, down_sum, query_sum, key_sum, value_sum, out_sum, *rest = finish(
            sums, (result, input_grad), small, persist_keys.shape
        )
        result, input_grad, gain_attn_sum, gain_ffn_sum, persist_k_sum, persist_v_sum, rms_stats = rest
    else:
        resid = inputs[0].astype(f32)
        scale_attn = rows_scale(resid)
        near, far = gather_rows((resid * scale_attn * gain_attn).astype(bf16))
        w_qkv = jnp.concatenate([w_query, w_key, w_value], 1)
        qkv = jnp.concatenate([mul(near, w_qkv).astype(bf16), mul(far, w_qkv).astype(bf16)], 0)
        normed_attn = jnp.concatenate([near, far], 0)
        mixed, log_total, states, grams = attend_and_recall(*rates, qkv, persist_keys, persist_values, parts)
        branch_attn = scatter_rows(mul(mixed[:half], w_out), mul(mixed[half:], w_out))
        middle = resid + branch_attn
        scale_ffn = rows_scale(middle)
        normed_ffn = jnp.concatenate(gather_rows((middle * scale_ffn * gain_ffn).astype(bf16)), 0)

        out_grad = cotangent[0].astype(f32) * own_valid
        out_full = jnp.concatenate(gather_rows(out_grad.astype(bf16)), 0)
        gate = mul(normed_ffn, w_gate)
        up = mul(normed_ffn, w_up)
        sigmoid = jax.nn.sigmoid(gate)
        silu = gate * sigmoid
        hidden = (silu * up).astype(bf16)
        branch_ffn = scatter_rows(mul(hidden[:half], w_down), mul(hidden[half:], w_down))
        result = middle + branch_ffn
        hidden_grad = mul_nt(out_full, w_down)
        gate_grad = (hidden_grad * up * sigmoid * (1.0 + gate * (1.0 - sigmoid))).astype(bf16)
        up_grad = (hidden_grad * silu).astype(bf16)

        def masked(value_in):
            return jnp.sum(own_valid * (value_in * value_in))

        squares = jnp.stack(
            [masked(resid), masked(middle), masked(result), masked(branch_attn), masked(branch_ffn), jnp.sum(own_valid)]
        )
        grad_down = mul_tn(hidden, out_full).astype(bf16)
        grad_gate = mul_tn(gate_grad, normed_ffn).astype(bf16)
        grad_up = mul_tn(up_grad, normed_ffn).astype(bf16)
        normed_ffn_grad = scatter_rows(
            mul_nt(gate_grad[:half], w_gate) + mul_nt(up_grad[:half], w_up),
            mul_nt(gate_grad[half:], w_gate) + mul_nt(up_grad[half:], w_up),
        )
        gain_ffn_part = jnp.sum(normed_ffn_grad * middle * scale_ffn, axis=0)
        middle_grad = out_grad + norm_back(middle, scale_ffn, gain_ffn, normed_ffn_grad)
        middle_full = jnp.concatenate(gather_rows(middle_grad.astype(bf16)), 0)
        mixed_grad = mul_nt(middle_full, w_out).astype(bf16)
        qkv_grad, persist_k_grad, persist_v_grad = attend_and_recall_back(
            *rates, qkv, mixed_grad, persist_keys, persist_values, log_total, states, grams, parts
        )
        normed_attn_grad = scatter_rows(mul_nt(qkv_grad[:half], w_qkv), mul_nt(qkv_grad[half:], w_qkv))
        gain_attn_part = jnp.sum(normed_attn_grad * resid * scale_attn, axis=0)
        input_grad = (middle_grad + norm_back(resid, scale_attn, gain_attn, normed_attn_grad)).astype(bf16)
        gate_sum, up_sum, down_sum, wide, out_sum, persist_sums = lax.psum(
            (grad_gate, grad_up, grad_down, mul_tn(normed_attn, qkv_grad).astype(bf16),
             mul_tn(mixed, middle_full).astype(bf16), jnp.stack([persist_k_grad, persist_v_grad])), "dp"
        )
        query_sum, key_sum, value_sum = wide[:, :cols], wide[:, cols:2 * cols], wide[:, 2 * cols:]
        gains, squares = lax.psum((jnp.concatenate([gain_attn_part, gain_ffn_part]), squares), ("dp", "tensor"))
        gain_attn_sum, gain_ffn_sum = gains[:width], gains[width:]
        persist_k_sum, persist_v_sum = persist_sums[0], persist_sums[1]
        rms_stats = jnp.sqrt(squares[:5] / (squares[5] * width))
    return (
        result.astype(bf16)[None],
        input_grad[None],
        gain_attn_sum.reshape(-1),
        query_sum.astype(f32),
        key_sum.astype(f32),
        value_sum.astype(f32),
        out_sum.astype(f32),
        persist_k_sum,
        persist_v_sum,
        gain_ffn_sum.reshape(-1),
        gate_sum.astype(f32).T,
        up_sum.astype(f32).T,
        down_sum.astype(f32),
        rms_stats,
    )


def solution(mesh):
    in_specs = (
        P("dp", "tensor", None),
        P("dp", "tensor", None),
        P("dp"),
        P(),
        P(None, "tensor"),
        P(None, "tensor"),
        P(None, "tensor"),
        P("tensor", None),
        P("tensor", None, None),
        P("tensor", None, None),
        P(),
        P(None, "tensor"),
        P(None, "tensor"),
        P("tensor", None),
        P("dp", None, "tensor"),
        P("dp", None, "tensor"),
        P("dp", None, "tensor"),
    )
    out_specs = (
        P("dp", "tensor", None),
        P("dp", "tensor", None),
        P(),
        P(None, "tensor"),
        P(None, "tensor"),
        P(None, "tensor"),
        P("tensor", None),
        P("tensor", None, None),
        P("tensor", None, None),
        P(),
        P(None, "tensor"),
        P(None, "tensor"),
        P("tensor", None),
        P(),
    )
    return jax.shard_map(body, mesh=mesh, in_specs=in_specs, out_specs=out_specs, check_vma=False)
```

```python
import functools
import jax
import jax.numpy as jnp
from jax import lax
from jax.sharding import PartitionSpec as P
import jax.experimental.pallas as pl
import jax.experimental.pallas.tpu as pltpu

norm_eps = 1e-05
unit_eps = 1e-06
f32 = jnp.float32
bf16 = jnp.bfloat16
log2_e = 1.4426950408889634


def dot_nn(left, right):
    return lax.dot_general(left, right, (((1,), (0,)), ((), ())), preferred_element_type=f32)


def dot_nt(left, right):
    return lax.dot_general(left, right, (((1,), (1,)), ((), ())), preferred_element_type=f32)


def dot_tn(left, right):
    return lax.dot_general(left, right, (((0,), (0,)), ((), ())), preferred_element_type=f32)


def halves(value):
    high = value.astype(bf16)
    return high, (value - high.astype(f32)).astype(bf16)


def dot3(dot, left, right):
    (lh, ll), (rh, rl) = left, right
    return dot(lh, rh) + dot(ll, rh) + dot(lh, rl)


def unit_rows(value):
    wide = value.astype(f32)
    scale = lax.rsqrt(jnp.sum(wide * wide, axis=-1, keepdims=True) + unit_eps)
    return wide * scale, scale


def block_rows(start, width):
    return pl.ds(pl.multiple_of(start, width), width)


def forward_kernel(
    heads, blocks, parts,
    place, length, momentum, decay, step_size, qkv, persist_k, persist_v,
    mixed, log_total, states, grams,
    ordered, reads,
):
    seq_len, wide = qkv.shape
    size = persist_k.shape[2]
    cols = heads * size
    rows = seq_len // parts
    width = seq_len // blocks
    me = place[0]
    count = length[0]
    for b in range(parts):
        ordered[b * rows:(b + 1) * rows, :] = qkv[block_rows(jnp.bitwise_xor(me, b) * rows, rows), :]

    carried = [(jnp.zeros((size, size), f32), jnp.zeros((size, size), f32)) for _ in range(heads)]
    for c in range(blocks):
        span = slice(c * width, (c + 1) * width)
        live = (c * width + lax.broadcasted_iota(jnp.int32, (width, 1), 0) < count).astype(f32)
        for h in range(heads):
            col = h * size
            key_unit, _ = unit_rows(ordered[span, cols + col:cols + col + size])
            query_unit, _ = unit_rows(ordered[span, col:col + size])
            value = ordered[span, 2 * cols + col:2 * cols + col + size]
            key_h, key_l = halves(key_unit)
            live_h, live_l = halves(key_unit * live)
            gram = dot3(dot_tn, (live_h, live_l), (key_h, key_l))
            target = dot_tn(value, live_h) + dot_tn(value, live_l)
            memory, velocity = carried[h]
            states[h, c] = memory.astype(bf16)
            grams[h, c] = gram
            parts_m = halves(memory)
            reads[span, col:col + size] = dot_nt(query_unit.astype(bf16), parts_m[0])
            change = dot3(dot_nn, parts_m, halves(gram)) - target
            velocity = momentum[c, h] * velocity - step_size[c, h] * change
            memory = (1.0 - decay[c, h]) * memory + velocity
            carried[h] = (memory, velocity)

    factor = size ** (-0.5) * log2_e
    diagonal = lax.broadcasted_iota(jnp.int32, (rows, rows), 0) <= lax.broadcasted_iota(jnp.int32, (rows, rows), 1)
    for h in range(heads):
        col = h * size
        value_t = ordered[:, 2 * cols + col:2 * cols + col + size].T
        persist_t = persist_v[h].astype(f32).T.astype(bf16)
        for i in range(parts):
            span = slice(i * rows, (i + 1) * rows)
            seen = (i + 1) * rows
            query = ordered[span, col:col + size]
            scores = dot_nt(ordered[:seen, cols + col:cols + col + size], query)
            last = jnp.where(diagonal, scores[seen - rows:], -1e30)
            scores = last if i == 0 else jnp.concatenate([scores[:seen - rows], last], axis=0)
            extra = dot_nt(persist_k[h], query)
            top = jnp.maximum(jnp.max(scores, axis=0, keepdims=True), jnp.max(extra, axis=0, keepdims=True))
            lifted = jnp.exp2((scores - top) * factor)
            lifted_extra = jnp.exp2((extra - top) * factor)
            total = jnp.sum(lifted, axis=0, keepdims=True) + jnp.sum(lifted_extra, axis=0, keepdims=True)
            attended = dot_nn(value_t[:, :seen], lifted.astype(bf16)) + dot_nn(persist_t, lifted_extra.astype(bf16))
            attended = attended * (1.0 / total)
            log_total[h:h + 1, span] = top * factor + jnp.log2(total)
            together = attended.T + reads[span, col:col + size]
            mixed[block_rows(jnp.bitwise_xor(me, i) * rows, rows), col:col + size] = together.astype(bf16)


def backward_kernel(
    heads, blocks, parts,
    place, length, momentum, decay, step_size, qkv, mixed_grad, persist_k, persist_v,
    log_total, states, grams,
    qkv_grad, persist_k_grad, persist_v_grad,
    ordered, upstream, slopes, key_sum, value_sum, query_sum,
):
    seq_len, wide = qkv.shape
    size = persist_k.shape[2]
    cols = heads * size
    rows = seq_len // parts
    width = seq_len // blocks
    me = place[0]
    count = length[0]
    for b in range(parts):
        source = block_rows(jnp.bitwise_xor(me, b) * rows, rows)
        ordered[b * rows:(b + 1) * rows, :] = qkv[source, :]
        upstream[b * rows:(b + 1) * rows, :] = mixed_grad[source, :]

    carried = [(jnp.zeros((size, size), f32), jnp.zeros((size, size), f32)) for _ in range(heads)]
    for c in reversed(range(blocks)):
        span = slice(c * width, (c + 1) * width)
        for h in range(heads):
            col = h * size
            query_unit, _ = unit_rows(ordered[span, col:col + size])
            query_h, query_l = halves(query_unit)
            rise = upstream[span, col:col + size]
            entry = dot_tn(rise, query_h) + dot_tn(rise, query_l)
            memory, velocity = carried[h]
            velocity = velocity + memory
            change = (-step_size[c, h]) * velocity
            slopes[h, c] = change
            memory = (1.0 - decay[c, h]) * memory + entry + dot3(dot_nn, halves(change), halves(grams[h, c]))
            velocity = momentum[c, h] * velocity
            carried[h] = (memory, velocity)

    for h in range(heads):
        col = h * size
        for c in range(blocks):
            span = slice(c * width, (c + 1) * width)
            live = (c * width + lax.broadcasted_iota(jnp.int32, (width, 1), 0) < count).astype(f32)
            query_unit, query_scale = unit_rows(ordered[span, col:col + size])
            key_unit, key_scale = unit_rows(ordered[span, cols + col:cols + col + size])
            value = ordered[span, 2 * cols + col:2 * cols + col + size].astype(f32)
            rise = upstream[span, col:col + size]
            state = states[h, c]
            slope = slopes[h, c].astype(bf16)
            key_b = key_unit.astype(bf16)
            error = (dot_nt(key_b, state) - value) * live
            error_grad = dot_nt(key_b, slope) * live
            unit_grad = dot_nn(error.astype(bf16), slope) + dot_nn(error_grad.astype(bf16), state)
            key_sum[span, :] = key_scale * (unit_grad - key_unit * jnp.sum(unit_grad * key_unit, axis=-1, keepdims=True))
            value_sum[span, :] = -error_grad
            read_grad = dot_nn(rise, state)
            query_sum[span, :] = query_scale * (read_grad - query_unit * jnp.sum(read_grad * query_unit, axis=-1, keepdims=True))

        factor = size ** (-0.5)
        diagonal = lax.broadcasted_iota(jnp.int32, (rows, rows), 0) <= lax.broadcasted_iota(jnp.int32, (rows, rows), 1)
        key_t = ordered[:, cols + col:cols + col + size].T
        persist_t = persist_k[h].astype(f32).T.astype(bf16)
        persist_k_total = jnp.zeros(persist_k.shape[1:], f32)
        persist_v_total = jnp.zeros(persist_k.shape[1:], f32)
        for i in range(parts):
            span = slice(i * rows, (i + 1) * rows)
            seen = (i + 1) * rows
            query = ordered[span, col:col + size]
            rise = upstream[span, col:col + size]
            scores = dot_nt(ordered[:seen, cols + col:cols + col + size], query)
            last = jnp.where(diagonal, scores[seen - rows:], -1e30)
            scores = last if i == 0 else jnp.concatenate([scores[:seen - rows], last], axis=0)
            extra = dot_nt(persist_k[h], query)
            base = log_total[h:h + 1, span]
            probs = jnp.exp2(scores * (factor * log2_e) - base)
            probs_extra = jnp.exp2(extra * (factor * log2_e) - base)
            probs_grad = dot_nt(ordered[:seen, 2 * cols + col:2 * cols + col + size], rise)
            extra_grad = dot_nt(persist_v[h], rise)
            weighted = probs * probs_grad
            weighted_extra = probs_extra * extra_grad
            inner = jnp.sum(weighted, axis=0, keepdims=True) + jnp.sum(weighted_extra, axis=0, keepdims=True)
            scores_grad = (weighted - probs * inner).astype(bf16)
            scores_extra = (weighted_extra - probs_extra * inner).astype(bf16)
            query_t = dot_nn(key_t[:, :seen], scores_grad) + dot_nn(persist_t, scores_extra)
            query_sum[span, :] += query_t.T * factor
            key_sum[:seen, :] += dot_nn(scores_grad, query) * factor
            value_sum[:seen, :] += dot_nn(probs.astype(bf16), rise)
            persist_k_total += dot_nn(scores_extra, query) * factor
            persist_v_total += dot_nn(probs_extra.astype(bf16), rise)
        persist_k_grad[h] = persist_k_total
        persist_v_grad[h] = persist_v_total
        for b in range(parts):
            span = slice(b * rows, (b + 1) * rows)
            target = block_rows(jnp.bitwise_xor(me, b) * rows, rows)
            qkv_grad[target, col:col + size] = query_sum[span, :].astype(bf16)
            qkv_grad[target, cols + col:cols + col + size] = key_sum[span, :].astype(bf16)
            qkv_grad[target, 2 * cols + col:2 * cols + col + size] = value_sum[span, :].astype(bf16)


vmem = functools.partial(pl.BlockSpec, memory_space=pltpu.VMEM)
smem = functools.partial(pl.BlockSpec, memory_space=pltpu.SMEM)
vmem_limit = 56 << 20


def attend_and_recall(place, length, momentum, decay, step_size, qkv, persist_k, persist_v, parts):
    heads, _, size = persist_k.shape
    seq_len = qkv.shape[0]
    blocks = momentum.shape[0]
    cols = heads * size
    return pl.pallas_call(
        functools.partial(forward_kernel, heads, blocks, parts),
        out_shape=(
            jax.ShapeDtypeStruct((seq_len, cols), bf16),
            jax.ShapeDtypeStruct((heads, seq_len), f32),
            jax.ShapeDtypeStruct((heads, blocks, size, size), bf16),
            jax.ShapeDtypeStruct((heads, blocks, size, size), f32),
        ),
        in_specs=[smem()] * 5 + [vmem()] * 3,
        out_specs=(vmem(),) * 4,
        scratch_shapes=[pltpu.VMEM((seq_len, 3 * cols), bf16), pltpu.VMEM((seq_len, cols), f32)],
        compiler_params=pltpu.CompilerParams(vmem_limit_bytes=vmem_limit),
        cost_estimate=pl.CostEstimate(flops=12_000_000_000, bytes_accessed=8_000_000, transcendentals=2_000_000),
        name="attend_recall",
    )(place, length, momentum, decay, step_size, qkv, persist_k, persist_v)


def attend_and_recall_back(
    place, length, momentum, decay, step_size, qkv, mixed_grad, persist_k, persist_v, log_total, states, grams, parts
):
    heads, persistent, size = persist_k.shape
    seq_len = qkv.shape[0]
    blocks = momentum.shape[0]
    cols = heads * size
    return pl.pallas_call(
        functools.partial(backward_kernel, heads, blocks, parts),
        out_shape=(
            jax.ShapeDtypeStruct((seq_len, 3 * cols), bf16),
            jax.ShapeDtypeStruct((heads, persistent, size), f32),
            jax.ShapeDtypeStruct((heads, persistent, size), f32),
        ),
        in_specs=[smem()] * 5 + [vmem()] * 7,
        out_specs=(vmem(),) * 3,
        scratch_shapes=[
            pltpu.VMEM((seq_len, 3 * cols), bf16),
            pltpu.VMEM((seq_len, cols), bf16),
            pltpu.VMEM((heads, blocks, size, size), f32),
            pltpu.VMEM((seq_len, size), f32),
            pltpu.VMEM((seq_len, size), f32),
            pltpu.VMEM((seq_len, size), f32),
        ],
        compiler_params=pltpu.CompilerParams(vmem_limit_bytes=vmem_limit),
        cost_estimate=pl.CostEstimate(flops=25_000_000_000, bytes_accessed=12_000_000, transcendentals=2_000_000),
        name="attend_recall_back",
    )(place, length, momentum, decay, step_size, qkv, mixed_grad, persist_k, persist_v, log_total, states, grams)


def ring_place(index, count):
    odd = index % 2
    return (1 - odd) * (index // 2) + odd * (count - 1 - index // 2)


def ring_index(place, count):
    late = place // (count // 2)
    return (1 - late) * (2 * place) + late * (2 * (count - 1 - place) + 1)


def flip(index, bit):
    return index + bit * (1 - 2 * ((index // bit) % 2))


def bits_below(count):
    return [1 << k for k in range(count.bit_length() - 1)]


def relative(index, block):
    for bit in (1, 2):
        if block & bit:
            index = flip(index, bit)
    return index


def remote(source, target, send_sem, recv_sem, device):
    return pltpu.make_async_remote_copy(
        src_ref=source, dst_ref=target, send_sem=send_sem, recv_sem=recv_sem,
        device_id=device, device_id_type=pl.DeviceIdType.MESH,
    )


class Ring:
    def __init__(self, count, by_rows, source, out, slots, send_sem, recv_sem, home, home_sem):
        self.homeward = pltpu.make_async_copy(out, home, home_sem)
        self.count, self.by_rows = count, by_rows
        self.source, self.out, self.slots = source, out, slots
        self.send_sem, self.recv_sem = send_sem, recv_sem
        index = lax.axis_index("dp")
        self.place = ring_place(index, count)
        self.peers = (
            {"dp": ring_index((self.place + 1) % count, count)},
            {"dp": ring_index((self.place + count - 1) % count, count)},
        )
        self.step = 0
        self.copies = [None, None]
        self.sent = [[], []]

    def piece(self, ref, way, chunk):
        rows, cols = ref.shape
        chunk = chunk % self.count
        if self.by_rows:
            size = rows // (2 * self.count)
            return ref.at[pl.ds(pl.multiple_of(chunk * (2 * size) + way * size, size), size), :]
        size, width = rows // 2, cols // self.count
        return ref.at[way * size:(way + 1) * size, pl.ds(pl.multiple_of(chunk * width, width), width)]

    def chunk(self, way, step):
        return self.place + self.count + (2 * self.count - step if way == 0 else step)

    def launch(self, way, step, source, target):
        copy = remote(source, target, self.send_sem.at[way, step % 2], self.recv_sem.at[way, step % self.count], self.peers[way])
        if step > 1:
            self.sent[way].pop(0).wait_send()
        copy.start()
        self.copies[way] = copy
        self.sent[way].append(copy)

    def start_way(self, way):
        self.launch(way, 0, self.piece(self.source, way, self.chunk(way, 0)), self.slots.at[way, 0])

    def start(self):
        for way in range(2):
            self.start_way(way)

    def advance(self):
        count, step = self.count, self.step
        for way in range(2):
            self.copies[way].wait_recv()
            if step < count - 1:
                chunk = self.chunk(way, step + 1)
                total = self.slots[way, step].astype(f32) + self.piece(self.source, way, chunk)[...].astype(f32)
                if step < count - 2:
                    self.slots[way, step] = total.astype(bf16)
                    source, target = self.slots.at[way, step], self.slots.at[way, step + 1]
                else:
                    source = target = self.piece(self.out, way, chunk)
                    source[...] = total.astype(bf16)
            else:
                source = target = self.piece(self.out, way, self.chunk(way, step + 1 - count))
            if step < 2 * count - 3:
                self.launch(way, step + 1, source, target)
        self.step += 1
        if self.step < 2 * count - 2:
            return True
        for copy in self.sent[0] + self.sent[1]:
            copy.wait_send()
        self.homeward.start()
        return False

    def left(self):
        return 2 * self.count - 2 - self.step


class SmallSum:
    def __init__(self, value, slots, shared, send_sem, recv_sem, count, parts):
        self.value, self.slots, self.shared = value, slots, shared
        self.send_sem, self.recv_sem = send_sem, recv_sem
        index, inner = lax.axis_index("dp"), lax.axis_index("tensor")
        self.inner = len(bits_below(parts))
        self.peers = [{"tensor": flip(inner, bit)} for bit in bits_below(parts)]
        self.peers += [{"dp": flip(index, bit)} for bit in bits_below(count)]
        self.step = 0

    def start(self):
        used = slice(0, self.shared if self.step < self.inner else self.value.shape[0])
        self.used = used
        self.copy = remote(
            self.value.at[used], self.slots.at[self.step, used], self.send_sem.at[self.step],
            self.recv_sem.at[self.step], self.peers[self.step],
        )
        self.copy.start()

    def left(self):
        return len(self.peers) - self.step

    def advance(self):
        self.copy.wait()
        self.value[self.used] += self.slots[self.step, self.used]
        self.step += 1
        if self.step < len(self.peers):
            self.start()
        return self.step < len(self.peers)


class Rounds:
    def __init__(self):
        self.queue = []

    def add(self, *flows):
        for flow in flows:
            flow.start()
            self.queue.append(flow)

    def spread(self, fast, slow):
        fast = [flow for flow in fast if flow in self.queue]
        slow = [flow for flow in slow if flow in self.queue]
        counts = {flow: flow.left() for flow in fast + slow}
        rest = [flow for k in range(max([counts[flow] for flow in slow], default=0)) for flow in slow if k < counts[flow]]
        turns = max(counts[flow] for flow in fast)
        self.queue = []
        for k in range(turns):
            self.queue += [flow for flow in fast if k < counts[flow]]
            self.queue += rest[k * len(rest) // turns:(k + 1) * len(rest) // turns]

    def mix(self, flow):
        for k in range(flow.left()):
            self.queue.insert(min(6 * k + 4, len(self.queue)), flow)

    def tick(self, count=1):
        for _ in range(count):
            if self.queue:
                flow = self.queue.pop(0)
                if flow.advance() and flow not in self.queue:
                    self.queue.append(flow)

    def finish(self):
        while self.queue:
            self.tick()


def rows_scale(value):
    return lax.rsqrt(jnp.mean(value * value, axis=-1, keepdims=True) + norm_eps)


class Scatter:
    def __init__(self, sent, landed, hold, send_sem, recv_sem):
        self.sent, self.landed, self.hold = sent, landed, hold
        self.send_sem, self.recv_sem = send_sem, recv_sem
        self.rows = hold.shape[0] // 2
        inner = lax.axis_index("tensor")
        self.sibling, self.across = {"tensor": flip(inner, 1)}, {"tensor": flip(inner, 2)}

    def span(self, j):
        return slice(j * self.rows, (j + 1) * self.rows)

    def copy(self, k, j, device):
        return remote(
            self.sent.at[k, self.span(j)], self.landed.at[k, self.span(j)],
            self.send_sem.at[k, j], self.recv_sem.at[k, j], device,
        )

    def begin(self, block, tick):
        first = [self.copy(0, j, self.sibling) for j in range(2)]
        self.second = [self.copy(1, j, self.across) for j in range(2)]
        self.third = [self.copy(2, j, self.sibling) for j in range(2)]
        for j in range(2):
            self.sent[0, self.span(j)] = block(3, j).astype(bf16)
            first[j].start()
        for j in range(2):
            self.hold[self.span(j), :] = block(2, j)
        tick()
        for j in range(2):
            first[j].wait()
            self.sent[1, self.span(j)] = (
                self.hold[self.span(j), :] + self.landed[0, self.span(j)].astype(f32)
            ).astype(bf16)
            self.second[j].start()
        for j in range(2):
            self.sent[2, self.span(j)] = block(1, j).astype(bf16)
            self.third[j].start()
        tick()
        for j in range(2):
            self.hold[self.span(j), :] = block(0, j)

    def finish(self, j):
        span = self.span(j)
        self.third[j].wait()
        self.second[j].wait()
        return self.hold[span, :] + self.landed[2, span].astype(f32) + self.landed[1, span].astype(f32)


class Gather:
    def __init__(self, full, parts, send_sem, recv_sem):
        self.full, self.rows = full, full.shape[0] // (2 * parts)
        self.send_sem, self.recv_sem = send_sem, recv_sem
        inner = lax.axis_index("tensor")
        self.sibling, self.across = {"tensor": flip(inner, 1)}, {"tensor": flip(inner, 2)}
        self.far, self.near, self.both = [None] * 2, [None] * 2, [None] * 2

    def copy(self, source, target, k, j, device):
        def piece(b):
            first = (2 * b + j) * self.rows
            return self.full.at[first:first + self.rows, :]

        return remote(piece(source), piece(target), self.send_sem.at[k, j], self.recv_sem.at[k, j], device)

    def begin(self, j):
        self.far[j], self.near[j] = self.copy(0, 2, 0, j, self.across), self.copy(0, 1, 1, j, self.sibling)
        self.far[j].start()
        self.near[j].start()

    def forward(self, then=lambda j: None):
        for j in range(2):
            self.far[j].wait()
            then(j)
            self.both[j] = self.copy(2, 3, 2, j, self.sibling)
            self.both[j].start()

    def wait(self, copies):
        for copy in copies:
            copy.wait()


def dot_pair(high, low, right):
    return dot_nn(jnp.concatenate([high, low], axis=1), jnp.concatenate([right, right], axis=0))


def layer_kernel(
    heads, blocks, parts, count, shared, pace,
    length, momentum, decay, step_size,
    inputs_h, cotangent_h, gain_attn, gain_ffn_h, persist_k_h, persist_v_h,
    w_query_h, w_key_h, w_value_h, w_out_h, w_gate_h, w_up_h, w_down_h,
    gate_home, up_home, down_home, query_home, key_home, value_home, out_home, result_home, input_grad_home, small,
    w_qkv, w_out, w_gate, w_up, w_down,
    normed_attn, ordered, mixed, states, grams, log_total,
    middle, hold, middle_grad, normed_ffn, out_full, gate_grad, up_grad, hidden,
    gate_source, up_source, down_source, query_source, key_source, value_source, out_source,
    gate_slots, up_slots, down_slots, query_slots, key_slots, value_slots, out_slots, small_slots,
    gate_out, up_out, down_out, query_out, key_out, value_out, out_out, result, input_grad,
    inputs, cotangent, gain_ffn, persist_k, persist_v, sent_a, landed_a, sent_b, landed_b, middle_full, upstream, slopes, key_sum, value_sum, query_sum, qkv_grad,
    load_sem, home_sem, ring_send, ring_recv, small_send, small_recv, move_send, move_recv,
):
    size = persist_k.shape[2]
    many = persist_k.shape[1]
    cols = heads * size
    seq_len, width = middle_full.shape
    units = gate_grad.shape[0]
    rows = seq_len // parts
    span_rows = seq_len // blocks
    inner = lax.axis_index("tensor")
    valid_count = length[0]
    factor = size ** (-0.5)

    rounds = Rounds()
    rings = [
        Ring(count, by_rows, source, out, slots, ring_send.at[k], ring_recv.at[k], home, home_sem.at[k])
        for k, (by_rows, source, out, slots, home) in enumerate((
            (False, down_source, down_out, down_slots, down_home),
            (False, gate_source, gate_out, gate_slots, gate_home),
            (False, up_source, up_out, up_slots, up_home),
            (False, out_source, out_out, out_slots, out_home),
            (True, query_source, query_out, query_slots, query_home),
            (True, key_source, key_out, key_slots, key_home),
            (True, value_source, value_out, value_slots, value_home),
        ))
    ]
    small_sum = SmallSum(small, small_slots, shared, small_send, small_recv, count, parts)
    barrier = pltpu.get_barrier_semaphore()
    peers = list(rings[0].peers) + small_sum.peers
    for peer in peers:
        pl.semaphore_signal(barrier, inc=1, device_id=peer, device_id_type=pl.DeviceIdType.MESH)

    loads = []

    def load(source, target):
        copy = pltpu.make_async_copy(source, target, load_sem.at[len(loads)])
        copy.start()
        loads.append(copy)
        return copy

    input_load, cotangent_load = load(inputs_h, inputs), load(cotangent_h, cotangent)
    qkv_loads = [
        load(source, w_qkv.at[:, k * cols:(k + 1) * cols]) for k, source in enumerate((w_query_h, w_key_h, w_value_h))
    ]
    persist_loads = [load(persist_k_h, persist_k), load(persist_v_h, persist_v), load(gain_ffn_h, gain_ffn)]
    out_load = load(w_out_h, w_out)
    ffn_loads = [load(w_gate_h, w_gate), load(w_up_h, w_up), load(w_down_h, w_down)]

    def true_rows(b):
        return pl.ds(pl.multiple_of(relative(inner, b) * rows, rows), rows)

    def block_of(b):
        return slice(b * rows, (b + 1) * rows)

    row_place = inner * rows + lax.broadcasted_iota(jnp.int32, (rows, 1), 0)
    own_valid = (row_place < valid_count).astype(f32)
    stat_row = 2 * width // size

    def half_rows(j):
        return slice(j * (rows // 2), (j + 1) * (rows // 2))

    def part_of(b, j):
        return slice((2 * b + j) * (rows // 2), (2 * b + j + 1) * (rows // 2))

    def note(k, value, j):
        total = jnp.sum(jnp.sum(value, axis=1, keepdims=True) * own_valid[half_rows(j)], axis=0, keepdims=True)
        small[stat_row + k:stat_row + k + 1, :] += jnp.broadcast_to(total, (1, size))

    gather_attn = Gather(normed_attn, parts, move_send.at[0], move_recv.at[0])
    small[stat_row:stat_row + 8, :] = jnp.zeros((8, size), f32)

    def attn_norm(j):
        resid = inputs[half_rows(j), :].astype(f32)
        normed_attn[half_rows(j), :] = (resid * rows_scale(resid) * gain_attn[...]).astype(bf16)
        note(0, resid * resid, j)

    input_load.wait()
    attn_norm(0)
    pl.semaphore_wait(barrier, len(peers))
    gather_attn.begin(0)
    attn_norm(1)
    gather_attn.begin(1)
    cotangent_load.wait()
    out_full[0:rows, :] = (cotangent[...].astype(f32) * own_valid).astype(bf16)
    for j in range(2):
        note(5, jnp.ones((rows // 2, 1), f32), j)
    for copy in qkv_loads:
        copy.wait()

    def qkv_block(b):
        made = dot_nn(normed_attn[block_of(b), :], w_qkv[...])
        ordered[true_rows(b), :] = made.astype(bf16)
        first = relative(inner, b) * (rows // span_rows)
        place = lax.broadcasted_iota(jnp.int32, (rows, 1), 0)
        live = (relative(inner, b) * rows + place < valid_count).astype(f32)
        for h in range(heads):
            col = h * size
            key_unit, _ = unit_rows(made[:, cols + col:cols + col + size].astype(bf16))
            value = made[:, 2 * cols + col:2 * cols + col + size].astype(bf16)
            live_unit = (key_unit * live).astype(bf16)
            empty = jnp.zeros((span_rows, size), bf16)
            spread = jnp.concatenate([
                jnp.concatenate([
                    live_unit[k * span_rows:(k + 1) * span_rows] if k == m else empty for m in range(rows // span_rows)
                ], axis=1) for k in range(rows // span_rows)
            ], axis=0)
            both = dot_nn(jnp.concatenate([value, key_unit.astype(bf16)], axis=1).T, spread).astype(bf16)
            for k in range(rows // span_rows):
                slopes[h, first + k] = both[:size, k * size:(k + 1) * size]
                grams[h, first + k] = both[size:, k * size:(k + 1) * size]

    qkv_block(0)
    gather_attn.wait(gather_attn.near)
    qkv_block(1)
    gather_cot = Gather(out_full, parts, move_send.at[1], move_recv.at[1])
    gather_attn.forward(gather_cot.begin)
    qkv_block(2)
    gather_attn.wait(gather_attn.both)
    qkv_block(3)

    for copy in persist_loads:
        copy.wait()
    diagonal = lax.broadcasted_iota(jnp.int32, (rows, rows), 0) <= lax.broadcasted_iota(jnp.int32, (rows, rows), 1)
    tiles = [(h, i) for i in range(parts) for h in range(heads)]

    def masked_scores(h, i, query):
        seen = (i + 1) * rows
        scores = dot_nt(ordered[:seen, cols + h * size:cols + (h + 1) * size], query)
        last = jnp.where(diagonal, scores[seen - rows:], -1e30)
        return last if i == 0 else jnp.concatenate([scores[:seen - rows], last], axis=0)

    value_t = [ordered[:, 2 * cols + h * size:2 * cols + (h + 1) * size].T for h in range(heads)]
    persist_t = [persist_v[h].astype(f32).T.astype(bf16) for h in range(heads)]

    def attend(h, i):
        seen, col = (i + 1) * rows, h * size
        query = ordered[block_of(i), col:col + size]
        scores = masked_scores(h, i, query)
        extra = dot_nt(persist_k[h], query)
        top = jnp.maximum(jnp.max(scores, axis=0, keepdims=True), jnp.max(extra, axis=0, keepdims=True))
        lifted = jnp.exp2((scores - top) * (factor * log2_e))
        lifted_extra = jnp.exp2((extra - top) * (factor * log2_e))
        total = jnp.sum(lifted, axis=0, keepdims=True) + jnp.sum(lifted_extra, axis=0, keepdims=True)
        attended = dot_nn(value_t[h][:, :seen], lifted.astype(bf16)) + dot_nn(persist_t[h], lifted_extra.astype(bf16))
        log_total[h:h + 1, block_of(i)] = top * (factor * log2_e) + jnp.log2(total)
        query_sum[block_of(i), col:col + size] = (attended * (1.0 / total)).T

    carried = [(jnp.zeros((size, size), f32), jnp.zeros((size, size), f32)) for _ in range(heads)]
    for c in range(blocks):
        for h in range(heads):
            memory, velocity = carried[h]
            high, low_part = halves(memory)
            states[h, c] = high
            change = dot_pair(high, low_part, grams[h, c]) - slopes[h, c].astype(f32)
            velocity = momentum[h, c] * velocity - step_size[h, c] * change
            memory = (1.0 - decay[h, c]) * memory + velocity
            carried[h] = (memory, velocity)
        for h, i in tiles[c * len(tiles) // blocks:(c + 1) * len(tiles) // blocks]:
            attend(h, i)
    def mix(b):
        span, first = true_rows(b), relative(inner, b) * (rows // span_rows)
        for h in range(heads):
            wide = slice(h * size, (h + 1) * size)
            query_unit = unit_rows(ordered[span, wide])[0].astype(bf16)
            reads = [
                dot_nt(query_unit[k * span_rows:(k + 1) * span_rows], states[h, first + k])
                for k in range(rows // span_rows)
            ]
            mixed[block_of(b), wide] = (query_sum[span, wide] + jnp.concatenate(reads, axis=0)).astype(bf16)

    def project(b, j):
        if j == 0:
            mix(b)
        return dot_nn(mixed[part_of(b, j), :], w_out[...])

    out_load.wait()
    scatter = Scatter(sent_a, landed_a, hold, move_send.at[2], move_recv.at[2])
    scatter.begin(project, rounds.tick)
    gather_cot.wait(gather_cot.near)
    gather_cot.forward()
    gather_ffn = Gather(normed_ffn, parts, move_send.at[0], move_recv.at[0])
    for j in range(2):
        branch = scatter.finish(j)
        value = inputs[half_rows(j), :].astype(f32) + branch
        middle[half_rows(j), :] = value
        normed_ffn[half_rows(j), :] = (value * rows_scale(value) * gain_ffn[...]).astype(bf16)
        gather_ffn.begin(j)
        note(3, branch * branch, j)
        note(1, value * value, j)
    for copy in ffn_loads:
        copy.wait()
    gather_cot.wait(gather_cot.both)
    gather_ffn.wait(gather_ffn.near)

    piece = units // 4

    def feed(tokens):
        for k in range(4):
            span = slice(k * piece, (k + 1) * piece)
            gate = dot_nt(w_gate[span, :], normed_ffn[tokens, :])
            up = dot_nt(w_up[span, :], normed_ffn[tokens, :])
            hidden_grad = dot_nt(w_down[span, :], out_full[tokens, :])
            sigmoid = jax.nn.sigmoid(gate)
            silu = gate * sigmoid
            hidden[span, tokens] = (silu * up).astype(bf16)
            up_grad[span, tokens] = (hidden_grad * silu).astype(bf16)
            gate_grad[span, tokens] = (hidden_grad * up * sigmoid * (1.0 + gate * (1.0 - sigmoid))).astype(bf16)

    feed(slice(0, 2 * rows))
    gather_ffn.forward()
    feed(block_of(2))
    gather_ffn.wait(gather_ffn.both)
    feed(block_of(3))
    for source, left, right, ring in (
        (down_source, hidden, out_full, rings[0]), (gate_source, gate_grad, normed_ffn, rings[1]),
        (up_source, up_grad, normed_ffn, rings[2]),
    ):
        for way in range(2):
            span = slice(way * (units // 2), (way + 1) * (units // 2))
            source[span, :] = dot_nn(left[span, :], right[...]).astype(bf16)
            ring.start_way(way)
        rounds.queue.append(ring)

    scatter = Scatter(sent_b, landed_b, hold, move_send.at[3], move_recv.at[3])
    scatter.begin(
        lambda b, j: dot_tn(gate_grad[:, part_of(b, j)], w_gate[...]) + dot_tn(up_grad[:, part_of(b, j)], w_up[...]),
        rounds.tick,
    )
    rounds.tick(pace[0])
    for b in range(parts):
        normed_ffn[:, block_of(b)] = normed_attn[block_of(b), :].T
        rounds.tick(pace[9])
    gather_middle = Gather(middle_full, parts, move_send.at[1], move_recv.at[1])
    gain_row = jnp.zeros((1, width), f32)
    for j in range(2):
        normed_grad = scatter.finish(j)
        value = middle[half_rows(j), :]
        scale = rows_scale(value)
        weighted = normed_grad * gain_ffn[...]
        grad = (
            cotangent[half_rows(j), :].astype(f32) * own_valid[half_rows(j)] + scale * weighted
            - value * (scale * scale * scale) * jnp.mean(weighted * value, axis=-1, keepdims=True)
        )
        middle_grad[half_rows(j), :] = grad
        middle_full[half_rows(j), :] = grad.astype(bf16)
        gather_middle.begin(j)
        gain_row = gain_row + jnp.sum(normed_grad * value * scale, axis=0, keepdims=True)
        if j == 0:
            rounds.tick(pace[8])
    for k in range(width // size):
        small[width // size + k:width // size + k + 1, :] = gain_row[:, k * size:(k + 1) * size]
    rounds.tick(pace[1])
    gather_middle.wait(gather_middle.near)

    def mixed_block(b):
        upstream[true_rows(b), :] = dot_nt(middle_full[block_of(b), :], w_out[...]).astype(bf16)

    mixed_block(0)
    mixed_block(1)
    gather_middle.forward()
    mixed_block(2)
    gather_middle.wait(gather_middle.both)
    mixed_block(3)
    scatter = Scatter(sent_a, landed_a, hold, move_send.at[2], move_recv.at[2])
    scatter.begin(lambda b, j: dot_tn(hidden[:, part_of(b, j)], w_down[...]), rounds.tick)
    rounds.tick(pace[2])
    out_source[...] = dot_tn(mixed[...], middle_full[...]).astype(bf16)
    rounds.add(rings[3])

    key_t = [ordered[:, cols + h * size:cols + (h + 1) * size].T for h in range(heads)]
    persist_t = [persist_k[h].astype(f32).T.astype(bf16) for h in range(heads)]
    persist_sums = [[jnp.zeros((many, size), f32), jnp.zeros((many, size), f32)] for _ in range(heads)]

    def attend_back(h, i):
        span, seen, col = block_of(i), (i + 1) * rows, h * size
        wide = slice(col, col + size)
        query = ordered[span, wide]
        rise = upstream[span, wide]
        scores = masked_scores(h, i, query)
        extra = dot_nt(persist_k[h], query)
        base = log_total[h:h + 1, span]
        probs = jnp.exp2(scores * (factor * log2_e) - base)
        probs_extra = jnp.exp2(extra * (factor * log2_e) - base)
        probs_grad = dot_nt(ordered[:seen, 2 * cols + col:2 * cols + col + size], rise)
        extra_grad = dot_nt(persist_v[h], rise)
        weighted = probs * probs_grad
        weighted_extra = probs_extra * extra_grad
        inner_sum = jnp.sum(weighted, axis=0, keepdims=True) + jnp.sum(weighted_extra, axis=0, keepdims=True)
        scores_grad = (weighted - probs * inner_sum).astype(bf16)
        scores_extra = (weighted_extra - probs_extra * inner_sum).astype(bf16)
        query_t = dot_nn(key_t[h][:, :seen], scores_grad) + dot_nn(persist_t[h], scores_extra)
        query_sum[span, wide] = query_t.T * factor
        key_part = dot_nn(scores_grad, query) * factor
        value_part = dot_nn(probs.astype(bf16), rise)
        for ref, part in ((key_sum, key_part), (value_sum, value_part)):
            ref[span, wide] = part[seen - rows:]
            if i:
                ref[:seen - rows, wide] += part[:seen - rows]
        persist_sums[h][0] += dot_nn(scores_extra, query) * factor
        persist_sums[h][1] += dot_nn(probs_extra.astype(bf16), rise)

    carried = [(jnp.zeros((size, size), f32), jnp.zeros((size, size), f32)) for _ in range(heads)]
    for c in reversed(range(blocks)):
        span = slice(c * span_rows, (c + 1) * span_rows)
        for h in range(heads):
            col = h * size
            query_unit, _ = unit_rows(ordered[span, col:col + size])
            rise = upstream[span, col:col + size]
            entry = dot_tn(rise, query_unit.astype(bf16))
            memory, velocity = carried[h]
            velocity = velocity + memory
            change = (-step_size[h, c]) * velocity
            slopes[h, c] = change.astype(bf16)
            memory = (1.0 - decay[h, c]) * memory + entry + dot_pair(*halves(change), grams[h, c])
            velocity = momentum[h, c] * velocity
            carried[h] = (memory, velocity)
        done = blocks - 1 - c
        for h, i in tiles[done * len(tiles) // blocks:(done + 1) * len(tiles) // blocks]:
            attend_back(h, i)
        rounds.tick(pace[3][done])

    for h in range(heads):
        col = h * size
        wide = slice(col, col + size)
        for c in range(blocks):
            span = slice(c * span_rows, (c + 1) * span_rows)
            live = (c * span_rows + lax.broadcasted_iota(jnp.int32, (span_rows, 1), 0) < valid_count).astype(f32)
            query_unit, query_scale = unit_rows(ordered[span, wide])
            key_unit, key_scale = unit_rows(ordered[span, cols + col:cols + col + size])
            value = ordered[span, 2 * cols + col:2 * cols + col + size].astype(f32)
            rise = upstream[span, wide]
            state = states[h, c]
            slope = slopes[h, c]
            error = (dot_nt(key_unit.astype(bf16), state) - value) * live
            error_grad = dot_nt(key_unit.astype(bf16), slope) * live
            unit_grad = dot_nn(error.astype(bf16), slope) + dot_nn(error_grad.astype(bf16), state)
            key_sum[span, wide] += key_scale * (
                unit_grad - key_unit * jnp.sum(unit_grad * key_unit, axis=-1, keepdims=True)
            )
            value_sum[span, wide] -= error_grad
            read_grad = dot_nn(rise, state)
            query_sum[span, wide] += query_scale * (
                read_grad - query_unit * jnp.sum(read_grad * query_unit, axis=-1, keepdims=True)
            )
            rounds.tick(pace[4][c])
        small[shared + h * many:shared + (h + 1) * many, :] = persist_sums[h][0]
        small[shared + (heads + h) * many:shared + (heads + h + 1) * many, :] = persist_sums[h][1]
    for b in range(parts):
        target = true_rows(b)
        qkv_grad[target, 0:cols] = query_sum[block_of(b), :].astype(bf16)
        qkv_grad[target, cols:2 * cols] = key_sum[block_of(b), :].astype(bf16)
        qkv_grad[target, 2 * cols:3 * cols] = value_sum[block_of(b), :].astype(bf16)

    for j in range(2):
        branch = scatter.finish(j)
        note(4, branch * branch, j)
        value = middle[half_rows(j), :] + branch
        note(2, value * value, j)
        result[half_rows(j), :] = value.astype(bf16)
    homes = [pltpu.make_async_copy(result, result_home, home_sem.at[len(rings)])]
    homes[0].start()

    for b in range(parts):
        span = block_of(b)
        grad = dot_nn(normed_ffn[span, :], qkv_grad[...])
        for k, source in enumerate((query_source, key_source, value_source)):
            source[span, :] = grad[:, k * cols:(k + 1) * cols].astype(bf16)
        rounds.tick(pace[6])
    rounds.add(*rings[4:])
    rounds.spread(rings[3:], rings[:3])
    scatter = Scatter(sent_b, landed_b, hold, move_send.at[3], move_recv.at[3])
    scatter.begin(lambda b, j: dot_nt(qkv_grad[part_of(b, j), :], w_qkv[...]), lambda: rounds.tick(pace[10]))
    for b in range(parts):
        span = block_of(b)
        products = sum(
            source[span, :].astype(f32) * w_qkv[span, k * cols:(k + 1) * cols].astype(f32)
            for k, source in enumerate((query_source, key_source, value_source))
        )
        gain_row = jnp.sum(products.T, axis=0, keepdims=True) / gain_attn[:, span]
        for k in range(rows // size):
            row = b * (rows // size) + k
            small[row:row + 1, :] = gain_row[:, k * size:(k + 1) * size]
        rounds.tick(pace[7])
    small_sum.start()
    rounds.mix(small_sum)
    for j in range(2):
        normed_grad = scatter.finish(j)
        value = inputs[half_rows(j), :].astype(f32)
        scale = rows_scale(value)
        weighted = normed_grad * gain_attn[...]
        input_grad[half_rows(j), :] = (
            middle_grad[half_rows(j), :] + scale * weighted
            - value * (scale * scale * scale) * jnp.mean(weighted * value, axis=-1, keepdims=True)
        ).astype(bf16)
    homes.append(pltpu.make_async_copy(input_grad, input_grad_home, home_sem.at[len(rings) + 1]))
    homes[1].start()
    rounds.finish()
    for copy in homes + [ring.homeward for ring in rings]:
        copy.wait()


def whole_layer(
    length, momentum, decay, step_size, inputs, cotangent, gain_attn, gain_ffn, persist_k, persist_v,
    w_query, w_key, w_value, w_out, w_gate, w_up, w_down, count, parts,
):
    heads, many, size = persist_k.shape
    blocks = momentum.shape[1]
    cols = heads * size
    rows, width = inputs.shape
    seq_len = rows * parts
    units = w_gate.shape[0]
    shared = 2 * width // size + 8
    small_rows = shared + 2 * heads * many
    flows = len(bits_below(count)) + len(bits_below(parts))

    def row_slots(*shape):
        return pltpu.VMEM((2, count - 1, shape[0] // (2 * count), shape[1]), bf16)

    def col_slots(*shape):
        return pltpu.VMEM((2, count - 1, shape[0] // 2, shape[1] // count), bf16)

    def low(*shape):
        return pltpu.VMEM(shape, bf16)

    def full(*shape):
        return pltpu.VMEM(shape, f32)

    def semaphores(*shape):
        return pltpu.SemaphoreType.DMA(shape)

    ffn = (units, width)
    return pl.pallas_call(
        functools.partial(layer_kernel, heads, blocks, parts, count, shared, pace),
        out_shape=(
            jax.ShapeDtypeStruct(ffn, bf16),
            jax.ShapeDtypeStruct(ffn, bf16),
            jax.ShapeDtypeStruct(ffn, bf16),
            jax.ShapeDtypeStruct((width, cols), bf16),
            jax.ShapeDtypeStruct((width, cols), bf16),
            jax.ShapeDtypeStruct((width, cols), bf16),
            jax.ShapeDtypeStruct((cols, width), bf16),
            jax.ShapeDtypeStruct((rows, width), bf16),
            jax.ShapeDtypeStruct((rows, width), bf16),
            jax.ShapeDtypeStruct((small_rows, size), f32),
        ),
        in_specs=[smem()] * 4 + [pl.BlockSpec(memory_space=pl.ANY)] * 2 + [vmem()] + [pl.BlockSpec(memory_space=pl.ANY)] * 10,
        out_specs=(pl.BlockSpec(memory_space=pl.ANY),) * 9 + (vmem(),),
        scratch_shapes=[
            low(width, 3 * cols), low(cols, width), low(*ffn), low(*ffn), low(*ffn),
            low(seq_len, width), low(seq_len, 3 * cols), low(seq_len, cols),
            low(heads, blocks, size, size), low(heads, blocks, size, size), full(heads, seq_len),
            full(rows, width), full(rows, width), full(rows, width), low(seq_len, width), low(seq_len, width),
            low(units, seq_len), low(units, seq_len), low(units, seq_len),
            low(*ffn), low(*ffn), low(*ffn), low(width, cols), low(width, cols), low(width, cols), low(cols, width),
            col_slots(*ffn), col_slots(*ffn), col_slots(*ffn),
            row_slots(width, cols), row_slots(width, cols), row_slots(width, cols), col_slots(cols, width),
            full(flows, small_rows, size),
            low(*ffn), low(*ffn), low(*ffn), low(width, cols), low(width, cols), low(width, cols), low(cols, width),
            low(rows, width), low(rows, width), low(rows, width), low(rows, width),
            full(1, width), low(heads, many, size), low(heads, many, size),
            low(3, rows, width), low(3, rows, width), low(3, rows, width), low(3, rows, width),
            low(seq_len, width), low(seq_len, cols), low(heads, blocks, size, size),
            full(seq_len, cols), full(seq_len, cols), full(seq_len, cols), low(seq_len, 3 * cols),
            semaphores(12), semaphores(9), semaphores(7, 2, 2), semaphores(7, 2, count),
            semaphores(flows), semaphores(flows), semaphores(4, 3, 2), semaphores(4, 3, 2),
        ],
        compiler_params=pltpu.CompilerParams(
            vmem_limit_bytes=layer_limit, collective_id=0, has_side_effects=True
        ),
        cost_estimate=pl.CostEstimate(flops=150_000_000_000, bytes_accessed=40_000_000, transcendentals=4_000_000),
        name="whole_layer",
    )(
        length, momentum, decay, step_size, inputs, cotangent, gain_attn, gain_ffn, persist_k, persist_v,
        w_query, w_key, w_value, w_out, w_gate, w_up, w_down,
    )


def finish_kernel(casts, moves, *refs):
    total = casts + moves
    sources, small = refs[:total], refs[total]
    targets, refs = refs[total + 1:2 * total + 1], refs[2 * total + 1:]
    gain_attn, gain_ffn, persist_k, persist_v, roots = refs[:5]
    held, cast, semaphores = refs[5:5 + total], refs[5 + total:5 + total + casts], refs[5 + total + casts]
    arrive = [pltpu.make_async_copy(sources[k], held[k], semaphores.at[0, k]) for k in range(total)]
    leave = [
        pltpu.make_async_copy(cast[k] if k < casts else held[k], targets[k], semaphores.at[1, k])
        for k in range(total)
    ]
    ahead = total
    for copy in arrive[:ahead]:
        copy.start()
    lines = gain_attn.shape[0]
    heads, many, size = persist_k.shape
    gain_attn[...] = small[0:lines, :]
    gain_ffn[...] = small[lines:2 * lines, :]
    stats = small[2 * lines:2 * lines + 8, :]
    stats = jnp.sqrt(stats / (stats[5:6, :] * (lines * size)))
    for k in range(5):
        roots[k] = stats[k, 0]
    for h in range(heads):
        first = 2 * lines + 8 + h * many
        persist_k[h] = small[first:first + many, :]
        persist_v[h] = small[first + heads * many:first + (heads + 1) * many, :]
    for k in range(total):
        arrive[k].wait()
        if k + ahead < total:
            arrive[k + ahead].start()
        if k < casts:
            cast[k][...] = held[k][...].astype(f32)
        leave[k].start()
    for copy in leave:
        copy.wait()


def finish(sums, rest, small, persist_shape):
    casts, moves = len(sums), len(rest)
    size = small.shape[1]
    lines = (small.shape[0] - 2 * persist_shape[0] * persist_shape[1] - 8) // 2
    anywhere = pl.BlockSpec(memory_space=pl.ANY)
    return pl.pallas_call(
        functools.partial(finish_kernel, casts, moves),
        out_shape=tuple(jax.ShapeDtypeStruct(value.shape, f32) for value in sums)
        + tuple(jax.ShapeDtypeStruct(value.shape, value.dtype) for value in rest)
        + (jax.ShapeDtypeStruct((lines, size), f32),) * 2
        + (jax.ShapeDtypeStruct(persist_shape, f32),) * 2
        + (jax.ShapeDtypeStruct((5,), f32),),
        in_specs=[anywhere] * (casts + moves) + [vmem()],
        out_specs=(anywhere,) * (casts + moves) + (vmem(),) * 4 + (smem(),),
        scratch_shapes=[pltpu.VMEM(value.shape, value.dtype) for value in (*sums, *rest)]
        + [pltpu.VMEM(value.shape, f32) for value in sums]
        + [pltpu.SemaphoreType.DMA((2, casts + moves))],
        compiler_params=pltpu.CompilerParams(vmem_limit_bytes=vmem_limit),
        name="finish",
    )(*sums, *rest, small)


pace = (0, 6, 0, (0, 1) * 8, (0, 0, 0, 0, 0, 0, 0, 1) * 2, None, 0, 3, 2, 1, 3)
layer_limit = 63 << 20


def swap(value, axis, bit):
    count = lax.axis_size(axis)
    return lax.ppermute(value, axis, [(i, i ^ bit) for i in range(count)])


def norm_back(value, scale, gain, upstream):
    weighted = upstream * gain
    return scale * weighted - value * (scale * scale * scale) * jnp.mean(
        weighted * value, axis=-1, keepdims=True
    )


def gather_rows(own):
    far = swap(own, "tensor", 2)
    near = swap(own, "tensor", 1)
    both = swap(far, "tensor", 1)
    return jnp.concatenate([own, near], 0), jnp.concatenate([far, both], 0)


def scatter_rows(near, far):
    rows = near.shape[0] // 2
    far_sum = far[:rows] + swap(far[rows:].astype(bf16), "tensor", 1).astype(f32)
    far_in = swap(far_sum.astype(bf16), "tensor", 2).astype(f32)
    near_in = swap(near[rows:].astype(bf16), "tensor", 1).astype(f32)
    return near[:rows] + near_in + far_in


def mul(left, right):
    return jnp.dot(left, right, preferred_element_type=f32)


def mul_nt(left, right):
    return jnp.einsum("ab,cb->ac", left, right, preferred_element_type=f32)


def mul_tn(left, right):
    return jnp.einsum("ab,ac->bc", left, right, preferred_element_type=f32)


def fits_ring(count, parts, *shapes):
    if count & (count - 1) or parts != 4 or count < 4:
        return False
    return all(rows % (32 * count) == 0 or (rows % 32 == 0 and cols % (128 * count) == 0) for rows, cols in shapes)


def body(
    inputs, cotangent, lengths, gain_attn, w_query, w_key, w_value, w_out, persist_keys, persist_values,
    gain_ffn, w_gate, w_up, w_down, momentum, decay, step_size,
):
    parts = lax.axis_size("tensor")
    count = lax.axis_size("dp")
    rows = inputs.shape[1]
    width = inputs.shape[2]
    half = 2 * rows
    cols = w_query.shape[1]
    size = persist_keys.shape[2]
    place = lax.axis_index("tensor")
    first_row = place * rows
    own_valid = (first_row + jnp.arange(rows, dtype=jnp.int32) < lengths[0]).astype(f32)[:, None]
    places = place.astype(jnp.int32).reshape(1)
    rates = (places, lengths, momentum[0], decay[0], step_size[0])

    if fits_ring(count, parts, (w_down.shape), (width, 3 * cols), (cols, width)):
        *sums, result, input_grad, small = whole_layer(
            lengths, momentum[0].T, decay[0].T, step_size[0].T, inputs[0], cotangent[0], gain_attn[None], gain_ffn[None], persist_keys, persist_values,
            w_query, w_key, w_value, w_out, w_gate.T, w_up.T, w_down, count, parts,
        )
        gate_sum, up_sum, down_sum, query_sum, key_sum, value_sum, out_sum, *rest = finish(
            sums, (result, input_grad), small, persist_keys.shape
        )
        result, input_grad, gain_attn_sum, gain_ffn_sum, persist_k_sum, persist_v_sum, rms_stats = rest
    else:
        resid = inputs[0].astype(f32)
        scale_attn = rows_scale(resid)
        near, far = gather_rows((resid * scale_attn * gain_attn).astype(bf16))
        w_qkv = jnp.concatenate([w_query, w_key, w_value], 1)
        qkv = jnp.concatenate([mul(near, w_qkv).astype(bf16), mul(far, w_qkv).astype(bf16)], 0)
        normed_attn = jnp.concatenate([near, far], 0)
        mixed, log_total, states, grams = attend_and_recall(*rates, qkv, persist_keys, persist_values, parts)
        branch_attn = scatter_rows(mul(mixed[:half], w_out), mul(mixed[half:], w_out))
        middle = resid + branch_attn
        scale_ffn = rows_scale(middle)
        normed_ffn = jnp.concatenate(gather_rows((middle * scale_ffn * gain_ffn).astype(bf16)), 0)

        out_grad = cotangent[0].astype(f32) * own_valid
        out_full = jnp.concatenate(gather_rows(out_grad.astype(bf16)), 0)
        gate = mul(normed_ffn, w_gate)
        up = mul(normed_ffn, w_up)
        sigmoid = jax.nn.sigmoid(gate)
        silu = gate * sigmoid
        hidden = (silu * up).astype(bf16)
        branch_ffn = scatter_rows(mul(hidden[:half], w_down), mul(hidden[half:], w_down))
        result = middle + branch_ffn
        hidden_grad = mul_nt(out_full, w_down)
        gate_grad = (hidden_grad * up * sigmoid * (1.0 + gate * (1.0 - sigmoid))).astype(bf16)
        up_grad = (hidden_grad * silu).astype(bf16)

        def masked(value_in):
            return jnp.sum(own_valid * (value_in * value_in))

        squares = jnp.stack(
            [masked(resid), masked(middle), masked(result), masked(branch_attn), masked(branch_ffn), jnp.sum(own_valid)]
        )
        grad_down = mul_tn(hidden, out_full).astype(bf16)
        grad_gate = mul_tn(gate_grad, normed_ffn).astype(bf16)
        grad_up = mul_tn(up_grad, normed_ffn).astype(bf16)
        normed_ffn_grad = scatter_rows(
            mul_nt(gate_grad[:half], w_gate) + mul_nt(up_grad[:half], w_up),
            mul_nt(gate_grad[half:], w_gate) + mul_nt(up_grad[half:], w_up),
        )
        gain_ffn_part = jnp.sum(normed_ffn_grad * middle * scale_ffn, axis=0)
        middle_grad = out_grad + norm_back(middle, scale_ffn, gain_ffn, normed_ffn_grad)
        middle_full = jnp.concatenate(gather_rows(middle_grad.astype(bf16)), 0)
        mixed_grad = mul_nt(middle_full, w_out).astype(bf16)
        qkv_grad, persist_k_grad, persist_v_grad = attend_and_recall_back(
            *rates, qkv, mixed_grad, persist_keys, persist_values, log_total, states, grams, parts
        )
        normed_attn_grad = scatter_rows(mul_nt(qkv_grad[:half], w_qkv), mul_nt(qkv_grad[half:], w_qkv))
        gain_attn_part = jnp.sum(normed_attn_grad * resid * scale_attn, axis=0)
        input_grad = (middle_grad + norm_back(resid, scale_attn, gain_attn, normed_attn_grad)).astype(bf16)
        gate_sum, up_sum, down_sum, wide, out_sum, persist_sums = lax.psum(
            (grad_gate, grad_up, grad_down, mul_tn(normed_attn, qkv_grad).astype(bf16),
             mul_tn(mixed, middle_full).astype(bf16), jnp.stack([persist_k_grad, persist_v_grad])), "dp"
        )
        query_sum, key_sum, value_sum = wide[:, :cols], wide[:, cols:2 * cols], wide[:, 2 * cols:]
        gains, squares = lax.psum((jnp.concatenate([gain_attn_part, gain_ffn_part]), squares), ("dp", "tensor"))
        gain_attn_sum, gain_ffn_sum = gains[:width], gains[width:]
        persist_k_sum, persist_v_sum = persist_sums[0], persist_sums[1]
        rms_stats = jnp.sqrt(squares[:5] / (squares[5] * width))
    return (
        result.astype(bf16)[None],
        input_grad[None],
        gain_attn_sum.reshape(-1),
        query_sum.astype(f32),
        key_sum.astype(f32),
        value_sum.astype(f32),
        out_sum.astype(f32),
        persist_k_sum,
        persist_v_sum,
        gain_ffn_sum.reshape(-1),
        gate_sum.astype(f32).T,
        up_sum.astype(f32).T,
        down_sum.astype(f32),
        rms_stats,
    )


def solution(mesh):
    in_specs = (
        P("dp", "tensor", None),
        P("dp", "tensor", None),
        P("dp"),
        P(),
        P(None, "tensor"),
        P(None, "tensor"),
        P(None, "tensor"),
        P("tensor", None),
        P("tensor", None, None),
        P("tensor", None, None),
        P(),
        P(None, "tensor"),
        P(None, "tensor"),
        P("tensor", None),
        P("dp", None, "tensor"),
        P("dp", None, "tensor"),
        P("dp", None, "tensor"),
    )
    out_specs = (
        P("dp", "tensor", None),
        P("dp", "tensor", None),
        P(),
        P(None, "tensor"),
        P(None, "tensor"),
        P(None, "tensor"),
        P("tensor", None),
        P("tensor", None, None),
        P("tensor", None, None),
        P(),
        P(None, "tensor"),
        P(None, "tensor"),
        P("tensor", None),
        P(),
    )
    return jax.shard_map(body, mesh=mesh, in_specs=in_specs, out_specs=out_specs, check_vma=False)
```

```python
import functools
import jax
import jax.numpy as jnp
from jax import lax
from jax.sharding import PartitionSpec as P
import jax.experimental.pallas as pl
import jax.experimental.pallas.tpu as pltpu

norm_eps = 1e-05
unit_eps = 1e-06
f32 = jnp.float32
bf16 = jnp.bfloat16
log2_e = 1.4426950408889634


def dot_nn(left, right):
    return lax.dot_general(left, right, (((1,), (0,)), ((), ())), preferred_element_type=f32)


def dot_nt(left, right):
    return lax.dot_general(left, right, (((1,), (1,)), ((), ())), preferred_element_type=f32)


def dot_tn(left, right):
    return lax.dot_general(left, right, (((0,), (0,)), ((), ())), preferred_element_type=f32)


def halves(value):
    high = value.astype(bf16)
    return high, (value - high.astype(f32)).astype(bf16)


def dot3(dot, left, right):
    (lh, ll), (rh, rl) = left, right
    return dot(lh, rh) + dot(ll, rh) + dot(lh, rl)


def unit_rows(value):
    wide = value.astype(f32)
    scale = lax.rsqrt(jnp.sum(wide * wide, axis=-1, keepdims=True) + unit_eps)
    return wide * scale, scale


def block_rows(start, width):
    return pl.ds(pl.multiple_of(start, width), width)


def forward_kernel(
    heads, blocks, parts,
    place, length, momentum, decay, step_size, qkv, persist_k, persist_v,
    mixed, log_total, states, grams,
    ordered, reads,
):
    seq_len, wide = qkv.shape
    size = persist_k.shape[2]
    cols = heads * size
    rows = seq_len // parts
    width = seq_len // blocks
    me = place[0]
    count = length[0]
    for b in range(parts):
        ordered[b * rows:(b + 1) * rows, :] = qkv[block_rows(jnp.bitwise_xor(me, b) * rows, rows), :]

    carried = [(jnp.zeros((size, size), f32), jnp.zeros((size, size), f32)) for _ in range(heads)]
    for c in range(blocks):
        span = slice(c * width, (c + 1) * width)
        live = (c * width + lax.broadcasted_iota(jnp.int32, (width, 1), 0) < count).astype(f32)
        for h in range(heads):
            col = h * size
            key_unit, _ = unit_rows(ordered[span, cols + col:cols + col + size])
            query_unit, _ = unit_rows(ordered[span, col:col + size])
            value = ordered[span, 2 * cols + col:2 * cols + col + size]
            key_h, key_l = halves(key_unit)
            live_h, live_l = halves(key_unit * live)
            gram = dot3(dot_tn, (live_h, live_l), (key_h, key_l))
            target = dot_tn(value, live_h) + dot_tn(value, live_l)
            memory, velocity = carried[h]
            states[h, c] = memory.astype(bf16)
            grams[h, c] = gram
            parts_m = halves(memory)
            reads[span, col:col + size] = dot_nt(query_unit.astype(bf16), parts_m[0])
            change = dot3(dot_nn, parts_m, halves(gram)) - target
            velocity = momentum[c, h] * velocity - step_size[c, h] * change
            memory = (1.0 - decay[c, h]) * memory + velocity
            carried[h] = (memory, velocity)

    factor = size ** (-0.5) * log2_e
    diagonal = lax.broadcasted_iota(jnp.int32, (rows, rows), 0) <= lax.broadcasted_iota(jnp.int32, (rows, rows), 1)
    for h in range(heads):
        col = h * size
        value_t = ordered[:, 2 * cols + col:2 * cols + col + size].T
        persist_t = persist_v[h].astype(f32).T.astype(bf16)
        for i in range(parts):
            span = slice(i * rows, (i + 1) * rows)
            seen = (i + 1) * rows
            query = ordered[span, col:col + size]
            scores = dot_nt(ordered[:seen, cols + col:cols + col + size], query)
            last = jnp.where(diagonal, scores[seen - rows:], -1e30)
            scores = last if i == 0 else jnp.concatenate([scores[:seen - rows], last], axis=0)
            extra = dot_nt(persist_k[h], query)
            top = jnp.maximum(jnp.max(scores, axis=0, keepdims=True), jnp.max(extra, axis=0, keepdims=True))
            lifted = jnp.exp2((scores - top) * factor)
            lifted_extra = jnp.exp2((extra - top) * factor)
            total = jnp.sum(lifted, axis=0, keepdims=True) + jnp.sum(lifted_extra, axis=0, keepdims=True)
            attended = dot_nn(value_t[:, :seen], lifted.astype(bf16)) + dot_nn(persist_t, lifted_extra.astype(bf16))
            attended = attended * (1.0 / total)
            log_total[h:h + 1, span] = top * factor + jnp.log2(total)
            together = attended.T + reads[span, col:col + size]
            mixed[block_rows(jnp.bitwise_xor(me, i) * rows, rows), col:col + size] = together.astype(bf16)


def backward_kernel(
    heads, blocks, parts,
    place, length, momentum, decay, step_size, qkv, mixed_grad, persist_k, persist_v,
    log_total, states, grams,
    qkv_grad, persist_k_grad, persist_v_grad,
    ordered, upstream, slopes, key_sum, value_sum, query_sum,
):
    seq_len, wide = qkv.shape
    size = persist_k.shape[2]
    cols = heads * size
    rows = seq_len // parts
    width = seq_len // blocks
    me = place[0]
    count = length[0]
    for b in range(parts):
        source = block_rows(jnp.bitwise_xor(me, b) * rows, rows)
        ordered[b * rows:(b + 1) * rows, :] = qkv[source, :]
        upstream[b * rows:(b + 1) * rows, :] = mixed_grad[source, :]

    carried = [(jnp.zeros((size, size), f32), jnp.zeros((size, size), f32)) for _ in range(heads)]
    for c in reversed(range(blocks)):
        span = slice(c * width, (c + 1) * width)
        for h in range(heads):
            col = h * size
            query_unit, _ = unit_rows(ordered[span, col:col + size])
            query_h, query_l = halves(query_unit)
            rise = upstream[span, col:col + size]
            entry = dot_tn(rise, query_h) + dot_tn(rise, query_l)
            memory, velocity = carried[h]
            velocity = velocity + memory
            change = (-step_size[c, h]) * velocity
            slopes[h, c] = change
            memory = (1.0 - decay[c, h]) * memory + entry + dot3(dot_nn, halves(change), halves(grams[h, c]))
            velocity = momentum[c, h] * velocity
            carried[h] = (memory, velocity)

    for h in range(heads):
        col = h * size
        for c in range(blocks):
            span = slice(c * width, (c + 1) * width)
            live = (c * width + lax.broadcasted_iota(jnp.int32, (width, 1), 0) < count).astype(f32)
            query_unit, query_scale = unit_rows(ordered[span, col:col + size])
            key_unit, key_scale = unit_rows(ordered[span, cols + col:cols + col + size])
            value = ordered[span, 2 * cols + col:2 * cols + col + size].astype(f32)
            rise = upstream[span, col:col + size]
            state = states[h, c]
            slope = slopes[h, c].astype(bf16)
            key_b = key_unit.astype(bf16)
            error = (dot_nt(key_b, state) - value) * live
            error_grad = dot_nt(key_b, slope) * live
            unit_grad = dot_nn(error.astype(bf16), slope) + dot_nn(error_grad.astype(bf16), state)
            key_sum[span, :] = key_scale * (unit_grad - key_unit * jnp.sum(unit_grad * key_unit, axis=-1, keepdims=True))
            value_sum[span, :] = -error_grad
            read_grad = dot_nn(rise, state)
            query_sum[span, :] = query_scale * (read_grad - query_unit * jnp.sum(read_grad * query_unit, axis=-1, keepdims=True))

        factor = size ** (-0.5)
        diagonal = lax.broadcasted_iota(jnp.int32, (rows, rows), 0) <= lax.broadcasted_iota(jnp.int32, (rows, rows), 1)
        key_t = ordered[:, cols + col:cols + col + size].T
        persist_t = persist_k[h].astype(f32).T.astype(bf16)
        persist_k_total = jnp.zeros(persist_k.shape[1:], f32)
        persist_v_total = jnp.zeros(persist_k.shape[1:], f32)
        for i in range(parts):
            span = slice(i * rows, (i + 1) * rows)
            seen = (i + 1) * rows
            query = ordered[span, col:col + size]
            rise = upstream[span, col:col + size]
            scores = dot_nt(ordered[:seen, cols + col:cols + col + size], query)
            last = jnp.where(diagonal, scores[seen - rows:], -1e30)
            scores = last if i == 0 else jnp.concatenate([scores[:seen - rows], last], axis=0)
            extra = dot_nt(persist_k[h], query)
            base = log_total[h:h + 1, span]
            probs = jnp.exp2(scores * (factor * log2_e) - base)
            probs_extra = jnp.exp2(extra * (factor * log2_e) - base)
            probs_grad = dot_nt(ordered[:seen, 2 * cols + col:2 * cols + col + size], rise)
            extra_grad = dot_nt(persist_v[h], rise)
            weighted = probs * probs_grad
            weighted_extra = probs_extra * extra_grad
            inner = jnp.sum(weighted, axis=0, keepdims=True) + jnp.sum(weighted_extra, axis=0, keepdims=True)
            scores_grad = (weighted - probs * inner).astype(bf16)
            scores_extra = (weighted_extra - probs_extra * inner).astype(bf16)
            query_t = dot_nn(key_t[:, :seen], scores_grad) + dot_nn(persist_t, scores_extra)
            query_sum[span, :] += query_t.T * factor
            key_sum[:seen, :] += dot_nn(scores_grad, query) * factor
            value_sum[:seen, :] += dot_nn(probs.astype(bf16), rise)
            persist_k_total += dot_nn(scores_extra, query) * factor
            persist_v_total += dot_nn(probs_extra.astype(bf16), rise)
        persist_k_grad[h] = persist_k_total
        persist_v_grad[h] = persist_v_total
        for b in range(parts):
            span = slice(b * rows, (b + 1) * rows)
            target = block_rows(jnp.bitwise_xor(me, b) * rows, rows)
            qkv_grad[target, col:col + size] = query_sum[span, :].astype(bf16)
            qkv_grad[target, cols + col:cols + col + size] = key_sum[span, :].astype(bf16)
            qkv_grad[target, 2 * cols + col:2 * cols + col + size] = value_sum[span, :].astype(bf16)


vmem = functools.partial(pl.BlockSpec, memory_space=pltpu.VMEM)
smem = functools.partial(pl.BlockSpec, memory_space=pltpu.SMEM)
vmem_limit = 56 << 20


def attend_and_recall(place, length, momentum, decay, step_size, qkv, persist_k, persist_v, parts):
    heads, _, size = persist_k.shape
    seq_len = qkv.shape[0]
    blocks = momentum.shape[0]
    cols = heads * size
    return pl.pallas_call(
        functools.partial(forward_kernel, heads, blocks, parts),
        out_shape=(
            jax.ShapeDtypeStruct((seq_len, cols), bf16),
            jax.ShapeDtypeStruct((heads, seq_len), f32),
            jax.ShapeDtypeStruct((heads, blocks, size, size), bf16),
            jax.ShapeDtypeStruct((heads, blocks, size, size), f32),
        ),
        in_specs=[smem()] * 5 + [vmem()] * 3,
        out_specs=(vmem(),) * 4,
        scratch_shapes=[pltpu.VMEM((seq_len, 3 * cols), bf16), pltpu.VMEM((seq_len, cols), f32)],
        compiler_params=pltpu.CompilerParams(vmem_limit_bytes=vmem_limit),
        cost_estimate=pl.CostEstimate(flops=12_000_000_000, bytes_accessed=8_000_000, transcendentals=2_000_000),
        name="attend_recall",
    )(place, length, momentum, decay, step_size, qkv, persist_k, persist_v)


def attend_and_recall_back(
    place, length, momentum, decay, step_size, qkv, mixed_grad, persist_k, persist_v, log_total, states, grams, parts
):
    heads, persistent, size = persist_k.shape
    seq_len = qkv.shape[0]
    blocks = momentum.shape[0]
    cols = heads * size
    return pl.pallas_call(
        functools.partial(backward_kernel, heads, blocks, parts),
        out_shape=(
            jax.ShapeDtypeStruct((seq_len, 3 * cols), bf16),
            jax.ShapeDtypeStruct((heads, persistent, size), f32),
            jax.ShapeDtypeStruct((heads, persistent, size), f32),
        ),
        in_specs=[smem()] * 5 + [vmem()] * 7,
        out_specs=(vmem(),) * 3,
        scratch_shapes=[
            pltpu.VMEM((seq_len, 3 * cols), bf16),
            pltpu.VMEM((seq_len, cols), bf16),
            pltpu.VMEM((heads, blocks, size, size), f32),
            pltpu.VMEM((seq_len, size), f32),
            pltpu.VMEM((seq_len, size), f32),
            pltpu.VMEM((seq_len, size), f32),
        ],
        compiler_params=pltpu.CompilerParams(vmem_limit_bytes=vmem_limit),
        cost_estimate=pl.CostEstimate(flops=25_000_000_000, bytes_accessed=12_000_000, transcendentals=2_000_000),
        name="attend_recall_back",
    )(place, length, momentum, decay, step_size, qkv, mixed_grad, persist_k, persist_v, log_total, states, grams)


def ring_place(index, count):
    odd = index % 2
    return (1 - odd) * (index // 2) + odd * (count - 1 - index // 2)


def ring_index(place, count):
    late = place // (count // 2)
    return (1 - late) * (2 * place) + late * (2 * (count - 1 - place) + 1)


def flip(index, bit):
    return index + bit * (1 - 2 * ((index // bit) % 2))


def bits_below(count):
    return [1 << k for k in range(count.bit_length() - 1)]


def relative(index, block):
    for bit in (1, 2):
        if block & bit:
            index = flip(index, bit)
    return index


def remote(source, target, send_sem, recv_sem, device):
    return pltpu.make_async_remote_copy(
        src_ref=source, dst_ref=target, send_sem=send_sem, recv_sem=recv_sem,
        device_id=device, device_id_type=pl.DeviceIdType.MESH,
    )


class Ring:
    def __init__(self, count, by_rows, source, out, slots, send_sem, recv_sem, home, home_sem):
        self.homeward = pltpu.make_async_copy(out, home, home_sem)
        self.count, self.by_rows = count, by_rows
        self.source, self.out, self.slots = source, out, slots
        self.send_sem, self.recv_sem = send_sem, recv_sem
        index = lax.axis_index("dp")
        self.place = ring_place(index, count)
        self.peers = (
            {"dp": ring_index((self.place + 1) % count, count)},
            {"dp": ring_index((self.place + count - 1) % count, count)},
        )
        self.step = 0
        self.copies = [None, None]
        self.sent = [[], []]

    def piece(self, ref, way, chunk):
        rows, cols = ref.shape
        chunk = chunk % self.count
        if self.by_rows:
            size = rows // (2 * self.count)
            return ref.at[pl.ds(pl.multiple_of(chunk * (2 * size) + way * size, size), size), :]
        size, width = rows // 2, cols // self.count
        return ref.at[way * size:(way + 1) * size, pl.ds(pl.multiple_of(chunk * width, width), width)]

    def chunk(self, way, step):
        return self.place + self.count + (2 * self.count - step if way == 0 else step)

    def launch(self, way, step, source, target):
        copy = remote(source, target, self.send_sem.at[way, step % 2], self.recv_sem.at[way, step % self.count], self.peers[way])
        if step > 1:
            self.sent[way].pop(0).wait_send()
        copy.start()
        self.copies[way] = copy
        self.sent[way].append(copy)

    def start_way(self, way):
        self.launch(way, 0, self.piece(self.source, way, self.chunk(way, 0)), self.slots.at[way, 0])

    def start(self):
        for way in range(2):
            self.start_way(way)

    def advance(self):
        count, step = self.count, self.step
        for way in range(2):
            self.copies[way].wait_recv()
            if step < count - 1:
                chunk = self.chunk(way, step + 1)
                total = self.slots[way, step].astype(f32) + self.piece(self.source, way, chunk)[...].astype(f32)
                if step < count - 2:
                    self.slots[way, step] = total.astype(bf16)
                    source, target = self.slots.at[way, step], self.slots.at[way, step + 1]
                else:
                    source = target = self.piece(self.out, way, chunk)
                    source[...] = total.astype(bf16)
            else:
                source = target = self.piece(self.out, way, self.chunk(way, step + 1 - count))
            if step < 2 * count - 3:
                self.launch(way, step + 1, source, target)
        self.step += 1
        if self.step < 2 * count - 2:
            return True
        for copy in self.sent[0] + self.sent[1]:
            copy.wait_send()
        self.homeward.start()
        return False

    def left(self):
        return 2 * self.count - 2 - self.step


class SmallSum:
    def __init__(self, value, slots, shared, send_sem, recv_sem, count, parts):
        self.value, self.slots, self.shared = value, slots, shared
        self.send_sem, self.recv_sem = send_sem, recv_sem
        index, inner = lax.axis_index("dp"), lax.axis_index("tensor")
        self.inner = len(bits_below(parts))
        self.peers = [{"tensor": flip(inner, bit)} for bit in bits_below(parts)]
        self.peers += [{"dp": flip(index, bit)} for bit in bits_below(count)]
        self.step = 0

    def start(self):
        used = slice(0, self.shared if self.step < self.inner else self.value.shape[0])
        self.used = used
        self.copy = remote(
            self.value.at[used], self.slots.at[self.step, used], self.send_sem.at[self.step],
            self.recv_sem.at[self.step], self.peers[self.step],
        )
        self.copy.start()

    def left(self):
        return len(self.peers) - self.step

    def advance(self):
        self.copy.wait()
        self.value[self.used] += self.slots[self.step, self.used]
        self.step += 1
        if self.step < len(self.peers):
            self.start()
        return self.step < len(self.peers)


class Rounds:
    def __init__(self):
        self.queue = []

    def add(self, *flows):
        for flow in flows:
            flow.start()
            self.queue.append(flow)

    def spread(self, fast, slow):
        fast = [flow for flow in fast if flow in self.queue]
        slow = [flow for flow in slow if flow in self.queue]
        counts = {flow: flow.left() for flow in fast + slow}
        rest = [flow for k in range(max([counts[flow] for flow in slow], default=0)) for flow in slow if k < counts[flow]]
        turns = max(counts[flow] for flow in fast)
        self.queue = []
        for k in range(turns):
            self.queue += [flow for flow in fast if k < counts[flow]]
            self.queue += rest[k * len(rest) // turns:(k + 1) * len(rest) // turns]

    def mix(self, flow):
        for k in range(flow.left()):
            self.queue.insert(min(6 * k + 4, len(self.queue)), flow)

    def tick(self, count=1):
        for _ in range(count):
            if self.queue:
                flow = self.queue.pop(0)
                if flow.advance() and flow not in self.queue:
                    self.queue.append(flow)

    def finish(self):
        while self.queue:
            self.tick()


def rows_scale(value):
    return lax.rsqrt(jnp.mean(value * value, axis=-1, keepdims=True) + norm_eps)


class Scatter:
    def __init__(self, sent, landed, hold, send_sem, recv_sem):
        self.sent, self.landed, self.hold = sent, landed, hold
        self.send_sem, self.recv_sem = send_sem, recv_sem
        self.rows = hold.shape[0] // 2
        inner = lax.axis_index("tensor")
        self.sibling, self.across = {"tensor": flip(inner, 1)}, {"tensor": flip(inner, 2)}

    def span(self, j):
        return slice(j * self.rows, (j + 1) * self.rows)

    def copy(self, k, j, device):
        return remote(
            self.sent.at[k, self.span(j)], self.landed.at[k, self.span(j)],
            self.send_sem.at[k, j], self.recv_sem.at[k, j], device,
        )

    def begin(self, block, tick):
        first = [self.copy(0, j, self.sibling) for j in range(2)]
        self.second = [self.copy(1, j, self.across) for j in range(2)]
        self.third = [self.copy(2, j, self.sibling) for j in range(2)]
        for j in range(2):
            self.sent[0, self.span(j)] = block(3, j).astype(bf16)
            first[j].start()
        for j in range(2):
            self.hold[self.span(j), :] = block(2, j)
        tick()
        for j in range(2):
            first[j].wait()
            self.sent[1, self.span(j)] = (
                self.hold[self.span(j), :] + self.landed[0, self.span(j)].astype(f32)
            ).astype(bf16)
            self.second[j].start()
        for j in range(2):
            self.sent[2, self.span(j)] = block(1, j).astype(bf16)
            self.third[j].start()
        tick()
        for j in range(2):
            self.hold[self.span(j), :] = block(0, j)

    def finish(self, j):
        span = self.span(j)
        self.third[j].wait()
        self.second[j].wait()
        return self.hold[span, :] + self.landed[2, span].astype(f32) + self.landed[1, span].astype(f32)


class Gather:
    def __init__(self, full, parts, send_sem, recv_sem):
        self.full, self.rows = full, full.shape[0] // (2 * parts)
        self.send_sem, self.recv_sem = send_sem, recv_sem
        inner = lax.axis_index("tensor")
        self.sibling, self.across = {"tensor": flip(inner, 1)}, {"tensor": flip(inner, 2)}
        self.far, self.near, self.both = [None] * 2, [None] * 2, [None] * 2

    def copy(self, source, target, k, j, device):
        def piece(b):
            first = (2 * b + j) * self.rows
            return self.full.at[first:first + self.rows, :]

        return remote(piece(source), piece(target), self.send_sem.at[k, j], self.recv_sem.at[k, j], device)

    def begin(self, j):
        self.far[j], self.near[j] = self.copy(0, 2, 0, j, self.across), self.copy(0, 1, 1, j, self.sibling)
        self.far[j].start()
        self.near[j].start()

    def forward(self, then=lambda j: None):
        for j in range(2):
            self.far[j].wait()
            then(j)
            self.both[j] = self.copy(2, 3, 2, j, self.sibling)
            self.both[j].start()

    def wait(self, copies):
        for copy in copies:
            copy.wait()


def dot_pair(high, low, right):
    return dot_nn(jnp.concatenate([high, low], axis=1), jnp.concatenate([right, right], axis=0))


def layer_kernel(
    heads, blocks, parts, count, shared, pace,
    length, momentum, decay, step_size,
    inputs_h, cotangent_h, gain_attn_h, gain_ffn_h, persist_k_h, persist_v_h,
    w_query_h, w_key_h, w_value_h, w_out_h, w_gate_h, w_up_h, w_down_h,
    gate_home, up_home, down_home, query_home, key_home, value_home, out_home, result_home, input_grad_home, small,
    w_qkv, w_out, w_gate, w_up, w_down,
    normed_attn, ordered, mixed, states, grams, log_total,
    middle, hold, middle_grad, normed_ffn, out_full, gate_grad, up_grad, hidden,
    gate_source, up_source, down_source, query_source, key_source, value_source, out_source,
    gate_slots, up_slots, down_slots, query_slots, key_slots, value_slots, out_slots, small_slots,
    gate_out, up_out, down_out, query_out, key_out, value_out, out_out, result, input_grad,
    inputs, cotangent, gain_attn, gain_ffn, persist_k, persist_v, sent_a, landed_a, sent_b, landed_b, middle_full, upstream, slopes, key_sum, value_sum, query_sum, qkv_grad,
    load_sem, home_sem, ring_send, ring_recv, small_send, small_recv, move_send, move_recv,
):
    size = persist_k.shape[2]
    many = persist_k.shape[1]
    cols = heads * size
    seq_len, width = middle_full.shape
    units = gate_grad.shape[0]
    rows = seq_len // parts
    span_rows = seq_len // blocks
    inner = lax.axis_index("tensor")
    valid_count = length[0]
    factor = size ** (-0.5)

    rounds = Rounds()
    rings = [
        Ring(count, by_rows, source, out, slots, ring_send.at[k], ring_recv.at[k], home, home_sem.at[k])
        for k, (by_rows, source, out, slots, home) in enumerate((
            (False, down_source, down_out, down_slots, down_home),
            (False, gate_source, gate_out, gate_slots, gate_home),
            (False, up_source, up_out, up_slots, up_home),
            (False, out_source, out_out, out_slots, out_home),
            (True, query_source, query_out, query_slots, query_home),
            (True, key_source, key_out, key_slots, key_home),
            (True, value_source, value_out, value_slots, value_home),
        ))
    ]
    small_sum = SmallSum(small, small_slots, shared, small_send, small_recv, count, parts)
    barrier = pltpu.get_barrier_semaphore()
    peers = list(rings[0].peers) + small_sum.peers
    for peer in peers:
        pl.semaphore_signal(barrier, inc=1, device_id=peer, device_id_type=pl.DeviceIdType.MESH)

    loads = []

    def load(source, target):
        copy = pltpu.make_async_copy(source, target, load_sem.at[len(loads)])
        copy.start()
        loads.append(copy)
        return copy

    input_load, cotangent_load = load(inputs_h, inputs), load(cotangent_h, cotangent)
    gain_load = load(gain_attn_h, gain_attn)
    qkv_loads = [
        load(source, w_qkv.at[:, k * cols:(k + 1) * cols]) for k, source in enumerate((w_query_h, w_key_h, w_value_h))
    ]
    persist_loads = [load(persist_k_h, persist_k), load(persist_v_h, persist_v), load(gain_ffn_h, gain_ffn)]
    out_load = load(w_out_h, w_out)
    ffn_loads = [load(w_gate_h, w_gate), load(w_up_h, w_up), load(w_down_h, w_down)]

    def true_rows(b):
        return pl.ds(pl.multiple_of(relative(inner, b) * rows, rows), rows)

    def block_of(b):
        return slice(b * rows, (b + 1) * rows)

    row_place = inner * rows + lax.broadcasted_iota(jnp.int32, (rows, 1), 0)
    own_valid = (row_place < valid_count).astype(f32)
    stat_row = 2 * width // size

    def half_rows(j):
        return slice(j * (rows // 2), (j + 1) * (rows // 2))

    def part_of(b, j):
        return slice((2 * b + j) * (rows // 2), (2 * b + j + 1) * (rows // 2))

    def note(k, value, j):
        total = jnp.sum(jnp.sum(value, axis=1, keepdims=True) * own_valid[half_rows(j)], axis=0, keepdims=True)
        small[stat_row + k:stat_row + k + 1, :] += jnp.broadcast_to(total, (1, size))

    gather_attn = Gather(normed_attn, parts, move_send.at[0], move_recv.at[0])
    small[stat_row:stat_row + 8, :] = jnp.zeros((8, size), f32)

    def attn_norm(j):
        resid = inputs[half_rows(j), :].astype(f32)
        normed_attn[half_rows(j), :] = (resid * rows_scale(resid) * gain_attn[...]).astype(bf16)
        note(0, resid * resid, j)

    input_load.wait()
    gain_load.wait()
    attn_norm(0)
    pl.semaphore_wait(barrier, len(peers))
    gather_attn.begin(0)
    attn_norm(1)
    gather_attn.begin(1)
    cotangent_load.wait()
    out_full[0:rows, :] = (cotangent[...].astype(f32) * own_valid).astype(bf16)
    for j in range(2):
        note(5, jnp.ones((rows // 2, 1), f32), j)
    for copy in qkv_loads:
        copy.wait()

    def qkv_block(b):
        made = dot_nn(normed_attn[block_of(b), :], w_qkv[...])
        ordered[true_rows(b), :] = made.astype(bf16)
        first = relative(inner, b) * (rows // span_rows)
        place = lax.broadcasted_iota(jnp.int32, (rows, 1), 0)
        live = (relative(inner, b) * rows + place < valid_count).astype(f32)
        for h in range(heads):
            col = h * size
            key_unit, _ = unit_rows(made[:, cols + col:cols + col + size].astype(bf16))
            value = made[:, 2 * cols + col:2 * cols + col + size].astype(bf16)
            live_unit = (key_unit * live).astype(bf16)
            empty = jnp.zeros((span_rows, size), bf16)
            spread = jnp.concatenate([
                jnp.concatenate([
                    live_unit[k * span_rows:(k + 1) * span_rows] if k == m else empty for m in range(rows // span_rows)
                ], axis=1) for k in range(rows // span_rows)
            ], axis=0)
            both = dot_nn(jnp.concatenate([value, key_unit.astype(bf16)], axis=1).T, spread).astype(bf16)
            for k in range(rows // span_rows):
                slopes[h, first + k] = both[:size, k * size:(k + 1) * size]
                grams[h, first + k] = both[size:, k * size:(k + 1) * size]

    qkv_block(0)
    gather_attn.wait(gather_attn.near)
    qkv_block(1)
    gather_cot = Gather(out_full, parts, move_send.at[1], move_recv.at[1])
    gather_attn.forward(gather_cot.begin)
    qkv_block(2)
    gather_attn.wait(gather_attn.both)
    qkv_block(3)

    for copy in persist_loads:
        copy.wait()
    diagonal = lax.broadcasted_iota(jnp.int32, (rows, rows), 0) <= lax.broadcasted_iota(jnp.int32, (rows, rows), 1)
    tiles = [(h, i) for i in range(parts) for h in range(heads)]

    def masked_scores(h, i, query):
        seen = (i + 1) * rows
        scores = dot_nt(ordered[:seen, cols + h * size:cols + (h + 1) * size], query)
        last = jnp.where(diagonal, scores[seen - rows:], -1e30)
        return last if i == 0 else jnp.concatenate([scores[:seen - rows], last], axis=0)

    value_t = [ordered[:, 2 * cols + h * size:2 * cols + (h + 1) * size].T for h in range(heads)]
    persist_t = [persist_v[h].astype(f32).T.astype(bf16) for h in range(heads)]

    def attend(h, i):
        seen, col = (i + 1) * rows, h * size
        query = ordered[block_of(i), col:col + size]
        scores = masked_scores(h, i, query)
        extra = dot_nt(persist_k[h], query)
        top = jnp.maximum(jnp.max(scores, axis=0, keepdims=True), jnp.max(extra, axis=0, keepdims=True))
        lifted = jnp.exp2((scores - top) * (factor * log2_e))
        lifted_extra = jnp.exp2((extra - top) * (factor * log2_e))
        total = jnp.sum(lifted, axis=0, keepdims=True) + jnp.sum(lifted_extra, axis=0, keepdims=True)
        attended = dot_nn(value_t[h][:, :seen], lifted.astype(bf16)) + dot_nn(persist_t[h], lifted_extra.astype(bf16))
        log_total[h:h + 1, block_of(i)] = top * (factor * log2_e) + jnp.log2(total)
        query_sum[block_of(i), col:col + size] = (attended * (1.0 / total)).T

    carried = [(jnp.zeros((size, size), f32), jnp.zeros((size, size), f32)) for _ in range(heads)]
    for c in range(blocks):
        for h in range(heads):
            memory, velocity = carried[h]
            high, low_part = halves(memory)
            states[h, c] = high
            change = dot_pair(high, low_part, grams[h, c]) - slopes[h, c].astype(f32)
            velocity = momentum[h, c] * velocity - step_size[h, c] * change
            memory = (1.0 - decay[h, c]) * memory + velocity
            carried[h] = (memory, velocity)
        for h, i in tiles[c * len(tiles) // blocks:(c + 1) * len(tiles) // blocks]:
            attend(h, i)
    def mix(b):
        span, first = true_rows(b), relative(inner, b) * (rows // span_rows)
        for h in range(heads):
            wide = slice(h * size, (h + 1) * size)
            query_unit = unit_rows(ordered[span, wide])[0].astype(bf16)
            reads = [
                dot_nt(query_unit[k * span_rows:(k + 1) * span_rows], states[h, first + k])
                for k in range(rows // span_rows)
            ]
            mixed[block_of(b), wide] = (query_sum[span, wide] + jnp.concatenate(reads, axis=0)).astype(bf16)

    def project(b, j):
        if j == 0:
            mix(b)
        return dot_nn(mixed[part_of(b, j), :], w_out[...])

    out_load.wait()
    scatter = Scatter(sent_a, landed_a, hold, move_send.at[2], move_recv.at[2])
    scatter.begin(project, rounds.tick)
    gather_cot.wait(gather_cot.near)
    gather_cot.forward()
    gather_ffn = Gather(normed_ffn, parts, move_send.at[0], move_recv.at[0])
    for j in range(2):
        branch = scatter.finish(j)
        value = inputs[half_rows(j), :].astype(f32) + branch
        middle[half_rows(j), :] = value
        normed_ffn[half_rows(j), :] = (value * rows_scale(value) * gain_ffn[...]).astype(bf16)
        gather_ffn.begin(j)
        note(3, branch * branch, j)
        note(1, value * value, j)
    for copy in ffn_loads:
        copy.wait()
    gather_cot.wait(gather_cot.both)
    gather_ffn.wait(gather_ffn.near)

    piece = units // 4

    def feed(tokens):
        for k in range(4):
            span = slice(k * piece, (k + 1) * piece)
            gate = dot_nt(w_gate[span, :], normed_ffn[tokens, :])
            up = dot_nt(w_up[span, :], normed_ffn[tokens, :])
            hidden_grad = dot_nt(w_down[span, :], out_full[tokens, :])
            sigmoid = jax.nn.sigmoid(gate)
            silu = gate * sigmoid
            hidden[span, tokens] = (silu * up).astype(bf16)
            up_grad[span, tokens] = (hidden_grad * silu).astype(bf16)
            gate_grad[span, tokens] = (hidden_grad * up * sigmoid * (1.0 + gate * (1.0 - sigmoid))).astype(bf16)

    feed(slice(0, 2 * rows))
    gather_ffn.forward()
    feed(block_of(2))
    gather_ffn.wait(gather_ffn.both)
    feed(block_of(3))
    for source, left, right, ring in (
        (down_source, hidden, out_full, rings[0]), (gate_source, gate_grad, normed_ffn, rings[1]),
        (up_source, up_grad, normed_ffn, rings[2]),
    ):
        for way in range(2):
            span = slice(way * (units // 2), (way + 1) * (units // 2))
            source[span, :] = dot_nn(left[span, :], right[...]).astype(bf16)
            ring.start_way(way)
        rounds.queue.append(ring)

    scatter = Scatter(sent_b, landed_b, hold, move_send.at[3], move_recv.at[3])
    scatter.begin(
        lambda b, j: dot_tn(gate_grad[:, part_of(b, j)], w_gate[...]) + dot_tn(up_grad[:, part_of(b, j)], w_up[...]),
        rounds.tick,
    )
    rounds.tick(pace[0])
    for b in range(parts):
        normed_ffn[:, block_of(b)] = normed_attn[block_of(b), :].T
        rounds.tick(pace[9])
    gather_middle = Gather(middle_full, parts, move_send.at[1], move_recv.at[1])
    gain_row = jnp.zeros((1, width), f32)
    for j in range(2):
        normed_grad = scatter.finish(j)
        value = middle[half_rows(j), :]
        scale = rows_scale(value)
        weighted = normed_grad * gain_ffn[...]
        grad = (
            cotangent[half_rows(j), :].astype(f32) * own_valid[half_rows(j)] + scale * weighted
            - value * (scale * scale * scale) * jnp.mean(weighted * value, axis=-1, keepdims=True)
        )
        middle_grad[half_rows(j), :] = grad
        middle_full[half_rows(j), :] = grad.astype(bf16)
        gather_middle.begin(j)
        gain_row = gain_row + jnp.sum(normed_grad * value * scale, axis=0, keepdims=True)
        if j == 0:
            rounds.tick(pace[8])
    for k in range(width // size):
        small[width // size + k:width // size + k + 1, :] = gain_row[:, k * size:(k + 1) * size]
    rounds.tick(pace[1])
    gather_middle.wait(gather_middle.near)

    def mixed_block(b):
        upstream[true_rows(b), :] = dot_nt(middle_full[block_of(b), :], w_out[...]).astype(bf16)

    mixed_block(0)
    mixed_block(1)
    gather_middle.forward()
    mixed_block(2)
    gather_middle.wait(gather_middle.both)
    mixed_block(3)
    scatter = Scatter(sent_a, landed_a, hold, move_send.at[2], move_recv.at[2])
    scatter.begin(lambda b, j: dot_tn(hidden[:, part_of(b, j)], w_down[...]), rounds.tick)
    rounds.tick(pace[2])
    out_source[...] = dot_tn(mixed[...], middle_full[...]).astype(bf16)
    rounds.add(rings[3])

    key_t = [ordered[:, cols + h * size:cols + (h + 1) * size].T for h in range(heads)]
    persist_t = [persist_k[h].astype(f32).T.astype(bf16) for h in range(heads)]
    persist_sums = [[jnp.zeros((many, size), f32), jnp.zeros((many, size), f32)] for _ in range(heads)]

    def attend_back(h, i):
        span, seen, col = block_of(i), (i + 1) * rows, h * size
        wide = slice(col, col + size)
        query = ordered[span, wide]
        rise = upstream[span, wide]
        scores = masked_scores(h, i, query)
        extra = dot_nt(persist_k[h], query)
        base = log_total[h:h + 1, span]
        probs = jnp.exp2(scores * (factor * log2_e) - base)
        probs_extra = jnp.exp2(extra * (factor * log2_e) - base)
        probs_grad = dot_nt(ordered[:seen, 2 * cols + col:2 * cols + col + size], rise)
        extra_grad = dot_nt(persist_v[h], rise)
        weighted = probs * probs_grad
        weighted_extra = probs_extra * extra_grad
        inner_sum = jnp.sum(weighted, axis=0, keepdims=True) + jnp.sum(weighted_extra, axis=0, keepdims=True)
        scores_grad = (weighted - probs * inner_sum).astype(bf16)
        scores_extra = (weighted_extra - probs_extra * inner_sum).astype(bf16)
        query_t = dot_nn(key_t[h][:, :seen], scores_grad) + dot_nn(persist_t[h], scores_extra)
        query_sum[span, wide] = query_t.T * factor
        key_part = dot_nn(scores_grad, query) * factor
        value_part = dot_nn(probs.astype(bf16), rise)
        for ref, part in ((key_sum, key_part), (value_sum, value_part)):
            ref[span, wide] = part[seen - rows:]
            if i:
                ref[:seen - rows, wide] += part[:seen - rows]
        persist_sums[h][0] += dot_nn(scores_extra, query) * factor
        persist_sums[h][1] += dot_nn(probs_extra.astype(bf16), rise)

    carried = [(jnp.zeros((size, size), f32), jnp.zeros((size, size), f32)) for _ in range(heads)]
    for c in reversed(range(blocks)):
        span = slice(c * span_rows, (c + 1) * span_rows)
        for h in range(heads):
            col = h * size
            query_unit, _ = unit_rows(ordered[span, col:col + size])
            rise = upstream[span, col:col + size]
            entry = dot_tn(rise, query_unit.astype(bf16))
            memory, velocity = carried[h]
            velocity = velocity + memory
            change = (-step_size[h, c]) * velocity
            slopes[h, c] = change.astype(bf16)
            memory = (1.0 - decay[h, c]) * memory + entry + dot_pair(*halves(change), grams[h, c])
            velocity = momentum[h, c] * velocity
            carried[h] = (memory, velocity)
        done = blocks - 1 - c
        for h, i in tiles[done * len(tiles) // blocks:(done + 1) * len(tiles) // blocks]:
            attend_back(h, i)
        rounds.tick(pace[3][done])

    for h in range(heads):
        col = h * size
        wide = slice(col, col + size)
        for c in range(blocks):
            span = slice(c * span_rows, (c + 1) * span_rows)
            live = (c * span_rows + lax.broadcasted_iota(jnp.int32, (span_rows, 1), 0) < valid_count).astype(f32)
            query_unit, query_scale = unit_rows(ordered[span, wide])
            key_unit, key_scale = unit_rows(ordered[span, cols + col:cols + col + size])
            value = ordered[span, 2 * cols + col:2 * cols + col + size].astype(f32)
            rise = upstream[span, wide]
            state = states[h, c]
            slope = slopes[h, c]
            error = (dot_nt(key_unit.astype(bf16), state) - value) * live
            error_grad = dot_nt(key_unit.astype(bf16), slope) * live
            unit_grad = dot_nn(error.astype(bf16), slope) + dot_nn(error_grad.astype(bf16), state)
            key_sum[span, wide] += key_scale * (
                unit_grad - key_unit * jnp.sum(unit_grad * key_unit, axis=-1, keepdims=True)
            )
            value_sum[span, wide] -= error_grad
            read_grad = dot_nn(rise, state)
            query_sum[span, wide] += query_scale * (
                read_grad - query_unit * jnp.sum(read_grad * query_unit, axis=-1, keepdims=True)
            )
            rounds.tick(pace[4][c])
        small[shared + h * many:shared + (h + 1) * many, :] = persist_sums[h][0]
        small[shared + (heads + h) * many:shared + (heads + h + 1) * many, :] = persist_sums[h][1]
    for b in range(parts):
        target = true_rows(b)
        qkv_grad[target, 0:cols] = query_sum[block_of(b), :].astype(bf16)
        qkv_grad[target, cols:2 * cols] = key_sum[block_of(b), :].astype(bf16)
        qkv_grad[target, 2 * cols:3 * cols] = value_sum[block_of(b), :].astype(bf16)

    for j in range(2):
        branch = scatter.finish(j)
        note(4, branch * branch, j)
        value = middle[half_rows(j), :] + branch
        note(2, value * value, j)
        result[half_rows(j), :] = value.astype(bf16)
    homes = [pltpu.make_async_copy(result, result_home, home_sem.at[len(rings)])]
    homes[0].start()

    for b in range(parts):
        span = block_of(b)
        grad = dot_nn(normed_ffn[span, :], qkv_grad[...])
        for k, source in enumerate((query_source, key_source, value_source)):
            source[span, :] = grad[:, k * cols:(k + 1) * cols].astype(bf16)
        rounds.tick(pace[6])
    rounds.add(*rings[4:])
    rounds.spread(rings[3:], rings[:3])
    scatter = Scatter(sent_b, landed_b, hold, move_send.at[3], move_recv.at[3])
    scatter.begin(lambda b, j: dot_nt(qkv_grad[part_of(b, j), :], w_qkv[...]), lambda: rounds.tick(pace[10]))
    for b in range(parts):
        span = block_of(b)
        products = sum(
            source[span, :].astype(f32) * w_qkv[span, k * cols:(k + 1) * cols].astype(f32)
            for k, source in enumerate((query_source, key_source, value_source))
        )
        gain_row = jnp.sum(products.T, axis=0, keepdims=True) / gain_attn[:, span]
        for k in range(rows // size):
            row = b * (rows // size) + k
            small[row:row + 1, :] = gain_row[:, k * size:(k + 1) * size]
        rounds.tick(pace[7])
    small_sum.start()
    rounds.mix(small_sum)
    for j in range(2):
        normed_grad = scatter.finish(j)
        value = inputs[half_rows(j), :].astype(f32)
        scale = rows_scale(value)
        weighted = normed_grad * gain_attn[...]
        input_grad[half_rows(j), :] = (
            middle_grad[half_rows(j), :] + scale * weighted
            - value * (scale * scale * scale) * jnp.mean(weighted * value, axis=-1, keepdims=True)
        ).astype(bf16)
    homes.append(pltpu.make_async_copy(input_grad, input_grad_home, home_sem.at[len(rings) + 1]))
    homes[1].start()
    rounds.finish()
    for copy in homes + [ring.homeward for ring in rings]:
        copy.wait()


def whole_layer(
    length, momentum, decay, step_size, inputs, cotangent, gain_attn, gain_ffn, persist_k, persist_v,
    w_query, w_key, w_value, w_out, w_gate, w_up, w_down, count, parts,
):
    heads, many, size = persist_k.shape
    blocks = momentum.shape[1]
    cols = heads * size
    rows, width = inputs.shape
    seq_len = rows * parts
    units = w_gate.shape[0]
    shared = 2 * width // size + 8
    small_rows = shared + 2 * heads * many
    flows = len(bits_below(count)) + len(bits_below(parts))

    def row_slots(*shape):
        return pltpu.VMEM((2, count - 1, shape[0] // (2 * count), shape[1]), bf16)

    def col_slots(*shape):
        return pltpu.VMEM((2, count - 1, shape[0] // 2, shape[1] // count), bf16)

    def low(*shape):
        return pltpu.VMEM(shape, bf16)

    def full(*shape):
        return pltpu.VMEM(shape, f32)

    def semaphores(*shape):
        return pltpu.SemaphoreType.DMA(shape)

    ffn = (units, width)
    return pl.pallas_call(
        functools.partial(layer_kernel, heads, blocks, parts, count, shared, pace),
        out_shape=(
            jax.ShapeDtypeStruct(ffn, bf16),
            jax.ShapeDtypeStruct(ffn, bf16),
            jax.ShapeDtypeStruct(ffn, bf16),
            jax.ShapeDtypeStruct((width, cols), bf16),
            jax.ShapeDtypeStruct((width, cols), bf16),
            jax.ShapeDtypeStruct((width, cols), bf16),
            jax.ShapeDtypeStruct((cols, width), bf16),
            jax.ShapeDtypeStruct((rows, width), bf16),
            jax.ShapeDtypeStruct((rows, width), bf16),
            jax.ShapeDtypeStruct((small_rows, size), f32),
        ),
        in_specs=[smem()] * 4 + [pl.BlockSpec(memory_space=pl.ANY)] * 13,
        out_specs=(pl.BlockSpec(memory_space=pl.ANY),) * 9 + (vmem(),),
        scratch_shapes=[
            low(width, 3 * cols), low(cols, width), low(*ffn), low(*ffn), low(*ffn),
            low(seq_len, width), low(seq_len, 3 * cols), low(seq_len, cols),
            low(heads, blocks, size, size), low(heads, blocks, size, size), full(heads, seq_len),
            full(rows, width), full(rows, width), full(rows, width), low(seq_len, width), low(seq_len, width),
            low(units, seq_len), low(units, seq_len), low(units, seq_len),
            low(*ffn), low(*ffn), low(*ffn), low(width, cols), low(width, cols), low(width, cols), low(cols, width),
            col_slots(*ffn), col_slots(*ffn), col_slots(*ffn),
            row_slots(width, cols), row_slots(width, cols), row_slots(width, cols), col_slots(cols, width),
            full(flows, small_rows, size),
            low(*ffn), low(*ffn), low(*ffn), low(width, cols), low(width, cols), low(width, cols), low(cols, width),
            low(rows, width), low(rows, width), low(rows, width), low(rows, width),
            full(1, width), full(1, width), low(heads, many, size), low(heads, many, size),
            low(3, rows, width), low(3, rows, width), low(3, rows, width), low(3, rows, width),
            low(seq_len, width), low(seq_len, cols), low(heads, blocks, size, size),
            full(seq_len, cols), full(seq_len, cols), full(seq_len, cols), low(seq_len, 3 * cols),
            semaphores(13), semaphores(9), semaphores(7, 2, 2), semaphores(7, 2, count),
            semaphores(flows), semaphores(flows), semaphores(4, 3, 2), semaphores(4, 3, 2),
        ],
        compiler_params=pltpu.CompilerParams(
            vmem_limit_bytes=layer_limit, collective_id=0, has_side_effects=True
        ),
        cost_estimate=pl.CostEstimate(flops=150_000_000_000, bytes_accessed=40_000_000, transcendentals=4_000_000),
        name="whole_layer",
    )(
        length, momentum, decay, step_size, inputs, cotangent, gain_attn, gain_ffn, persist_k, persist_v,
        w_query, w_key, w_value, w_out, w_gate, w_up, w_down,
    )


def finish_kernel(casts, moves, *refs):
    total = casts + moves
    sources, small = refs[:total], refs[total]
    targets, refs = refs[total + 1:2 * total + 1], refs[2 * total + 1:]
    gain_attn, gain_ffn, persist_k, persist_v, roots = refs[:5]
    held, cast, semaphores = refs[5:5 + total], refs[5 + total:5 + total + casts], refs[5 + total + casts]
    arrive = [pltpu.make_async_copy(sources[k], held[k], semaphores.at[0, k]) for k in range(total)]
    leave = [
        pltpu.make_async_copy(cast[k] if k < casts else held[k], targets[k], semaphores.at[1, k])
        for k in range(total)
    ]
    ahead = total
    for copy in arrive[:ahead]:
        copy.start()
    lines = gain_attn.shape[0]
    heads, many, size = persist_k.shape
    gain_attn[...] = small[0:lines, :]
    gain_ffn[...] = small[lines:2 * lines, :]
    stats = small[2 * lines:2 * lines + 8, :]
    stats = jnp.sqrt(stats / (stats[5:6, :] * (lines * size)))
    for k in range(5):
        roots[k] = stats[k, 0]
    for h in range(heads):
        first = 2 * lines + 8 + h * many
        persist_k[h] = small[first:first + many, :]
        persist_v[h] = small[first + heads * many:first + (heads + 1) * many, :]
    for k in range(total):
        arrive[k].wait()
        if k + ahead < total:
            arrive[k + ahead].start()
        if k < casts:
            cast[k][...] = held[k][...].astype(f32)
        leave[k].start()
    for copy in leave:
        copy.wait()


def finish(sums, rest, small, persist_shape):
    casts, moves = len(sums), len(rest)
    size = small.shape[1]
    lines = (small.shape[0] - 2 * persist_shape[0] * persist_shape[1] - 8) // 2
    anywhere = pl.BlockSpec(memory_space=pl.ANY)
    return pl.pallas_call(
        functools.partial(finish_kernel, casts, moves),
        out_shape=tuple(jax.ShapeDtypeStruct(value.shape, f32) for value in sums)
        + tuple(jax.ShapeDtypeStruct(value.shape, value.dtype) for value in rest)
        + (jax.ShapeDtypeStruct((lines, size), f32),) * 2
        + (jax.ShapeDtypeStruct(persist_shape, f32),) * 2
        + (jax.ShapeDtypeStruct((5,), f32),),
        in_specs=[anywhere] * (casts + moves) + [vmem()],
        out_specs=(anywhere,) * (casts + moves) + (vmem(),) * 4 + (smem(),),
        scratch_shapes=[pltpu.VMEM(value.shape, value.dtype) for value in (*sums, *rest)]
        + [pltpu.VMEM(value.shape, f32) for value in sums]
        + [pltpu.SemaphoreType.DMA((2, casts + moves))],
        compiler_params=pltpu.CompilerParams(vmem_limit_bytes=vmem_limit),
        name="finish",
    )(*sums, *rest, small)


pace = (0, 6, 0, (0, 1) * 8, (0, 0, 0, 0, 0, 0, 0, 1) * 2, None, 0, 3, 2, 1, 3)
layer_limit = 63 << 20


def swap(value, axis, bit):
    count = lax.axis_size(axis)
    return lax.ppermute(value, axis, [(i, i ^ bit) for i in range(count)])


def norm_back(value, scale, gain, upstream):
    weighted = upstream * gain
    return scale * weighted - value * (scale * scale * scale) * jnp.mean(
        weighted * value, axis=-1, keepdims=True
    )


def gather_rows(own):
    far = swap(own, "tensor", 2)
    near = swap(own, "tensor", 1)
    both = swap(far, "tensor", 1)
    return jnp.concatenate([own, near], 0), jnp.concatenate([far, both], 0)


def scatter_rows(near, far):
    rows = near.shape[0] // 2
    far_sum = far[:rows] + swap(far[rows:].astype(bf16), "tensor", 1).astype(f32)
    far_in = swap(far_sum.astype(bf16), "tensor", 2).astype(f32)
    near_in = swap(near[rows:].astype(bf16), "tensor", 1).astype(f32)
    return near[:rows] + near_in + far_in


def mul(left, right):
    return jnp.dot(left, right, preferred_element_type=f32)


def mul_nt(left, right):
    return jnp.einsum("ab,cb->ac", left, right, preferred_element_type=f32)


def mul_tn(left, right):
    return jnp.einsum("ab,ac->bc", left, right, preferred_element_type=f32)


def fits_ring(count, parts, *shapes):
    if count & (count - 1) or parts != 4 or count < 4:
        return False
    return all(rows % (32 * count) == 0 or (rows % 32 == 0 and cols % (128 * count) == 0) for rows, cols in shapes)


def body(
    inputs, cotangent, lengths, gain_attn, w_query, w_key, w_value, w_out, persist_keys, persist_values,
    gain_ffn, w_gate, w_up, w_down, momentum, decay, step_size,
):
    parts = lax.axis_size("tensor")
    count = lax.axis_size("dp")
    rows = inputs.shape[1]
    width = inputs.shape[2]
    half = 2 * rows
    cols = w_query.shape[1]
    size = persist_keys.shape[2]
    place = lax.axis_index("tensor")
    first_row = place * rows
    own_valid = (first_row + jnp.arange(rows, dtype=jnp.int32) < lengths[0]).astype(f32)[:, None]
    places = place.astype(jnp.int32).reshape(1)
    rates = (places, lengths, momentum[0], decay[0], step_size[0])

    if fits_ring(count, parts, (w_down.shape), (width, 3 * cols), (cols, width)):
        *sums, result, input_grad, small = whole_layer(
            lengths, momentum[0].T, decay[0].T, step_size[0].T, inputs[0], cotangent[0], gain_attn[None], gain_ffn[None], persist_keys, persist_values,
            w_query, w_key, w_value, w_out, w_gate.T, w_up.T, w_down, count, parts,
        )
        gate_sum, up_sum, down_sum, query_sum, key_sum, value_sum, out_sum, *rest = finish(
            sums, (result, input_grad), small, persist_keys.shape
        )
        result, input_grad, gain_attn_sum, gain_ffn_sum, persist_k_sum, persist_v_sum, rms_stats = rest
    else:
        resid = inputs[0].astype(f32)
        scale_attn = rows_scale(resid)
        near, far = gather_rows((resid * scale_attn * gain_attn).astype(bf16))
        w_qkv = jnp.concatenate([w_query, w_key, w_value], 1)
        qkv = jnp.concatenate([mul(near, w_qkv).astype(bf16), mul(far, w_qkv).astype(bf16)], 0)
        normed_attn = jnp.concatenate([near, far], 0)
        mixed, log_total, states, grams = attend_and_recall(*rates, qkv, persist_keys, persist_values, parts)
        branch_attn = scatter_rows(mul(mixed[:half], w_out), mul(mixed[half:], w_out))
        middle = resid + branch_attn
        scale_ffn = rows_scale(middle)
        normed_ffn = jnp.concatenate(gather_rows((middle * scale_ffn * gain_ffn).astype(bf16)), 0)

        out_grad = cotangent[0].astype(f32) * own_valid
        out_full = jnp.concatenate(gather_rows(out_grad.astype(bf16)), 0)
        gate = mul(normed_ffn, w_gate)
        up = mul(normed_ffn, w_up)
        sigmoid = jax.nn.sigmoid(gate)
        silu = gate * sigmoid
        hidden = (silu * up).astype(bf16)
        branch_ffn = scatter_rows(mul(hidden[:half], w_down), mul(hidden[half:], w_down))
        result = middle + branch_ffn
        hidden_grad = mul_nt(out_full, w_down)
        gate_grad = (hidden_grad * up * sigmoid * (1.0 + gate * (1.0 - sigmoid))).astype(bf16)
        up_grad = (hidden_grad * silu).astype(bf16)

        def masked(value_in):
            return jnp.sum(own_valid * (value_in * value_in))

        squares = jnp.stack(
            [masked(resid), masked(middle), masked(result), masked(branch_attn), masked(branch_ffn), jnp.sum(own_valid)]
        )
        grad_down = mul_tn(hidden, out_full).astype(bf16)
        grad_gate = mul_tn(gate_grad, normed_ffn).astype(bf16)
        grad_up = mul_tn(up_grad, normed_ffn).astype(bf16)
        normed_ffn_grad = scatter_rows(
            mul_nt(gate_grad[:half], w_gate) + mul_nt(up_grad[:half], w_up),
            mul_nt(gate_grad[half:], w_gate) + mul_nt(up_grad[half:], w_up),
        )
        gain_ffn_part = jnp.sum(normed_ffn_grad * middle * scale_ffn, axis=0)
        middle_grad = out_grad + norm_back(middle, scale_ffn, gain_ffn, normed_ffn_grad)
        middle_full = jnp.concatenate(gather_rows(middle_grad.astype(bf16)), 0)
        mixed_grad = mul_nt(middle_full, w_out).astype(bf16)
        qkv_grad, persist_k_grad, persist_v_grad = attend_and_recall_back(
            *rates, qkv, mixed_grad, persist_keys, persist_values, log_total, states, grams, parts
        )
        normed_attn_grad = scatter_rows(mul_nt(qkv_grad[:half], w_qkv), mul_nt(qkv_grad[half:], w_qkv))
        gain_attn_part = jnp.sum(normed_attn_grad * resid * scale_attn, axis=0)
        input_grad = (middle_grad + norm_back(resid, scale_attn, gain_attn, normed_attn_grad)).astype(bf16)
        gate_sum, up_sum, down_sum, wide, out_sum, persist_sums = lax.psum(
            (grad_gate, grad_up, grad_down, mul_tn(normed_attn, qkv_grad).astype(bf16),
             mul_tn(mixed, middle_full).astype(bf16), jnp.stack([persist_k_grad, persist_v_grad])), "dp"
        )
        query_sum, key_sum, value_sum = wide[:, :cols], wide[:, cols:2 * cols], wide[:, 2 * cols:]
        gains, squares = lax.psum((jnp.concatenate([gain_attn_part, gain_ffn_part]), squares), ("dp", "tensor"))
        gain_attn_sum, gain_ffn_sum = gains[:width], gains[width:]
        persist_k_sum, persist_v_sum = persist_sums[0], persist_sums[1]
        rms_stats = jnp.sqrt(squares[:5] / (squares[5] * width))
    return (
        result.astype(bf16)[None],
        input_grad[None],
        gain_attn_sum.reshape(-1),
        query_sum.astype(f32),
        key_sum.astype(f32),
        value_sum.astype(f32),
        out_sum.astype(f32),
        persist_k_sum,
        persist_v_sum,
        gain_ffn_sum.reshape(-1),
        gate_sum.astype(f32).T,
        up_sum.astype(f32).T,
        down_sum.astype(f32),
        rms_stats,
    )


def solution(mesh):
    in_specs = (
        P("dp", "tensor", None),
        P("dp", "tensor", None),
        P("dp"),
        P(),
        P(None, "tensor"),
        P(None, "tensor"),
        P(None, "tensor"),
        P("tensor", None),
        P("tensor", None, None),
        P("tensor", None, None),
        P(),
        P(None, "tensor"),
        P(None, "tensor"),
        P("tensor", None),
        P("dp", None, "tensor"),
        P("dp", None, "tensor"),
        P("dp", None, "tensor"),
    )
    out_specs = (
        P("dp", "tensor", None),
        P("dp", "tensor", None),
        P(),
        P(None, "tensor"),
        P(None, "tensor"),
        P(None, "tensor"),
        P("tensor", None),
        P("tensor", None, None),
        P("tensor", None, None),
        P(),
        P(None, "tensor"),
        P(None, "tensor"),
        P("tensor", None),
        P(),
    )
    return jax.shard_map(body, mesh=mesh, in_specs=in_specs, out_specs=out_specs, check_vma=False)
```
